32 devices in a mesh: section: 2 (over y), dp: 16 (over z, x, core).
Axes of the slice: x: 2, y: 2, z: 4, core: 2. Of those that a mesh axis runs over, the one named last changes fastest.
Arguments:
- inputs: bfloat16 [8192, 1024], P('dp'), may hold values from -6 to 6
- out_grad: bfloat16 [8192, 1024], P('dp'), may hold values from -6 to 6
- doc_ids: int32 [32, 256], P('dp'), may hold values from 0 to 3, never falling along the last dimension, each value on 1 to 128 neighbouring positions
- row_live: int32 [32], P('dp'), may hold values from 64 to 256, as said below
- pre_gain: float32 [2, 1024], P('section'), may hold values from 0.5 to 1.5
- mlp_gain: float32 [2, 1024], P('section'), may hold values from 0.5 to 1.5
- mixer_gain: float32 [2, 1536], P('section'), may hold values from 0.5 to 1.5
- conv_weight: float32 [2, 4, 1792], P('section'), may hold values from -0.5 to 0.5
- conv_bias: float32 [2, 1792], P('section'), may hold values from -0.5 to 0.5
- step_bias: float32 [2, 24], P('section'), may hold values from -4 to -1
- decay_log: float32 [2, 24], P('section'), may hold values from -4 to 1
- skip_scale: float32 [2, 24], P('section'), may hold values from 0.5 to 1.5
- mixer_in_weight: bfloat16 [2, 1024, 3352], P('section', 'dp'), may hold values from -0.1875 to 0.1875
- mixer_out_weight: bfloat16 [2, 1536, 1024], P('section', None, 'dp'), may hold values from -0.15625 to 0.15625
- query_weight: bfloat16 [2, 1024, 512], P('section', 'dp'), may hold values from -0.1875 to 0.1875
- key_weight: bfloat16 [2, 1024, 128], P('section', 'dp'), may hold values from -0.1875 to 0.1875
- value_weight: bfloat16 [2, 1024, 128], P('section', 'dp'), may hold values from -0.1875 to 0.1875
- attend_weight: bfloat16 [2, 512, 1024], P('section', None, 'dp'), may hold values from -0.75 to 0.75
- gate_up_weight: bfloat16 [2, 1024, 4096], P('section', 'dp'), may hold values from -0.1875 to 0.1875
- down_weight: bfloat16 [2, 2048, 1024], P('section', None, 'dp'), may hold values from -0.125 to 0.125
Outputs:
- section_out: bfloat16 [2, 8192, 1024], P('section', 'dp')
- section_in_grad: float32 [2, 8192, 1024], P('section', 'dp')
- pre_gain_grad: float32 [2, 1024], P('section')
- mlp_gain_grad: float32 [2, 1024], P('section')
- mixer_gain_grad: float32 [2, 1536], P('section')
- conv_weight_grad: float32 [2, 4, 1792], P('section')
- conv_bias_grad: float32 [2, 1792], P('section')
- step_bias_grad: float32 [2, 24], P('section')
- decay_log_grad: float32 [2, 24], P('section')
- skip_scale_grad: float32 [2, 24], P('section')
- mixer_in_grad: float32 [2, 1024, 3352], P('section', 'dp')
- mixer_out_grad: float32 [2, 1536, 1024], P('section', None, 'dp')
- query_grad: float32 [2, 1024, 512], P('section', 'dp')
- key_grad: float32 [2, 1024, 128], P('section', 'dp')
- value_grad: float32 [2, 1024, 128], P('section', 'dp')
- attend_grad: float32 [2, 512, 1024], P('section', None, 'dp')
- gate_up_grad: float32 [2, 1024, 4096], P('section', 'dp')
- down_grad: float32 [2, 2048, 1024], P('section', None, 'dp')
The draws below stay inside these ranges and needn't reach their ends.
Inputs may be any that keep to these rules, and one draw needn't show every extreme that they name: `doc_ids`: each row of 256 positions holds 4 documents in order, numbered from 0, each at most 128 positions long. The loss counts the first row_live positions of each row; some row is counted in full.
All inputs are finite; a program needn't handle non-finite values.
Results may differ from the reference program's by a relative error of at most 0.02.
Values may be sent and summed in bfloat16 or wider, within the bound.
No kernel may reach another device: no remote copies, remote signals or barrier semaphores. Data moves between devices by JAX's collectives and lax.ppermute only.
A program may use at most 320 MiB of HBM per device.

```python
import math
import jax
import jax.numpy as jnp
import numpy as np
from jax import lax

D = 1024
FF = 2048
MH = 24
MP = 64
NS = 128
AH = 8
KVH = 2
HD = 64
CONV = 4
MB = 2
TOK_MB = 256
E = 1536
CH = 1792
PROJ = 3352
ROWS = 32
TOKENS = 8192
N_DP = 16


def draw_row_live(key, part):
    key = jax.random.fold_in(key, 11)
    key_counts, key_full = jax.random.split(key)
    counts = jax.random.randint(key_counts, (ROWS,), TOK_MB // 4, TOK_MB + 1)
    full_row = jax.random.randint(key_full, (), 0, ROWS)
    return jnp.where(jnp.arange(ROWS) == full_row, TOK_MB, counts).astype(jnp.int32)


def level_of(stream_key, shape, shards, low, top_value):
    factor_of, own = 1.0, jax.random.fold_in(stream_key, 6)
    for position, shards_of in shards:
        draws = jnp.exp(jax.random.uniform(jax.random.fold_in(own, position), (shards_of,), jnp.float32, low / len(shards), top_value / len(shards)))
        factor_of = factor_of * jnp.repeat(draws, shape[position] // shards_of).reshape([-1 if axis == position else 1 for axis in range(len(shape))])
    return factor_of


def split_up(amount, total, reach, skew):
    loads = [(1 << 20) // math.isqrt(rank ** skew) + 1 for rank in range(2, amount + 1)]
    rest, given = total - reach - (amount - 1), [1] * (amount - 1)
    while rest > 0:
        movable = [i for i in range(amount - 1) if given[i] < reach]
        pool, remaining = sum([loads[i] for i in movable]), rest
        for i in movable:
            addition = min(reach - given[i], max(1, remaining * loads[i] // pool), rest)
            given[i] = given[i] + addition
            rest = rest - addition
    return np.array([reach] + given)


def uneven(own_key, count, total, limit, slope):
    if count == 2:
        one = jax.random.randint(own_key, (), max(1, total - limit), min(limit, total - 1) + 1)
        return jnp.stack([one, total - one])
    lengths = jnp.asarray(split_up(count, total, limit, slope), jnp.int32)
    couples = (count - 1) // 2
    giver, sink = lengths[1:1 + 2 * couples:2], lengths[2:2 + 2 * couples:2]
    margin = jnp.minimum(giver - 1, limit - sink)
    moved = jax.random.randint(jax.random.fold_in(own_key, 1), (couples,), 0, 1 << 20) % (margin + 1)
    lengths = lengths.at[1:1 + 2 * couples:2].set(giver - moved).at[2:2 + 2 * couples:2].set(sink + moved)
    return lengths[jax.random.permutation(jax.random.fold_in(own_key, 2), count)]


def gaussian(stream_key, dims, width, limit, cuts=(), held_as=jnp.bfloat16):
    values = width * jax.random.normal(stream_key, dims, jnp.float32)
    if cuts:
        values = values * level_of(stream_key, dims, cuts, -0.22, 0.18)
    return jnp.clip(values, -limit, limit).astype(held_as)


def setup_inputs(seed: int = 0) -> dict:
    arg_keys = jax.random.split(jax.random.key(seed), 21)
    return {
        "inputs": gaussian(arg_keys[0], (TOKENS, D), 1.0, 6.0, ((0, 16),)),
        "out_grad": gaussian(arg_keys[1], (TOKENS, D), 1.0, 6.0, ((0, 16),)),
        "doc_ids": jax.vmap(lambda own: jnp.searchsorted(jnp.cumsum(uneven(own, 4, TOK_MB, TOK_MB // 2, 0)), jnp.arange(TOK_MB), side="right"))(jax.random.split(arg_keys[2], ROWS)).reshape((ROWS, TOK_MB)).astype(jnp.int32),
        "row_live": draw_row_live(jax.random.fold_in(arg_keys[20], 71), 0),
        "pre_gain": jnp.clip(1.0 + 0.1 * jax.random.normal(arg_keys[4], (2, D), jnp.float32), 0.5, 1.5),
        "mlp_gain": jnp.clip(1.0 + 0.1 * jax.random.normal(arg_keys[5], (2, D), jnp.float32), 0.5, 1.5),
        "mixer_gain": jnp.clip(1.0 + 0.1 * jax.random.normal(arg_keys[6], (2, E), jnp.float32), 0.5, 1.5),
        "conv_weight": jnp.clip(jax.random.uniform(arg_keys[7], (2, CONV, CH), jnp.float32, -0.5, 0.5) * level_of(arg_keys[7], (2, CONV, CH), ((0, 2),), -0.4, 0.0), -0.5, 0.5),
        "conv_bias": jnp.clip(jax.random.uniform(arg_keys[8], (2, CH), jnp.float32, -0.5, 0.5) * level_of(arg_keys[8], (2, CH), ((0, 2),), -0.4, 0.0), -0.5, 0.5),
        "step_bias": jnp.clip(-4.0 + 3.0 * jax.random.uniform(arg_keys[9], (2, MH), jnp.float32) ** level_of(arg_keys[9], (2, MH), ((0, 2),), -0.2, 0.2), -4.0, -1.0),
        "decay_log": jnp.clip(-4.0 + 5.0 * jax.random.uniform(arg_keys[10], (2, MH), jnp.float32) ** level_of(arg_keys[10], (2, MH), ((0, 2),), -0.2, 0.2), -4.0, 1.0),
        "skip_scale": jnp.clip(0.5 + 1.0 * jax.random.uniform(arg_keys[11], (2, MH), jnp.float32) ** level_of(arg_keys[11], (2, MH), ((0, 2),), -0.2, 0.2), 0.5, 1.5),
        "mixer_in_weight": gaussian(arg_keys[12], (2, D, PROJ), D ** -0.5, 0.1875, ((0, 2), (1, 16))),
        "mixer_out_weight": gaussian(arg_keys[13], (2, E, D), E ** -0.5, 0.15625, ((0, 2), (2, 16))),
        "query_weight": gaussian(arg_keys[14], (2, D, AH * HD), D ** -0.5, 0.1875, ((0, 2), (1, 16))),
        "key_weight": gaussian(arg_keys[15], (2, D, KVH * HD), D ** -0.5, 0.1875, ((0, 2), (1, 16))),
        "value_weight": gaussian(arg_keys[16], (2, D, KVH * HD), D ** -0.5, 0.1875, ((0, 2), (1, 16))),
        "attend_weight": gaussian(arg_keys[17], (2, AH * HD, D), (AH * HD // 8) ** -0.5, 0.75, ((0, 2), (2, 16))),
        "gate_up_weight": gaussian(arg_keys[18], (2, D, 2 * FF), D ** -0.5, 0.1875, ((0, 2), (1, 16))),
        "down_weight": gaussian(arg_keys[19], (2, FF, D), FF ** -0.5, 0.125, ((0, 2), (2, 16))),
    }


highest = lax.Precision.HIGHEST
epsilon = 1e-05
rope_base = 100000000000.0

@jax.custom_vjp
def low(v):
    return lax.optimization_barrier(v.astype(jnp.bfloat16)).astype(jnp.float32)

@jax.custom_vjp
def low_back(v):
    return v

def low_keep(v):
    return (low(v), None)

def low_pass(kept, grad):
    return (grad,)

def back_keep(v):
    return (v, None)

def back_low(kept, grad):
    return (low(grad),)
low.defvjp(low_keep, low_pass)
low_back.defvjp(back_keep, back_low)

def rms_scale(values, scale_gain):
    return values * lax.rsqrt(lax.optimization_barrier(jnp.mean(values * values, axis=-1, keepdims=True)) + epsilon) * scale_gain

def doc_layout(doc_row):
    positions = jnp.arange(doc_row.shape[0], dtype=jnp.int32)
    earlier = lax.optimization_barrier(jnp.sum((doc_row[None, :] < doc_row[:, None]).astype(jnp.int32), axis=1))
    places = positions - earlier
    allowed = (positions[:, None] >= positions[None, :]) & (doc_row[:, None] == doc_row[None, :])
    return (places, allowed)

def conv_mix(channels, doc_row, conv_weight, conv_bias):
    tap_count = conv_weight.shape[0]
    row_count = channels.shape[0]
    summed = conv_bias[None, :] + conv_weight[tap_count - 1][None, :] * channels
    for offset in range(1, tap_count):
        shifted = jnp.pad(channels, ((offset, 0), (0, 0)))[:row_count]
        earlier_doc = jnp.pad(doc_row, (offset, 0), constant_values=-1)[:row_count]
        same_doc = (earlier_doc == doc_row)[:, None]
        summed = summed + conv_weight[tap_count - 1 - offset][None, :] * jnp.where(same_doc, shifted, 0.0)
    return jax.nn.silu(summed)

def mixer_core(projected, doc_row, allowed, conv_weight, conv_bias, step_bias, decay_log, skip_scale, mixer_gain):
    row_count = projected.shape[0]
    gate_part = projected[:, :E]
    channels = conv_mix(projected[:, E:2 * E + 2 * NS], doc_row, conv_weight, conv_bias)
    heads_in = channels[:, :E].reshape(row_count, MH, MP)
    inward = channels[:, E:E + NS]
    outward = channels[:, E + NS:]
    step_size = jax.nn.softplus(projected[:, 2 * E + 2 * NS:] + step_bias)
    log_rates = -step_size * jnp.exp(decay_log)
    totals = jnp.cumsum(log_rates, axis=0)
    pair_dots = jnp.dot(outward, inward.T, precision=highest)
    masked = allowed[:, :, None]
    decays = jnp.where(masked, jnp.exp(jnp.where(masked, totals[:, None, :] - totals[None, :, :], 0.0)), 0.0)
    mixing = pair_dots[:, :, None] * decays * step_size[None, :, :]
    result = jnp.einsum('tsh,shp->thp', mixing, heads_in, precision=highest) + skip_scale[None, :, None] * heads_in
    gated_rows = result.reshape(row_count, E) * jax.nn.silu(gate_part)
    return rms_scale(gated_rows, mixer_gain)

def rotate(vectors, places):
    half_dim = vectors.shape[-1] // 2
    inverse_freq = rope_base ** (-jnp.arange(half_dim, dtype=jnp.float32) / half_dim)
    angles = places.astype(jnp.float32)[:, None] * inverse_freq[None, :]
    cosine = jnp.cos(angles)[:, None, :]
    sine_part = jnp.sin(angles)[:, None, :]
    first_half = vectors[..., :half_dim]
    second_half = vectors[..., half_dim:]
    return jnp.concatenate([first_half * cosine - second_half * sine_part, second_half * cosine + first_half * sine_part], axis=-1)

def attend_core(query_rows, key_rows, value_rows, places, allowed):
    row_count = query_rows.shape[0]
    per_group = AH // KVH
    queries = rotate(query_rows.reshape(row_count, AH, HD), places).reshape(row_count, KVH, per_group, HD)
    key_heads = rotate(key_rows.reshape(row_count, KVH, HD), places)
    value_heads = value_rows.reshape(row_count, KVH, HD)
    scores = jnp.einsum('tkgd,skd->kgts', queries, key_heads, precision=highest) * (1.0 / math.sqrt(HD))
    scores = jnp.where(allowed[None, None], scores, -1e+30)
    attention = jax.nn.softmax(scores, axis=-1)
    blended = jnp.einsum('kgts,skd->tkgd', attention, value_heads, precision=highest)
    return blended.reshape(row_count, AH * HD)

def swiglu(gate_up):
    return jax.nn.silu(gate_up[:, :FF]) * gate_up[:, FF:]

def matmul(left, right):
    return jnp.dot(left, right, precision=highest)

def layer(hidden, doc_row, places, allowed, params):
    pre_gain, mlp_gain, mixer_gain, conv_weight, conv_bias, step_bias, decay_log, skip_scale, mixer_in_weight, mixer_out_weight, query_weight, key_weight, value_weight, attend_weight, gate_up_weight, down_weight = params
    normed = low(rms_scale(hidden, pre_gain))
    projected = low_back(matmul(normed, mixer_in_weight))
    query_rows = low_back(matmul(normed, query_weight))
    key_rows = low_back(matmul(normed, key_weight))
    value_rows = low_back(matmul(normed, value_weight))
    mixed_low = low(mixer_core(projected, doc_row, allowed, conv_weight, conv_bias, step_bias, decay_log, skip_scale, mixer_gain))
    attended = low(attend_core(query_rows, key_rows, value_rows, places, allowed))
    middle = hidden + low_back(matmul(mixed_low, mixer_out_weight)) + low_back(matmul(attended, attend_weight))
    normed_two = low(rms_scale(middle, mlp_gain))
    gate_up = low_back(matmul(normed_two, gate_up_weight))
    activated = low(swiglu(gate_up))
    return middle + low_back(matmul(activated, down_weight))

def reference(inputs, out_grad, doc_ids, row_live, pre_gain, mlp_gain, mixer_gain, conv_weight, conv_bias, step_bias, decay_log, skip_scale, mixer_in_weight, mixer_out_weight, query_weight, key_weight, value_weight, attend_weight, gate_up_weight, down_weight):
    params = tuple((parameter.astype(jnp.float32) for parameter in (pre_gain, mlp_gain, mixer_gain, conv_weight, conv_bias, step_bias, decay_log, skip_scale, mixer_in_weight, mixer_out_weight, query_weight, key_weight, value_weight, attend_weight, gate_up_weight, down_weight)))
    params_zero = tuple((parameter[0] for parameter in params))
    params_one = tuple((parameter[1] for parameter in params))
    starts = inputs.astype(jnp.float32).reshape(N_DP, MB, TOK_MB, D)
    live_all = row_live.reshape(N_DP, MB)
    live_mask = (jnp.arange(TOK_MB, dtype=jnp.int32)[None, None, :] < live_all[:, :, None]).astype(jnp.float32)
    cotangents = out_grad.astype(jnp.float32).reshape(N_DP, MB, TOK_MB, D) * live_mask[..., None]
    docs_all = doc_ids.reshape(N_DP, MB, TOK_MB)

    def group_step(running, batch_in):
        start_rows, cotangent, doc_rows = batch_in
        layouts = [doc_layout(doc_rows[row_index]) for row_index in range(MB)]

        def forward(begin_rows, probe_in, first_params, second_params):
            outputs = []
            middles = []
            for row_index in range(MB):
                places, allowed = layouts[row_index]
                handed = low_back(low(layer(begin_rows[row_index], doc_rows[row_index], places, allowed, first_params))) + probe_in[row_index]
                outputs.append(layer(handed, doc_rows[row_index], places, allowed, second_params))
                middles.append(handed)
            return (jnp.stack(outputs), jnp.stack(middles))
        probe_in = jnp.zeros_like(start_rows)
        result, pullback, middles = jax.vjp(forward, start_rows, probe_in, params_zero, params_one, has_aux=True)
        start_grad, probe_grad, first_grads, second_grads = pullback(cotangent)
        running = jax.tree.map(jnp.add, running, (first_grads, second_grads))
        return (running, (middles.astype(jnp.bfloat16), result.astype(jnp.bfloat16), start_grad, probe_grad))
    empty_sums = jax.tree.map(jnp.zeros_like, (params_zero, params_one))
    sums_both, stacked = lax.scan(group_step, empty_sums, (starts, cotangents, docs_all))
    middles_all, results_all, start_grads, probe_grads = stacked
    section_out = jnp.stack([middles_all.reshape(TOKENS, D), results_all.reshape(TOKENS, D)])
    section_in_grad = jnp.stack([start_grads.reshape(TOKENS, D), probe_grads.reshape(TOKENS, D)])
    grads = [jnp.stack([first_one, second_one]) for first_one, second_one in zip(sums_both[0], sums_both[1])]
    return (section_out, section_in_grad, grads[0], grads[1], grads[2], grads[3], grads[4], grads[5], grads[6], grads[7], grads[8], grads[9], grads[10], grads[11], grads[12], grads[13], grads[14], grads[15])
```

```python
import functools
import math

import jax
import jax.numpy as jnp
from jax import lax
from jax.experimental import pallas as pl
from jax.experimental.pallas import tpu as pltpu
from jax.sharding import PartitionSpec as P

D = 1024
FF = 2048
MH = 24
MP = 64
NS = 128
AH = 8
KVH = 2
HD = 64
MB = 2
TOK = 256
E = 1536
CH = 1792
HALF = TOK // 2
PAIRS = MH // 2
LANES = 128

AT_W = E
AT_Q = E + CH
AT_K = AT_Q + AH * HD
AT_V = AT_K + KVH * HD
AT_DT = AT_V + KVH * HD
WIDE_A = AT_DT + LANES
MIXED = E + AH * HD
AT_GU = MIXED
AT_DN = AT_GU + 2 * FF
WIDE_B = AT_DN + FF

highest = lax.Precision.HIGHEST
epsilon = 1e-05
rope_base = 100000000000.0
bf16 = jnp.bfloat16
f32 = jnp.float32


def dot_nn(left, right):
    return lax.dot_general(left, right, (((1,), (0,)), ((), ())), preferred_element_type=f32)


def dot_nt(left, right):
    return lax.dot_general(left, right, (((1,), (1,)), ((), ())), preferred_element_type=f32)


def dot_tn(left, right):
    return lax.dot_general(left, right, (((0,), (0,)), ((), ())), preferred_element_type=f32)


def dot_exact(left, right):
    return lax.dot_general(
        left, right, (((1,), (0,)), ((), ())), precision=highest, preferred_element_type=f32
    )


def softplus(value):
    return jnp.maximum(value, 0.0) + jnp.log1p(jnp.exp(-jnp.abs(value)))


def lane_low(rows):
    return lax.broadcasted_iota(jnp.int32, (rows, LANES), 1) < HD


def rope_halves(rows):
    return (lax.broadcasted_iota(jnp.int32, (rows, LANES), 1) & (HD - 1)) < HD // 2


def rope_turn(tile, cosine, sine):
    swapped = jnp.where(
        rope_halves(tile.shape[0]),
        -pltpu.roll(tile, LANES - HD // 2, 1),
        pltpu.roll(tile, HD // 2, 1),
    )
    return tile * cosine + swapped * sine


def rope_back(tile, cosine, sine):
    swapped = jnp.where(
        rope_halves(tile.shape[0]),
        pltpu.roll(tile, LANES - HD // 2, 1),
        -pltpu.roll(tile, HD // 2, 1),
    )
    return tile * cosine + swapped * sine


def both_halves(tile):
    swapped = pltpu.roll(tile, HD, 1)
    low = lane_low(tile.shape[0])
    return (jnp.where(low, tile, swapped), jnp.where(low, swapped, tile))


def tile_at(index):
    return pl.ds(pl.multiple_of(index * LANES, LANES), LANES)


def tile_from(start, index):
    return pl.ds(pl.multiple_of(start + index * LANES, LANES), LANES)


def allowed_pairs(doc_col_ref, doc_row_ref):
    later = lax.broadcasted_iota(jnp.int32, (TOK, TOK), 0)
    early = lax.broadcasted_iota(jnp.int32, (TOK, TOK), 1)
    same = doc_col_ref[:, 0:1] == doc_row_ref[0:1, :]
    return (later >= early) & same


def core_forward_kernel(
    pa_ref, rope_ref, mask_ref, doc_col_ref, doc_row_ref, taps_ref, head_ref, wide_ref,
    xb_ref, pre_ref, yns_ref,
    conv_s, cb_s, sum_s,
):
    def conv_tile(index, carry):
        rows = pa_ref[:, tile_from(AT_W, index)]
        at = tile_at(index)
        total = taps_ref[4:5, at] + taps_ref[3:4, at] * rows
        for shift in (1, 2, 3):
            moved = mask_ref[:, (shift - 1) * LANES : shift * LANES] * pltpu.roll(rows, shift, 0)
            total = total + taps_ref[3 - shift : 4 - shift, at] * moved
        pre_ref[:, at] = total
        conv_s[:, at] = total * jax.nn.sigmoid(total)
        return carry

    lax.fori_loop(0, CH // LANES, conv_tile, 0)

    allowed = allowed_pairs(doc_col_ref, doc_row_ref)
    steps = softplus(pa_ref[:, AT_DT:] + head_ref[0:1, :])
    rates = -steps * head_ref[1:2, :]
    totals = dot_exact(jnp.where(allowed, 1.0, 0.0), rates)
    totals_t = totals.T
    inward = conv_s[:, E : E + NS].astype(bf16)
    outward = conv_s[:, E + NS :].astype(bf16)
    cb_s[...] = jnp.where(allowed, dot_nt(outward, inward), 0.0)
    low = lane_low(TOK)
    for pair in range(PAIRS):
        lanes = slice(pair * LANES, (pair + 1) * LANES)
        first = 2 * pair
        step_pair = jnp.where(low, steps[:, first : first + 1], steps[:, first + 1 : first + 2])
        scaled = (conv_s[:, lanes] * step_pair).astype(bf16)
        halves = []
        for head in (first, first + 1):
            col = totals[:, head : head + 1]
            row = totals_t[head : head + 1, :]
            top = jnp.exp(jnp.minimum(col[:HALF] - row[:, :HALF], 0.0)) * cb_s[:HALF, :HALF]
            end = jnp.exp(jnp.minimum(col[HALF:] - row, 0.0)) * cb_s[HALF:, :]
            halves.append(
                jnp.concatenate(
                    [dot_nn(top.astype(bf16), scaled[:HALF]), dot_nn(end.astype(bf16), scaled)],
                    axis=0,
                )
            )
        yns_ref[:, lanes] = jnp.where(low, halves[0], halves[1])

    sum_s[...] = jnp.zeros((TOK, LANES), f32)

    def gate_tile(index, carry):
        at = tile_at(index)
        gate = pa_ref[:, at]
        rows = yns_ref[:, at] + wide_ref[0:1, at] * conv_s[:, at]
        gated = rows * (gate * jax.nn.sigmoid(gate))
        sum_s[...] += gated * gated
        conv_s[:, at] = gated
        return carry

    lax.fori_loop(0, E // LANES, gate_tile, 0)
    scale = lax.rsqrt(jnp.sum(sum_s[...], axis=1, keepdims=True) * (1.0 / E) + epsilon)

    def norm_tile(index, carry):
        at = tile_at(index)
        xb_ref[:, at] = (conv_s[:, at] * scale * wide_ref[1:2, at]).astype(bf16)
        return carry

    lax.fori_loop(0, E // LANES, norm_tile, 0)

    cosine = rope_ref[:, :LANES]
    sine = rope_ref[:, LANES:]
    keys = both_halves(rope_turn(pa_ref[:, AT_K:AT_V], cosine, sine))
    values = both_halves(pa_ref[:, AT_V:AT_DT])
    keys = tuple(part.astype(bf16) for part in keys)
    values = tuple(part.astype(bf16) for part in values)
    for pair in range(AH // 2):
        group = pair // (AH // (2 * KVH))
        at = AT_Q + pair * LANES
        turned = rope_turn(pa_ref[:, at : at + LANES], cosine, sine) * (1.0 / math.sqrt(HD))
        halves = []
        for side in range(2):
            chosen = low if side == 0 else jnp.logical_not(low)
            query = jnp.where(chosen, turned, 0.0).astype(bf16)
            parts = []
            for rows, cols in ((slice(0, HALF), HALF), (slice(HALF, TOK), TOK)):
                scores = dot_nt(query[rows], keys[group][:cols])
                scores = jnp.where(allowed[rows, :cols], scores, -1e30)
                top = jnp.max(scores, axis=1, keepdims=True)
                weights = jnp.exp(scores - top)
                share = 1.0 / jnp.sum(weights, axis=1, keepdims=True)
                parts.append(dot_nn(weights.astype(bf16), values[group][:cols]) * share)
            halves.append(jnp.concatenate(parts, axis=0))
        out = jnp.where(low, halves[0], halves[1])
        xb_ref[:, E + pair * LANES : E + (pair + 1) * LANES] = out.astype(bf16)


def silu_slope(value, gate):
    return gate * (1.0 + value * (1.0 - gate))


def core_backward_kernel(
    pick_ref,
    pa_ref, pre_ref, yns_ref, dxb_ref, rope_ref, mask_ref, doc_col_ref, doc_row_ref,
    taps_ref, head_ref, wide_ref,
    pg_ref, small_ref,
    x_s, dx_s, dyb_s, cbt_s, dcbt_s, sum_s, ssum_s,
):
    small_ref[...] = jnp.zeros_like(small_ref)
    sum_s[...] = jnp.zeros((TOK, LANES), f32)
    ssum_s[...] = jnp.zeros((TOK, LANES), f32)

    def start_tile(index, carry):
        at = tile_at(index)
        pre = pre_ref[:, at]
        heads_in = pre * jax.nn.sigmoid(pre)
        x_s[:, at] = heads_in
        gate = pa_ref[:, at]
        rows = yns_ref[:, at] + wide_ref[0:1, at] * heads_in
        gated = rows * (gate * jax.nn.sigmoid(gate))
        sum_s[...] += gated * gated
        ssum_s[...] += dxb_ref[:, at] * wide_ref[1:2, at] * gated
        return carry

    lax.fori_loop(0, E // LANES, start_tile, 0)
    scale = lax.rsqrt(jnp.sum(sum_s[...], axis=1, keepdims=True) * (1.0 / E) + epsilon)
    pull = jnp.sum(ssum_s[...], axis=1, keepdims=True) * (1.0 / E) * scale * scale * scale

    def gate_tile(index, carry):
        at = tile_at(index)
        heads_in = x_s[:, at]
        skip = wide_ref[0:1, at]
        gate = pa_ref[:, at]
        opened = jax.nn.sigmoid(gate)
        rows = yns_ref[:, at] + skip * heads_in
        gated = rows * (gate * opened)
        arrived = dxb_ref[:, at]
        d_gated = scale * (arrived * wide_ref[1:2, at]) - gated * pull
        small_ref[5:6, at] = jnp.sum(arrived * gated * scale, axis=0, keepdims=True)
        d_rows = d_gated * (gate * opened)
        pg_ref[:, at] = (d_gated * rows * silu_slope(gate, opened)).astype(bf16)
        small_ref[6:7, at] = jnp.sum(d_rows * heads_in, axis=0, keepdims=True)
        dyb_s[:, at] = d_rows.astype(bf16)
        dx_s[:, at] = skip * d_rows
        return carry

    lax.fori_loop(0, E // LANES, gate_tile, 0)

    def state_tile(index, carry):
        at = tile_from(E, index)
        pre = pre_ref[:, at]
        x_s[:, at] = pre * jax.nn.sigmoid(pre)
        return carry

    lax.fori_loop(0, 2, state_tile, 0)

    later = lax.broadcasted_iota(jnp.int32, (TOK, TOK), 1)
    early = lax.broadcasted_iota(jnp.int32, (TOK, TOK), 0)
    allowed_t = (later >= early) & (doc_col_ref[:, 0:1] == doc_row_ref[0:1, :])
    allowed = allowed_pairs(doc_col_ref, doc_row_ref)
    raw = pa_ref[:, AT_DT:] + head_ref[0:1, :]
    steps = softplus(raw)
    decay = head_ref[1:2, :]
    rates = -steps * decay
    totals = dot_exact(jnp.where(allowed, 1.0, 0.0), rates)
    totals_t = totals.T
    inward = x_s[:, E : E + NS].astype(bf16)
    outward = x_s[:, E + NS :].astype(bf16)
    cbt_s[...] = jnp.where(allowed_t, dot_nt(inward, outward), 0.0)
    dcbt_s[...] = jnp.zeros((TOK, TOK), f32)
    low = lane_low(TOK)
    spread_row = lax.broadcasted_iota(jnp.int32, (LANES, LANES), 0) >= HD
    spread_col = lax.broadcasted_iota(jnp.int32, (LANES, LANES), 1)
    sum_s[...] = jnp.zeros((TOK, LANES), f32)
    ssum_s[...] = jnp.zeros((TOK, LANES), f32)
    for pair in range(PAIRS):
        lanes = slice(pair * LANES, (pair + 1) * LANES)
        first = 2 * pair
        step_pair = jnp.where(low, steps[:, first : first + 1], steps[:, first + 1 : first + 2])
        heads_in = x_s[:, lanes]
        scaled = (heads_in * step_pair).astype(bf16)
        d_rows = dyb_s[:, lanes]
        halves = []
        for side, head in enumerate((first, first + 1)):
            chosen = low if side == 0 else jnp.logical_not(low)
            own = jnp.where(chosen, scaled, jnp.zeros_like(scaled))
            col = totals[:, head : head + 1]
            row = totals_t[head : head + 1, :]
            top = jnp.exp(jnp.minimum(row - col[:HALF], 0.0))
            end = jnp.exp(jnp.minimum(row[:, HALF:] - col[HALF:], 0.0))
            top_mix = (top * cbt_s[:HALF, :]).astype(bf16)
            end_mix = (end * cbt_s[HALF:, HALF:]).astype(bf16)
            dcbt_s[:HALF, :] += dot_nt(own[:HALF], d_rows) * top
            dcbt_s[HALF:, HALF:] += dot_nt(own[HALF:], d_rows[HALF:]) * end
            halves.append(
                jnp.concatenate(
                    [dot_nn(top_mix, d_rows), dot_nn(end_mix, d_rows[HALF:])], axis=0
                )
            )
        d_scaled = jnp.where(low, halves[0], halves[1])
        dx_s[:, lanes] += d_scaled * step_pair
        spread = (spread_col == jnp.where(spread_row, first + 1, first)).astype(bf16)
        for value, into in (
            (d_scaled * heads_in, sum_s),
            (d_rows.astype(f32) * yns_ref[:, lanes] - scaled.astype(f32) * d_scaled, ssum_s),
        ):
            coarse = value.astype(bf16)
            fine = (value - coarse.astype(f32)).astype(bf16)
            into[...] += dot_nn(coarse, spread) + dot_nn(fine, spread)

    d_rates = dot_exact(jnp.where(allowed_t, 1.0, 0.0), ssum_s[...])
    d_steps = sum_s[...] - decay * d_rates
    d_raw = d_steps * jax.nn.sigmoid(raw)
    pg_ref[:, AT_DT:] = d_raw.astype(bf16)
    small_ref[7:8, :LANES] = jnp.sum(d_raw, axis=0, keepdims=True)
    small_ref[7:8, LANES : 2 * LANES] = jnp.sum(d_rates * rates, axis=0, keepdims=True)
    d_pairs = jnp.where(allowed_t, dcbt_s[...], 0.0).astype(bf16)
    dx_s[:, E : E + NS] = dot_nn(d_pairs, outward)
    dx_s[:, E + NS :] = dot_tn(d_pairs, inward)

    def conv_tile(index, carry):
        at = tile_at(index)
        pre = pre_ref[:, at]
        d_pre = dx_s[:, at] * silu_slope(pre, jax.nn.sigmoid(pre))
        rows = pa_ref[:, tile_from(AT_W, index)]
        small_ref[4:5, at] = jnp.sum(d_pre, axis=0, keepdims=True)
        small_ref[3:4, at] = jnp.sum(d_pre * rows, axis=0, keepdims=True)
        back = taps_ref[3:4, at] * d_pre
        for shift in (1, 2, 3):
            held = mask_ref[:, (shift - 1) * LANES : shift * LANES] * d_pre
            small_ref[3 - shift : 4 - shift, at] = jnp.sum(
                held * pltpu.roll(rows, shift, 0), axis=0, keepdims=True
            )
            back = back + taps_ref[3 - shift : 4 - shift, at] * pltpu.roll(held, TOK - shift, 0)
        pg_ref[:, tile_from(AT_W, index)] = back.astype(bf16)
        return carry

    lax.fori_loop(0, CH // LANES, conv_tile, 0)

    cosine = rope_ref[:, :LANES]
    sine = rope_ref[:, LANES:]
    keys = both_halves(rope_turn(pa_ref[:, AT_K:AT_V], cosine, sine))
    values = both_halves(pa_ref[:, AT_V:AT_DT])
    keys = tuple(part.astype(bf16) for part in keys)
    values = tuple(part.astype(bf16) for part in values)
    root = 1.0 / math.sqrt(HD)
    d_keys = []
    d_values = []
    for group in range(KVH):
        key = keys[group]
        value = values[group]
        d_key = jnp.zeros((TOK, LANES), f32)
        d_value = jnp.zeros((TOK, LANES), f32)
        for pair in range(group * (AH // (2 * KVH)), (group + 1) * (AH // (2 * KVH))):
            at = AT_Q + pair * LANES
            turned = rope_turn(pa_ref[:, at : at + LANES], cosine, sine) * root
            arrived = dxb_ref[:, E + pair * LANES : E + (pair + 1) * LANES]
            halves = []
            for side in range(2):
                chosen = low if side == 0 else jnp.logical_not(low)
                query = jnp.where(chosen, turned, 0.0).astype(bf16)
                d_out = jnp.where(chosen, arrived, 0.0).astype(bf16)
                scores = jnp.where(allowed_t, dot_nt(key, query), -1e30)
                peak = jnp.max(scores, axis=0, keepdims=True)
                weights = jnp.exp(scores - peak)
                weights = weights * (1.0 / jnp.sum(weights, axis=0, keepdims=True))
                d_weights = dot_nt(value, d_out)
                offset = jnp.sum(weights * d_weights, axis=0, keepdims=True)
                d_scores = (weights * (d_weights - offset)).astype(bf16)
                d_value = d_value + dot_nn(weights.astype(bf16), d_out)
                d_key = d_key + dot_nn(d_scores, query)
                halves.append(dot_tn(d_scores, key))
            d_query = rope_back(jnp.where(low, halves[0], halves[1]) * root, cosine, sine)
            pg_ref[:, at : at + LANES] = d_query.astype(bf16)
        d_keys.append(d_key + pltpu.roll(d_key, HD, 1))
        d_values.append(d_value + pltpu.roll(d_value, HD, 1))
    d_key = rope_back(jnp.where(low, d_keys[0], d_keys[1]), cosine, sine)
    pg_ref[:, AT_K:AT_V] = d_key.astype(bf16)
    pg_ref[:, AT_V:AT_DT] = jnp.where(low, d_values[0], d_values[1]).astype(bf16)


def row_block(width):
    return pl.BlockSpec((None, TOK, width), lambda row: (row, 0, 0))


def whole_block(shape):
    return pl.BlockSpec(shape, lambda row: (0,) * len(shape))


def core_forward(projected, layout, params):
    rope, masks, doc_cols, doc_rows = layout
    taps, heads, wide = params
    rows = projected.shape[0]
    return pl.pallas_call(
        core_forward_kernel,
        grid=(rows,),
        in_specs=[
            row_block(WIDE_A),
            row_block(2 * LANES),
            row_block(3 * LANES),
            row_block(LANES),
            pl.BlockSpec((None, 8, TOK), lambda row: (row, 0, 0)),
            whole_block(taps.shape),
            whole_block(heads.shape),
            whole_block(wide.shape),
        ],
        out_specs=[row_block(MIXED), row_block(CH), row_block(E)],
        out_shape=[
            jax.ShapeDtypeStruct((rows, TOK, MIXED), bf16),
            jax.ShapeDtypeStruct((rows, TOK, CH), f32),
            jax.ShapeDtypeStruct((rows, TOK, E), f32),
        ],
        scratch_shapes=[
            pltpu.VMEM((TOK, CH), f32),
            pltpu.VMEM((TOK, TOK), f32),
            pltpu.VMEM((TOK, LANES), f32),
        ],
        compiler_params=pltpu.CompilerParams(vmem_limit_bytes=48 * 2**20),
        cost_estimate=pl.CostEstimate(
            flops=rows * 4 * 10**8, bytes_accessed=rows * 12 * 2**20, transcendentals=rows * 10**6
        ),
        name="core_forward",
    )(projected, rope, masks, doc_cols, doc_rows, taps, heads, wide)


def core_backward(row, projected, pre, yns, d_mixed, layout, params):
    rope, masks, doc_cols, doc_rows = layout
    taps, heads, wide = params

    def picked(width, depth=TOK):
        return pl.BlockSpec((None, depth, width), lambda step, pick: (pick[0], 0, 0))

    def plain(shape):
        return pl.BlockSpec(shape, lambda step, pick: (0,) * len(shape))

    return pl.pallas_call(
        core_backward_kernel,
        grid_spec=pltpu.PrefetchScalarGridSpec(
            num_scalar_prefetch=1,
            grid=(1,),
            in_specs=[
                picked(WIDE_A),
                picked(CH),
                picked(E),
                plain((TOK, MIXED)),
                picked(2 * LANES),
                picked(3 * LANES),
                picked(LANES),
                picked(TOK, 8),
                plain(taps.shape),
                plain(heads.shape),
                plain(wide.shape),
            ],
            out_specs=[plain((TOK, WIDE_A)), plain((8, CH))],
            scratch_shapes=[
                pltpu.VMEM((TOK, CH), f32),
                pltpu.VMEM((TOK, CH), f32),
                pltpu.VMEM((TOK, E), bf16),
                pltpu.VMEM((TOK, TOK), f32),
                pltpu.VMEM((TOK, TOK), f32),
                pltpu.VMEM((TOK, LANES), f32),
                pltpu.VMEM((TOK, LANES), f32),
            ],
        ),
        out_shape=[
            jax.ShapeDtypeStruct((TOK, WIDE_A), bf16),
            jax.ShapeDtypeStruct((8, CH), f32),
        ],
        compiler_params=pltpu.CompilerParams(vmem_limit_bytes=48 * 2**20),
        cost_estimate=pl.CostEstimate(
            flops=10**9, bytes_accessed=16 * 2**20, transcendentals=2 * 10**6
        ),
        name="core_backward",
    )(
        row.reshape(1), projected, pre, yns, d_mixed, rope, masks, doc_cols, doc_rows,
        taps, heads, wide,
    )


def passed_along(value, axis, steps):
    count = lax.axis_size(axis)
    leading, last = (max(0, -steps), min(count, count - steps))
    return lax.ppermute(value, axis, [(source, source + steps) for source in range(leading, last)])


def norm_scale(values):
    return lax.rsqrt(jnp.mean(values * values, axis=-1, keepdims=True) + epsilon)


def norm_back(values, gain, arrived):
    scale = norm_scale(values)
    weighted = arrived * gain
    pull = jnp.mean(weighted * values, axis=-1, keepdims=True) * scale * scale * scale
    gain_grad = jnp.sum(arrived * values * scale, axis=0)
    return (weighted * scale - values * pull, gain_grad)


def row_layout(doc_ids):
    rows = doc_ids.shape[0]
    positions = jnp.arange(TOK, dtype=jnp.int32)
    earlier = jnp.sum((doc_ids[:, None, :] < doc_ids[:, :, None]).astype(jnp.int32), axis=2)
    places = positions[None, :] - earlier
    half_dim = HD // 2
    inverse_freq = rope_base ** (-jnp.arange(half_dim, dtype=f32) / half_dim)
    angles = places.astype(f32)[:, :, None] * inverse_freq[None, None, :]
    repeats = LANES // half_dim
    rope = jnp.concatenate([jnp.cos(angles)] * repeats + [jnp.sin(angles)] * repeats, axis=-1)
    masks = jnp.concatenate(
        [
            jnp.broadcast_to((places >= shift).astype(f32)[:, :, None], (rows, TOK, LANES))
            for shift in (1, 2, 3)
        ],
        axis=-1,
    )
    doc_cols = jnp.broadcast_to(doc_ids[:, :, None], (rows, TOK, LANES))
    doc_rows = jnp.broadcast_to(doc_ids[:, None, :], (rows, 8, TOK))
    return (rope, masks, doc_cols, doc_rows)


def core_params(conv_weight, conv_bias, step_bias, decay_log, skip_scale, mixer_gain):
    taps = jnp.concatenate([conv_weight, conv_bias[None], jnp.zeros((3, CH), f32)], axis=0)
    heads = jnp.zeros((8, LANES), f32)
    heads = heads.at[0, :MH].set(step_bias).at[1, :MH].set(jnp.exp(decay_log))
    wide = jnp.concatenate(
        [jnp.repeat(skip_scale, MP)[None], mixer_gain[None], jnp.zeros((6, E), f32)], axis=0
    )
    return (taps, heads, wide)


def stage_a(start_rows, pre_gain, weight_a):
    normed = (start_rows * norm_scale(start_rows) * pre_gain).astype(bf16)
    return (normed, dot_nn(normed, weight_a))


def stage_b(start_rows, mixed, mlp_gain, weight_b):
    middle = start_rows + dot_nt(mixed, weight_b[:, :MIXED])
    normed = (middle * norm_scale(middle) * mlp_gain).astype(bf16)
    gate_up = dot_nn(normed, weight_b[:, AT_GU:AT_DN])
    gate = gate_up[:, :FF]
    act = (gate * jax.nn.sigmoid(gate) * gate_up[:, FF:]).astype(bf16)
    result = middle + dot_nt(act, weight_b[:, AT_DN:])
    return (result, middle, normed, gate_up, act)


def layer_forward(start_rows, layout, params, pre_gain, mlp_gain, weight_a, weight_b):
    rows = start_rows.shape[0] // TOK
    normed, projected = stage_a(start_rows, pre_gain, weight_a)
    projected = projected.reshape(rows, TOK, WIDE_A)
    mixed, pre, yns = core_forward(projected, layout, params)
    mixed = mixed.reshape(rows * TOK, MIXED)
    result, middle, normed_two, gate_up, act = stage_b(start_rows, mixed, mlp_gain, weight_b)
    return result, (
        start_rows, normed, projected, pre, yns, mixed, middle, normed_two, gate_up, act,
    )


def layer_backward(row, saved, cotangent, layout, params, pre_gain, mlp_gain, weight_a, weight_b):
    start_rows, _, projected, pre, yns, _, middle, _, gate_up, _ = saved

    def own(array):
        return lax.dynamic_slice_in_dim(array, row * TOK, TOK, axis=0)

    out_low = cotangent.astype(bf16)
    act_grad = dot_nn(out_low, weight_b[:, AT_DN:])
    gate_up_rows = own(gate_up)
    gate = gate_up_rows[:, :FF]
    opened = jax.nn.sigmoid(gate)
    d_gate = act_grad * gate_up_rows[:, FF:] * silu_slope(gate, opened)
    d_up = act_grad * (gate * opened)
    gate_up_low = jnp.concatenate([d_gate.astype(bf16), d_up.astype(bf16)], axis=1)
    normed_two_grad = dot_nt(gate_up_low, weight_b[:, AT_GU:AT_DN])
    middle_norm_grad, mlp_gain_grad = norm_back(own(middle), mlp_gain, normed_two_grad)
    middle_grad = cotangent + middle_norm_grad
    middle_low = middle_grad.astype(bf16)
    d_mixed = dot_nn(middle_low, weight_b[:, :MIXED])
    proj_low, small = core_backward(row, projected, pre, yns, d_mixed, layout, params)
    normed_grad = dot_nt(proj_low, weight_a)
    start_norm_grad, pre_gain_grad = norm_back(own(start_rows), pre_gain, normed_grad)
    start_grad = middle_grad + start_norm_grad
    return start_grad, (out_low, gate_up_low, middle_low, proj_low), (
        pre_gain_grad, mlp_gain_grad, small,
    )


def per_device(
    inputs, out_grad, doc_ids, row_live, pre_gain, mlp_gain, mixer_gain, conv_weight, conv_bias,
    step_bias, decay_log, skip_scale, mixer_in_weight, mixer_out_weight, query_weight, key_weight,
    value_weight, attend_weight, gate_up_weight, down_weight,
):
    is_first = lax.axis_index("section") == 0
    shard = mixer_in_weight.shape[1]
    packed_a = jnp.concatenate(
        [
            mixer_in_weight[0, :, :AT_Q],
            query_weight[0],
            key_weight[0],
            value_weight[0],
            mixer_in_weight[0, :, AT_Q:],
            jnp.zeros((shard, LANES - MH), bf16),
        ],
        axis=1,
    )
    packed_b = jnp.concatenate(
        [mixer_out_weight[0].T, attend_weight[0].T, gate_up_weight[0], down_weight[0].T], axis=1
    )
    weight_a = lax.all_gather(packed_a, "dp", axis=0, tiled=True)
    weight_b = lax.all_gather(packed_b, "dp", axis=0, tiled=True)

    layout = row_layout(doc_ids)
    params = core_params(
        conv_weight[0], conv_bias[0], step_bias[0], decay_log[0], skip_scale[0], mixer_gain[0]
    )
    gains = (pre_gain[0], mlp_gain[0])
    weights = (weight_a, weight_b)
    first_rows = inputs.astype(f32)
    handed, _ = layer_forward(first_rows, layout, params, *gains, *weights)
    received = passed_along(handed.astype(bf16), "section", 1)
    start_rows = jnp.where(is_first, first_rows, received.astype(f32))
    result, saved = layer_forward(start_rows, layout, params, *gains, *weights)
    section_out = result.astype(bf16)[None]

    positions = jnp.arange(TOK, dtype=jnp.int32)
    live = (positions[None, :] < row_live[:, None]).astype(f32).reshape(MB * TOK, 1)
    from_loss = out_grad.astype(f32) * live

    received = jnp.zeros((TOK, D), bf16)
    done = []
    for tick in range(3):
        row = jnp.where(is_first, (1, 1, 0)[tick], (1, 0, 1)[tick]).astype(jnp.int32)
        loss_row = (1, 0, 1)[tick]
        cotangent = jnp.where(
            is_first,
            received.astype(f32),
            from_loss[loss_row * TOK : (loss_row + 1) * TOK],
        )
        step = layer_backward(row, saved, cotangent, layout, params, *gains, *weights)
        done.append(step)
        if tick < 2:
            received = passed_along(step[0].astype(bf16), "section", -1)

    def in_order(first, second):
        return jnp.concatenate(
            [jnp.where(is_first, second, first), jnp.where(is_first, first, second)], axis=0
        )

    start_grad = in_order(done[1][0], done[2][0])[None]
    out_low, gate_up_low, middle_low, proj_low = (
        in_order(one, two) for one, two in zip(done[1][1], done[2][1])
    )
    normed, mixed, normed_two, act = saved[1], saved[5], saved[7], saved[9]
    grad_b = jnp.concatenate(
        [
            dot_tn(middle_low, mixed).astype(bf16),
            dot_tn(normed_two, gate_up_low).astype(bf16),
            dot_tn(out_low, act).astype(bf16),
        ],
        axis=1,
    )
    grad_a = dot_tn(normed, proj_low).astype(bf16)
    share_b = lax.psum_scatter(grad_b, "dp", scatter_dimension=0, tiled=True).astype(f32)
    share_a = lax.psum_scatter(grad_a, "dp", scatter_dimension=0, tiled=True).astype(f32)

    pre_sum, mlp_sum, small = lax.psum(
        tuple(one + two for one, two in zip(done[1][2], done[2][2])), "dp"
    )
    skip_sum = jnp.sum(small[6, :E].reshape(MH, MP), axis=1)
    mixer_in_grad = jnp.concatenate([share_a[:, :AT_Q], share_a[:, AT_DT : AT_DT + MH]], axis=1)
    return (
        section_out,
        start_grad,
        pre_sum[None],
        mlp_sum[None],
        small[5:6, :E],
        small[None, :4],
        small[4:5],
        small[7:8, :MH],
        small[7:8, LANES : LANES + MH],
        skip_sum[None],
        mixer_in_grad[None],
        share_b[:, :E].T[None],
        share_a[:, AT_Q:AT_K][None],
        share_a[:, AT_K:AT_V][None],
        share_a[:, AT_V:AT_DT][None],
        share_b[:, E:MIXED].T[None],
        share_b[:, AT_GU:AT_DN][None],
        share_b[:, AT_DN:].T[None],
    )


def solution(mesh):
    rows = P("dp", None)
    small = P("section", None)
    by_row = P("section", "dp", None)
    by_col = P("section", None, "dp")
    small_specs = (small, small, small, P("section", None, None), small, small, small, small)
    big_specs = (by_row, by_col, by_row, by_row, by_row, by_col, by_row, by_col)
    in_specs = (rows, rows, rows, P("dp")) + small_specs + big_specs
    out_specs = (by_row, by_row) + small_specs + big_specs
    return jax.shard_map(
        per_device, mesh=mesh, in_specs=in_specs, out_specs=out_specs, check_vma=False
    )
```

```python
import functools
import math

import jax
import jax.numpy as jnp
from jax import lax
from jax.experimental import pallas as pl
from jax.experimental.pallas import tpu as pltpu
from jax.sharding import Mesh
from jax.sharding import PartitionSpec as P

D = 1024
FF = 2048
MH = 24
MP = 64
NS = 128
AH = 8
KVH = 2
HD = 64
MB = 2
TOK = 256
E = 1536
CH = 1792
HALF = TOK // 2
PAIRS = MH // 2
LANES = 128
SIDE = D // 2

AT_W = E
AT_Q = E + CH
AT_K = AT_Q + AH * HD
AT_V = AT_K + KVH * HD
AT_DT = AT_V + KVH * HD
WIDE_A = AT_DT + LANES
MIXED = E + AH * HD
AT_GU = MIXED
AT_DN = AT_GU + 2 * FF
WIDE_B = AT_DN + FF

highest = lax.Precision.HIGHEST
epsilon = 1e-05
rope_base = 100000000000.0
bf16 = jnp.bfloat16
f32 = jnp.float32


def dot_nn(left, right):
    return lax.dot_general(left, right, (((1,), (0,)), ((), ())), preferred_element_type=f32)


def dot_nt(left, right):
    return lax.dot_general(left, right, (((1,), (1,)), ((), ())), preferred_element_type=f32)


def dot_tn(left, right):
    return lax.dot_general(left, right, (((0,), (0,)), ((), ())), preferred_element_type=f32)


def dot_exact(left, right):
    return lax.dot_general(
        left, right, (((1,), (0,)), ((), ())), precision=highest, preferred_element_type=f32
    )


def softplus(value):
    return jnp.maximum(value, 0.0) + jnp.log1p(jnp.exp(-jnp.abs(value)))


def lane_low(rows):
    return lax.broadcasted_iota(jnp.int32, (rows, LANES), 1) < HD


def rope_halves(rows):
    return (lax.broadcasted_iota(jnp.int32, (rows, LANES), 1) & (HD - 1)) < HD // 2


def rope_turn(tile, cosine, sine):
    swapped = jnp.where(
        rope_halves(tile.shape[0]),
        -pltpu.roll(tile, LANES - HD // 2, 1),
        pltpu.roll(tile, HD // 2, 1),
    )
    return tile * cosine + swapped * sine


def rope_back(tile, cosine, sine):
    swapped = jnp.where(
        rope_halves(tile.shape[0]),
        pltpu.roll(tile, LANES - HD // 2, 1),
        -pltpu.roll(tile, HD // 2, 1),
    )
    return tile * cosine + swapped * sine


def both_halves(tile):
    swapped = pltpu.roll(tile, HD, 1)
    low = lane_low(tile.shape[0])
    return (jnp.where(low, tile, swapped), jnp.where(low, swapped, tile))


def tile_at(index):
    return pl.ds(pl.multiple_of(index * LANES, LANES), LANES)


def tile_from(start, index):
    return pl.ds(pl.multiple_of(start + index * LANES, LANES), LANES)


def allowed_pairs(doc_col_ref, doc_row_ref):
    later = lax.broadcasted_iota(jnp.int32, (TOK, TOK), 0)
    early = lax.broadcasted_iota(jnp.int32, (TOK, TOK), 1)
    same = doc_col_ref[:, 0:1] == doc_row_ref[0:1, :]
    return (later >= early) & same


def core_forward_kernel(
    pa_ref, rope_ref, mask_ref, doc_col_ref, doc_row_ref, taps_ref, head_ref, wide_ref,
    xb_ref, pre_ref, yns_ref,
    conv_s, cb_s, sum_s,
):
    def conv_tile(index, carry):
        rows = pa_ref[:, tile_from(AT_W, index)]
        at = tile_at(index)
        total = taps_ref[4:5, at] + taps_ref[3:4, at] * rows
        for shift in (1, 2, 3):
            moved = mask_ref[:, (shift - 1) * LANES : shift * LANES] * pltpu.roll(rows, shift, 0)
            total = total + taps_ref[3 - shift : 4 - shift, at] * moved
        pre_ref[:, at] = total
        conv_s[:, at] = total * jax.nn.sigmoid(total)
        return carry

    lax.fori_loop(0, CH // LANES, conv_tile, 0)

    allowed = allowed_pairs(doc_col_ref, doc_row_ref)
    steps = softplus(pa_ref[:, AT_DT:] + head_ref[0:1, :])
    rates = -steps * head_ref[1:2, :]
    totals = dot_exact(jnp.where(allowed, 1.0, 0.0), rates)
    totals_t = totals.T
    inward = conv_s[:, E : E + NS].astype(bf16)
    outward = conv_s[:, E + NS :].astype(bf16)
    cb_s[...] = jnp.where(allowed, dot_nt(outward, inward), 0.0)
    low = lane_low(TOK)
    for pair in range(PAIRS):
        lanes = slice(pair * LANES, (pair + 1) * LANES)
        first = 2 * pair
        step_pair = jnp.where(low, steps[:, first : first + 1], steps[:, first + 1 : first + 2])
        scaled = (conv_s[:, lanes] * step_pair).astype(bf16)
        halves = []
        for head in (first, first + 1):
            col = totals[:, head : head + 1]
            row = totals_t[head : head + 1, :]
            top = jnp.exp(jnp.minimum(col[:HALF] - row[:, :HALF], 0.0)) * cb_s[:HALF, :HALF]
            end = jnp.exp(jnp.minimum(col[HALF:] - row, 0.0)) * cb_s[HALF:, :]
            halves.append(
                jnp.concatenate(
                    [dot_nn(top.astype(bf16), scaled[:HALF]), dot_nn(end.astype(bf16), scaled)],
                    axis=0,
                )
            )
        yns_ref[:, lanes] = jnp.where(low, halves[0], halves[1])

    sum_s[...] = jnp.zeros((TOK, LANES), f32)

    def gate_tile(index, carry):
        at = tile_at(index)
        gate = pa_ref[:, at]
        rows = yns_ref[:, at] + wide_ref[0:1, at] * conv_s[:, at]
        gated = rows * (gate * jax.nn.sigmoid(gate))
        sum_s[...] += gated * gated
        conv_s[:, at] = gated
        return carry

    lax.fori_loop(0, E // LANES, gate_tile, 0)
    scale = lax.rsqrt(jnp.sum(sum_s[...], axis=1, keepdims=True) * (1.0 / E) + epsilon)

    def norm_tile(index, carry):
        at = tile_at(index)
        xb_ref[:, at] = (conv_s[:, at] * scale * wide_ref[1:2, at]).astype(bf16)
        return carry

    lax.fori_loop(0, E // LANES, norm_tile, 0)

    cosine = rope_ref[:, :LANES]
    sine = rope_ref[:, LANES:]
    keys = both_halves(rope_turn(pa_ref[:, AT_K:AT_V], cosine, sine))
    values = both_halves(pa_ref[:, AT_V:AT_DT])
    keys = tuple(part.astype(bf16) for part in keys)
    values = tuple(part.astype(bf16) for part in values)
    for pair in range(AH // 2):
        group = pair // (AH // (2 * KVH))
        at = AT_Q + pair * LANES
        turned = rope_turn(pa_ref[:, at : at + LANES], cosine, sine) * (1.0 / math.sqrt(HD))
        halves = []
        for side in range(2):
            chosen = low if side == 0 else jnp.logical_not(low)
            query = jnp.where(chosen, turned, 0.0).astype(bf16)
            parts = []
            for rows, cols in ((slice(0, HALF), HALF), (slice(HALF, TOK), TOK)):
                scores = dot_nt(query[rows], keys[group][:cols])
                scores = jnp.where(allowed[rows, :cols], scores, -1e30)
                top = jnp.max(scores, axis=1, keepdims=True)
                weights = jnp.exp(scores - top)
                share = 1.0 / jnp.sum(weights, axis=1, keepdims=True)
                parts.append(dot_nn(weights.astype(bf16), values[group][:cols]) * share)
            halves.append(jnp.concatenate(parts, axis=0))
        out = jnp.where(low, halves[0], halves[1])
        xb_ref[:, E + pair * LANES : E + (pair + 1) * LANES] = out.astype(bf16)


def silu_slope(value, gate):
    return gate * (1.0 + value * (1.0 - gate))


def core_backward_kernel(
    pick_ref,
    pa_ref, pre_ref, yns_ref, dxb_ref, rope_ref, mask_ref, doc_col_ref, doc_row_ref,
    taps_ref, head_ref, wide_ref,
    pg_ref, small_ref,
    x_s, dx_s, dyb_s, cbt_s, dcbt_s, sum_s, ssum_s,
):
    small_ref[...] = jnp.zeros_like(small_ref)
    sum_s[...] = jnp.zeros((TOK, LANES), f32)
    ssum_s[...] = jnp.zeros((TOK, LANES), f32)

    def start_tile(index, carry):
        at = tile_at(index)
        pre = pre_ref[:, at]
        heads_in = pre * jax.nn.sigmoid(pre)
        x_s[:, at] = heads_in
        gate = pa_ref[:, at]
        rows = yns_ref[:, at] + wide_ref[0:1, at] * heads_in
        gated = rows * (gate * jax.nn.sigmoid(gate))
        sum_s[...] += gated * gated
        ssum_s[...] += dxb_ref[:, at] * wide_ref[1:2, at] * gated
        return carry

    lax.fori_loop(0, E // LANES, start_tile, 0)
    scale = lax.rsqrt(jnp.sum(sum_s[...], axis=1, keepdims=True) * (1.0 / E) + epsilon)
    pull = jnp.sum(ssum_s[...], axis=1, keepdims=True) * (1.0 / E) * scale * scale * scale

    def gate_tile(index, carry):
        at = tile_at(index)
        heads_in = x_s[:, at]
        skip = wide_ref[0:1, at]
        gate = pa_ref[:, at]
        opened = jax.nn.sigmoid(gate)
        rows = yns_ref[:, at] + skip * heads_in
        gated = rows * (gate * opened)
        arrived = dxb_ref[:, at]
        d_gated = scale * (arrived * wide_ref[1:2, at]) - gated * pull
        small_ref[5:6, at] = jnp.sum(arrived * gated * scale, axis=0, keepdims=True)
        d_rows = d_gated * (gate * opened)
        pg_ref[:, at] = (d_gated * rows * silu_slope(gate, opened)).astype(bf16)
        small_ref[6:7, at] = jnp.sum(d_rows * heads_in, axis=0, keepdims=True)
        dyb_s[:, at] = d_rows.astype(bf16)
        dx_s[:, at] = skip * d_rows
        return carry

    lax.fori_loop(0, E // LANES, gate_tile, 0)

    def state_tile(index, carry):
        at = tile_from(E, index)
        pre = pre_ref[:, at]
        x_s[:, at] = pre * jax.nn.sigmoid(pre)
        return carry

    lax.fori_loop(0, 2, state_tile, 0)

    later = lax.broadcasted_iota(jnp.int32, (TOK, TOK), 1)
    early = lax.broadcasted_iota(jnp.int32, (TOK, TOK), 0)
    allowed_t = (later >= early) & (doc_col_ref[:, 0:1] == doc_row_ref[0:1, :])
    allowed = allowed_pairs(doc_col_ref, doc_row_ref)
    raw = pa_ref[:, AT_DT:] + head_ref[0:1, :]
    steps = softplus(raw)
    decay = head_ref[1:2, :]
    rates = -steps * decay
    totals = dot_exact(jnp.where(allowed, 1.0, 0.0), rates)
    totals_t = totals.T
    inward = x_s[:, E : E + NS].astype(bf16)
    outward = x_s[:, E + NS :].astype(bf16)
    cbt_s[...] = jnp.where(allowed_t, dot_nt(inward, outward), 0.0)
    dcbt_s[...] = jnp.zeros((TOK, TOK), f32)
    low = lane_low(TOK)
    spread_row = lax.broadcasted_iota(jnp.int32, (LANES, LANES), 0) >= HD
    spread_col = lax.broadcasted_iota(jnp.int32, (LANES, LANES), 1)
    sum_s[...] = jnp.zeros((TOK, LANES), f32)
    ssum_s[...] = jnp.zeros((TOK, LANES), f32)
    for pair in range(PAIRS):
        lanes = slice(pair * LANES, (pair + 1) * LANES)
        first = 2 * pair
        step_pair = jnp.where(low, steps[:, first : first + 1], steps[:, first + 1 : first + 2])
        heads_in = x_s[:, lanes]
        scaled = (heads_in * step_pair).astype(bf16)
        d_rows = dyb_s[:, lanes]
        halves = []
        for side, head in enumerate((first, first + 1)):
            chosen = low if side == 0 else jnp.logical_not(low)
            own = jnp.where(chosen, scaled, jnp.zeros_like(scaled))
            col = totals[:, head : head + 1]
            row = totals_t[head : head + 1, :]
            top = jnp.exp(jnp.minimum(row - col[:HALF], 0.0))
            end = jnp.exp(jnp.minimum(row[:, HALF:] - col[HALF:], 0.0))
            top_mix = (top * cbt_s[:HALF, :]).astype(bf16)
            end_mix = (end * cbt_s[HALF:, HALF:]).astype(bf16)
            dcbt_s[:HALF, :] += dot_nt(own[:HALF], d_rows) * top
            dcbt_s[HALF:, HALF:] += dot_nt(own[HALF:], d_rows[HALF:]) * end
            halves.append(
                jnp.concatenate(
                    [dot_nn(top_mix, d_rows), dot_nn(end_mix, d_rows[HALF:])], axis=0
                )
            )
        d_scaled = jnp.where(low, halves[0], halves[1])
        dx_s[:, lanes] += d_scaled * step_pair
        spread = (spread_col == jnp.where(spread_row, first + 1, first)).astype(bf16)
        for value, into in (
            (d_scaled * heads_in, sum_s),
            (d_rows.astype(f32) * yns_ref[:, lanes] - scaled.astype(f32) * d_scaled, ssum_s),
        ):
            coarse = value.astype(bf16)
            fine = (value - coarse.astype(f32)).astype(bf16)
            into[...] += dot_nn(coarse, spread) + dot_nn(fine, spread)

    d_rates = dot_exact(jnp.where(allowed_t, 1.0, 0.0), ssum_s[...])
    d_steps = sum_s[...] - decay * d_rates
    d_raw = d_steps * jax.nn.sigmoid(raw)
    pg_ref[:, AT_DT:] = d_raw.astype(bf16)
    small_ref[7:8, :LANES] = jnp.sum(d_raw, axis=0, keepdims=True)
    small_ref[7:8, LANES : 2 * LANES] = jnp.sum(d_rates * rates, axis=0, keepdims=True)
    d_pairs = jnp.where(allowed_t, dcbt_s[...], 0.0).astype(bf16)
    dx_s[:, E : E + NS] = dot_nn(d_pairs, outward)
    dx_s[:, E + NS :] = dot_tn(d_pairs, inward)

    def conv_tile(index, carry):
        at = tile_at(index)
        pre = pre_ref[:, at]
        d_pre = dx_s[:, at] * silu_slope(pre, jax.nn.sigmoid(pre))
        rows = pa_ref[:, tile_from(AT_W, index)]
        small_ref[4:5, at] = jnp.sum(d_pre, axis=0, keepdims=True)
        small_ref[3:4, at] = jnp.sum(d_pre * rows, axis=0, keepdims=True)
        back = taps_ref[3:4, at] * d_pre
        for shift in (1, 2, 3):
            held = mask_ref[:, (shift - 1) * LANES : shift * LANES] * d_pre
            small_ref[3 - shift : 4 - shift, at] = jnp.sum(
                held * pltpu.roll(rows, shift, 0), axis=0, keepdims=True
            )
            back = back + taps_ref[3 - shift : 4 - shift, at] * pltpu.roll(held, TOK - shift, 0)
        pg_ref[:, tile_from(AT_W, index)] = back.astype(bf16)
        return carry

    lax.fori_loop(0, CH // LANES, conv_tile, 0)

    cosine = rope_ref[:, :LANES]
    sine = rope_ref[:, LANES:]
    keys = both_halves(rope_turn(pa_ref[:, AT_K:AT_V], cosine, sine))
    values = both_halves(pa_ref[:, AT_V:AT_DT])
    keys = tuple(part.astype(bf16) for part in keys)
    values = tuple(part.astype(bf16) for part in values)
    root = 1.0 / math.sqrt(HD)
    d_keys = []
    d_values = []
    for group in range(KVH):
        key = keys[group]
        value = values[group]
        d_key = jnp.zeros((TOK, LANES), f32)
        d_value = jnp.zeros((TOK, LANES), f32)
        for pair in range(group * (AH // (2 * KVH)), (group + 1) * (AH // (2 * KVH))):
            at = AT_Q + pair * LANES
            turned = rope_turn(pa_ref[:, at : at + LANES], cosine, sine) * root
            arrived = dxb_ref[:, E + pair * LANES : E + (pair + 1) * LANES]
            halves = []
            for side in range(2):
                chosen = low if side == 0 else jnp.logical_not(low)
                query = jnp.where(chosen, turned, 0.0).astype(bf16)
                d_out = jnp.where(chosen, arrived, 0.0).astype(bf16)
                scores = jnp.where(allowed_t, dot_nt(key, query), -1e30)
                peak = jnp.max(scores, axis=0, keepdims=True)
                weights = jnp.exp(scores - peak)
                weights = weights * (1.0 / jnp.sum(weights, axis=0, keepdims=True))
                d_weights = dot_nt(value, d_out)
                offset = jnp.sum(weights * d_weights, axis=0, keepdims=True)
                d_scores = (weights * (d_weights - offset)).astype(bf16)
                d_value = d_value + dot_nn(weights.astype(bf16), d_out)
                d_key = d_key + dot_nn(d_scores, query)
                halves.append(dot_tn(d_scores, key))
            d_query = rope_back(jnp.where(low, halves[0], halves[1]) * root, cosine, sine)
            pg_ref[:, at : at + LANES] = d_query.astype(bf16)
        d_keys.append(d_key + pltpu.roll(d_key, HD, 1))
        d_values.append(d_value + pltpu.roll(d_value, HD, 1))
    d_key = rope_back(jnp.where(low, d_keys[0], d_keys[1]), cosine, sine)
    pg_ref[:, AT_K:AT_V] = d_key.astype(bf16)
    pg_ref[:, AT_V:AT_DT] = jnp.where(low, d_values[0], d_values[1]).astype(bf16)


def row_block(width):
    return pl.BlockSpec((None, TOK, width), lambda row: (row, 0, 0))


def whole_block(shape):
    return pl.BlockSpec(shape, lambda row: (0,) * len(shape))


def core_forward(projected, layout, params):
    rope, masks, doc_cols, doc_rows = layout
    taps, heads, wide = params
    rows = projected.shape[0]
    return pl.pallas_call(
        core_forward_kernel,
        grid=(rows,),
        in_specs=[
            row_block(WIDE_A),
            row_block(2 * LANES),
            row_block(3 * LANES),
            row_block(LANES),
            pl.BlockSpec((None, 8, TOK), lambda row: (row, 0, 0)),
            whole_block(taps.shape),
            whole_block(heads.shape),
            whole_block(wide.shape),
        ],
        out_specs=[row_block(MIXED), row_block(CH), row_block(E)],
        out_shape=[
            jax.ShapeDtypeStruct((rows, TOK, MIXED), bf16),
            jax.ShapeDtypeStruct((rows, TOK, CH), f32),
            jax.ShapeDtypeStruct((rows, TOK, E), f32),
        ],
        scratch_shapes=[
            pltpu.VMEM((TOK, CH), f32),
            pltpu.VMEM((TOK, TOK), f32),
            pltpu.VMEM((TOK, LANES), f32),
        ],
        compiler_params=pltpu.CompilerParams(vmem_limit_bytes=48 * 2**20),
        cost_estimate=pl.CostEstimate(
            flops=rows * 4 * 10**8, bytes_accessed=rows * 12 * 2**20, transcendentals=rows * 10**6
        ),
        name="core_forward",
    )(projected, rope, masks, doc_cols, doc_rows, taps, heads, wide)


def core_backward(row, projected, pre, yns, d_mixed, layout, params):
    rope, masks, doc_cols, doc_rows = layout
    taps, heads, wide = params

    def picked(width, depth=TOK):
        return pl.BlockSpec((None, depth, width), lambda step, pick: (pick[0], 0, 0))

    def plain(shape):
        return pl.BlockSpec(shape, lambda step, pick: (0,) * len(shape))

    return pl.pallas_call(
        core_backward_kernel,
        grid_spec=pltpu.PrefetchScalarGridSpec(
            num_scalar_prefetch=1,
            grid=(1,),
            in_specs=[
                picked(WIDE_A),
                picked(CH),
                picked(E),
                plain((TOK, MIXED)),
                picked(2 * LANES),
                picked(3 * LANES),
                picked(LANES),
                picked(TOK, 8),
                plain(taps.shape),
                plain(heads.shape),
                plain(wide.shape),
            ],
            out_specs=[plain((TOK, WIDE_A)), plain((8, CH))],
            scratch_shapes=[
                pltpu.VMEM((TOK, CH), f32),
                pltpu.VMEM((TOK, CH), f32),
                pltpu.VMEM((TOK, E), bf16),
                pltpu.VMEM((TOK, TOK), f32),
                pltpu.VMEM((TOK, TOK), f32),
                pltpu.VMEM((TOK, LANES), f32),
                pltpu.VMEM((TOK, LANES), f32),
            ],
        ),
        out_shape=[
            jax.ShapeDtypeStruct((TOK, WIDE_A), bf16),
            jax.ShapeDtypeStruct((8, CH), f32),
        ],
        compiler_params=pltpu.CompilerParams(vmem_limit_bytes=48 * 2**20),
        cost_estimate=pl.CostEstimate(
            flops=10**9, bytes_accessed=16 * 2**20, transcendentals=2 * 10**6
        ),
        name="core_backward",
    )(
        row, projected, pre, yns, d_mixed, rope, masks, doc_cols, doc_rows,
        taps, heads, wide,
    )


def passed_along(value, axis, steps):
    count = lax.axis_size(axis)
    leading, last = (max(0, -steps), min(count, count - steps))
    return lax.ppermute(value, axis, [(source, source + steps) for source in range(leading, last)])


def norm_rows(values):
    return lax.rsqrt(jnp.mean(values * values, axis=-1, keepdims=True) + epsilon)


def norm_back(values, gain, arrived):
    scale = norm_rows(values)
    weighted = arrived * gain
    pull = jnp.mean(weighted * values, axis=-1, keepdims=True) * scale * scale * scale
    gain_grad = jnp.sum(arrived * values * scale, axis=0, keepdims=True)
    return (weighted * scale - values * pull, gain_grad)


def project_kernel(rows_ref, gain_ref, own_ref, other_ref, normed_ref, out_ref):
    @pl.when(pl.program_id(0) == 0)
    def _():
        rows = rows_ref[...].astype(f32)
        normed_ref[...] = (rows * norm_rows(rows) * gain_ref[...]).astype(bf16)

    out_ref[...] = dot_nn(normed_ref[:, :SIDE], own_ref[...]) + dot_nn(
        normed_ref[:, SIDE:], other_ref[...]
    )


def project(rows, gain, own, other):
    count = rows.shape[0]
    tile = WIDE_A // 3
    weight = pl.BlockSpec((SIDE, tile), lambda step: (0, step))
    return pl.pallas_call(
        project_kernel,
        grid=(3,),
        in_specs=[whole_block((count, D)), whole_block((1, D)), weight, weight],
        out_specs=[whole_block((count, D)), pl.BlockSpec((count, tile), lambda step: (0, step))],
        out_shape=[
            jax.ShapeDtypeStruct((count, D), bf16),
            jax.ShapeDtypeStruct((count, WIDE_A), f32),
        ],
        compiler_params=pltpu.CompilerParams(vmem_limit_bytes=40 * 2**20),
        cost_estimate=pl.CostEstimate(
            flops=2 * count * D * WIDE_A,
            bytes_accessed=2 * D * WIDE_A + 4 * count * WIDE_A,
            transcendentals=0,
        ),
        name="project",
    )(rows, gain, own, other)


def feed_forward_kernel(
    keep, rows_ref, mixed_ref, gain_ref,
    out_own, out_other, gate_own, gate_other, up_own, up_other, down_own, down_other,
    *refs,
):
    if keep:
        low_ref, middle_ref, normed_ref, gate_ref, up_ref, act_ref, total_s = refs
    else:
        low_ref, middle_ref, normed_ref, total_s = refs
    step = pl.program_id(0)

    @pl.when(step == 0)
    def _():
        middle_ref[...] = rows_ref[...].astype(f32)

    @pl.when(step < 4)
    def _():
        mixed = mixed_ref[...]
        middle_ref[:, :SIDE] += dot_nt(mixed, out_own[...])
        middle_ref[:, SIDE:] += dot_nt(mixed, out_other[...])

    @pl.when(step == 3)
    def _():
        middle = middle_ref[...]
        normed_ref[...] = (middle * norm_rows(middle) * gain_ref[...]).astype(bf16)
        total_s[...] = middle

    @pl.when(step >= 4)
    def _():
        left = normed_ref[:, :SIDE]
        right = normed_ref[:, SIDE:]
        gate = dot_nn(left, gate_own[...]) + dot_nn(right, gate_other[...])
        up = dot_nn(left, up_own[...]) + dot_nn(right, up_other[...])
        act = (gate * jax.nn.sigmoid(gate) * up).astype(bf16)
        if keep:
            gate_ref[...] = gate
            up_ref[...] = up
            act_ref[...] = act
        total_s[:, :SIDE] += dot_nt(act, down_own[...])
        total_s[:, SIDE:] += dot_nt(act, down_other[...])

    @pl.when(step == 7)
    def _():
        low_ref[...] = total_s[...].astype(bf16)


def b_block(start, skipped):
    return pl.BlockSpec(
        (SIDE, 512), lambda step, *pick: (0, start + jnp.clip(step - skipped, 0, 3))
    )


def b_blocks(parts):
    return [b_block(start, skipped) for start, skipped in parts for _ in range(2)]


def feed_forward(rows, mixed, gain, own, other, keep):
    count = rows.shape[0]
    wide = pl.BlockSpec((count, 512), lambda step: (0, jnp.clip(step - 4, 0, 3)))
    out_specs = [whole_block((count, D))]
    out_shape = [jax.ShapeDtypeStruct((count, D), bf16)]
    scratch = [pltpu.VMEM((count, D), f32)]
    if keep:
        out_specs += [whole_block((count, D)), whole_block((count, D)), wide, wide, wide]
        out_shape += [
            jax.ShapeDtypeStruct((count, D), f32),
            jax.ShapeDtypeStruct((count, D), bf16),
            jax.ShapeDtypeStruct((count, FF), f32),
            jax.ShapeDtypeStruct((count, FF), f32),
            jax.ShapeDtypeStruct((count, FF), bf16),
        ]
    else:
        scratch = [pltpu.VMEM((count, D), f32), pltpu.VMEM((count, D), bf16)] + scratch
    return pl.pallas_call(
        functools.partial(feed_forward_kernel, keep),
        grid=(8,),
        in_specs=[
            whole_block((count, D)),
            pl.BlockSpec((count, 512), lambda step: (0, jnp.clip(step, 0, 3))),
            whole_block((1, D)),
        ]
        + b_blocks(((0, 0), (4, 4), (8, 4), (12, 4))),
        out_specs=out_specs,
        out_shape=out_shape,
        scratch_shapes=scratch,
        compiler_params=pltpu.CompilerParams(vmem_limit_bytes=48 * 2**20),
        cost_estimate=pl.CostEstimate(
            flops=2 * count * D * WIDE_B, bytes_accessed=2 * D * WIDE_B, transcendentals=0
        ),
        name="feed_forward",
    )(rows, mixed, gain, *([own, other] * 4))


def feed_back_kernel(
    pick_ref, cot_ref, gate_ref, up_ref, middle_ref, gain_ref,
    down_own, down_other, gate_own, gate_other, up_own, up_other, out_own, out_other,
    d_gate_ref, d_up_ref, d_middle_ref, low_ref, d_mixed_ref, gain_grad_ref,
    total_s,
):
    step = pl.program_id(0)

    @pl.when(step == 0)
    def _():
        total_s[...] = jnp.zeros_like(total_s)

    @pl.when(step < 4)
    def _():
        arrived = dot_nn(cot_ref[:, :SIDE], down_own[...]) + dot_nn(
            cot_ref[:, SIDE:], down_other[...]
        )
        gate = gate_ref[...]
        opened = jax.nn.sigmoid(gate)
        d_gate = (arrived * up_ref[...] * silu_slope(gate, opened)).astype(bf16)
        d_up = (arrived * (gate * opened)).astype(bf16)
        d_gate_ref[...] = d_gate
        d_up_ref[...] = d_up
        total_s[:, :SIDE] += dot_nt(d_gate, gate_own[...]) + dot_nt(d_up, up_own[...])
        total_s[:, SIDE:] += dot_nt(d_gate, gate_other[...]) + dot_nt(d_up, up_other[...])

    @pl.when(step == 3)
    def _():
        d_norm, gain_grad = norm_back(middle_ref[...], gain_ref[...], total_s[...])
        d_middle = cot_ref[...].astype(f32) + d_norm
        d_middle_ref[...] = d_middle
        low_ref[...] = d_middle.astype(bf16)
        gain_grad_ref[...] = gain_grad

    @pl.when(step >= 4)
    def _():
        d_mixed_ref[...] = dot_nn(low_ref[:, :SIDE], out_own[...]) + dot_nn(
            low_ref[:, SIDE:], out_other[...]
        )


def feed_back(row, cotangent, gate, up, middle, gain, own, other):
    saved = pl.BlockSpec((TOK, 512), lambda step, pick: (pick[0], jnp.clip(step, 0, 3)))
    early = pl.BlockSpec((TOK, 512), lambda step, pick: (0, jnp.clip(step, 0, 3)))
    late = pl.BlockSpec((TOK, 512), lambda step, pick: (0, jnp.clip(step - 4, 0, 3)))
    full = pl.BlockSpec((TOK, D), lambda step, pick: (0, 0))
    gain_block = pl.BlockSpec((1, D), lambda step, pick: (0, 0))
    return pl.pallas_call(
        feed_back_kernel,
        grid_spec=pltpu.PrefetchScalarGridSpec(
            num_scalar_prefetch=1,
            grid=(8,),
            in_specs=[
                full,
                saved,
                saved,
                pl.BlockSpec((TOK, D), lambda step, pick: (pick[0], 0)),
                gain_block,
            ]
            + b_blocks(((12, 0), (4, 0), (8, 0), (0, 4))),
            out_specs=[early, early, full, full, late, gain_block],
            scratch_shapes=[pltpu.VMEM((TOK, D), f32)],
        ),
        out_shape=[
            jax.ShapeDtypeStruct((TOK, FF), bf16),
            jax.ShapeDtypeStruct((TOK, FF), bf16),
            jax.ShapeDtypeStruct((TOK, D), f32),
            jax.ShapeDtypeStruct((TOK, D), bf16),
            jax.ShapeDtypeStruct((TOK, MIXED), f32),
            jax.ShapeDtypeStruct((1, D), f32),
        ],
        compiler_params=pltpu.CompilerParams(vmem_limit_bytes=48 * 2**20),
        cost_estimate=pl.CostEstimate(
            flops=2 * TOK * D * WIDE_B, bytes_accessed=2 * D * WIDE_B, transcendentals=0
        ),
        name="feed_back",
    )(row, cotangent, gate, up, middle, gain, *([own, other] * 4))


def project_back_kernel(
    pick_ref, grad_ref, rows_ref, d_middle_ref, gain_ref, own_ref, other_ref,
    d_rows_ref, low_ref, gain_grad_ref, total_s,
):
    step = pl.program_id(0)

    @pl.when(step == 0)
    def _():
        total_s[...] = jnp.zeros_like(total_s)

    total_s[:, :SIDE] += dot_nt(grad_ref[...], own_ref[...])
    total_s[:, SIDE:] += dot_nt(grad_ref[...], other_ref[...])

    @pl.when(step == 2)
    def _():
        d_norm, gain_grad = norm_back(rows_ref[...].astype(f32), gain_ref[...], total_s[...])
        d_rows = d_middle_ref[...] + d_norm
        d_rows_ref[...] = d_rows
        low_ref[...] = d_rows.astype(bf16)
        gain_grad_ref[...] = gain_grad


def project_back(row, proj_low, start_rows, d_middle, gain, own, other):
    tile = WIDE_A // 3
    weight = pl.BlockSpec((SIDE, tile), lambda step, pick: (0, step))
    full = pl.BlockSpec((TOK, D), lambda step, pick: (0, 0))
    gain_block = pl.BlockSpec((1, D), lambda step, pick: (0, 0))
    return pl.pallas_call(
        project_back_kernel,
        grid_spec=pltpu.PrefetchScalarGridSpec(
            num_scalar_prefetch=1,
            grid=(3,),
            in_specs=[
                pl.BlockSpec((TOK, tile), lambda step, pick: (0, step)),
                pl.BlockSpec((TOK, D), lambda step, pick: (pick[0], 0)),
                full,
                gain_block,
                weight,
                weight,
            ],
            out_specs=[full, full, gain_block],
            scratch_shapes=[pltpu.VMEM((TOK, D), f32)],
        ),
        out_shape=[
            jax.ShapeDtypeStruct((TOK, D), f32),
            jax.ShapeDtypeStruct((TOK, D), bf16),
            jax.ShapeDtypeStruct((1, D), f32),
        ],
        compiler_params=pltpu.CompilerParams(vmem_limit_bytes=40 * 2**20),
        cost_estimate=pl.CostEstimate(
            flops=2 * TOK * D * WIDE_A, bytes_accessed=2 * D * WIDE_A, transcendentals=0
        ),
        name="project_back",
    )(row, proj_low, start_rows, d_middle, gain, own, other)


def turned_pair(one_ref, two_ref):
    return jnp.concatenate(
        [one_ref[...].astype(f32).T.astype(bf16), two_ref[...].astype(f32).T.astype(bf16)], axis=1
    )


def weight_grad_b_kernel(
    added, pick_ref,
    mid_one, mid_two, norm_one, norm_two, out_one, out_two,
    mixed_one, mixed_two, gate_one, gate_two, up_one, up_two, act_one, act_two, *refs,
):
    if added:
        arrived_ref, sum_ref, left_s = refs
    else:
        sum_ref, left_s = refs
    step = pl.program_id(0)
    for start, one_ref, two_ref in (
        (0, mid_one, mid_two), (2, norm_one, norm_two), (6, out_one, out_two),
    ):
        @pl.when(step == start)
        def _(one_ref=one_ref, two_ref=two_ref):
            left_s[...] = turned_pair(one_ref, two_ref)

    for start, one_ref, two_ref in (
        (0, mixed_one, mixed_two), (2, gate_one, gate_two), (4, up_one, up_two),
        (6, act_one, act_two),
    ):
        @pl.when((step >= start) & (step < start + 2))
        def _(one_ref=one_ref, two_ref=two_ref):
            total = dot_nn(left_s[:, :TOK], one_ref[...]) + dot_nn(left_s[:, TOK:], two_ref[...])
            if added:
                total = total + arrived_ref[...].astype(f32)
            sum_ref[...] = total.astype(bf16)


def weight_grad_b(picks, side, ticks, normed_two, mixed, act, arrived=None):
    def tick_left():
        return pl.BlockSpec((TOK, SIDE), lambda step, pick: (0, side))

    def saved_left(which):
        return pl.BlockSpec((TOK, SIDE), lambda step, pick: (pick[which], side))

    def tick_right(start):
        return pl.BlockSpec((TOK, 1024), lambda step, pick: (0, jnp.clip(step - start, 0, 1)))

    def saved_right(which, start):
        return pl.BlockSpec(
            (TOK, 1024), lambda step, pick: (pick[which], jnp.clip(step - start, 0, 1))
        )

    (cot_one, gate_one, up_one, mid_one), (cot_two, gate_two, up_two, mid_two) = ticks
    tile = pl.BlockSpec((SIDE, 1024), lambda step, pick: (0, step))
    operands = [
        mid_one, mid_two, normed_two, normed_two, cot_one, cot_two,
        mixed, mixed, gate_one, gate_two, up_one, up_two, act, act,
    ]
    in_specs = [
        tick_left(), tick_left(), saved_left(0), saved_left(1), tick_left(), tick_left(),
        saved_right(0, 0), saved_right(1, 0), tick_right(2), tick_right(2), tick_right(4),
        tick_right(4), saved_right(0, 6), saved_right(1, 6),
    ]
    if arrived is not None:
        operands.append(arrived)
        in_specs.append(tile)
    return pl.pallas_call(
        functools.partial(weight_grad_b_kernel, arrived is not None),
        grid_spec=pltpu.PrefetchScalarGridSpec(
            num_scalar_prefetch=1,
            grid=(8,),
            in_specs=in_specs,
            out_specs=tile,
            scratch_shapes=[pltpu.VMEM((SIDE, MB * TOK), bf16)],
        ),
        out_shape=jax.ShapeDtypeStruct((SIDE, WIDE_B), bf16),
        compiler_params=pltpu.CompilerParams(vmem_limit_bytes=48 * 2**20),
        cost_estimate=pl.CostEstimate(
            flops=2 * MB * TOK * SIDE * WIDE_B, bytes_accessed=4 * SIDE * WIDE_B, transcendentals=0
        ),
        name="weight_grad_b",
    )(picks, *operands)


def weight_grad_a_kernel(added, pick_ref, norm_one, norm_two, one_ref, two_ref, *refs):
    if added:
        arrived_ref, sum_ref, left_s = refs
    else:
        sum_ref, left_s = refs

    @pl.when(pl.program_id(0) == 0)
    def _():
        left_s[...] = turned_pair(norm_one, norm_two)

    total = dot_nn(left_s[:, :TOK], one_ref[...]) + dot_nn(left_s[:, TOK:], two_ref[...])
    if added:
        total = total + arrived_ref[...].astype(f32)
    sum_ref[...] = total.astype(bf16)


def weight_grad_a(picks, side, proj_one, proj_two, normed, arrived=None):
    wide = WIDE_A // 3
    tile = pl.BlockSpec((SIDE, wide), lambda step, pick: (0, step))
    right = pl.BlockSpec((TOK, wide), lambda step, pick: (0, step))
    operands = [normed, normed, proj_one, proj_two]
    in_specs = [
        pl.BlockSpec((TOK, SIDE), lambda step, pick: (pick[0], side)),
        pl.BlockSpec((TOK, SIDE), lambda step, pick: (pick[1], side)),
        right,
        right,
    ]
    if arrived is not None:
        operands.append(arrived)
        in_specs.append(tile)
    return pl.pallas_call(
        functools.partial(weight_grad_a_kernel, arrived is not None),
        grid_spec=pltpu.PrefetchScalarGridSpec(
            num_scalar_prefetch=1,
            grid=(3,),
            in_specs=in_specs,
            out_specs=tile,
            scratch_shapes=[pltpu.VMEM((SIDE, MB * TOK), bf16)],
        ),
        out_shape=jax.ShapeDtypeStruct((SIDE, WIDE_A), bf16),
        compiler_params=pltpu.CompilerParams(vmem_limit_bytes=48 * 2**20),
        cost_estimate=pl.CostEstimate(
            flops=2 * MB * TOK * SIDE * WIDE_A, bytes_accessed=4 * SIDE * WIDE_A, transcendentals=0
        ),
        name="weight_grad_a",
    )(picks, *operands)


def row_layout(doc_ids):
    rows = doc_ids.shape[0]
    positions = jnp.arange(TOK, dtype=jnp.int32)
    earlier = jnp.sum((doc_ids[:, None, :] < doc_ids[:, :, None]).astype(jnp.int32), axis=2)
    places = positions[None, :] - earlier
    half_dim = HD // 2
    inverse_freq = rope_base ** (-jnp.arange(half_dim, dtype=f32) / half_dim)
    angles = places.astype(f32)[:, :, None] * inverse_freq[None, None, :]
    repeats = LANES // half_dim
    rope = jnp.concatenate([jnp.cos(angles)] * repeats + [jnp.sin(angles)] * repeats, axis=-1)
    masks = jnp.concatenate(
        [
            jnp.broadcast_to((places >= shift).astype(f32)[:, :, None], (rows, TOK, LANES))
            for shift in (1, 2, 3)
        ],
        axis=-1,
    )
    doc_cols = jnp.broadcast_to(doc_ids[:, :, None], (rows, TOK, LANES))
    doc_rows = jnp.broadcast_to(doc_ids[:, None, :], (rows, 8, TOK))
    return (rope, masks, doc_cols, doc_rows)


def core_params(conv_weight, conv_bias, step_bias, decay_log, skip_scale, mixer_gain):
    taps = jnp.concatenate([conv_weight, conv_bias[None], jnp.zeros((3, CH), f32)], axis=0)
    heads = jnp.zeros((8, LANES), f32)
    heads = heads.at[0, :MH].set(step_bias).at[1, :MH].set(jnp.exp(decay_log))
    wide = jnp.concatenate(
        [jnp.repeat(skip_scale, MP)[None], mixer_gain[None], jnp.zeros((6, E), f32)], axis=0
    )
    return (taps, heads, wide)


def swapped(value):
    return lax.ppermute(value, "core", [(0, 1), (1, 0)])


def summed_small(value):
    chips = lax.axis_size("chip")
    if chips & (chips - 1):
        return lax.psum(value, ("chip", "core"))
    value = value + swapped(value)
    step = 1
    while step < chips:
        value = value + lax.ppermute(value, "chip", [(chip, chip ^ step) for chip in range(chips)])
        step *= 2
    return value


def own_first(values, core):
    lead = values.shape[:-1]
    parts = values.reshape(lead + (-1, 2, values.shape[-1] // (2 * lax.axis_size("chip"))))
    left = parts[..., 0, :].reshape(lead + (SIDE,))
    right = parts[..., 1, :].reshape(lead + (SIDE,))
    return jnp.concatenate(
        [jnp.where(core == 0, left, right), jnp.where(core == 0, right, left)], axis=-1
    )


def in_place(values, core):
    lead = values.shape[:-1]
    chips = lax.axis_size("chip")
    one = values[..., :SIDE].reshape(lead + (chips, 1, SIDE // chips))
    two = values[..., SIDE:].reshape(lead + (chips, 1, SIDE // chips))
    left = jnp.where(core == 0, one, two)
    right = jnp.where(core == 0, two, one)
    return jnp.concatenate([left, right], axis=-2).reshape(lead + (D,))


def per_device(
    inputs, out_grad, doc_ids, row_live, pre_gain, mlp_gain, mixer_gain, conv_weight, conv_bias,
    step_bias, decay_log, skip_scale, mixer_in_weight, mixer_out_weight, query_weight, key_weight,
    value_weight, attend_weight, gate_up_weight, down_weight,
):
    is_first = lax.axis_index("section") == 0
    core = lax.axis_index("core")
    shard = mixer_in_weight.shape[1]
    packed_a = jnp.concatenate(
        [
            mixer_in_weight[0, :, :AT_Q],
            query_weight[0],
            key_weight[0],
            value_weight[0],
            mixer_in_weight[0, :, AT_Q:],
            jnp.zeros((shard, LANES - MH), bf16),
        ],
        axis=1,
    )
    packed_b = jnp.concatenate(
        [mixer_out_weight[0].T, attend_weight[0].T, gate_up_weight[0], down_weight[0].T], axis=1
    )
    own_a = lax.all_gather(packed_a, "chip", axis=0, tiled=True)
    own_b = lax.all_gather(packed_b, "chip", axis=0, tiled=True)
    pair_a = (own_a, swapped(own_a))
    pair_b = (own_b, swapped(own_b))

    layout = row_layout(doc_ids)
    params = core_params(
        conv_weight[0], conv_bias[0], step_bias[0], decay_log[0], skip_scale[0], mixer_gain[0]
    )
    pre_row = own_first(pre_gain, core)
    mlp_row = own_first(mlp_gain, core)
    first_rows = own_first(inputs, core)

    def mixed_of(projected):
        mixed, pre, yns = core_forward(projected.reshape(MB, TOK, WIDE_A), layout, params)
        return mixed.reshape(MB * TOK, MIXED), pre, yns

    _, projected = project(first_rows, pre_row, *pair_a)
    mixed, _, _ = mixed_of(projected)
    (handed,) = feed_forward(first_rows, mixed, mlp_row, *pair_b, keep=False)
    received = passed_along(handed, "section", 1)
    start_rows = jnp.where(is_first, first_rows, received)
    normed, projected = project(start_rows, pre_row, *pair_a)
    mixed, pre, yns = mixed_of(projected)
    result, middle, normed_two, gate, up, act = feed_forward(
        start_rows, mixed, mlp_row, *pair_b, keep=True
    )
    projected = projected.reshape(MB, TOK, WIDE_A)

    positions = jnp.arange(TOK, dtype=jnp.int32)
    live = (positions[None, :] < row_live[:, None]).reshape(MB * TOK, 1)
    from_loss = own_first(jnp.where(live, out_grad, jnp.zeros_like(out_grad)), core)

    received = jnp.zeros((TOK, D), bf16)
    done = []
    rows = []
    picks = jnp.where(is_first, jnp.array([1, 0]), jnp.array([0, 1])).astype(jnp.int32)
    sent_b = None
    for tick in range(3):
        row = jnp.where(is_first, (1, 1, 0)[tick], (1, 0, 1)[tick]).astype(jnp.int32).reshape(1)
        loss_row = (1, 0, 1)[tick]
        cotangent = jnp.where(
            is_first, received, from_loss[loss_row * TOK : (loss_row + 1) * TOK]
        )
        d_gate, d_up, d_middle, middle_low, d_mixed, mlp_grad = feed_back(
            row, cotangent, gate, up, middle, mlp_row, *pair_b
        )
        done.append((cotangent, d_gate, d_up, middle_low))
        if tick == 2:
            ticks = (done[1], done[2])
            sent_b = weight_grad_b(picks, 1, ticks, normed_two, mixed, act)
            d_mixed, sent_b = lax.optimization_barrier((d_mixed, sent_b))
            arrived_b = swapped(sent_b)
            sum_b = weight_grad_b(picks, 0, ticks, normed_two, mixed, act, arrived_b)
            share_b = lax.psum_scatter(sum_b, "chip", scatter_dimension=0, tiled=True)
        proj_low, small = core_backward(row, projected, pre, yns, d_mixed, layout, params)
        d_rows, d_low, pre_grad = project_back(
            row, proj_low, start_rows, d_middle, pre_row, *pair_a
        )
        rows.append((d_rows, proj_low, pre_grad, mlp_grad, small))
        if tick < 2:
            received = passed_along(d_low, "section", -1)

    proj_one, proj_two = rows[1][1], rows[2][1]
    arrived_a = swapped(weight_grad_a(picks, 1, proj_one, proj_two, normed))
    sum_a = weight_grad_a(picks, 0, proj_one, proj_two, normed, arrived_a)
    share_a = lax.psum_scatter(sum_a, "chip", scatter_dimension=0, tiled=True)

    start_grad = jnp.concatenate(
        [
            jnp.where(is_first, rows[2][0], rows[1][0]),
            jnp.where(is_first, rows[1][0], rows[2][0]),
        ],
        axis=0,
    )
    pre_sum, mlp_sum, small = (one + two for one, two in zip(rows[1][2:], rows[2][2:]))
    gain_sums = in_place(jnp.concatenate([pre_sum, mlp_sum], axis=0), core)
    packed = jnp.concatenate(
        [small, jnp.pad(gain_sums, ((0, 6), (0, CH - D)))], axis=0
    )
    packed, sum_a = lax.optimization_barrier((packed, sum_a))
    small = summed_small(packed)
    skip_sum = jnp.sum(small[6, :E].reshape(MH, MP), axis=1)
    share_a = share_a.astype(f32)
    share_b = share_b.astype(f32)
    mixer_in_grad = jnp.concatenate([share_a[:, :AT_Q], share_a[:, AT_DT : AT_DT + MH]], axis=1)
    return (
        in_place(result, core)[None],
        in_place(start_grad, core)[None],
        small[8:9, :D],
        small[9:10, :D],
        small[5:6, :E],
        small[None, :4],
        small[4:5],
        small[7:8, :MH],
        small[7:8, LANES : LANES + MH],
        skip_sum[None],
        mixer_in_grad[None],
        share_b[:, :E].T[None],
        share_a[:, AT_Q:AT_K][None],
        share_a[:, AT_K:AT_V][None],
        share_a[:, AT_V:AT_DT][None],
        share_b[:, E:MIXED].T[None],
        share_b[:, AT_GU:AT_DN][None],
        share_b[:, AT_DN:].T[None],
    )


def solution(mesh):
    dp = mesh.shape["dp"]
    devices = mesh.devices.reshape(mesh.shape["section"], dp // 2, 2)
    paired = Mesh(devices, ("section", "chip", "core"))
    over = ("chip", "core")
    rows = P(over, None)
    small = P("section", None)
    by_row = P("section", over, None)
    by_col = P("section", None, over)
    small_specs = (small, small, small, P("section", None, None), small, small, small, small)
    big_specs = (by_row, by_col, by_row, by_row, by_row, by_col, by_row, by_col)
    in_specs = (rows, rows, rows, P(over)) + small_specs + big_specs
    out_specs = (by_row, by_row) + small_specs + big_specs
    return jax.shard_map(
        per_device, mesh=paired, in_specs=in_specs, out_specs=out_specs, check_vma=False
    )
```

```python
import functools
import math

import jax
import jax.numpy as jnp
from jax import lax
from jax.experimental import pallas as pl
from jax.experimental.pallas import tpu as pltpu
from jax.sharding import Mesh
from jax.sharding import PartitionSpec as P

D = 1024
FF = 2048
MH = 24
MP = 64
NS = 128
AH = 8
KVH = 2
HD = 64
MB = 2
TOK = 256
E = 1536
CH = 1792
HALF = TOK // 2
PAIRS = MH // 2
LANES = 128
SIDE = D // 2

AT_W = E
AT_Q = E + CH
AT_K = AT_Q + AH * HD
AT_V = AT_K + KVH * HD
AT_DT = AT_V + KVH * HD
WIDE_A = AT_DT + LANES
MIXED = E + AH * HD
AT_GU = MIXED
AT_DN = AT_GU + 2 * FF
WIDE_B = AT_DN + FF

highest = lax.Precision.HIGHEST
epsilon = 1e-05
rope_base = 100000000000.0
bf16 = jnp.bfloat16
f32 = jnp.float32


def dot_nn(left, right):
    return lax.dot_general(left, right, (((1,), (0,)), ((), ())), preferred_element_type=f32)


def dot_nt(left, right):
    return lax.dot_general(left, right, (((1,), (1,)), ((), ())), preferred_element_type=f32)


def dot_tn(left, right):
    return lax.dot_general(left, right, (((0,), (0,)), ((), ())), preferred_element_type=f32)


def dot_exact(left, right):
    return lax.dot_general(
        left, right, (((1,), (0,)), ((), ())), precision=highest, preferred_element_type=f32
    )


def softplus(value):
    return jnp.maximum(value, 0.0) + jnp.log1p(jnp.exp(-jnp.abs(value)))


def lane_low(rows):
    return lax.broadcasted_iota(jnp.int32, (rows, LANES), 1) < HD


def rope_halves(rows):
    return (lax.broadcasted_iota(jnp.int32, (rows, LANES), 1) & (HD - 1)) < HD // 2


def rope_turn(tile, cosine, sine):
    swapped = jnp.where(
        rope_halves(tile.shape[0]),
        -pltpu.roll(tile, LANES - HD // 2, 1),
        pltpu.roll(tile, HD // 2, 1),
    )
    return tile * cosine + swapped * sine


def rope_back(tile, cosine, sine):
    swapped = jnp.where(
        rope_halves(tile.shape[0]),
        pltpu.roll(tile, LANES - HD // 2, 1),
        -pltpu.roll(tile, HD // 2, 1),
    )
    return tile * cosine + swapped * sine


def both_halves(tile):
    swapped = pltpu.roll(tile, HD, 1)
    low = lane_low(tile.shape[0])
    return (jnp.where(low, tile, swapped), jnp.where(low, swapped, tile))


def tile_at(index):
    return pl.ds(pl.multiple_of(index * LANES, LANES), LANES)


def tile_from(start, index):
    return pl.ds(pl.multiple_of(start + index * LANES, LANES), LANES)


def allowed_pairs(doc_col_ref, doc_row_ref):
    later = lax.broadcasted_iota(jnp.int32, (TOK, TOK), 0)
    early = lax.broadcasted_iota(jnp.int32, (TOK, TOK), 1)
    same = doc_col_ref[:, 0:1] == doc_row_ref[0:1, :]
    return (later >= early) & same


def core_forward_kernel(
    pa_ref, rope_ref, mask_ref, doc_col_ref, doc_row_ref, taps_ref, head_ref, wide_ref,
    xb_ref, pre_ref, yns_ref,
    conv_s, cb_s, sum_s,
):
    def conv_tile(index, carry):
        rows = pa_ref[:, tile_from(AT_W, index)]
        at = tile_at(index)
        total = taps_ref[4:5, at] + taps_ref[3:4, at] * rows
        for shift in (1, 2, 3):
            moved = mask_ref[:, (shift - 1) * LANES : shift * LANES] * pltpu.roll(rows, shift, 0)
            total = total + taps_ref[3 - shift : 4 - shift, at] * moved
        pre_ref[:, at] = total
        conv_s[:, at] = total * jax.nn.sigmoid(total)
        return carry

    lax.fori_loop(0, CH // LANES, conv_tile, 0)

    allowed = allowed_pairs(doc_col_ref, doc_row_ref)
    steps = softplus(pa_ref[:, AT_DT:] + head_ref[0:1, :])
    rates = -steps * head_ref[1:2, :]
    totals = dot_exact(jnp.where(allowed, 1.0, 0.0), rates)
    totals_t = totals.T
    inward = conv_s[:, E : E + NS].astype(bf16)
    outward = conv_s[:, E + NS :].astype(bf16)
    cb_s[...] = jnp.where(allowed, dot_nt(outward, inward), 0.0)
    low = lane_low(TOK)
    for pair in range(PAIRS):
        lanes = slice(pair * LANES, (pair + 1) * LANES)
        first = 2 * pair
        step_pair = jnp.where(low, steps[:, first : first + 1], steps[:, first + 1 : first + 2])
        scaled = (conv_s[:, lanes] * step_pair).astype(bf16)
        halves = []
        for head in (first, first + 1):
            col = totals[:, head : head + 1]
            row = totals_t[head : head + 1, :]
            top = jnp.exp(jnp.minimum(col[:HALF] - row[:, :HALF], 0.0)) * cb_s[:HALF, :HALF]
            end = jnp.exp(jnp.minimum(col[HALF:] - row, 0.0)) * cb_s[HALF:, :]
            halves.append(
                jnp.concatenate(
                    [dot_nn(top.astype(bf16), scaled[:HALF]), dot_nn(end.astype(bf16), scaled)],
                    axis=0,
                )
            )
        yns_ref[:, lanes] = jnp.where(low, halves[0], halves[1])

    sum_s[...] = jnp.zeros((TOK, LANES), f32)

    def gate_tile(index, carry):
        at = tile_at(index)
        gate = pa_ref[:, at]
        rows = yns_ref[:, at] + wide_ref[0:1, at] * conv_s[:, at]
        gated = rows * (gate * jax.nn.sigmoid(gate))
        sum_s[...] += gated * gated
        conv_s[:, at] = gated
        return carry

    lax.fori_loop(0, E // LANES, gate_tile, 0)
    scale = lax.rsqrt(jnp.sum(sum_s[...], axis=1, keepdims=True) * (1.0 / E) + epsilon)

    def norm_tile(index, carry):
        at = tile_at(index)
        xb_ref[:, at] = (conv_s[:, at] * scale * wide_ref[1:2, at]).astype(bf16)
        return carry

    lax.fori_loop(0, E // LANES, norm_tile, 0)

    cosine = rope_ref[:, :LANES]
    sine = rope_ref[:, LANES:]
    keys = both_halves(rope_turn(pa_ref[:, AT_K:AT_V], cosine, sine))
    values = both_halves(pa_ref[:, AT_V:AT_DT])
    keys = tuple(part.astype(bf16) for part in keys)
    values = tuple(part.astype(bf16) for part in values)
    for pair in range(AH // 2):
        group = pair // (AH // (2 * KVH))
        at = AT_Q + pair * LANES
        turned = rope_turn(pa_ref[:, at : at + LANES], cosine, sine) * (1.0 / math.sqrt(HD))
        halves = []
        for side in range(2):
            chosen = low if side == 0 else jnp.logical_not(low)
            query = jnp.where(chosen, turned, 0.0).astype(bf16)
            parts = []
            for rows, cols in ((slice(0, HALF), HALF), (slice(HALF, TOK), TOK)):
                scores = dot_nt(query[rows], keys[group][:cols])
                scores = jnp.where(allowed[rows, :cols], scores, -1e30)
                top = jnp.max(scores, axis=1, keepdims=True)
                weights = jnp.exp(scores - top)
                share = 1.0 / jnp.sum(weights, axis=1, keepdims=True)
                parts.append(dot_nn(weights.astype(bf16), values[group][:cols]) * share)
            halves.append(jnp.concatenate(parts, axis=0))
        out = jnp.where(low, halves[0], halves[1])
        xb_ref[:, E + pair * LANES : E + (pair + 1) * LANES] = out.astype(bf16)


def silu_slope(value, gate):
    return gate * (1.0 + value * (1.0 - gate))


def core_backward_kernel(
    pick_ref,
    pa_ref, pre_ref, yns_ref, dxb_ref, rope_ref, mask_ref, doc_col_ref, doc_row_ref,
    taps_ref, head_ref, wide_ref,
    pg_ref, small_ref,
    x_s, dx_s, dyb_s, cbt_s, dcbt_s, sum_s, ssum_s,
):
    small_ref[...] = jnp.zeros_like(small_ref)
    sum_s[...] = jnp.zeros((TOK, LANES), f32)
    ssum_s[...] = jnp.zeros((TOK, LANES), f32)

    def start_tile(index, carry):
        at = tile_at(index)
        pre = pre_ref[:, at]
        heads_in = pre * jax.nn.sigmoid(pre)
        x_s[:, at] = heads_in
        gate = pa_ref[:, at]
        rows = yns_ref[:, at] + wide_ref[0:1, at] * heads_in
        gated = rows * (gate * jax.nn.sigmoid(gate))
        sum_s[...] += gated * gated
        ssum_s[...] += dxb_ref[:, at] * wide_ref[1:2, at] * gated
        return carry

    lax.fori_loop(0, E // LANES, start_tile, 0)
    scale = lax.rsqrt(jnp.sum(sum_s[...], axis=1, keepdims=True) * (1.0 / E) + epsilon)
    pull = jnp.sum(ssum_s[...], axis=1, keepdims=True) * (1.0 / E) * scale * scale * scale

    def gate_tile(index, carry):
        at = tile_at(index)
        heads_in = x_s[:, at]
        skip = wide_ref[0:1, at]
        gate = pa_ref[:, at]
        opened = jax.nn.sigmoid(gate)
        rows = yns_ref[:, at] + skip * heads_in
        gated = rows * (gate * opened)
        arrived = dxb_ref[:, at]
        d_gated = scale * (arrived * wide_ref[1:2, at]) - gated * pull
        small_ref[5:6, at] = jnp.sum(arrived * gated * scale, axis=0, keepdims=True)
        d_rows = d_gated * (gate * opened)
        pg_ref[:, at] = (d_gated * rows * silu_slope(gate, opened)).astype(bf16)
        small_ref[6:7, at] = jnp.sum(d_rows * heads_in, axis=0, keepdims=True)
        dyb_s[:, at] = d_rows.astype(bf16)
        dx_s[:, at] = skip * d_rows
        return carry

    lax.fori_loop(0, E // LANES, gate_tile, 0)

    def state_tile(index, carry):
        at = tile_from(E, index)
        pre = pre_ref[:, at]
        x_s[:, at] = pre * jax.nn.sigmoid(pre)
        return carry

    lax.fori_loop(0, 2, state_tile, 0)

    later = lax.broadcasted_iota(jnp.int32, (TOK, TOK), 1)
    early = lax.broadcasted_iota(jnp.int32, (TOK, TOK), 0)
    allowed_t = (later >= early) & (doc_col_ref[:, 0:1] == doc_row_ref[0:1, :])
    allowed = allowed_pairs(doc_col_ref, doc_row_ref)
    raw = pa_ref[:, AT_DT:] + head_ref[0:1, :]
    steps = softplus(raw)
    decay = head_ref[1:2, :]
    rates = -steps * decay
    totals = dot_exact(jnp.where(allowed, 1.0, 0.0), rates)
    totals_t = totals.T
    inward = x_s[:, E : E + NS].astype(bf16)
    outward = x_s[:, E + NS :].astype(bf16)
    cbt_s[...] = jnp.where(allowed_t, dot_nt(inward, outward), 0.0)
    dcbt_s[...] = jnp.zeros((TOK, TOK), f32)
    low = lane_low(TOK)
    spread_row = lax.broadcasted_iota(jnp.int32, (LANES, LANES), 0) >= HD
    spread_col = lax.broadcasted_iota(jnp.int32, (LANES, LANES), 1)
    sum_s[...] = jnp.zeros((TOK, LANES), f32)
    ssum_s[...] = jnp.zeros((TOK, LANES), f32)
    for pair in range(PAIRS):
        lanes = slice(pair * LANES, (pair + 1) * LANES)
        first = 2 * pair
        step_pair = jnp.where(low, steps[:, first : first + 1], steps[:, first + 1 : first + 2])
        heads_in = x_s[:, lanes]
        scaled = (heads_in * step_pair).astype(bf16)
        d_rows = dyb_s[:, lanes]
        halves = []
        for side, head in enumerate((first, first + 1)):
            chosen = low if side == 0 else jnp.logical_not(low)
            own = jnp.where(chosen, scaled, jnp.zeros_like(scaled))
            col = totals[:, head : head + 1]
            row = totals_t[head : head + 1, :]
            top = jnp.exp(jnp.minimum(row - col[:HALF], 0.0))
            end = jnp.exp(jnp.minimum(row[:, HALF:] - col[HALF:], 0.0))
            top_mix = (top * cbt_s[:HALF, :]).astype(bf16)
            end_mix = (end * cbt_s[HALF:, HALF:]).astype(bf16)
            dcbt_s[:HALF, :] += dot_nt(own[:HALF], d_rows) * top
            dcbt_s[HALF:, HALF:] += dot_nt(own[HALF:], d_rows[HALF:]) * end
            halves.append(
                jnp.concatenate(
                    [dot_nn(top_mix, d_rows), dot_nn(end_mix, d_rows[HALF:])], axis=0
                )
            )
        d_scaled = jnp.where(low, halves[0], halves[1])
        dx_s[:, lanes] += d_scaled * step_pair
        spread = (spread_col == jnp.where(spread_row, first + 1, first)).astype(bf16)
        for value, into in (
            (d_scaled * heads_in, sum_s),
            (d_rows.astype(f32) * yns_ref[:, lanes] - scaled.astype(f32) * d_scaled, ssum_s),
        ):
            coarse = value.astype(bf16)
            fine = (value - coarse.astype(f32)).astype(bf16)
            into[...] += dot_nn(coarse, spread) + dot_nn(fine, spread)

    d_rates = dot_exact(jnp.where(allowed_t, 1.0, 0.0), ssum_s[...])
    d_steps = sum_s[...] - decay * d_rates
    d_raw = d_steps * jax.nn.sigmoid(raw)
    pg_ref[:, AT_DT:] = d_raw.astype(bf16)
    small_ref[7:8, :LANES] = jnp.sum(d_raw, axis=0, keepdims=True)
    small_ref[7:8, LANES : 2 * LANES] = jnp.sum(d_rates * rates, axis=0, keepdims=True)
    d_pairs = jnp.where(allowed_t, dcbt_s[...], 0.0).astype(bf16)
    dx_s[:, E : E + NS] = dot_nn(d_pairs, outward)
    dx_s[:, E + NS :] = dot_tn(d_pairs, inward)

    def conv_tile(index, carry):
        at = tile_at(index)
        pre = pre_ref[:, at]
        d_pre = dx_s[:, at] * silu_slope(pre, jax.nn.sigmoid(pre))
        rows = pa_ref[:, tile_from(AT_W, index)]
        small_ref[4:5, at] = jnp.sum(d_pre, axis=0, keepdims=True)
        small_ref[3:4, at] = jnp.sum(d_pre * rows, axis=0, keepdims=True)
        back = taps_ref[3:4, at] * d_pre
        for shift in (1, 2, 3):
            held = mask_ref[:, (shift - 1) * LANES : shift * LANES] * d_pre
            small_ref[3 - shift : 4 - shift, at] = jnp.sum(
                held * pltpu.roll(rows, shift, 0), axis=0, keepdims=True
            )
            back = back + taps_ref[3 - shift : 4 - shift, at] * pltpu.roll(held, TOK - shift, 0)
        pg_ref[:, tile_from(AT_W, index)] = back.astype(bf16)
        return carry

    lax.fori_loop(0, CH // LANES, conv_tile, 0)

    cosine = rope_ref[:, :LANES]
    sine = rope_ref[:, LANES:]
    keys = both_halves(rope_turn(pa_ref[:, AT_K:AT_V], cosine, sine))
    values = both_halves(pa_ref[:, AT_V:AT_DT])
    keys = tuple(part.astype(bf16) for part in keys)
    values = tuple(part.astype(bf16) for part in values)
    root = 1.0 / math.sqrt(HD)
    d_keys = []
    d_values = []
    for group in range(KVH):
        key = keys[group]
        value = values[group]
        d_key = jnp.zeros((TOK, LANES), f32)
        d_value = jnp.zeros((TOK, LANES), f32)
        for pair in range(group * (AH // (2 * KVH)), (group + 1) * (AH // (2 * KVH))):
            at = AT_Q + pair * LANES
            turned = rope_turn(pa_ref[:, at : at + LANES], cosine, sine) * root
            arrived = dxb_ref[:, E + pair * LANES : E + (pair + 1) * LANES]
            halves = []
            for side in range(2):
                chosen = low if side == 0 else jnp.logical_not(low)
                query = jnp.where(chosen, turned, 0.0).astype(bf16)
                d_out = jnp.where(chosen, arrived, 0.0).astype(bf16)
                scores = jnp.where(allowed_t, dot_nt(key, query), -1e30)
                peak = jnp.max(scores, axis=0, keepdims=True)
                weights = jnp.exp(scores - peak)
                weights = weights * (1.0 / jnp.sum(weights, axis=0, keepdims=True))
                d_weights = dot_nt(value, d_out)
                offset = jnp.sum(weights * d_weights, axis=0, keepdims=True)
                d_scores = (weights * (d_weights - offset)).astype(bf16)
                d_value = d_value + dot_nn(weights.astype(bf16), d_out)
                d_key = d_key + dot_nn(d_scores, query)
                halves.append(dot_tn(d_scores, key))
            d_query = rope_back(jnp.where(low, halves[0], halves[1]) * root, cosine, sine)
            pg_ref[:, at : at + LANES] = d_query.astype(bf16)
        d_keys.append(d_key + pltpu.roll(d_key, HD, 1))
        d_values.append(d_value + pltpu.roll(d_value, HD, 1))
    d_key = rope_back(jnp.where(low, d_keys[0], d_keys[1]), cosine, sine)
    pg_ref[:, AT_K:AT_V] = d_key.astype(bf16)
    pg_ref[:, AT_V:AT_DT] = jnp.where(low, d_values[0], d_values[1]).astype(bf16)


def row_block(width):
    return pl.BlockSpec((None, TOK, width), lambda row: (row, 0, 0))


def whole_block(shape):
    return pl.BlockSpec(shape, lambda row: (0,) * len(shape))


def core_forward(projected, layout, params):
    rope, masks, doc_cols, doc_rows = layout
    taps, heads, wide = params
    rows = projected.shape[0]
    return pl.pallas_call(
        core_forward_kernel,
        grid=(rows,),
        in_specs=[
            row_block(WIDE_A),
            row_block(2 * LANES),
            row_block(3 * LANES),
            row_block(LANES),
            pl.BlockSpec((None, 8, TOK), lambda row: (row, 0, 0)),
            whole_block(taps.shape),
            whole_block(heads.shape),
            whole_block(wide.shape),
        ],
        out_specs=[row_block(MIXED), row_block(CH), row_block(E)],
        out_shape=[
            jax.ShapeDtypeStruct((rows, TOK, MIXED), bf16),
            jax.ShapeDtypeStruct((rows, TOK, CH), f32),
            jax.ShapeDtypeStruct((rows, TOK, E), f32),
        ],
        scratch_shapes=[
            pltpu.VMEM((TOK, CH), f32),
            pltpu.VMEM((TOK, TOK), f32),
            pltpu.VMEM((TOK, LANES), f32),
        ],
        compiler_params=pltpu.CompilerParams(vmem_limit_bytes=48 * 2**20),
        cost_estimate=pl.CostEstimate(
            flops=rows * 4 * 10**8, bytes_accessed=rows * 12 * 2**20, transcendentals=rows * 10**6
        ),
        name="core_forward",
    )(projected, rope, masks, doc_cols, doc_rows, taps, heads, wide)


def core_backward(row, projected, pre, yns, d_mixed, layout, params):
    rope, masks, doc_cols, doc_rows = layout
    taps, heads, wide = params

    def picked(width, depth=TOK):
        return pl.BlockSpec((None, depth, width), lambda step, pick: (pick[0], 0, 0))

    def plain(shape):
        return pl.BlockSpec(shape, lambda step, pick: (0,) * len(shape))

    return pl.pallas_call(
        core_backward_kernel,
        grid_spec=pltpu.PrefetchScalarGridSpec(
            num_scalar_prefetch=1,
            grid=(1,),
            in_specs=[
                picked(WIDE_A),
                picked(CH),
                picked(E),
                plain((TOK, MIXED)),
                picked(2 * LANES),
                picked(3 * LANES),
                picked(LANES),
                picked(TOK, 8),
                plain(taps.shape),
                plain(heads.shape),
                plain(wide.shape),
            ],
            out_specs=[plain((TOK, WIDE_A)), plain((8, CH))],
            scratch_shapes=[
                pltpu.VMEM((TOK, CH), f32),
                pltpu.VMEM((TOK, CH), f32),
                pltpu.VMEM((TOK, E), bf16),
                pltpu.VMEM((TOK, TOK), f32),
                pltpu.VMEM((TOK, TOK), f32),
                pltpu.VMEM((TOK, LANES), f32),
                pltpu.VMEM((TOK, LANES), f32),
            ],
        ),
        out_shape=[
            jax.ShapeDtypeStruct((TOK, WIDE_A), bf16),
            jax.ShapeDtypeStruct((8, CH), f32),
        ],
        compiler_params=pltpu.CompilerParams(vmem_limit_bytes=48 * 2**20),
        cost_estimate=pl.CostEstimate(
            flops=10**9, bytes_accessed=16 * 2**20, transcendentals=2 * 10**6
        ),
        name="core_backward",
    )(
        row, projected, pre, yns, d_mixed, rope, masks, doc_cols, doc_rows,
        taps, heads, wide,
    )


def passed_along(value, axis, steps):
    count = lax.axis_size(axis)
    leading, last = (max(0, -steps), min(count, count - steps))
    return lax.ppermute(value, axis, [(source, source + steps) for source in range(leading, last)])


def norm_rows(values):
    return lax.rsqrt(jnp.mean(values * values, axis=-1, keepdims=True) + epsilon)


def norm_back(values, gain, arrived):
    scale = norm_rows(values)
    weighted = arrived * gain
    pull = jnp.mean(weighted * values, axis=-1, keepdims=True) * scale * scale * scale
    gain_grad = jnp.sum(arrived * values * scale, axis=0, keepdims=True)
    return (weighted * scale - values * pull, gain_grad)


def project_kernel(rows_ref, gain_ref, own_ref, other_ref, normed_ref, out_ref):
    @pl.when(pl.program_id(0) == 0)
    def _():
        rows = rows_ref[...].astype(f32)
        normed_ref[...] = (rows * norm_rows(rows) * gain_ref[...]).astype(bf16)

    out_ref[...] = dot_nn(normed_ref[:, :SIDE], own_ref[...]) + dot_nn(
        normed_ref[:, SIDE:], other_ref[...]
    )


def project(rows, gain, own, other):
    count = rows.shape[0]
    tile = WIDE_A // 3
    weight = pl.BlockSpec((SIDE, tile), lambda step: (0, step))
    return pl.pallas_call(
        project_kernel,
        grid=(3,),
        in_specs=[whole_block((count, D)), whole_block((1, D)), weight, weight],
        out_specs=[whole_block((count, D)), pl.BlockSpec((count, tile), lambda step: (0, step))],
        out_shape=[
            jax.ShapeDtypeStruct((count, D), bf16),
            jax.ShapeDtypeStruct((count, WIDE_A), f32),
        ],
        compiler_params=pltpu.CompilerParams(vmem_limit_bytes=40 * 2**20),
        cost_estimate=pl.CostEstimate(
            flops=2 * count * D * WIDE_A,
            bytes_accessed=2 * D * WIDE_A + 4 * count * WIDE_A,
            transcendentals=0,
        ),
        name="project",
    )(rows, gain, own, other)


def feed_forward_kernel(
    keep, rows_ref, mixed_ref, gain_ref,
    out_own, out_other, gate_own, gate_other, up_own, up_other, down_own, down_other,
    *refs,
):
    if keep:
        low_ref, middle_ref, normed_ref, gate_ref, up_ref, act_ref, total_s = refs
    else:
        low_ref, middle_ref, normed_ref, total_s = refs
    step = pl.program_id(0)

    @pl.when(step == 0)
    def _():
        middle_ref[...] = rows_ref[...].astype(f32)

    @pl.when(step < 4)
    def _():
        mixed = mixed_ref[...]
        middle_ref[:, :SIDE] += dot_nt(mixed, out_own[...])
        middle_ref[:, SIDE:] += dot_nt(mixed, out_other[...])

    @pl.when(step == 3)
    def _():
        middle = middle_ref[...]
        normed_ref[...] = (middle * norm_rows(middle) * gain_ref[...]).astype(bf16)
        total_s[...] = middle

    @pl.when(step >= 4)
    def _():
        left = normed_ref[:, :SIDE]
        right = normed_ref[:, SIDE:]
        gate = dot_nn(left, gate_own[...]) + dot_nn(right, gate_other[...])
        up = dot_nn(left, up_own[...]) + dot_nn(right, up_other[...])
        act = (gate * jax.nn.sigmoid(gate) * up).astype(bf16)
        if keep:
            gate_ref[...] = gate
            up_ref[...] = up
            act_ref[...] = act
        total_s[:, :SIDE] += dot_nt(act, down_own[...])
        total_s[:, SIDE:] += dot_nt(act, down_other[...])

    @pl.when(step == 7)
    def _():
        low_ref[...] = total_s[...].astype(bf16)


def b_block(start, skipped):
    return pl.BlockSpec(
        (SIDE, 512), lambda step, *pick: (0, start + jnp.clip(step - skipped, 0, 3))
    )


def b_blocks(parts):
    return [b_block(start, skipped) for start, skipped in parts for _ in range(2)]


def feed_forward(rows, mixed, gain, own, other, own_down, other_down, keep):
    count = rows.shape[0]
    wide = pl.BlockSpec((count, 512), lambda step: (0, jnp.clip(step - 4, 0, 3)))
    out_specs = [whole_block((count, D))]
    out_shape = [jax.ShapeDtypeStruct((count, D), bf16)]
    scratch = [pltpu.VMEM((count, D), f32)]
    if keep:
        out_specs += [whole_block((count, D)), whole_block((count, D)), wide, wide, wide]
        out_shape += [
            jax.ShapeDtypeStruct((count, D), f32),
            jax.ShapeDtypeStruct((count, D), bf16),
            jax.ShapeDtypeStruct((count, FF), f32),
            jax.ShapeDtypeStruct((count, FF), f32),
            jax.ShapeDtypeStruct((count, FF), bf16),
        ]
    else:
        scratch = [pltpu.VMEM((count, D), f32), pltpu.VMEM((count, D), bf16)] + scratch
    return pl.pallas_call(
        functools.partial(feed_forward_kernel, keep),
        grid=(8,),
        in_specs=[
            whole_block((count, D)),
            pl.BlockSpec((count, 512), lambda step: (0, jnp.clip(step, 0, 3))),
            whole_block((1, D)),
        ]
        + b_blocks(((0, 0), (4, 4), (8, 4), (0, 4))),
        out_specs=out_specs,
        out_shape=out_shape,
        scratch_shapes=scratch,
        compiler_params=pltpu.CompilerParams(vmem_limit_bytes=48 * 2**20),
        cost_estimate=pl.CostEstimate(
            flops=2 * count * D * WIDE_B, bytes_accessed=2 * D * WIDE_B, transcendentals=0
        ),
        name="feed_forward",
    )(rows, mixed, gain, *([own, other] * 3), own_down, other_down)


def feed_back_kernel(
    pick_ref, cot_ref, gate_ref, up_ref, middle_ref, gain_ref,
    down_own, down_other, gate_own, gate_other, up_own, up_other, out_own, out_other,
    d_gate_ref, d_up_ref, d_middle_ref, low_ref, d_mixed_ref, gain_grad_ref,
    total_s,
):
    step = pl.program_id(0)

    @pl.when(step == 0)
    def _():
        total_s[...] = jnp.zeros_like(total_s)

    @pl.when(step < 4)
    def _():
        arrived = dot_nn(cot_ref[:, :SIDE], down_own[...]) + dot_nn(
            cot_ref[:, SIDE:], down_other[...]
        )
        gate = gate_ref[...]
        opened = jax.nn.sigmoid(gate)
        d_gate = (arrived * up_ref[...] * silu_slope(gate, opened)).astype(bf16)
        d_up = (arrived * (gate * opened)).astype(bf16)
        d_gate_ref[...] = d_gate
        d_up_ref[...] = d_up
        total_s[:, :SIDE] += dot_nt(d_gate, gate_own[...]) + dot_nt(d_up, up_own[...])
        total_s[:, SIDE:] += dot_nt(d_gate, gate_other[...]) + dot_nt(d_up, up_other[...])

    @pl.when(step == 3)
    def _():
        d_norm, gain_grad = norm_back(middle_ref[...], gain_ref[...], total_s[...])
        d_middle = cot_ref[...].astype(f32) + d_norm
        d_middle_ref[...] = d_middle
        low_ref[...] = d_middle.astype(bf16)
        gain_grad_ref[...] = gain_grad

    @pl.when(step >= 4)
    def _():
        d_mixed_ref[...] = dot_nn(low_ref[:, :SIDE], out_own[...]) + dot_nn(
            low_ref[:, SIDE:], out_other[...]
        )


def feed_back(row, cotangent, gate, up, middle, gain, own, other, own_down, other_down):
    saved = pl.BlockSpec((TOK, 512), lambda step, pick: (pick[0], jnp.clip(step, 0, 3)))
    early = pl.BlockSpec((TOK, 512), lambda step, pick: (0, jnp.clip(step, 0, 3)))
    late = pl.BlockSpec((TOK, 512), lambda step, pick: (0, jnp.clip(step - 4, 0, 3)))
    full = pl.BlockSpec((TOK, D), lambda step, pick: (0, 0))
    gain_block = pl.BlockSpec((1, D), lambda step, pick: (0, 0))
    return pl.pallas_call(
        feed_back_kernel,
        grid_spec=pltpu.PrefetchScalarGridSpec(
            num_scalar_prefetch=1,
            grid=(8,),
            in_specs=[
                full,
                saved,
                saved,
                pl.BlockSpec((TOK, D), lambda step, pick: (pick[0], 0)),
                gain_block,
            ]
            + b_blocks(((0, 0), (4, 0), (8, 0), (0, 4))),
            out_specs=[early, early, full, full, late, gain_block],
            scratch_shapes=[pltpu.VMEM((TOK, D), f32)],
        ),
        out_shape=[
            jax.ShapeDtypeStruct((TOK, FF), bf16),
            jax.ShapeDtypeStruct((TOK, FF), bf16),
            jax.ShapeDtypeStruct((TOK, D), f32),
            jax.ShapeDtypeStruct((TOK, D), bf16),
            jax.ShapeDtypeStruct((TOK, MIXED), f32),
            jax.ShapeDtypeStruct((1, D), f32),
        ],
        compiler_params=pltpu.CompilerParams(vmem_limit_bytes=48 * 2**20),
        cost_estimate=pl.CostEstimate(
            flops=2 * TOK * D * WIDE_B, bytes_accessed=2 * D * WIDE_B, transcendentals=0
        ),
        name="feed_back",
    )(row, cotangent, gate, up, middle, gain, own_down, other_down, *([own, other] * 3))


def project_back_kernel(
    pick_ref, grad_ref, rows_ref, d_middle_ref, gain_ref, own_ref, other_ref,
    d_rows_ref, low_ref, gain_grad_ref, total_s,
):
    step = pl.program_id(0)

    @pl.when(step == 0)
    def _():
        total_s[...] = jnp.zeros_like(total_s)

    total_s[:, :SIDE] += dot_nt(grad_ref[...], own_ref[...])
    total_s[:, SIDE:] += dot_nt(grad_ref[...], other_ref[...])

    @pl.when(step == 2)
    def _():
        d_norm, gain_grad = norm_back(rows_ref[...].astype(f32), gain_ref[...], total_s[...])
        d_rows = d_middle_ref[...] + d_norm
        d_rows_ref[...] = d_rows
        low_ref[...] = d_rows.astype(bf16)
        gain_grad_ref[...] = gain_grad


def project_back(row, proj_low, start_rows, d_middle, gain, own, other):
    tile = WIDE_A // 3
    weight = pl.BlockSpec((SIDE, tile), lambda step, pick: (0, step))
    full = pl.BlockSpec((TOK, D), lambda step, pick: (0, 0))
    gain_block = pl.BlockSpec((1, D), lambda step, pick: (0, 0))
    return pl.pallas_call(
        project_back_kernel,
        grid_spec=pltpu.PrefetchScalarGridSpec(
            num_scalar_prefetch=1,
            grid=(3,),
            in_specs=[
                pl.BlockSpec((TOK, tile), lambda step, pick: (0, step)),
                pl.BlockSpec((TOK, D), lambda step, pick: (pick[0], 0)),
                full,
                gain_block,
                weight,
                weight,
            ],
            out_specs=[full, full, gain_block],
            scratch_shapes=[pltpu.VMEM((TOK, D), f32)],
        ),
        out_shape=[
            jax.ShapeDtypeStruct((TOK, D), f32),
            jax.ShapeDtypeStruct((TOK, D), bf16),
            jax.ShapeDtypeStruct((1, D), f32),
        ],
        compiler_params=pltpu.CompilerParams(vmem_limit_bytes=40 * 2**20),
        cost_estimate=pl.CostEstimate(
            flops=2 * TOK * D * WIDE_A, bytes_accessed=2 * D * WIDE_A, transcendentals=0
        ),
        name="project_back",
    )(row, proj_low, start_rows, d_middle, gain, own, other)


def weight_grad_kernel(groups, pick_ref, *refs):
    lefts = refs[: 4 * len(groups)]
    rights = refs[4 * len(groups) : 8 * len(groups)]
    sum_ref, left_s = refs[8 * len(groups) :]
    step = pl.program_id(0)
    for index, (start, count) in enumerate(groups):
        four = lefts[4 * index : 4 * index + 4]
        blocks = rights[4 * index : 4 * index + 4]

        @pl.when(step == start)
        def _(four=four):
            for place, ref in enumerate(four):
                left_s[:, place * TOK : (place + 1) * TOK] = ref[...].astype(f32).T.astype(bf16)

        @pl.when((step >= start) & (step < start + count))
        def _(blocks=blocks):
            right = jnp.concatenate([ref[...] for ref in blocks], axis=0)
            sum_ref[...] = dot_nn(left_s[...], right).astype(bf16)


def weight_grad(picks, tile, groups):
    steps = []
    in_left = []
    in_right = []
    operands_left = []
    operands_right = []
    start = 0
    for left, right in groups:
        count = right[0][0].shape[1] // tile
        steps.append((start, count))
        for array, which, column in left:
            in_left.append(
                pl.BlockSpec(
                    (TOK, SIDE),
                    lambda step, pick, which=which, column=column: (
                        0 if which is None else pick[which],
                        column,
                    ),
                )
            )
            operands_left.append(array)
        for array, which in right:
            in_right.append(
                pl.BlockSpec(
                    (TOK, tile),
                    lambda step, pick, which=which, start=start, count=count: (
                        0 if which is None else pick[which],
                        jnp.clip(step - start, 0, count - 1),
                    ),
                )
            )
            operands_right.append(array)
        start += count
    return pl.pallas_call(
        functools.partial(weight_grad_kernel, tuple(steps)),
        grid_spec=pltpu.PrefetchScalarGridSpec(
            num_scalar_prefetch=1,
            grid=(start,),
            in_specs=in_left + in_right,
            out_specs=pl.BlockSpec((SIDE, tile), lambda step, pick: (0, step)),
            scratch_shapes=[pltpu.VMEM((SIDE, 4 * TOK), bf16)],
        ),
        out_shape=jax.ShapeDtypeStruct((SIDE, start * tile), bf16),
        compiler_params=pltpu.CompilerParams(vmem_limit_bytes=56 * 2**20),
        cost_estimate=pl.CostEstimate(
            flops=8 * TOK * SIDE * start * tile,
            bytes_accessed=4 * SIDE * start * tile,
            transcendentals=0,
        ),
        name="weight_grad",
    )(picks, *operands_left, *operands_right)


def row_layout(doc_ids):
    rows = doc_ids.shape[0]
    positions = jnp.arange(TOK, dtype=jnp.int32)
    earlier = jnp.sum((doc_ids[:, None, :] < doc_ids[:, :, None]).astype(jnp.int32), axis=2)
    places = positions[None, :] - earlier
    half_dim = HD // 2
    inverse_freq = rope_base ** (-jnp.arange(half_dim, dtype=f32) / half_dim)
    angles = places.astype(f32)[:, :, None] * inverse_freq[None, None, :]
    repeats = LANES // half_dim
    rope = jnp.concatenate([jnp.cos(angles)] * repeats + [jnp.sin(angles)] * repeats, axis=-1)
    masks = jnp.concatenate(
        [
            jnp.broadcast_to((places >= shift).astype(f32)[:, :, None], (rows, TOK, LANES))
            for shift in (1, 2, 3)
        ],
        axis=-1,
    )
    doc_cols = jnp.broadcast_to(doc_ids[:, :, None], (rows, TOK, LANES))
    doc_rows = jnp.broadcast_to(doc_ids[:, None, :], (rows, 8, TOK))
    return (rope, masks, doc_cols, doc_rows)


def core_params(conv_weight, conv_bias, step_bias, decay_log, skip_scale, mixer_gain):
    taps = jnp.concatenate([conv_weight, conv_bias[None], jnp.zeros((3, CH), f32)], axis=0)
    heads = jnp.zeros((8, LANES), f32)
    heads = heads.at[0, :MH].set(step_bias).at[1, :MH].set(jnp.exp(decay_log))
    wide = jnp.concatenate(
        [jnp.repeat(skip_scale, MP)[None], mixer_gain[None], jnp.zeros((6, E), f32)], axis=0
    )
    return (taps, heads, wide)


def swapped(value):
    return lax.ppermute(value, "core", [(0, 1), (1, 0)])


def ring_order(chips):
    return [2 * step for step in range(chips // 2)] + [
        2 * step + 1 for step in reversed(range(chips // 2))
    ]


def ring_place(chip, chips):
    return jnp.where(chip % 2 == 0, chip // 2, chips - 1 - chip // 2)


def onward(value, steps):
    order = ring_order(lax.axis_size("chip"))
    chips = len(order)
    return lax.ppermute(
        value, "chip", [(order[at], order[(at + steps) % chips]) for at in range(chips)]
    )


def slot_offsets(chips):
    offsets = [0]
    for far in range(1, chips // 2):
        offsets += [-far, far]
    return offsets + [chips // 2]


def gather_steps(shard):
    chips = lax.axis_size("chip")
    half = shard.shape[0] // 2
    ahead = back = shard
    slots = [shard]
    for _ in range(1, chips // 2):
        ahead, back = onward(ahead, 1), onward(back, -1)
        slots += [ahead, back]
    return slots + [onward(ahead[:half], 1), onward(back[half:], -1)]


def ring_reduce(sums):
    chips = lax.axis_size("chip")
    size = sums.shape[0] // chips
    half = size // 2
    far = chips // 2

    def slot(index, start=0, stop=size):
        return sums[index * size + start : index * size + stop]

    ahead = onward(slot(chips - 1, 0, half), 1)
    back = onward(slot(chips - 1, half, size), -1)
    for left in range(far - 1, 0, -1):
        own_ahead = slot(2 * left).astype(f32)
        own_back = slot(2 * left - 1).astype(f32)
        ahead, back = ahead.astype(f32), back.astype(f32)
        if left == far - 1:
            ahead = jnp.pad(ahead, ((0, half), (0, 0)))
            back = jnp.pad(back, ((half, 0), (0, 0)))
        ahead = onward((own_ahead + ahead).astype(bf16), 1)
        back = onward((own_back + back).astype(bf16), -1)
    return slot(0).astype(f32) + ahead.astype(f32) + back.astype(f32)


def summed_small(value):
    chips = lax.axis_size("chip")
    if chips & (chips - 1):
        return lax.psum(value, ("chip", "core"))
    value = value + swapped(value)
    step = 1
    while step < chips:
        value = value + lax.ppermute(value, "chip", [(chip, chip ^ step) for chip in range(chips)])
        step *= 2
    return value


def ring_columns(core):
    chips = lax.axis_size("chip")
    place = ring_place(lax.axis_index("chip"), chips)
    own = []
    for offset in slot_offsets(chips):
        at = (place + offset) % chips
        own.append(jnp.where(at < chips // 2, 2 * at, 2 * (chips - 1 - at) + 1))
    own = jnp.stack(own)
    width = D // (2 * chips)
    starts = jnp.concatenate([2 * own + core, 2 * own + 1 - core]) * width
    wanted = (starts[:, None] + jnp.arange(width)[None, :]).reshape(D)
    return (jnp.arange(D)[:, None] == wanted[None, :]).astype(bf16)


def per_device(
    inputs, out_grad, doc_ids, row_live, pre_gain, mlp_gain, mixer_gain, conv_weight, conv_bias,
    step_bias, decay_log, skip_scale, mixer_in_weight, mixer_out_weight, query_weight, key_weight,
    value_weight, attend_weight, gate_up_weight, down_weight,
):
    is_first = lax.axis_index("section") == 0
    core = lax.axis_index("core")
    shard = mixer_in_weight.shape[1]
    packed_a = jnp.concatenate(
        [
            mixer_in_weight[0, :, :AT_Q],
            query_weight[0],
            key_weight[0],
            value_weight[0],
            mixer_in_weight[0, :, AT_Q:],
            jnp.zeros((shard, LANES - MH), bf16),
        ],
        axis=1,
    )
    packed_b = jnp.concatenate(
        [mixer_out_weight[0].T, attend_weight[0].T, gate_up_weight[0]], axis=1
    )
    packed_c = down_weight[0].T
    slots_a = gather_steps(packed_a)
    packed_b, slots_a[2] = lax.optimization_barrier((packed_b, slots_a[2]))
    slots_b = gather_steps(packed_b)
    packed_c, slots_b[2] = lax.optimization_barrier((packed_c, slots_b[2]))
    slots_c = gather_steps(packed_c)
    own_a = jnp.concatenate(slots_a, axis=0)
    own_b = jnp.concatenate(slots_b, axis=0)
    own_c = jnp.concatenate(slots_c, axis=0)
    pair_a = (own_a, swapped(own_a))
    pair_b = (own_b, swapped(own_b), own_c, swapped(own_c))

    layout = row_layout(doc_ids)
    params = core_params(
        conv_weight[0], conv_bias[0], step_bias[0], decay_log[0], skip_scale[0], mixer_gain[0]
    )
    turn = ring_columns(core)

    def own_order(values):
        if values.dtype == bf16:
            return dot_nn(values, turn).astype(bf16)
        return dot_exact(values, turn.astype(f32))

    def whole_order(values):
        if values.dtype == bf16:
            return dot_nt(values, turn).astype(bf16)
        return dot_exact(values, turn.astype(f32).T)

    pre_row = own_order(pre_gain)
    mlp_row = own_order(mlp_gain)
    first_rows = own_order(inputs)

    def mixed_of(projected):
        mixed, pre, yns = core_forward(projected.reshape(MB, TOK, WIDE_A), layout, params)
        return mixed.reshape(MB * TOK, MIXED), pre, yns

    _, projected = project(first_rows, pre_row, *pair_a)
    mixed, _, _ = mixed_of(projected)
    (handed,) = feed_forward(first_rows, mixed, mlp_row, *pair_b, keep=False)
    received = passed_along(handed, "section", 1)
    start_rows = jnp.where(is_first, first_rows, received)
    normed, projected = project(start_rows, pre_row, *pair_a)
    mixed, pre, yns = mixed_of(projected)
    result, middle, normed_two, gate, up, act = feed_forward(
        start_rows, mixed, mlp_row, *pair_b, keep=True
    )
    projected = projected.reshape(MB, TOK, WIDE_A)
    their_mixed = swapped(mixed)
    their_act = swapped(act)
    their_normed = swapped(normed[:, SIDE:])
    their_normed_two = swapped(normed_two[:, SIDE:])

    positions = jnp.arange(TOK, dtype=jnp.int32)
    live = (positions[None, :] < row_live[:, None]).reshape(MB * TOK, 1)
    from_loss = own_order(jnp.where(live, out_grad, jnp.zeros_like(out_grad)))

    received = jnp.zeros((TOK, D), bf16)
    lefts = []
    rights = []
    rows = []
    picks = jnp.where(is_first, jnp.array([1, 0]), jnp.array([0, 1])).astype(jnp.int32)

    def tick_left(which):
        return [(lefts[1][which], None, 0), (lefts[2][which], None, 0)] + [
            (lefts[1][which + 2], None, 0), (lefts[2][which + 2], None, 0)
        ]

    def tick_right(which):
        return [(rights[tick][which + far], None) for far in (0, 2) for tick in (1, 2)]

    def saved_left(own, their):
        return [(own, 0, 0), (own, 1, 0), (their, 0, 0), (their, 1, 0)]

    def saved_right(own, their):
        return [(own, 0), (own, 1), (their, 0), (their, 1)]

    for tick in range(3):
        row = jnp.where(is_first, (1, 1, 0)[tick], (1, 0, 1)[tick]).astype(jnp.int32).reshape(1)
        loss_row = (1, 0, 1)[tick]
        cotangent = jnp.where(
            is_first, received, from_loss[loss_row * TOK : (loss_row + 1) * TOK]
        )
        d_gate, d_up, d_middle, middle_low, d_mixed, mlp_grad = feed_back(
            row, cotangent, gate, up, middle, mlp_row, *pair_b
        )
        lefts.append(
            (cotangent, middle_low, swapped(cotangent[:, SIDE:]), swapped(middle_low[:, SIDE:]))
        )
        rights.append((d_gate, d_up, swapped(d_gate), swapped(d_up)))
        if tick == 2:
            sum_c = weight_grad(picks, 1024, [(tick_left(0), saved_right(act, their_act))])
            sum_b = weight_grad(
                picks,
                1024,
                [
                    (tick_left(1), saved_right(mixed, their_mixed)),
                    (saved_left(normed_two, their_normed_two), tick_right(0)),
                    (saved_left(normed_two, their_normed_two), tick_right(1)),
                ],
            )
            d_mixed, sum_b, sum_c = lax.optimization_barrier((d_mixed, sum_b, sum_c))
            share_c = ring_reduce(sum_c)
            share_b = ring_reduce(sum_b)
        proj_low, small = core_backward(row, projected, pre, yns, d_mixed, layout, params)
        their_low = swapped(proj_low)
        if tick == 2:
            (p_one, their_one), (p_two, their_two) = rows[1][1], (proj_low, their_low)
            sum_a = weight_grad(
                picks,
                WIDE_A // 3,
                [
                    (
                        saved_left(normed, their_normed),
                        [(p_one, None), (p_two, None), (their_one, None), (their_two, None)],
                    )
                ],
            )
            d_middle, sum_a = lax.optimization_barrier((d_middle, sum_a))
            share_a = ring_reduce(sum_a)
        d_rows, d_low, pre_grad = project_back(
            row, proj_low, start_rows, d_middle, pre_row, *pair_a
        )
        rows.append((d_rows, (proj_low, their_low), pre_grad, mlp_grad, small))
        if tick < 2:
            received = passed_along(d_low, "section", -1)

    start_grad = jnp.concatenate(
        [
            jnp.where(is_first, rows[2][0], rows[1][0]),
            jnp.where(is_first, rows[1][0], rows[2][0]),
        ],
        axis=0,
    )
    pre_sum, mlp_sum, small = (one + two for one, two in zip(rows[1][2:], rows[2][2:]))
    gain_sums = whole_order(jnp.concatenate([pre_sum, mlp_sum], axis=0))
    small = summed_small(
        jnp.concatenate([small, jnp.pad(gain_sums, ((0, 6), (0, CH - D)))], axis=0)
    )
    skip_sum = jnp.sum(small[6, :E].reshape(MH, MP), axis=1)
    mixer_in_grad = jnp.concatenate([share_a[:, :AT_Q], share_a[:, AT_DT : AT_DT + MH]], axis=1)
    return (
        whole_order(result)[None],
        whole_order(start_grad)[None],
        small[8:9, :D],
        small[9:10, :D],
        small[5:6, :E],
        small[None, :4],
        small[4:5],
        small[7:8, :MH],
        small[7:8, LANES : LANES + MH],
        skip_sum[None],
        mixer_in_grad[None],
        share_b[:, :E].T[None],
        share_a[:, AT_Q:AT_K][None],
        share_a[:, AT_K:AT_V][None],
        share_a[:, AT_V:AT_DT][None],
        share_b[:, E:MIXED].T[None],
        share_b[:, AT_GU:AT_DN][None],
        share_c.T[None],
    )


def solution(mesh):
    dp = mesh.shape["dp"]
    devices = mesh.devices.reshape(mesh.shape["section"], dp // 2, 2)
    paired = Mesh(devices, ("section", "chip", "core"))
    over = ("chip", "core")
    rows = P(over, None)
    small = P("section", None)
    by_row = P("section", over, None)
    by_col = P("section", None, over)
    small_specs = (small, small, small, P("section", None, None), small, small, small, small)
    big_specs = (by_row, by_col, by_row, by_row, by_row, by_col, by_row, by_col)
    in_specs = (rows, rows, rows, P(over)) + small_specs + big_specs
    out_specs = (by_row, by_row) + small_specs + big_specs
    return jax.shard_map(
        per_device, mesh=paired, in_specs=in_specs, out_specs=out_specs, check_vma=False
    )
```

```python
import functools
import math

import jax
import jax.numpy as jnp
from jax import lax
from jax.experimental import pallas as pl
from jax.experimental.pallas import tpu as pltpu
from jax.sharding import Mesh
from jax.sharding import PartitionSpec as P

D = 1024
FF = 2048
MH = 24
MP = 64
NS = 128
AH = 8
KVH = 2
HD = 64
MB = 2
TOK = 256
E = 1536
CH = 1792
HALF = TOK // 2
PAIRS = MH // 2
LANES = 128
SIDE = D // 2

AT_W = E
AT_Q = E + CH
AT_K = AT_Q + AH * HD
AT_V = AT_K + KVH * HD
AT_DT = AT_V + KVH * HD
WIDE_A = AT_DT + LANES
MIXED = E + AH * HD
AT_GU = MIXED
AT_DN = AT_GU + 2 * FF
WIDE_B = AT_DN + FF

highest = lax.Precision.HIGHEST
epsilon = 1e-05
rope_base = 100000000000.0
bf16 = jnp.bfloat16
f32 = jnp.float32


def dot_nn(left, right):
    return lax.dot_general(left, right, (((1,), (0,)), ((), ())), preferred_element_type=f32)


def dot_nt(left, right):
    return lax.dot_general(left, right, (((1,), (1,)), ((), ())), preferred_element_type=f32)


def dot_tn(left, right):
    return lax.dot_general(left, right, (((0,), (0,)), ((), ())), preferred_element_type=f32)


def dot_exact(left, right):
    return lax.dot_general(
        left, right, (((1,), (0,)), ((), ())), precision=highest, preferred_element_type=f32
    )


def softplus(value):
    return jnp.maximum(value, 0.0) + jnp.log1p(jnp.exp(-jnp.abs(value)))


def lane_low(rows):
    return lax.broadcasted_iota(jnp.int32, (rows, LANES), 1) < HD


def rope_halves(rows):
    return (lax.broadcasted_iota(jnp.int32, (rows, LANES), 1) & (HD - 1)) < HD // 2


def rope_turn(tile, cosine, sine):
    swapped = jnp.where(
        rope_halves(tile.shape[0]),
        -pltpu.roll(tile, LANES - HD // 2, 1),
        pltpu.roll(tile, HD // 2, 1),
    )
    return tile * cosine + swapped * sine


def rope_back(tile, cosine, sine):
    swapped = jnp.where(
        rope_halves(tile.shape[0]),
        pltpu.roll(tile, LANES - HD // 2, 1),
        -pltpu.roll(tile, HD // 2, 1),
    )
    return tile * cosine + swapped * sine


def both_halves(tile):
    swapped = pltpu.roll(tile, HD, 1)
    low = lane_low(tile.shape[0])
    return (jnp.where(low, tile, swapped), jnp.where(low, swapped, tile))


def tile_at(index):
    return pl.ds(pl.multiple_of(index * LANES, LANES), LANES)


def tile_from(start, index):
    return pl.ds(pl.multiple_of(start + index * LANES, LANES), LANES)


def allowed_pairs(doc_col_ref, doc_row_ref):
    later = lax.broadcasted_iota(jnp.int32, (TOK, TOK), 0)
    early = lax.broadcasted_iota(jnp.int32, (TOK, TOK), 1)
    same = doc_col_ref[:, 0:1] == doc_row_ref[0:1, :]
    return (later >= early) & same


def core_forward_kernel(
    pa_ref, rope_ref, mask_ref, doc_col_ref, doc_row_ref, taps_ref, head_ref, wide_ref,
    xb_ref, pre_ref, yns_ref,
    conv_s, cb_s, sum_s,
):
    def conv_tile(index, carry):
        rows = pa_ref[:, tile_from(AT_W, index)]
        at = tile_at(index)
        total = taps_ref[4:5, at] + taps_ref[3:4, at] * rows
        for shift in (1, 2, 3):
            moved = mask_ref[:, (shift - 1) * LANES : shift * LANES] * pltpu.roll(rows, shift, 0)
            total = total + taps_ref[3 - shift : 4 - shift, at] * moved
        pre_ref[:, at] = total
        conv_s[:, at] = total * jax.nn.sigmoid(total)
        return carry

    lax.fori_loop(0, CH // LANES, conv_tile, 0)

    allowed = allowed_pairs(doc_col_ref, doc_row_ref)
    steps = softplus(pa_ref[:, AT_DT:] + head_ref[0:1, :])
    rates = -steps * head_ref[1:2, :]
    totals = dot_exact(jnp.where(allowed, 1.0, 0.0), rates)
    totals_t = totals.T
    inward = conv_s[:, E : E + NS].astype(bf16)
    outward = conv_s[:, E + NS :].astype(bf16)
    cb_s[...] = jnp.where(allowed, dot_nt(outward, inward), 0.0)
    low = lane_low(TOK)
    for pair in range(PAIRS):
        lanes = slice(pair * LANES, (pair + 1) * LANES)
        first = 2 * pair
        step_pair = jnp.where(low, steps[:, first : first + 1], steps[:, first + 1 : first + 2])
        scaled = (conv_s[:, lanes] * step_pair).astype(bf16)
        halves = []
        for head in (first, first + 1):
            col = totals[:, head : head + 1]
            row = totals_t[head : head + 1, :]
            top = jnp.exp(jnp.minimum(col[:HALF] - row[:, :HALF], 0.0)) * cb_s[:HALF, :HALF]
            end = jnp.exp(jnp.minimum(col[HALF:] - row, 0.0)) * cb_s[HALF:, :]
            halves.append(
                jnp.concatenate(
                    [dot_nn(top.astype(bf16), scaled[:HALF]), dot_nn(end.astype(bf16), scaled)],
                    axis=0,
                )
            )
        yns_ref[:, lanes] = jnp.where(low, halves[0], halves[1])

    sum_s[...] = jnp.zeros((TOK, LANES), f32)

    def gate_tile(index, carry):
        at = tile_at(index)
        gate = pa_ref[:, at]
        rows = yns_ref[:, at] + wide_ref[0:1, at] * conv_s[:, at]
        gated = rows * (gate * jax.nn.sigmoid(gate))
        sum_s[...] += gated * gated
        conv_s[:, at] = gated
        return carry

    lax.fori_loop(0, E // LANES, gate_tile, 0)
    scale = lax.rsqrt(jnp.sum(sum_s[...], axis=1, keepdims=True) * (1.0 / E) + epsilon)

    def norm_tile(index, carry):
        at = tile_at(index)
        xb_ref[:, at] = (conv_s[:, at] * scale * wide_ref[1:2, at]).astype(bf16)
        return carry

    lax.fori_loop(0, E // LANES, norm_tile, 0)

    cosine = rope_ref[:, :LANES]
    sine = rope_ref[:, LANES:]
    keys = both_halves(rope_turn(pa_ref[:, AT_K:AT_V], cosine, sine))
    values = both_halves(pa_ref[:, AT_V:AT_DT])
    keys = tuple(part.astype(bf16) for part in keys)
    values = tuple(part.astype(bf16) for part in values)
    for pair in range(AH // 2):
        group = pair // (AH // (2 * KVH))
        at = AT_Q + pair * LANES
        turned = rope_turn(pa_ref[:, at : at + LANES], cosine, sine) * (1.0 / math.sqrt(HD))
        halves = []
        for side in range(2):
            chosen = low if side == 0 else jnp.logical_not(low)
            query = jnp.where(chosen, turned, 0.0).astype(bf16)
            parts = []
            for rows, cols in ((slice(0, HALF), HALF), (slice(HALF, TOK), TOK)):
                scores = dot_nt(query[rows], keys[group][:cols])
                scores = jnp.where(allowed[rows, :cols], scores, -1e30)
                top = jnp.max(scores, axis=1, keepdims=True)
                weights = jnp.exp(scores - top)
                share = 1.0 / jnp.sum(weights, axis=1, keepdims=True)
                parts.append(dot_nn(weights.astype(bf16), values[group][:cols]) * share)
            halves.append(jnp.concatenate(parts, axis=0))
        out = jnp.where(low, halves[0], halves[1])
        xb_ref[:, E + pair * LANES : E + (pair + 1) * LANES] = out.astype(bf16)


def silu_slope(value, gate):
    return gate * (1.0 + value * (1.0 - gate))


def core_backward_kernel(
    pick_ref,
    pa_ref, pre_ref, yns_ref, dxb_ref, rope_ref, mask_ref, doc_col_ref, doc_row_ref,
    taps_ref, head_ref, wide_ref,
    pg_ref, small_ref,
    x_s, dx_s, dyb_s, cbt_s, dcbt_s, sum_s, ssum_s,
):
    small_ref[...] = jnp.zeros_like(small_ref)
    sum_s[...] = jnp.zeros((TOK, LANES), f32)
    ssum_s[...] = jnp.zeros((TOK, LANES), f32)

    def start_tile(index, carry):
        at = tile_at(index)
        pre = pre_ref[:, at]
        heads_in = pre * jax.nn.sigmoid(pre)
        x_s[:, at] = heads_in
        gate = pa_ref[:, at]
        rows = yns_ref[:, at] + wide_ref[0:1, at] * heads_in
        gated = rows * (gate * jax.nn.sigmoid(gate))
        sum_s[...] += gated * gated
        ssum_s[...] += dxb_ref[:, at] * wide_ref[1:2, at] * gated
        return carry

    lax.fori_loop(0, E // LANES, start_tile, 0)
    scale = lax.rsqrt(jnp.sum(sum_s[...], axis=1, keepdims=True) * (1.0 / E) + epsilon)
    pull = jnp.sum(ssum_s[...], axis=1, keepdims=True) * (1.0 / E) * scale * scale * scale

    def gate_tile(index, carry):
        at = tile_at(index)
        heads_in = x_s[:, at]
        skip = wide_ref[0:1, at]
        gate = pa_ref[:, at]
        opened = jax.nn.sigmoid(gate)
        rows = yns_ref[:, at] + skip * heads_in
        gated = rows * (gate * opened)
        arrived = dxb_ref[:, at]
        d_gated = scale * (arrived * wide_ref[1:2, at]) - gated * pull
        small_ref[5:6, at] = jnp.sum(arrived * gated * scale, axis=0, keepdims=True)
        d_rows = d_gated * (gate * opened)
        pg_ref[:, at] = (d_gated * rows * silu_slope(gate, opened)).astype(bf16)
        small_ref[6:7, at] = jnp.sum(d_rows * heads_in, axis=0, keepdims=True)
        dyb_s[:, at] = d_rows.astype(bf16)
        dx_s[:, at] = skip * d_rows
        return carry

    lax.fori_loop(0, E // LANES, gate_tile, 0)

    def state_tile(index, carry):
        at = tile_from(E, index)
        pre = pre_ref[:, at]
        x_s[:, at] = pre * jax.nn.sigmoid(pre)
        return carry

    lax.fori_loop(0, 2, state_tile, 0)

    later = lax.broadcasted_iota(jnp.int32, (TOK, TOK), 1)
    early = lax.broadcasted_iota(jnp.int32, (TOK, TOK), 0)
    allowed_t = (later >= early) & (doc_col_ref[:, 0:1] == doc_row_ref[0:1, :])
    allowed = allowed_pairs(doc_col_ref, doc_row_ref)
    raw = pa_ref[:, AT_DT:] + head_ref[0:1, :]
    steps = softplus(raw)
    decay = head_ref[1:2, :]
    rates = -steps * decay
    totals = dot_exact(jnp.where(allowed, 1.0, 0.0), rates)
    totals_t = totals.T
    inward = x_s[:, E : E + NS].astype(bf16)
    outward = x_s[:, E + NS :].astype(bf16)
    cbt_s[...] = jnp.where(allowed_t, dot_nt(inward, outward), 0.0)
    dcbt_s[...] = jnp.zeros((TOK, TOK), f32)
    low = lane_low(TOK)
    spread_row = lax.broadcasted_iota(jnp.int32, (LANES, LANES), 0) >= HD
    spread_col = lax.broadcasted_iota(jnp.int32, (LANES, LANES), 1)
    sum_s[...] = jnp.zeros((TOK, LANES), f32)
    ssum_s[...] = jnp.zeros((TOK, LANES), f32)
    for pair in range(PAIRS):
        lanes = slice(pair * LANES, (pair + 1) * LANES)
        first = 2 * pair
        step_pair = jnp.where(low, steps[:, first : first + 1], steps[:, first + 1 : first + 2])
        heads_in = x_s[:, lanes]
        scaled = (heads_in * step_pair).astype(bf16)
        d_rows = dyb_s[:, lanes]
        halves = []
        for side, head in enumerate((first, first + 1)):
            chosen = low if side == 0 else jnp.logical_not(low)
            own = jnp.where(chosen, scaled, jnp.zeros_like(scaled))
            col = totals[:, head : head + 1]
            row = totals_t[head : head + 1, :]
            top = jnp.exp(jnp.minimum(row - col[:HALF], 0.0))
            end = jnp.exp(jnp.minimum(row[:, HALF:] - col[HALF:], 0.0))
            top_mix = (top * cbt_s[:HALF, :]).astype(bf16)
            end_mix = (end * cbt_s[HALF:, HALF:]).astype(bf16)
            dcbt_s[:HALF, :] += dot_nt(own[:HALF], d_rows) * top
            dcbt_s[HALF:, HALF:] += dot_nt(own[HALF:], d_rows[HALF:]) * end
            halves.append(
                jnp.concatenate(
                    [dot_nn(top_mix, d_rows), dot_nn(end_mix, d_rows[HALF:])], axis=0
                )
            )
        d_scaled = jnp.where(low, halves[0], halves[1])
        dx_s[:, lanes] += d_scaled * step_pair
        spread = (spread_col == jnp.where(spread_row, first + 1, first)).astype(bf16)
        for value, into in (
            (d_scaled * heads_in, sum_s),
            (d_rows.astype(f32) * yns_ref[:, lanes] - scaled.astype(f32) * d_scaled, ssum_s),
        ):
            coarse = value.astype(bf16)
            fine = (value - coarse.astype(f32)).astype(bf16)
            into[...] += dot_nn(coarse, spread) + dot_nn(fine, spread)

    d_rates = dot_exact(jnp.where(allowed_t, 1.0, 0.0), ssum_s[...])
    d_steps = sum_s[...] - decay * d_rates
    d_raw = d_steps * jax.nn.sigmoid(raw)
    pg_ref[:, AT_DT:] = d_raw.astype(bf16)
    small_ref[7:8, :LANES] = jnp.sum(d_raw, axis=0, keepdims=True)
    small_ref[7:8, LANES : 2 * LANES] = jnp.sum(d_rates * rates, axis=0, keepdims=True)
    d_pairs = jnp.where(allowed_t, dcbt_s[...], 0.0).astype(bf16)
    dx_s[:, E : E + NS] = dot_nn(d_pairs, outward)
    dx_s[:, E + NS :] = dot_tn(d_pairs, inward)

    def conv_tile(index, carry):
        at = tile_at(index)
        pre = pre_ref[:, at]
        d_pre = dx_s[:, at] * silu_slope(pre, jax.nn.sigmoid(pre))
        rows = pa_ref[:, tile_from(AT_W, index)]
        small_ref[4:5, at] = jnp.sum(d_pre, axis=0, keepdims=True)
        small_ref[3:4, at] = jnp.sum(d_pre * rows, axis=0, keepdims=True)
        back = taps_ref[3:4, at] * d_pre
        for shift in (1, 2, 3):
            held = mask_ref[:, (shift - 1) * LANES : shift * LANES] * d_pre
            small_ref[3 - shift : 4 - shift, at] = jnp.sum(
                held * pltpu.roll(rows, shift, 0), axis=0, keepdims=True
            )
            back = back + taps_ref[3 - shift : 4 - shift, at] * pltpu.roll(held, TOK - shift, 0)
        pg_ref[:, tile_from(AT_W, index)] = back.astype(bf16)
        return carry

    lax.fori_loop(0, CH // LANES, conv_tile, 0)

    cosine = rope_ref[:, :LANES]
    sine = rope_ref[:, LANES:]
    keys = both_halves(rope_turn(pa_ref[:, AT_K:AT_V], cosine, sine))
    values = both_halves(pa_ref[:, AT_V:AT_DT])
    keys = tuple(part.astype(bf16) for part in keys)
    values = tuple(part.astype(bf16) for part in values)
    root = 1.0 / math.sqrt(HD)
    d_keys = []
    d_values = []
    for group in range(KVH):
        key = keys[group]
        value = values[group]
        d_key = jnp.zeros((TOK, LANES), f32)
        d_value = jnp.zeros((TOK, LANES), f32)
        for pair in range(group * (AH // (2 * KVH)), (group + 1) * (AH // (2 * KVH))):
            at = AT_Q + pair * LANES
            turned = rope_turn(pa_ref[:, at : at + LANES], cosine, sine) * root
            arrived = dxb_ref[:, E + pair * LANES : E + (pair + 1) * LANES]
            halves = []
            for side in range(2):
                chosen = low if side == 0 else jnp.logical_not(low)
                query = jnp.where(chosen, turned, 0.0).astype(bf16)
                d_out = jnp.where(chosen, arrived, 0.0).astype(bf16)
                scores = jnp.where(allowed_t, dot_nt(key, query), -1e30)
                peak = jnp.max(scores, axis=0, keepdims=True)
                weights = jnp.exp(scores - peak)
                weights = weights * (1.0 / jnp.sum(weights, axis=0, keepdims=True))
                d_weights = dot_nt(value, d_out)
                offset = jnp.sum(weights * d_weights, axis=0, keepdims=True)
                d_scores = (weights * (d_weights - offset)).astype(bf16)
                d_value = d_value + dot_nn(weights.astype(bf16), d_out)
                d_key = d_key + dot_nn(d_scores, query)
                halves.append(dot_tn(d_scores, key))
            d_query = rope_back(jnp.where(low, halves[0], halves[1]) * root, cosine, sine)
            pg_ref[:, at : at + LANES] = d_query.astype(bf16)
        d_keys.append(d_key + pltpu.roll(d_key, HD, 1))
        d_values.append(d_value + pltpu.roll(d_value, HD, 1))
    d_key = rope_back(jnp.where(low, d_keys[0], d_keys[1]), cosine, sine)
    pg_ref[:, AT_K:AT_V] = d_key.astype(bf16)
    pg_ref[:, AT_V:AT_DT] = jnp.where(low, d_values[0], d_values[1]).astype(bf16)


def row_block(width):
    return pl.BlockSpec((None, TOK, width), lambda row: (row, 0, 0))


def whole_block(shape):
    return pl.BlockSpec(shape, lambda row: (0,) * len(shape))


def core_forward(row, projected, layout, params, held=()):
    rope, masks, doc_cols, doc_rows = layout
    taps, heads, wide = params

    def block(width, depth=TOK):
        return pl.BlockSpec((None, depth, width), lambda step: (row, 0, 0))

    kernel = core_forward_kernel
    if held:
        def kernel(*refs):
            core_forward_kernel(*refs[:8], *refs[11:])

    return pl.pallas_call(
        kernel,
        grid=(1,),
        in_specs=[
            block(WIDE_A),
            block(2 * LANES),
            block(3 * LANES),
            block(LANES),
            block(TOK, 8),
            whole_block(taps.shape),
            whole_block(heads.shape),
            whole_block(wide.shape),
        ]
        + [pl.BlockSpec(memory_space=pl.ANY)] * len(held),
        out_specs=[block(MIXED), block(CH), block(E)],
        out_shape=[
            jax.ShapeDtypeStruct((MB, TOK, MIXED), bf16),
            jax.ShapeDtypeStruct((MB, TOK, CH), f32),
            jax.ShapeDtypeStruct((MB, TOK, E), f32),
        ],
        scratch_shapes=[
            pltpu.VMEM((TOK, CH), f32),
            pltpu.VMEM((TOK, TOK), f32),
            pltpu.VMEM((TOK, LANES), f32),
        ],
        input_output_aliases={8: 0, 9: 1, 10: 2} if held else {},
        compiler_params=pltpu.CompilerParams(vmem_limit_bytes=48 * 2**20),
        cost_estimate=pl.CostEstimate(
            flops=4 * 10**8, bytes_accessed=12 * 2**20, transcendentals=10**6
        ),
        name="core_forward",
    )(projected, rope, masks, doc_cols, doc_rows, taps, heads, wide, *held)


def core_backward(row, projected, pre, yns, d_mixed, layout, params):
    rope, masks, doc_cols, doc_rows = layout
    taps, heads, wide = params

    def picked(width, depth=TOK):
        return pl.BlockSpec((None, depth, width), lambda step, pick: (pick[0], 0, 0))

    def plain(shape):
        return pl.BlockSpec(shape, lambda step, pick: (0,) * len(shape))

    return pl.pallas_call(
        core_backward_kernel,
        grid_spec=pltpu.PrefetchScalarGridSpec(
            num_scalar_prefetch=1,
            grid=(1,),
            in_specs=[
                picked(WIDE_A),
                picked(CH),
                picked(E),
                plain((TOK, MIXED)),
                picked(2 * LANES),
                picked(3 * LANES),
                picked(LANES),
                picked(TOK, 8),
                plain(taps.shape),
                plain(heads.shape),
                plain(wide.shape),
            ],
            out_specs=[plain((TOK, WIDE_A)), plain((8, CH))],
            scratch_shapes=[
                pltpu.VMEM((TOK, CH), f32),
                pltpu.VMEM((TOK, CH), f32),
                pltpu.VMEM((TOK, E), bf16),
                pltpu.VMEM((TOK, TOK), f32),
                pltpu.VMEM((TOK, TOK), f32),
                pltpu.VMEM((TOK, LANES), f32),
                pltpu.VMEM((TOK, LANES), f32),
            ],
        ),
        out_shape=[
            jax.ShapeDtypeStruct((TOK, WIDE_A), bf16),
            jax.ShapeDtypeStruct((8, CH), f32),
        ],
        compiler_params=pltpu.CompilerParams(vmem_limit_bytes=48 * 2**20),
        cost_estimate=pl.CostEstimate(
            flops=10**9, bytes_accessed=16 * 2**20, transcendentals=2 * 10**6
        ),
        name="core_backward",
    )(
        row, projected, pre, yns, d_mixed, rope, masks, doc_cols, doc_rows,
        taps, heads, wide,
    )


def passed_along(value, axis, steps):
    count = lax.axis_size(axis)
    leading, last = (max(0, -steps), min(count, count - steps))
    return lax.ppermute(value, axis, [(source, source + steps) for source in range(leading, last)])


def norm_rows(values):
    return lax.rsqrt(jnp.mean(values * values, axis=-1, keepdims=True) + epsilon)


def norm_back(values, gain, arrived):
    scale = norm_rows(values)
    weighted = arrived * gain
    pull = jnp.mean(weighted * values, axis=-1, keepdims=True) * scale * scale * scale
    gain_grad = jnp.sum(arrived * values * scale, axis=0, keepdims=True)
    return (weighted * scale - values * pull, gain_grad)


def project_kernel(rows_ref, gain_ref, own_ref, other_ref, normed_ref, out_ref):
    @pl.when(pl.program_id(0) == 0)
    def _():
        rows = rows_ref[...].astype(f32)
        normed_ref[...] = (rows * norm_rows(rows) * gain_ref[...]).astype(bf16)

    out_ref[...] = dot_nn(normed_ref[:, :SIDE], own_ref[...]) + dot_nn(
        normed_ref[:, SIDE:], other_ref[...]
    )


def project(rows, gain, own, other, row=None, held=()):
    count = rows.shape[0]
    tile = WIDE_A // 3
    weight = pl.BlockSpec((SIDE, tile), lambda step: (0, step))
    at = row or 0
    total = count if row is None else MB * TOK
    kernel = project_kernel
    if held:
        def kernel(rows_ref, gain_ref, own_ref, other_ref, old_normed, old_out, *outs):
            project_kernel(rows_ref, gain_ref, own_ref, other_ref, *outs)

    return pl.pallas_call(
        kernel,
        grid=(3,),
        in_specs=[whole_block((count, D)), whole_block((1, D)), weight, weight]
        + [pl.BlockSpec(memory_space=pl.ANY)] * len(held),
        out_specs=[
            pl.BlockSpec((count, D), lambda step: (at, 0)),
            pl.BlockSpec((count, tile), lambda step: (at, step)),
        ],
        out_shape=[
            jax.ShapeDtypeStruct((total, D), bf16),
            jax.ShapeDtypeStruct((total, WIDE_A), f32),
        ],
        input_output_aliases={4: 0, 5: 1} if held else {},
        compiler_params=pltpu.CompilerParams(vmem_limit_bytes=40 * 2**20),
        cost_estimate=pl.CostEstimate(
            flops=2 * count * D * WIDE_A,
            bytes_accessed=2 * D * WIDE_A + 4 * count * WIDE_A,
            transcendentals=0,
        ),
        name="project",
    )(rows, gain, own, other, *held)


def feed_forward_kernel(
    keep, rows_ref, mixed_ref, gain_ref,
    out_own, out_other, gate_own, gate_other, up_own, up_other, down_own, down_other,
    *refs,
):
    if keep:
        low_ref, middle_ref, normed_ref, gate_ref, up_ref, act_ref, total_s = refs
    else:
        low_ref, middle_ref, normed_ref, total_s = refs
    step = pl.program_id(0)

    @pl.when(step == 0)
    def _():
        middle_ref[...] = rows_ref[...].astype(f32)

    @pl.when(step < 4)
    def _():
        mixed = mixed_ref[...]
        middle_ref[:, :SIDE] += dot_nt(mixed, out_own[...])
        middle_ref[:, SIDE:] += dot_nt(mixed, out_other[...])

    @pl.when(step == 3)
    def _():
        middle = middle_ref[...]
        normed_ref[...] = (middle * norm_rows(middle) * gain_ref[...]).astype(bf16)
        total_s[...] = middle

    @pl.when(step >= 4)
    def _():
        left = normed_ref[:, :SIDE]
        right = normed_ref[:, SIDE:]
        gate = dot_nn(left, gate_own[...]) + dot_nn(right, gate_other[...])
        up = dot_nn(left, up_own[...]) + dot_nn(right, up_other[...])
        act = (gate * jax.nn.sigmoid(gate) * up).astype(bf16)
        if keep:
            gate_ref[...] = gate
            up_ref[...] = up
            act_ref[...] = act
        total_s[:, :SIDE] += dot_nt(act, down_own[...])
        total_s[:, SIDE:] += dot_nt(act, down_other[...])

    @pl.when(step == 7)
    def _():
        low_ref[...] = total_s[...].astype(bf16)


def b_block(start, skipped):
    return pl.BlockSpec(
        (SIDE, 512), lambda step, *pick: (0, start + jnp.clip(step - skipped, 0, 3))
    )


def b_blocks(parts):
    return [b_block(start, skipped) for start, skipped in parts for _ in range(2)]


def feed_forward(rows, mixed, gain, own_b, other_b, own_c, other_c, keep):
    count = rows.shape[0]
    wide = pl.BlockSpec((count, 512), lambda step: (0, jnp.clip(step - 4, 0, 3)))
    out_specs = [whole_block((count, D))]
    out_shape = [jax.ShapeDtypeStruct((count, D), bf16)]
    scratch = [pltpu.VMEM((count, D), f32)]
    if keep:
        out_specs += [whole_block((count, D)), whole_block((count, D)), wide, wide, wide]
        out_shape += [
            jax.ShapeDtypeStruct((count, D), f32),
            jax.ShapeDtypeStruct((count, D), bf16),
            jax.ShapeDtypeStruct((count, FF), f32),
            jax.ShapeDtypeStruct((count, FF), f32),
            jax.ShapeDtypeStruct((count, FF), bf16),
        ]
    else:
        scratch = [pltpu.VMEM((count, D), f32), pltpu.VMEM((count, D), bf16)] + scratch
    return pl.pallas_call(
        functools.partial(feed_forward_kernel, keep),
        grid=(8,),
        in_specs=[
            whole_block((count, D)),
            pl.BlockSpec((count, 512), lambda step: (0, jnp.clip(step, 0, 3))),
            whole_block((1, D)),
        ]
        + b_blocks(((0, 0), (4, 4), (0, 4), (4, 4))),
        out_specs=out_specs,
        out_shape=out_shape,
        scratch_shapes=scratch,
        compiler_params=pltpu.CompilerParams(vmem_limit_bytes=48 * 2**20),
        cost_estimate=pl.CostEstimate(
            flops=2 * count * D * WIDE_B, bytes_accessed=2 * D * WIDE_B, transcendentals=0
        ),
        name="feed_forward",
    )(rows, mixed, gain, *([own_b, other_b] * 2), *([own_c, other_c] * 2))


def feed_back_kernel(
    pick_ref, cot_ref, gate_ref, up_ref, middle_ref, gain_ref,
    down_own, down_other, gate_own, gate_other, up_own, up_other, out_own, out_other,
    d_gate_ref, d_up_ref, d_middle_ref, low_ref, d_mixed_ref, gain_grad_ref,
    total_s,
):
    step = pl.program_id(0)

    @pl.when(step == 0)
    def _():
        total_s[...] = jnp.zeros_like(total_s)

    @pl.when(step < 4)
    def _():
        arrived = dot_nn(cot_ref[:, :SIDE], down_own[...]) + dot_nn(
            cot_ref[:, SIDE:], down_other[...]
        )
        gate = gate_ref[...]
        opened = jax.nn.sigmoid(gate)
        d_gate = (arrived * up_ref[...] * silu_slope(gate, opened)).astype(bf16)
        d_up = (arrived * (gate * opened)).astype(bf16)
        d_gate_ref[...] = d_gate
        d_up_ref[...] = d_up
        total_s[:, :SIDE] += dot_nt(d_gate, gate_own[...]) + dot_nt(d_up, up_own[...])
        total_s[:, SIDE:] += dot_nt(d_gate, gate_other[...]) + dot_nt(d_up, up_other[...])

    @pl.when(step == 3)
    def _():
        d_norm, gain_grad = norm_back(middle_ref[...], gain_ref[...], total_s[...])
        d_middle = cot_ref[...].astype(f32) + d_norm
        d_middle_ref[...] = d_middle
        low_ref[...] = d_middle.astype(bf16)
        gain_grad_ref[...] = gain_grad

    @pl.when(step >= 4)
    def _():
        d_mixed_ref[...] = dot_nn(low_ref[:, :SIDE], out_own[...]) + dot_nn(
            low_ref[:, SIDE:], out_other[...]
        )


def feed_back(row, cotangent, gate, up, middle, gain, own_b, other_b, own_c, other_c):
    saved = pl.BlockSpec((TOK, 512), lambda step, pick: (pick[0], jnp.clip(step, 0, 3)))
    early = pl.BlockSpec((TOK, 512), lambda step, pick: (0, jnp.clip(step, 0, 3)))
    late = pl.BlockSpec((TOK, 512), lambda step, pick: (0, jnp.clip(step - 4, 0, 3)))
    full = pl.BlockSpec((TOK, D), lambda step, pick: (0, 0))
    gain_block = pl.BlockSpec((1, D), lambda step, pick: (0, 0))
    return pl.pallas_call(
        feed_back_kernel,
        grid_spec=pltpu.PrefetchScalarGridSpec(
            num_scalar_prefetch=1,
            grid=(8,),
            in_specs=[
                full,
                saved,
                saved,
                pl.BlockSpec((TOK, D), lambda step, pick: (pick[0], 0)),
                gain_block,
            ]
            + b_blocks(((4, 0), (4, 0), (0, 0), (0, 4))),
            out_specs=[early, early, full, full, late, gain_block],
            scratch_shapes=[pltpu.VMEM((TOK, D), f32)],
        ),
        out_shape=[
            jax.ShapeDtypeStruct((TOK, FF), bf16),
            jax.ShapeDtypeStruct((TOK, FF), bf16),
            jax.ShapeDtypeStruct((TOK, D), f32),
            jax.ShapeDtypeStruct((TOK, D), bf16),
            jax.ShapeDtypeStruct((TOK, MIXED), f32),
            jax.ShapeDtypeStruct((1, D), f32),
        ],
        compiler_params=pltpu.CompilerParams(vmem_limit_bytes=48 * 2**20),
        cost_estimate=pl.CostEstimate(
            flops=2 * TOK * D * WIDE_B, bytes_accessed=2 * D * WIDE_B, transcendentals=0
        ),
        name="feed_back",
    )(
        row, cotangent, gate, up, middle, gain,
        own_c, other_c, own_b, other_b, own_c, other_c, own_b, other_b,
    )


def project_back_kernel(
    pick_ref, grad_ref, rows_ref, d_middle_ref, gain_ref, own_ref, other_ref,
    d_rows_ref, low_ref, gain_grad_ref, total_s,
):
    step = pl.program_id(0)

    @pl.when(step == 0)
    def _():
        total_s[...] = jnp.zeros_like(total_s)

    total_s[:, :SIDE] += dot_nt(grad_ref[...], own_ref[...])
    total_s[:, SIDE:] += dot_nt(grad_ref[...], other_ref[...])

    @pl.when(step == 2)
    def _():
        d_norm, gain_grad = norm_back(rows_ref[...].astype(f32), gain_ref[...], total_s[...])
        d_rows = d_middle_ref[...] + d_norm
        d_rows_ref[...] = d_rows
        low_ref[...] = d_rows.astype(bf16)
        gain_grad_ref[...] = gain_grad


def project_back(row, proj_low, start_rows, d_middle, gain, own, other):
    tile = WIDE_A // 3
    weight = pl.BlockSpec((SIDE, tile), lambda step, pick: (0, step))
    full = pl.BlockSpec((TOK, D), lambda step, pick: (0, 0))
    gain_block = pl.BlockSpec((1, D), lambda step, pick: (0, 0))
    return pl.pallas_call(
        project_back_kernel,
        grid_spec=pltpu.PrefetchScalarGridSpec(
            num_scalar_prefetch=1,
            grid=(3,),
            in_specs=[
                pl.BlockSpec((TOK, tile), lambda step, pick: (0, step)),
                pl.BlockSpec((TOK, D), lambda step, pick: (pick[0], 0)),
                full,
                gain_block,
                weight,
                weight,
            ],
            out_specs=[full, full, gain_block],
            scratch_shapes=[pltpu.VMEM((TOK, D), f32)],
        ),
        out_shape=[
            jax.ShapeDtypeStruct((TOK, D), f32),
            jax.ShapeDtypeStruct((TOK, D), bf16),
            jax.ShapeDtypeStruct((1, D), f32),
        ],
        compiler_params=pltpu.CompilerParams(vmem_limit_bytes=40 * 2**20),
        cost_estimate=pl.CostEstimate(
            flops=2 * TOK * D * WIDE_A, bytes_accessed=2 * D * WIDE_A, transcendentals=0
        ),
        name="project_back",
    )(row, proj_low, start_rows, d_middle, gain, own, other)


def weight_grad_kernel(groups, pick_ref, *refs):
    lefts = refs[: 4 * len(groups)]
    rights = refs[4 * len(groups) : 8 * len(groups)]
    sum_ref, left_s = refs[8 * len(groups) :]
    step = pl.program_id(0)
    for index, (start, count) in enumerate(groups):
        four = lefts[4 * index : 4 * index + 4]
        blocks = rights[4 * index : 4 * index + 4]

        @pl.when(step == start)
        def _(four=four):
            for place, ref in enumerate(four):
                left_s[:, place * TOK : (place + 1) * TOK] = ref[...].astype(f32).T.astype(bf16)

        @pl.when((step >= start) & (step < start + count))
        def _(blocks=blocks):
            right = jnp.concatenate([ref[...] for ref in blocks], axis=0)
            sum_ref[...] = dot_nn(left_s[...], right).astype(bf16)


def weight_grad(picks, tile, groups):
    steps = []
    in_left = []
    in_right = []
    operands_left = []
    operands_right = []
    start = 0
    for left, right in groups:
        count = right[0][0].shape[1] // tile
        steps.append((start, count))
        for array, which, column in left:
            in_left.append(
                pl.BlockSpec(
                    (TOK, SIDE),
                    lambda step, pick, which=which, column=column: (
                        0 if which is None else pick[which],
                        column,
                    ),
                )
            )
            operands_left.append(array)
        for array, which in right:
            in_right.append(
                pl.BlockSpec(
                    (TOK, tile),
                    lambda step, pick, which=which, start=start, count=count: (
                        0 if which is None else pick[which],
                        jnp.clip(step - start, 0, count - 1),
                    ),
                )
            )
            operands_right.append(array)
        start += count
    return pl.pallas_call(
        functools.partial(weight_grad_kernel, tuple(steps)),
        grid_spec=pltpu.PrefetchScalarGridSpec(
            num_scalar_prefetch=1,
            grid=(start,),
            in_specs=in_left + in_right,
            out_specs=pl.BlockSpec((SIDE, tile), lambda step, pick: (0, step)),
            scratch_shapes=[pltpu.VMEM((SIDE, 4 * TOK), bf16)],
        ),
        out_shape=jax.ShapeDtypeStruct((SIDE, start * tile), bf16),
        compiler_params=pltpu.CompilerParams(vmem_limit_bytes=56 * 2**20),
        cost_estimate=pl.CostEstimate(
            flops=8 * TOK * SIDE * start * tile,
            bytes_accessed=4 * SIDE * start * tile,
            transcendentals=0,
        ),
        name="weight_grad",
    )(picks, *operands_left, *operands_right)


def row_layout(doc_ids):
    rows = doc_ids.shape[0]
    positions = jnp.arange(TOK, dtype=jnp.int32)
    earlier = jnp.sum((doc_ids[:, None, :] < doc_ids[:, :, None]).astype(jnp.int32), axis=2)
    places = positions[None, :] - earlier
    half_dim = HD // 2
    inverse_freq = rope_base ** (-jnp.arange(half_dim, dtype=f32) / half_dim)
    angles = places.astype(f32)[:, :, None] * inverse_freq[None, None, :]
    repeats = LANES // half_dim
    rope = jnp.concatenate([jnp.cos(angles)] * repeats + [jnp.sin(angles)] * repeats, axis=-1)
    masks = jnp.concatenate(
        [
            jnp.broadcast_to((places >= shift).astype(f32)[:, :, None], (rows, TOK, LANES))
            for shift in (1, 2, 3)
        ],
        axis=-1,
    )
    doc_cols = jnp.broadcast_to(doc_ids[:, :, None], (rows, TOK, LANES))
    doc_rows = jnp.broadcast_to(doc_ids[:, None, :], (rows, 8, TOK))
    return (rope, masks, doc_cols, doc_rows)


def core_params(conv_weight, conv_bias, step_bias, decay_log, skip_scale, mixer_gain):
    taps = jnp.concatenate([conv_weight, conv_bias[None], jnp.zeros((3, CH), f32)], axis=0)
    heads = jnp.zeros((8, LANES), f32)
    heads = heads.at[0, :MH].set(step_bias).at[1, :MH].set(jnp.exp(decay_log))
    wide = jnp.concatenate(
        [jnp.repeat(skip_scale, MP)[None], mixer_gain[None], jnp.zeros((6, E), f32)], axis=0
    )
    return (taps, heads, wide)


def swapped(value):
    return lax.ppermute(value, "core", [(0, 1), (1, 0)])


def ring_order(chips):
    return [2 * step for step in range(chips // 2)] + [
        2 * step + 1 for step in reversed(range(chips // 2))
    ]


def ring_place(chip, chips):
    return jnp.where(chip % 2 == 0, chip // 2, chips - 1 - chip // 2)


def onward(value, steps):
    order = ring_order(lax.axis_size("chip"))
    chips = len(order)
    return lax.ppermute(
        value, "chip", [(order[at], order[(at + steps) % chips]) for at in range(chips)]
    )


def slot_offsets(chips):
    offsets = [0]
    for far in range(1, chips // 2):
        offsets += [-far, far]
    return offsets + [chips // 2]


def tied(*values):
    return lax.optimization_barrier(values)


class RingGather:
    def __init__(self, shard):
        self.slots = [shard]
        self.ahead = self.back = shard
        self.left = lax.axis_size("chip") // 2

    def operands(self):
        half = self.ahead.shape[0] // 2
        if self.left == 1:
            return self.ahead[:half], self.back[half:]
        return self.ahead, self.back

    def send(self, ahead, back):
        self.ahead, self.back = tied(onward(ahead, 1), onward(back, -1))
        self.slots += [self.ahead, self.back]
        self.left -= 1
        return self.ahead

    def step(self):
        return self.send(*self.operands())

    def last(self):
        while self.left > 1:
            self.step()

    def hold(self, value):
        self.ahead, self.back, _ = tied(self.ahead, self.back, value)
        self.slots[-2:] = [self.ahead, self.back]


class RingReduce:
    def __init__(self, sums):
        self.sums = sums
        self.chips = lax.axis_size("chip")
        self.size = sums.shape[0] // self.chips
        self.left = self.chips // 2
        self.ahead = self.back = None

    def slot(self, index, start=0, stop=None):
        stop = self.size if stop is None else stop
        return self.sums[index * self.size + start : index * self.size + stop]

    def operands(self):
        half = self.size // 2
        if self.ahead is None:
            last = self.chips - 1
            return self.slot(last, 0, half), self.slot(last, half)
        ahead, back = self.ahead.astype(f32), self.back.astype(f32)
        if self.left == self.chips // 2 - 1:
            ahead = jnp.pad(ahead, ((0, half), (0, 0)))
            back = jnp.pad(back, ((half, 0), (0, 0)))
        return (
            (self.slot(2 * self.left).astype(f32) + ahead).astype(bf16),
            (self.slot(2 * self.left - 1).astype(f32) + back).astype(bf16),
        )

    def send(self, ahead, back):
        self.ahead, self.back = tied(onward(ahead, 1), onward(back, -1))
        self.left -= 1
        return self.ahead

    def step(self):
        return self.send(*self.operands())

    def hold(self, value):
        self.ahead, self.back, _ = tied(self.ahead, self.back, value)

    def total(self):
        while self.left > 0:
            self.step()
        return self.slot(0).astype(f32) + self.ahead.astype(f32) + self.back.astype(f32)


def summed_small(value):
    chips = lax.axis_size("chip")
    if chips & (chips - 1):
        return lax.psum(value, ("chip", "core"))
    value = value + swapped(value)
    step = 1
    while step < chips:
        value = value + lax.ppermute(value, "chip", [(chip, chip ^ step) for chip in range(chips)])
        step *= 2
    return value


def ring_columns(core):
    chips = lax.axis_size("chip")
    place = ring_place(lax.axis_index("chip"), chips)
    own = []
    for offset in slot_offsets(chips):
        at = (place + offset) % chips
        own.append(jnp.where(at < chips // 2, 2 * at, 2 * (chips - 1 - at) + 1))
    own = jnp.stack(own)
    width = D // (2 * chips)
    starts = jnp.concatenate([2 * own + core, 2 * own + 1 - core]) * width
    wanted = (starts[:, None] + jnp.arange(width)[None, :]).reshape(D)
    return (jnp.arange(D)[:, None] == wanted[None, :]).astype(bf16)


def per_device(
    inputs, out_grad, doc_ids, row_live, pre_gain, mlp_gain, mixer_gain, conv_weight, conv_bias,
    step_bias, decay_log, skip_scale, mixer_in_weight, mixer_out_weight, query_weight, key_weight,
    value_weight, attend_weight, gate_up_weight, down_weight,
):
    is_first = lax.axis_index("section") == 0
    core = lax.axis_index("core")
    shard = mixer_in_weight.shape[1]
    packed_a = jnp.concatenate(
        [
            mixer_in_weight[0, :, :AT_Q],
            query_weight[0],
            key_weight[0],
            value_weight[0],
            mixer_in_weight[0, :, AT_Q:],
            jnp.zeros((shard, LANES - MH), bf16),
        ],
        axis=1,
    )
    packed_b = jnp.concatenate(
        [mixer_out_weight[0].T, attend_weight[0].T, gate_up_weight[0, :, :FF]], axis=1
    )
    packed_c = jnp.concatenate([gate_up_weight[0, :, FF:], down_weight[0].T], axis=1)

    layout = row_layout(doc_ids)
    params = core_params(
        conv_weight[0], conv_bias[0], step_bias[0], decay_log[0], skip_scale[0], mixer_gain[0]
    )
    turn = ring_columns(core)

    def own_order(values):
        if values.dtype == bf16:
            return dot_nn(values, turn).astype(bf16)
        return dot_exact(values, turn.astype(f32))

    def whole_order(values):
        if values.dtype == bf16:
            return dot_nt(values, turn).astype(bf16)
        return dot_exact(values, turn.astype(f32).T)

    pre_row = own_order(pre_gain)
    mlp_row = own_order(mlp_gain)
    first_rows = own_order(inputs)

    ring_a = RingGather(packed_a)
    ring_a.last()
    packed_b, packed_c, _ = tied(packed_b, packed_c, ring_a.ahead)
    ring_b = RingGather(packed_b)
    ring_b.step()
    ring_a.step()
    own_a = jnp.concatenate(ring_a.slots, axis=0)
    pair_a = (own_a, swapped(own_a))
    ring_c = RingGather(packed_c)

    def both_on(value):
        now_b, now_c, value = tied(ring_b.operands(), ring_c.operands(), value)
        ring_b.send(*now_b)
        ring_c.send(*now_c)
        return value

    both_on(pre_row)
    gain_now, _ = both_on((pre_row, pair_a[1]))
    _, projected = project(first_rows, gain_now, *pair_a)
    projected = projected.reshape(MB, TOK, WIDE_A)
    mixed = core_forward(0, projected, layout, params)
    mixed, _, _ = core_forward(1, projected, layout, params, held=mixed)
    ring_b.hold(mixed)
    ring_c.hold(mixed)
    mixed = both_on(mixed)
    while ring_b.left:
        ring_b.step()
    own_b = jnp.concatenate(ring_b.slots, axis=0)
    other_b = swapped(own_b)
    while ring_c.left:
        ring_c.step()
    own_c = jnp.concatenate(ring_c.slots, axis=0)
    other_c = jnp.concatenate([swapped(slot) for slot in ring_c.slots], axis=0)
    pair_b = (own_b, other_b, own_c, other_c)
    mixed = mixed.reshape(MB * TOK, MIXED)
    (handed,) = feed_forward(first_rows, mixed, mlp_row, *pair_b, keep=False)

    parts = [first_rows[row * TOK : (row + 1) * TOK] for row in range(MB)]
    received = [passed_along(handed[row * TOK : (row + 1) * TOK], "section", 1) for row in range(MB)]
    held, cores = (), ()
    starts = []
    for row in range(MB):
        start = jnp.where(is_first, parts[row], received[row])
        held = project(start, pre_row, *pair_a, row=row, held=held)
        starts.append(start)
        cores = core_forward(row, held[1].reshape(MB, TOK, WIDE_A), layout, params, held=cores)
        if row + 1 < MB:
            received[row + 1], cores, held = tied(received[row + 1], cores, held)
    start_rows = jnp.concatenate(starts, axis=0)
    normed, projected = held
    projected = projected.reshape(MB, TOK, WIDE_A)
    mixed, pre, yns = cores
    mixed = mixed.reshape(MB * TOK, MIXED)
    result, middle, normed_two, gate, up, act = feed_forward(
        start_rows, mixed, mlp_row, *pair_b, keep=True
    )
    their_mixed = swapped(mixed)
    their_act = swapped(act)
    their_normed = swapped(normed[:, SIDE:])
    their_normed_two = swapped(normed_two[:, SIDE:])

    positions = jnp.arange(TOK, dtype=jnp.int32)
    live = (positions[None, :] < row_live[:, None]).reshape(MB * TOK, 1)
    from_loss = own_order(jnp.where(live, out_grad, jnp.zeros_like(out_grad)))

    received = jnp.zeros((TOK, D), bf16)
    lefts = []
    rights = []
    rows = []
    picks = jnp.where(is_first, jnp.array([1, 0]), jnp.array([0, 1])).astype(jnp.int32)

    def tick_left(which):
        return [(lefts[1][which], None, 0), (lefts[2][which], None, 0)] + [
            (lefts[1][which + 2], None, 0), (lefts[2][which + 2], None, 0)
        ]

    def tick_right(which):
        return [(rights[tick][which + far], None) for far in (0, 2) for tick in (1, 2)]

    def saved_left(own, their):
        return [(own, 0, 0), (own, 1, 0), (their, 0, 0), (their, 1, 0)]

    def saved_right(own, their):
        return [(own, 0), (own, 1), (their, 0), (their, 1)]

    for tick in range(3):
        row = jnp.where(is_first, (1, 1, 0)[tick], (1, 0, 1)[tick]).astype(jnp.int32).reshape(1)
        if tick == 1:
            row, their_mixed, their_act, their_normed, their_normed_two = tied(
                row, their_mixed, their_act, their_normed, their_normed_two
            )
        if tick == 2:
            row, lefts[1], rights[1], rows[1] = tied(row, lefts[1], rights[1], rows[1])
        loss_row = (1, 0, 1)[tick]
        cotangent = jnp.where(
            is_first, received, from_loss[loss_row * TOK : (loss_row + 1) * TOK]
        )
        d_gate, d_up, d_middle, middle_low, d_mixed, mlp_grad = feed_back(
            row, cotangent, gate, up, middle, mlp_row, *pair_b
        )
        lefts.append(
            (cotangent, middle_low, swapped(cotangent[:, SIDE:]), swapped(middle_low[:, SIDE:]))
        )
        rights.append((d_gate, d_up, swapped(d_gate), swapped(d_up)))
        if tick == 2:
            sum_c = weight_grad(
                picks,
                1024,
                [
                    (tick_left(1), saved_right(mixed, their_mixed)),
                    (tick_left(0), saved_right(act, their_act)),
                ],
            )
            ring_c = RingReduce(sum_c)
            ring_c.step()
            picks_now, now_c, rights[2] = tied(picks, ring_c.operands(), rights[2])
            ring_c.send(*now_c)
            sum_b = weight_grad(
                picks_now,
                1024,
                [
                    (saved_left(normed_two, their_normed_two), tick_right(0)),
                    (saved_left(normed_two, their_normed_two), tick_right(1)),
                ],
            )
            ring_b = RingReduce(sum_b)
            ring_c.hold(sum_b)
            now_b, now_c, row = tied(ring_b.operands(), ring_c.operands(), row)
            ring_c.send(*now_c)
            ring_b.send(*now_b)
        proj_low, small = core_backward(row, projected, pre, yns, d_mixed, layout, params)
        if tick == 2:
            ring_b.hold(proj_low)
            ring_c.hold(proj_low)
            now_b, now_c, proj_low = tied(ring_b.operands(), ring_c.operands(), proj_low)
            ring_c.send(*now_c)
            ring_b.send(*now_b)
        their_low = swapped(proj_low)
        d_rows, d_low, pre_grad = project_back(
            row, proj_low, start_rows, d_middle, pre_row, *pair_a
        )
        if tick == 2:
            (p_one, their_one), (p_two, their_two) = rows[1][1], (proj_low, their_low)
            ring_b.hold(d_rows)
            now_b, d_rows, their_two = tied(ring_b.operands(), d_rows, their_two)
            ring_b.send(*now_b)
            picks_now, d_rows, now_b = tied(picks, d_rows, now_b)
            sum_a = weight_grad(
                picks_now,
                WIDE_A // 3,
                [
                    (
                        saved_left(normed, their_normed),
                        [(p_one, None), (p_two, None), (their_one, None), (their_two, None)],
                    )
                ],
            )
            ring_a = RingReduce(sum_a)
            ring_b.hold(sum_a)
            now_a, now_b, small, d_rows = tied(
                ring_a.operands(), ring_b.operands(), small, d_rows
            )
            ring_a.send(*now_a)
            ring_b.send(*now_b)
        rows.append((d_rows, (proj_low, their_low), pre_grad, mlp_grad, small))
        if tick < 2:
            received = passed_along(d_low, "section", -1)

    start_grad = jnp.concatenate(
        [
            jnp.where(is_first, rows[2][0], rows[1][0]),
            jnp.where(is_first, rows[1][0], rows[2][0]),
        ],
        axis=0,
    )
    pre_sum, mlp_sum, small = (one + two for one, two in zip(rows[1][2:], rows[2][2:]))
    gain_sums = whole_order(jnp.concatenate([pre_sum, mlp_sum], axis=0))
    small = summed_small(
        jnp.concatenate([small, jnp.pad(gain_sums, ((0, 6), (0, CH - D)))], axis=0)
    )
    share_c = ring_c.total()
    share_b = ring_b.total()
    share_a = ring_a.total()
    skip_sum = jnp.sum(small[6, :E].reshape(MH, MP), axis=1)
    mixer_in_grad = jnp.concatenate([share_a[:, :AT_Q], share_a[:, AT_DT : AT_DT + MH]], axis=1)
    return (
        whole_order(result)[None],
        whole_order(start_grad)[None],
        small[8:9, :D],
        small[9:10, :D],
        small[5:6, :E],
        small[None, :4],
        small[4:5],
        small[7:8, :MH],
        small[7:8, LANES : LANES + MH],
        skip_sum[None],
        mixer_in_grad[None],
        share_c[:, :E].T[None],
        share_a[:, AT_Q:AT_K][None],
        share_a[:, AT_K:AT_V][None],
        share_a[:, AT_V:AT_DT][None],
        share_c[:, E:MIXED].T[None],
        share_b[None],
        share_c[:, MIXED:].T[None],
    )


def solution(mesh):
    dp = mesh.shape["dp"]
    devices = mesh.devices.reshape(mesh.shape["section"], dp // 2, 2)
    paired = Mesh(devices, ("section", "chip", "core"))
    over = ("chip", "core")
    rows = P(over, None)
    small = P("section", None)
    by_row = P("section", over, None)
    by_col = P("section", None, over)
    small_specs = (small, small, small, P("section", None, None), small, small, small, small)
    big_specs = (by_row, by_col, by_row, by_row, by_row, by_col, by_row, by_col)
    in_specs = (rows, rows, rows, P(over)) + small_specs + big_specs
    out_specs = (by_row, by_row) + small_specs + big_specs
    return jax.shard_map(
        per_device, mesh=paired, in_specs=in_specs, out_specs=out_specs, check_vma=False
    )
```

```python
import functools
import math

import jax
import jax.numpy as jnp
from jax import lax
from jax.experimental import pallas as pl
from jax.experimental.pallas import tpu as pltpu
from jax.sharding import Mesh
from jax.sharding import PartitionSpec as P

D = 1024
FF = 2048
MH = 24
MP = 64
NS = 128
AH = 8
KVH = 2
HD = 64
MB = 2
TOK = 256
E = 1536
CH = 1792
HALF = TOK // 2
PAIRS = MH // 2
LANES = 128
SIDE = D // 2
VMEM = 60 * 2**20

AT_W = E
AT_Q = E + CH
AT_K = AT_Q + AH * HD
AT_V = AT_K + KVH * HD
AT_DT = AT_V + KVH * HD
WIDE_A = AT_DT + LANES
CUT_A = 16 * LANES
MIXED = E + AH * HD
AT_GU = MIXED
AT_DN = AT_GU + 2 * FF
WIDE_B = AT_DN + FF

highest = lax.Precision.HIGHEST
epsilon = 1e-05
rope_base = 100000000000.0
bf16 = jnp.bfloat16
f32 = jnp.float32


def dot_nn(left, right):
    return lax.dot_general(left, right, (((1,), (0,)), ((), ())), preferred_element_type=f32)


def dot_nt(left, right):
    return lax.dot_general(left, right, (((1,), (1,)), ((), ())), preferred_element_type=f32)


def dot_tn(left, right):
    return lax.dot_general(left, right, (((0,), (0,)), ((), ())), preferred_element_type=f32)


def dot_exact(left, right):
    return lax.dot_general(
        left, right, (((1,), (0,)), ((), ())), precision=highest, preferred_element_type=f32
    )


def softplus(value):
    return jnp.maximum(value, 0.0) + jnp.log1p(jnp.exp(-jnp.abs(value)))


def lane_low(rows):
    return lax.broadcasted_iota(jnp.int32, (rows, LANES), 1) < HD


def rope_halves(rows):
    return (lax.broadcasted_iota(jnp.int32, (rows, LANES), 1) & (HD - 1)) < HD // 2


def rope_turn(tile, cosine, sine):
    swapped = jnp.where(
        rope_halves(tile.shape[0]),
        -pltpu.roll(tile, LANES - HD // 2, 1),
        pltpu.roll(tile, HD // 2, 1),
    )
    return tile * cosine + swapped * sine


def rope_back(tile, cosine, sine):
    swapped = jnp.where(
        rope_halves(tile.shape[0]),
        pltpu.roll(tile, LANES - HD // 2, 1),
        -pltpu.roll(tile, HD // 2, 1),
    )
    return tile * cosine + swapped * sine


def both_halves(tile):
    swapped = pltpu.roll(tile, HD, 1)
    low = lane_low(tile.shape[0])
    return (jnp.where(low, tile, swapped), jnp.where(low, swapped, tile))


def tile_at(index):
    return pl.ds(pl.multiple_of(index * LANES, LANES), LANES)


def tile_from(start, index):
    return pl.ds(pl.multiple_of(start + index * LANES, LANES), LANES)


def allowed_pairs(doc_col_ref, doc_row_ref):
    later = lax.broadcasted_iota(jnp.int32, (TOK, TOK), 0)
    early = lax.broadcasted_iota(jnp.int32, (TOK, TOK), 1)
    same = doc_col_ref[:, 0:1] == doc_row_ref[0:1, :]
    return (later >= early) & same


def core_forward_kernel(
    pa_ref, rope_ref, mask_ref, doc_col_ref, doc_row_ref, taps_ref, head_ref, wide_ref,
    xb_ref, pre_ref, yns_ref,
    conv_s, cb_s, sum_s,
):
    def conv_tile(index, carry):
        rows = pa_ref[:, tile_from(AT_W, index)]
        at = tile_at(index)
        total = taps_ref[4:5, at] + taps_ref[3:4, at] * rows
        for shift in (1, 2, 3):
            moved = mask_ref[:, (shift - 1) * LANES : shift * LANES] * pltpu.roll(rows, shift, 0)
            total = total + taps_ref[3 - shift : 4 - shift, at] * moved
        pre_ref[:, at] = total
        conv_s[:, at] = total * jax.nn.sigmoid(total)
        return carry

    lax.fori_loop(0, CH // LANES, conv_tile, 0)

    allowed = allowed_pairs(doc_col_ref, doc_row_ref)
    steps = softplus(pa_ref[:, AT_DT:] + head_ref[0:1, :])
    rates = -steps * head_ref[1:2, :]
    totals = dot_exact(jnp.where(allowed, 1.0, 0.0), rates)
    totals_t = totals.T
    inward = conv_s[:, E : E + NS].astype(bf16)
    outward = conv_s[:, E + NS :].astype(bf16)
    cb_s[...] = jnp.where(allowed, dot_nt(outward, inward), 0.0)
    low = lane_low(TOK)
    for pair in range(PAIRS):
        lanes = slice(pair * LANES, (pair + 1) * LANES)
        first = 2 * pair
        step_pair = jnp.where(low, steps[:, first : first + 1], steps[:, first + 1 : first + 2])
        scaled = (conv_s[:, lanes] * step_pair).astype(bf16)
        halves = []
        for head in (first, first + 1):
            col = totals[:, head : head + 1]
            row = totals_t[head : head + 1, :]
            top = jnp.exp(jnp.minimum(col[:HALF] - row[:, :HALF], 0.0)) * cb_s[:HALF, :HALF]
            end = jnp.exp(jnp.minimum(col[HALF:] - row, 0.0)) * cb_s[HALF:, :]
            halves.append(
                jnp.concatenate(
                    [dot_nn(top.astype(bf16), scaled[:HALF]), dot_nn(end.astype(bf16), scaled)],
                    axis=0,
                )
            )
        yns_ref[:, lanes] = jnp.where(low, halves[0], halves[1])

    sum_s[...] = jnp.zeros((TOK, LANES), f32)

    def gate_tile(index, carry):
        at = tile_at(index)
        gate = pa_ref[:, at]
        rows = yns_ref[:, at] + wide_ref[0:1, at] * conv_s[:, at]
        gated = rows * (gate * jax.nn.sigmoid(gate))
        sum_s[...] += gated * gated
        conv_s[:, at] = gated
        return carry

    lax.fori_loop(0, E // LANES, gate_tile, 0)
    scale = lax.rsqrt(jnp.sum(sum_s[...], axis=1, keepdims=True) * (1.0 / E) + epsilon)

    def norm_tile(index, carry):
        at = tile_at(index)
        xb_ref[:, at] = (conv_s[:, at] * scale * wide_ref[1:2, at]).astype(bf16)
        return carry

    lax.fori_loop(0, E // LANES, norm_tile, 0)

    cosine = rope_ref[:, :LANES]
    sine = rope_ref[:, LANES:]
    keys = both_halves(rope_turn(pa_ref[:, AT_K:AT_V], cosine, sine))
    values = both_halves(pa_ref[:, AT_V:AT_DT])
    keys = tuple(part.astype(bf16) for part in keys)
    values = tuple(part.astype(bf16) for part in values)
    for pair in range(AH // 2):
        group = pair // (AH // (2 * KVH))
        at = AT_Q + pair * LANES
        turned = rope_turn(pa_ref[:, at : at + LANES], cosine, sine) * (1.0 / math.sqrt(HD))
        halves = []
        for side in range(2):
            chosen = low if side == 0 else jnp.logical_not(low)
            query = jnp.where(chosen, turned, 0.0).astype(bf16)
            parts = []
            for rows, cols in ((slice(0, HALF), HALF), (slice(HALF, TOK), TOK)):
                scores = dot_nt(query[rows], keys[group][:cols])
                scores = jnp.where(allowed[rows, :cols], scores, -1e30)
                top = jnp.max(scores, axis=1, keepdims=True)
                weights = jnp.exp(scores - top)
                share = 1.0 / jnp.sum(weights, axis=1, keepdims=True)
                parts.append(dot_nn(weights.astype(bf16), values[group][:cols]) * share)
            halves.append(jnp.concatenate(parts, axis=0))
        out = jnp.where(low, halves[0], halves[1])
        xb_ref[:, E + pair * LANES : E + (pair + 1) * LANES] = out.astype(bf16)


def silu_slope(value, gate):
    return gate * (1.0 + value * (1.0 - gate))


def core_backward_kernel(
    pick_ref,
    pa_ref, pre_ref, yns_ref, dxb_ref, rope_ref, mask_ref, doc_col_ref, doc_row_ref,
    taps_ref, head_ref, wide_ref,
    pg_ref, small_ref,
    x_s, dx_s, dyb_s, cbt_s, dcbt_s, sum_s, ssum_s,
):
    small_ref[...] = jnp.zeros_like(small_ref)
    sum_s[...] = jnp.zeros((TOK, LANES), f32)
    ssum_s[...] = jnp.zeros((TOK, LANES), f32)

    def start_tile(index, carry):
        at = tile_at(index)
        pre = pre_ref[:, at]
        heads_in = pre * jax.nn.sigmoid(pre)
        x_s[:, at] = heads_in
        gate = pa_ref[:, at]
        rows = yns_ref[:, at] + wide_ref[0:1, at] * heads_in
        gated = rows * (gate * jax.nn.sigmoid(gate))
        sum_s[...] += gated * gated
        ssum_s[...] += dxb_ref[:, at] * wide_ref[1:2, at] * gated
        return carry

    lax.fori_loop(0, E // LANES, start_tile, 0)
    scale = lax.rsqrt(jnp.sum(sum_s[...], axis=1, keepdims=True) * (1.0 / E) + epsilon)
    pull = jnp.sum(ssum_s[...], axis=1, keepdims=True) * (1.0 / E) * scale * scale * scale

    def gate_tile(index, carry):
        at = tile_at(index)
        heads_in = x_s[:, at]
        skip = wide_ref[0:1, at]
        gate = pa_ref[:, at]
        opened = jax.nn.sigmoid(gate)
        rows = yns_ref[:, at] + skip * heads_in
        gated = rows * (gate * opened)
        arrived = dxb_ref[:, at]
        d_gated = scale * (arrived * wide_ref[1:2, at]) - gated * pull
        small_ref[5:6, at] = jnp.sum(arrived * gated * scale, axis=0, keepdims=True)
        d_rows = d_gated * (gate * opened)
        pg_ref[:, at] = (d_gated * rows * silu_slope(gate, opened)).astype(bf16)
        small_ref[6:7, at] = jnp.sum(d_rows * heads_in, axis=0, keepdims=True)
        dyb_s[:, at] = d_rows.astype(bf16)
        dx_s[:, at] = skip * d_rows
        return carry

    lax.fori_loop(0, E // LANES, gate_tile, 0)

    def state_tile(index, carry):
        at = tile_from(E, index)
        pre = pre_ref[:, at]
        x_s[:, at] = pre * jax.nn.sigmoid(pre)
        return carry

    lax.fori_loop(0, 2, state_tile, 0)

    later = lax.broadcasted_iota(jnp.int32, (TOK, TOK), 1)
    early = lax.broadcasted_iota(jnp.int32, (TOK, TOK), 0)
    allowed_t = (later >= early) & (doc_col_ref[:, 0:1] == doc_row_ref[0:1, :])
    allowed = allowed_pairs(doc_col_ref, doc_row_ref)
    raw = pa_ref[:, AT_DT:] + head_ref[0:1, :]
    steps = softplus(raw)
    decay = head_ref[1:2, :]
    rates = -steps * decay
    totals = dot_exact(jnp.where(allowed, 1.0, 0.0), rates)
    totals_t = totals.T
    inward = x_s[:, E : E + NS].astype(bf16)
    outward = x_s[:, E + NS :].astype(bf16)
    cbt_s[...] = jnp.where(allowed_t, dot_nt(inward, outward), 0.0)
    dcbt_s[...] = jnp.zeros((TOK, TOK), f32)
    low = lane_low(TOK)
    spread_row = lax.broadcasted_iota(jnp.int32, (LANES, LANES), 0) >= HD
    spread_col = lax.broadcasted_iota(jnp.int32, (LANES, LANES), 1)
    sum_s[...] = jnp.zeros((TOK, LANES), f32)
    ssum_s[...] = jnp.zeros((TOK, LANES), f32)
    for pair in range(PAIRS):
        lanes = slice(pair * LANES, (pair + 1) * LANES)
        first = 2 * pair
        step_pair = jnp.where(low, steps[:, first : first + 1], steps[:, first + 1 : first + 2])
        heads_in = x_s[:, lanes]
        scaled = (heads_in * step_pair).astype(bf16)
        d_rows = dyb_s[:, lanes]
        halves = []
        for side, head in enumerate((first, first + 1)):
            chosen = low if side == 0 else jnp.logical_not(low)
            own = jnp.where(chosen, scaled, jnp.zeros_like(scaled))
            col = totals[:, head : head + 1]
            row = totals_t[head : head + 1, :]
            top = jnp.exp(jnp.minimum(row - col[:HALF], 0.0))
            end = jnp.exp(jnp.minimum(row[:, HALF:] - col[HALF:], 0.0))
            top_mix = (top * cbt_s[:HALF, :]).astype(bf16)
            end_mix = (end * cbt_s[HALF:, HALF:]).astype(bf16)
            dcbt_s[:HALF, :] += dot_nt(own[:HALF], d_rows) * top
            dcbt_s[HALF:, HALF:] += dot_nt(own[HALF:], d_rows[HALF:]) * end
            halves.append(
                jnp.concatenate(
                    [dot_nn(top_mix, d_rows), dot_nn(end_mix, d_rows[HALF:])], axis=0
                )
            )
        d_scaled = jnp.where(low, halves[0], halves[1])
        dx_s[:, lanes] += d_scaled * step_pair
        spread = (spread_col == jnp.where(spread_row, first + 1, first)).astype(bf16)
        for value, into in (
            (d_scaled * heads_in, sum_s),
            (d_rows.astype(f32) * yns_ref[:, lanes] - scaled.astype(f32) * d_scaled, ssum_s),
        ):
            coarse = value.astype(bf16)
            fine = (value - coarse.astype(f32)).astype(bf16)
            into[...] += dot_nn(coarse, spread) + dot_nn(fine, spread)

    d_rates = dot_exact(jnp.where(allowed_t, 1.0, 0.0), ssum_s[...])
    d_steps = sum_s[...] - decay * d_rates
    d_raw = d_steps * jax.nn.sigmoid(raw)
    pg_ref[:, AT_DT:] = d_raw.astype(bf16)
    small_ref[7:8, :LANES] = jnp.sum(d_raw, axis=0, keepdims=True)
    small_ref[7:8, LANES : 2 * LANES] = jnp.sum(d_rates * rates, axis=0, keepdims=True)
    d_pairs = jnp.where(allowed_t, dcbt_s[...], 0.0).astype(bf16)
    dx_s[:, E : E + NS] = dot_nn(d_pairs, outward)
    dx_s[:, E + NS :] = dot_tn(d_pairs, inward)

    def conv_tile(index, carry):
        at = tile_at(index)
        pre = pre_ref[:, at]
        d_pre = dx_s[:, at] * silu_slope(pre, jax.nn.sigmoid(pre))
        rows = pa_ref[:, tile_from(AT_W, index)]
        small_ref[4:5, at] = jnp.sum(d_pre, axis=0, keepdims=True)
        small_ref[3:4, at] = jnp.sum(d_pre * rows, axis=0, keepdims=True)
        back = taps_ref[3:4, at] * d_pre
        for shift in (1, 2, 3):
            held = mask_ref[:, (shift - 1) * LANES : shift * LANES] * d_pre
            small_ref[3 - shift : 4 - shift, at] = jnp.sum(
                held * pltpu.roll(rows, shift, 0), axis=0, keepdims=True
            )
            back = back + taps_ref[3 - shift : 4 - shift, at] * pltpu.roll(held, TOK - shift, 0)
        pg_ref[:, tile_from(AT_W, index)] = back.astype(bf16)
        return carry

    lax.fori_loop(0, CH // LANES, conv_tile, 0)

    cosine = rope_ref[:, :LANES]
    sine = rope_ref[:, LANES:]
    keys = both_halves(rope_turn(pa_ref[:, AT_K:AT_V], cosine, sine))
    values = both_halves(pa_ref[:, AT_V:AT_DT])
    keys = tuple(part.astype(bf16) for part in keys)
    values = tuple(part.astype(bf16) for part in values)
    root = 1.0 / math.sqrt(HD)
    d_keys = []
    d_values = []
    for group in range(KVH):
        key = keys[group]
        value = values[group]
        d_key = jnp.zeros((TOK, LANES), f32)
        d_value = jnp.zeros((TOK, LANES), f32)
        for pair in range(group * (AH // (2 * KVH)), (group + 1) * (AH // (2 * KVH))):
            at = AT_Q + pair * LANES
            turned = rope_turn(pa_ref[:, at : at + LANES], cosine, sine) * root
            arrived = dxb_ref[:, E + pair * LANES : E + (pair + 1) * LANES]
            halves = []
            for side in range(2):
                chosen = low if side == 0 else jnp.logical_not(low)
                query = jnp.where(chosen, turned, 0.0).astype(bf16)
                d_out = jnp.where(chosen, arrived, 0.0).astype(bf16)
                scores = jnp.where(allowed_t, dot_nt(key, query), -1e30)
                peak = jnp.max(scores, axis=0, keepdims=True)
                weights = jnp.exp(scores - peak)
                weights = weights * (1.0 / jnp.sum(weights, axis=0, keepdims=True))
                d_weights = dot_nt(value, d_out)
                offset = jnp.sum(weights * d_weights, axis=0, keepdims=True)
                d_scores = (weights * (d_weights - offset)).astype(bf16)
                d_value = d_value + dot_nn(weights.astype(bf16), d_out)
                d_key = d_key + dot_nn(d_scores, query)
                halves.append(dot_tn(d_scores, key))
            d_query = rope_back(jnp.where(low, halves[0], halves[1]) * root, cosine, sine)
            pg_ref[:, at : at + LANES] = d_query.astype(bf16)
        d_keys.append(d_key + pltpu.roll(d_key, HD, 1))
        d_values.append(d_value + pltpu.roll(d_value, HD, 1))
    d_key = rope_back(jnp.where(low, d_keys[0], d_keys[1]), cosine, sine)
    pg_ref[:, AT_K:AT_V] = d_key.astype(bf16)
    pg_ref[:, AT_V:AT_DT] = jnp.where(low, d_values[0], d_values[1]).astype(bf16)


def row_block(width):
    return pl.BlockSpec((None, TOK, width), lambda row: (row, 0, 0))


def whole_block(shape):
    return pl.BlockSpec(shape, lambda row: (0,) * len(shape))


def core_forward(row, projected, layout, params, held=()):
    rope, masks, doc_cols, doc_rows = layout
    taps, heads, wide = params

    def block(width, depth=TOK):
        return pl.BlockSpec((None, depth, width), lambda step: (row, 0, 0))

    kernel = core_forward_kernel
    if held:
        def kernel(*refs):
            core_forward_kernel(*refs[:8], *refs[11:])

    return pl.pallas_call(
        kernel,
        grid=(1,),
        in_specs=[
            block(WIDE_A),
            block(2 * LANES),
            block(3 * LANES),
            block(LANES),
            block(TOK, 8),
            whole_block(taps.shape),
            whole_block(heads.shape),
            whole_block(wide.shape),
        ]
        + [pl.BlockSpec(memory_space=pl.ANY)] * len(held),
        out_specs=[block(MIXED), block(CH), block(E)],
        out_shape=[
            jax.ShapeDtypeStruct((MB, TOK, MIXED), bf16),
            jax.ShapeDtypeStruct((MB, TOK, CH), f32),
            jax.ShapeDtypeStruct((MB, TOK, E), f32),
        ],
        scratch_shapes=[
            pltpu.VMEM((TOK, CH), f32),
            pltpu.VMEM((TOK, TOK), f32),
            pltpu.VMEM((TOK, LANES), f32),
        ],
        input_output_aliases={8: 0, 9: 1, 10: 2} if held else {},
        compiler_params=pltpu.CompilerParams(vmem_limit_bytes=VMEM),
        cost_estimate=pl.CostEstimate(
            flops=4 * 10**8, bytes_accessed=12 * 2**20, transcendentals=10**6
        ),
        name="core_forward",
    )(projected, rope, masks, doc_cols, doc_rows, taps, heads, wide, *held)


def core_backward(row, projected, pre, yns, d_mixed, layout, params):
    rope, masks, doc_cols, doc_rows = layout
    taps, heads, wide = params

    def picked(width, depth=TOK):
        return pl.BlockSpec((None, depth, width), lambda step, pick: (pick[0], 0, 0))

    def plain(shape):
        return pl.BlockSpec(shape, lambda step, pick: (0,) * len(shape))

    return pl.pallas_call(
        core_backward_kernel,
        grid_spec=pltpu.PrefetchScalarGridSpec(
            num_scalar_prefetch=1,
            grid=(1,),
            in_specs=[
                picked(WIDE_A),
                picked(CH),
                picked(E),
                plain((TOK, MIXED)),
                picked(2 * LANES),
                picked(3 * LANES),
                picked(LANES),
                picked(TOK, 8),
                plain(taps.shape),
                plain(heads.shape),
                plain(wide.shape),
            ],
            out_specs=[plain((TOK, WIDE_A)), plain((8, CH))],
            scratch_shapes=[
                pltpu.VMEM((TOK, CH), f32),
                pltpu.VMEM((TOK, CH), f32),
                pltpu.VMEM((TOK, E), bf16),
                pltpu.VMEM((TOK, TOK), f32),
                pltpu.VMEM((TOK, TOK), f32),
                pltpu.VMEM((TOK, LANES), f32),
                pltpu.VMEM((TOK, LANES), f32),
            ],
        ),
        out_shape=[
            jax.ShapeDtypeStruct((TOK, WIDE_A), bf16),
            jax.ShapeDtypeStruct((8, CH), f32),
        ],
        compiler_params=pltpu.CompilerParams(vmem_limit_bytes=VMEM),
        cost_estimate=pl.CostEstimate(
            flops=10**9, bytes_accessed=16 * 2**20, transcendentals=2 * 10**6
        ),
        name="core_backward",
    )(
        row, projected, pre, yns, d_mixed, rope, masks, doc_cols, doc_rows,
        taps, heads, wide,
    )


def passed_along(value, axis, steps):
    count = lax.axis_size(axis)
    leading, last = (max(0, -steps), min(count, count - steps))
    return lax.ppermute(value, axis, [(source, source + steps) for source in range(leading, last)])


def norm_rows(values):
    return lax.rsqrt(jnp.mean(values * values, axis=-1, keepdims=True) + epsilon)


def norm_back(values, gain, arrived):
    scale = norm_rows(values)
    weighted = arrived * gain
    pull = jnp.mean(weighted * values, axis=-1, keepdims=True) * scale * scale * scale
    gain_grad = jnp.sum(arrived * values * scale, axis=0, keepdims=True)
    return (weighted * scale - values * pull, gain_grad)


def project_kernel(rows_ref, gain_ref, own_ref, other_ref, normed_ref, out_ref):
    @pl.when(pl.program_id(0) == 0)
    def _():
        rows = rows_ref[...].astype(f32)
        normed_ref[...] = (rows * norm_rows(rows) * gain_ref[...]).astype(bf16)

    out_ref[...] = dot_nn(normed_ref[:, :SIDE], own_ref[...]) + dot_nn(
        normed_ref[:, SIDE:], other_ref[...]
    )


def project(rows, gain, own, other, row=None, held=()):
    count = rows.shape[0]
    tile = WIDE_A // 3
    weight = pl.BlockSpec((SIDE, tile), lambda step: (0, step))
    at = row or 0
    total = count if row is None else MB * TOK
    kernel = project_kernel
    if held:
        def kernel(rows_ref, gain_ref, own_ref, other_ref, old_normed, old_out, *outs):
            project_kernel(rows_ref, gain_ref, own_ref, other_ref, *outs)

    return pl.pallas_call(
        kernel,
        grid=(3,),
        in_specs=[whole_block((count, D)), whole_block((1, D)), weight, weight]
        + [pl.BlockSpec(memory_space=pl.ANY)] * len(held),
        out_specs=[
            pl.BlockSpec((count, D), lambda step: (at, 0)),
            pl.BlockSpec((count, tile), lambda step: (at, step)),
        ],
        out_shape=[
            jax.ShapeDtypeStruct((total, D), bf16),
            jax.ShapeDtypeStruct((total, WIDE_A), f32),
        ],
        input_output_aliases={4: 0, 5: 1} if held else {},
        compiler_params=pltpu.CompilerParams(vmem_limit_bytes=VMEM),
        cost_estimate=pl.CostEstimate(
            flops=2 * count * D * WIDE_A,
            bytes_accessed=2 * D * WIDE_A + 4 * count * WIDE_A,
            transcendentals=0,
        ),
        name="project",
    )(rows, gain, own, other, *held)


def feed_forward_kernel(
    keep, rows_ref, mixed_ref, gain_ref,
    out_own, out_other, gate_own, gate_other, up_own, up_other, down_own, down_other,
    *refs,
):
    if keep:
        low_ref, middle_ref, normed_ref, gate_ref, up_ref, act_ref, total_s = refs
    else:
        *row_refs, middle_ref, normed_ref, total_s = refs
    step = pl.program_id(0)

    @pl.when(step == 0)
    def _():
        middle_ref[...] = rows_ref[...].astype(f32)

    @pl.when(step < 4)
    def _():
        mixed = mixed_ref[...]
        middle_ref[:, :SIDE] += dot_nt(mixed, out_own[...])
        middle_ref[:, SIDE:] += dot_nt(mixed, out_other[...])

    @pl.when(step == 3)
    def _():
        middle = middle_ref[...]
        normed_ref[...] = (middle * norm_rows(middle) * gain_ref[...]).astype(bf16)
        total_s[...] = middle

    @pl.when(step >= 4)
    def _():
        left = normed_ref[:, :SIDE]
        right = normed_ref[:, SIDE:]
        gate = dot_nn(left, gate_own[...]) + dot_nn(right, gate_other[...])
        up = dot_nn(left, up_own[...]) + dot_nn(right, up_other[...])
        act = (gate * jax.nn.sigmoid(gate) * up).astype(bf16)
        if keep:
            gate_ref[...] = gate
            up_ref[...] = up
            act_ref[...] = act
        total_s[:, :SIDE] += dot_nt(act, down_own[...])
        total_s[:, SIDE:] += dot_nt(act, down_other[...])

    @pl.when(step == 7)
    def _():
        if keep:
            low_ref[...] = total_s[...].astype(bf16)
        else:
            for row, row_ref in enumerate(row_refs):
                row_ref[...] = total_s[row * TOK : (row + 1) * TOK, :].astype(bf16)


def b_block(start, skipped):
    return pl.BlockSpec(
        (SIDE, 512), lambda step, *pick: (0, start + jnp.clip(step - skipped, 0, 3))
    )


def b_blocks(parts):
    return [b_block(start, skipped) for start, skipped in parts for _ in range(2)]


def feed_forward(rows, mixed, gain, own, other, keep):
    count = rows.shape[0]
    wide = pl.BlockSpec((count, 512), lambda step: (0, jnp.clip(step - 4, 0, 3)))
    out_specs = [whole_block((count, D))]
    out_shape = [jax.ShapeDtypeStruct((count, D), bf16)]
    scratch = [pltpu.VMEM((count, D), f32)]
    if keep:
        out_specs += [whole_block((count, D)), whole_block((count, D)), wide, wide, wide]
        out_shape += [
            jax.ShapeDtypeStruct((count, D), f32),
            jax.ShapeDtypeStruct((count, D), bf16),
            jax.ShapeDtypeStruct((count, FF), f32),
            jax.ShapeDtypeStruct((count, FF), f32),
            jax.ShapeDtypeStruct((count, FF), bf16),
        ]
    else:
        out_specs = [whole_block((TOK, D))] * MB
        out_shape = [jax.ShapeDtypeStruct((TOK, D), bf16)] * MB
        scratch = [pltpu.VMEM((count, D), f32), pltpu.VMEM((count, D), bf16)] + scratch
    return pl.pallas_call(
        functools.partial(feed_forward_kernel, keep),
        grid=(8,),
        in_specs=[
            whole_block((count, D)),
            pl.BlockSpec((count, 512), lambda step: (0, jnp.clip(step, 0, 3))),
            whole_block((1, D)),
        ]
        + b_blocks(((0, 0), (4, 4), (8, 4), (12, 4))),
        out_specs=out_specs,
        out_shape=out_shape,
        scratch_shapes=scratch,
        compiler_params=pltpu.CompilerParams(vmem_limit_bytes=VMEM),
        cost_estimate=pl.CostEstimate(
            flops=2 * count * D * WIDE_B, bytes_accessed=2 * D * WIDE_B, transcendentals=0
        ),
        name="feed_forward",
    )(rows, mixed, gain, *([own, other] * 4))


def feed_back_kernel(
    pick_ref, cot_ref, gate_ref, up_ref, middle_ref, gain_ref,
    down_own, down_other, gate_own, gate_other, up_own, up_other, out_own, out_other,
    d_gate_ref, d_up_ref, d_middle_ref, low_ref, d_mixed_ref, gain_grad_ref,
    total_s,
):
    step = pl.program_id(0)

    @pl.when(step == 0)
    def _():
        total_s[...] = jnp.zeros_like(total_s)

    @pl.when(step < 4)
    def _():
        arrived = dot_nn(cot_ref[:, :SIDE], down_own[...]) + dot_nn(
            cot_ref[:, SIDE:], down_other[...]
        )
        gate = gate_ref[...]
        opened = jax.nn.sigmoid(gate)
        d_gate = (arrived * up_ref[...] * silu_slope(gate, opened)).astype(bf16)
        d_up = (arrived * (gate * opened)).astype(bf16)
        d_gate_ref[...] = d_gate
        d_up_ref[...] = d_up
        total_s[:, :SIDE] += dot_nt(d_gate, gate_own[...]) + dot_nt(d_up, up_own[...])
        total_s[:, SIDE:] += dot_nt(d_gate, gate_other[...]) + dot_nt(d_up, up_other[...])

    @pl.when(step == 3)
    def _():
        d_norm, gain_grad = norm_back(middle_ref[...], gain_ref[...], total_s[...])
        d_middle = cot_ref[...].astype(f32) + d_norm
        d_middle_ref[...] = d_middle
        low_ref[...] = d_middle.astype(bf16)
        gain_grad_ref[...] = gain_grad

    @pl.when(step >= 4)
    def _():
        d_mixed_ref[...] = dot_nn(low_ref[:, :SIDE], out_own[...]) + dot_nn(
            low_ref[:, SIDE:], out_other[...]
        )


def feed_back(row, cotangent, gate, up, middle, gain, own, other):
    saved = pl.BlockSpec((TOK, 512), lambda step, pick: (pick[0], jnp.clip(step, 0, 3)))
    early = pl.BlockSpec((TOK, 512), lambda step, pick: (0, jnp.clip(step, 0, 3)))
    late = pl.BlockSpec((TOK, 512), lambda step, pick: (0, jnp.clip(step - 4, 0, 3)))
    full = pl.BlockSpec((TOK, D), lambda step, pick: (0, 0))
    gain_block = pl.BlockSpec((1, D), lambda step, pick: (0, 0))
    return pl.pallas_call(
        feed_back_kernel,
        grid_spec=pltpu.PrefetchScalarGridSpec(
            num_scalar_prefetch=1,
            grid=(8,),
            in_specs=[
                full,
                saved,
                saved,
                pl.BlockSpec((TOK, D), lambda step, pick: (pick[0], 0)),
                gain_block,
            ]
            + b_blocks(((12, 0), (4, 0), (8, 0), (0, 4))),
            out_specs=[early, early, full, full, late, gain_block],
            scratch_shapes=[pltpu.VMEM((TOK, D), f32)],
        ),
        out_shape=[
            jax.ShapeDtypeStruct((TOK, FF), bf16),
            jax.ShapeDtypeStruct((TOK, FF), bf16),
            jax.ShapeDtypeStruct((TOK, D), f32),
            jax.ShapeDtypeStruct((TOK, D), bf16),
            jax.ShapeDtypeStruct((TOK, MIXED), f32),
            jax.ShapeDtypeStruct((1, D), f32),
        ],
        compiler_params=pltpu.CompilerParams(vmem_limit_bytes=VMEM),
        cost_estimate=pl.CostEstimate(
            flops=2 * TOK * D * WIDE_B, bytes_accessed=2 * D * WIDE_B, transcendentals=0
        ),
        name="feed_back",
    )(row, cotangent, gate, up, middle, gain, *([own, other] * 4))


def project_back_kernel(
    pick_ref, grad_ref, rows_ref, d_middle_ref, gain_ref, own_ref, other_ref,
    d_rows_ref, low_ref, gain_grad_ref, total_s,
):
    step = pl.program_id(0)

    @pl.when(step == 0)
    def _():
        total_s[...] = jnp.zeros_like(total_s)

    total_s[:, :SIDE] += dot_nt(grad_ref[...], own_ref[...])
    total_s[:, SIDE:] += dot_nt(grad_ref[...], other_ref[...])

    @pl.when(step == 2)
    def _():
        d_norm, gain_grad = norm_back(rows_ref[...].astype(f32), gain_ref[...], total_s[...])
        d_rows = d_middle_ref[...] + d_norm
        d_rows_ref[...] = d_rows
        low_ref[...] = d_rows.astype(bf16)
        gain_grad_ref[...] = gain_grad


def project_back(row, proj_low, start_rows, d_middle, gain, own, other):
    tile = WIDE_A // 3
    weight = pl.BlockSpec((SIDE, tile), lambda step, pick: (0, step))
    full = pl.BlockSpec((TOK, D), lambda step, pick: (0, 0))
    gain_block = pl.BlockSpec((1, D), lambda step, pick: (0, 0))
    return pl.pallas_call(
        project_back_kernel,
        grid_spec=pltpu.PrefetchScalarGridSpec(
            num_scalar_prefetch=1,
            grid=(3,),
            in_specs=[
                pl.BlockSpec((TOK, tile), lambda step, pick: (0, step)),
                pl.BlockSpec((TOK, D), lambda step, pick: (pick[0], 0)),
                full,
                gain_block,
                weight,
                weight,
            ],
            out_specs=[full, full, gain_block],
            scratch_shapes=[pltpu.VMEM((TOK, D), f32)],
        ),
        out_shape=[
            jax.ShapeDtypeStruct((TOK, D), f32),
            jax.ShapeDtypeStruct((TOK, D), bf16),
            jax.ShapeDtypeStruct((1, D), f32),
        ],
        compiler_params=pltpu.CompilerParams(vmem_limit_bytes=VMEM),
        cost_estimate=pl.CostEstimate(
            flops=2 * TOK * D * WIDE_A, bytes_accessed=2 * D * WIDE_A, transcendentals=0
        ),
        name="project_back",
    )(row, proj_low, start_rows, d_middle, gain, own, other)


def weight_grad_kernel(groups, pick_ref, *refs):
    lefts = refs[: 4 * len(groups)]
    rights = refs[4 * len(groups) : 8 * len(groups)]
    sum_ref, left_s = refs[8 * len(groups) :]
    step = pl.program_id(0)
    for index, (start, count) in enumerate(groups):
        four = lefts[4 * index : 4 * index + 4]
        blocks = rights[4 * index : 4 * index + 4]

        @pl.when(step == start)
        def _(four=four):
            for place, ref in enumerate(four):
                left_s[:, place * TOK : (place + 1) * TOK] = ref[...].astype(f32).T.astype(bf16)

        @pl.when((step >= start) & (step < start + count))
        def _(blocks=blocks):
            right = jnp.concatenate([ref[...] for ref in blocks], axis=0)
            sum_ref[...] = dot_nn(left_s[...], right).astype(bf16)


def weight_grad(picks, tile, groups):
    steps = []
    in_left = []
    in_right = []
    operands_left = []
    operands_right = []
    start = 0
    for left, right in groups:
        count = right[0][0].shape[1] // tile
        steps.append((start, count))
        for array, which, column in left:
            in_left.append(
                pl.BlockSpec(
                    (TOK, SIDE),
                    lambda step, pick, which=which, column=column: (
                        0 if which is None else pick[which],
                        column,
                    ),
                )
            )
            operands_left.append(array)
        for array, which in right:
            in_right.append(
                pl.BlockSpec(
                    (TOK, tile),
                    lambda step, pick, which=which, start=start, count=count: (
                        0 if which is None else pick[which],
                        jnp.clip(step - start, 0, count - 1),
                    ),
                )
            )
            operands_right.append(array)
        start += count
    return pl.pallas_call(
        functools.partial(weight_grad_kernel, tuple(steps)),
        grid_spec=pltpu.PrefetchScalarGridSpec(
            num_scalar_prefetch=1,
            grid=(start,),
            in_specs=in_left + in_right,
            out_specs=pl.BlockSpec((SIDE, tile), lambda step, pick: (0, step)),
            scratch_shapes=[pltpu.VMEM((SIDE, 4 * TOK), bf16)],
        ),
        out_shape=jax.ShapeDtypeStruct((SIDE, start * tile), bf16),
        compiler_params=pltpu.CompilerParams(vmem_limit_bytes=VMEM),
        cost_estimate=pl.CostEstimate(
            flops=8 * TOK * SIDE * start * tile,
            bytes_accessed=4 * SIDE * start * tile,
            transcendentals=0,
        ),
        name="weight_grad",
    )(picks, *operands_left, *operands_right)


def row_layout(doc_ids):
    rows = doc_ids.shape[0]
    positions = jnp.arange(TOK, dtype=jnp.int32)
    earlier = jnp.sum((doc_ids[:, None, :] < doc_ids[:, :, None]).astype(jnp.int32), axis=2)
    places = positions[None, :] - earlier
    half_dim = HD // 2
    inverse_freq = rope_base ** (-jnp.arange(half_dim, dtype=f32) / half_dim)
    angles = places.astype(f32)[:, :, None] * inverse_freq[None, None, :]
    repeats = LANES // half_dim
    rope = jnp.concatenate([jnp.cos(angles)] * repeats + [jnp.sin(angles)] * repeats, axis=-1)
    masks = jnp.concatenate(
        [
            jnp.broadcast_to((places >= shift).astype(f32)[:, :, None], (rows, TOK, LANES))
            for shift in (1, 2, 3)
        ],
        axis=-1,
    )
    doc_cols = jnp.broadcast_to(doc_ids[:, :, None], (rows, TOK, LANES))
    doc_rows = jnp.broadcast_to(doc_ids[:, None, :], (rows, 8, TOK))
    return (rope, masks, doc_cols, doc_rows)


def core_params(conv_weight, conv_bias, step_bias, decay_log, skip_scale, mixer_gain):
    taps = jnp.concatenate([conv_weight, conv_bias[None], jnp.zeros((3, CH), f32)], axis=0)
    heads = jnp.zeros((8, LANES), f32)
    heads = heads.at[0, :MH].set(step_bias).at[1, :MH].set(jnp.exp(decay_log))
    wide = jnp.concatenate(
        [jnp.repeat(skip_scale, MP)[None], mixer_gain[None], jnp.zeros((6, E), f32)], axis=0
    )
    return (taps, heads, wide)


def swapped(value):
    return lax.ppermute(value, "core", [(0, 1), (1, 0)])


def ring_order(chips):
    return [2 * step for step in range(chips // 2)] + [
        2 * step + 1 for step in reversed(range(chips // 2))
    ]


def ring_place(chip, chips):
    return jnp.where(chip % 2 == 0, chip // 2, chips - 1 - chip // 2)


def onward(value, steps):
    order = ring_order(lax.axis_size("chip"))
    chips = len(order)
    return lax.ppermute(
        value, "chip", [(order[at], order[(at + steps) % chips]) for at in range(chips)]
    )


def slot_offsets(chips):
    offsets = [0]
    for far in range(1, chips // 2):
        offsets += [-far, far]
    return offsets + [chips // 2]


def tied(*values):
    return lax.optimization_barrier(values)


class RingGather:
    def __init__(self, shard):
        self.slots = [shard]
        self.ahead = self.back = shard
        self.left = lax.axis_size("chip") // 2

    def operands(self):
        half = self.ahead.shape[0] // 2
        if self.left == 1:
            return self.ahead[:half], self.back[half:]
        return self.ahead, self.back

    def send(self, ahead, back):
        self.ahead, self.back = tied(onward(ahead, 1), onward(back, -1))
        self.slots += [self.ahead, self.back]
        self.left -= 1
        return self.ahead

    def step(self):
        return self.send(*self.operands())

    def last(self):
        while self.left > 1:
            self.step()

    def hold(self, value):
        self.ahead, self.back, _ = tied(self.ahead, self.back, value)
        self.slots[-2:] = [self.ahead, self.back]


class RingReduce:
    def __init__(self, sums):
        self.sums = sums
        self.chips = lax.axis_size("chip")
        self.size = sums.shape[0] // self.chips
        self.left = self.chips // 2
        self.ahead = self.back = None

    def slot(self, index, start=0, stop=None):
        stop = self.size if stop is None else stop
        return self.sums[index * self.size + start : index * self.size + stop]

    def operands(self):
        half = self.size // 2
        if self.ahead is None:
            last = self.chips - 1
            return self.slot(last, 0, half), self.slot(last, half)
        ahead, back = self.ahead.astype(f32), self.back.astype(f32)
        if self.left == self.chips // 2 - 1:
            ahead = jnp.pad(ahead, ((0, half), (0, 0)))
            back = jnp.pad(back, ((half, 0), (0, 0)))
        return (
            (self.slot(2 * self.left).astype(f32) + ahead).astype(bf16),
            (self.slot(2 * self.left - 1).astype(f32) + back).astype(bf16),
        )

    def send(self, ahead, back):
        self.ahead, self.back = tied(onward(ahead, 1), onward(back, -1))
        self.left -= 1
        return self.ahead

    def step(self):
        return self.send(*self.operands())

    def hold(self, value):
        self.ahead, self.back, _ = tied(self.ahead, self.back, value)

    def total(self):
        while self.left > 0:
            self.step()
        return self.slot(0).astype(f32) + self.ahead.astype(f32) + self.back.astype(f32)


def small_hops(chips):
    if chips & (chips - 1):
        return [lambda value: lax.psum(value, ("chip", "core"))]
    hops = [lambda value: value + swapped(value)]
    for bit in range(chips.bit_length() - 1):
        pairs = [(chip, chip ^ (1 << bit)) for chip in range(chips)]
        hops.append(lambda value, pairs=pairs: value + lax.ppermute(value, "chip", pairs))
    return hops


def ring_columns(core):
    chips = lax.axis_size("chip")
    place = ring_place(lax.axis_index("chip"), chips)
    own = []
    for offset in slot_offsets(chips):
        at = (place + offset) % chips
        own.append(jnp.where(at < chips // 2, 2 * at, 2 * (chips - 1 - at) + 1))
    own = jnp.stack(own)
    width = D // (2 * chips)
    starts = jnp.concatenate([2 * own + core, 2 * own + 1 - core]) * width
    wanted = (starts[:, None] + jnp.arange(width)[None, :]).reshape(D)
    return (jnp.arange(D)[:, None] == wanted[None, :]).astype(bf16)


def per_device(
    inputs, out_grad, doc_ids, row_live, pre_gain, mlp_gain, mixer_gain, conv_weight, conv_bias,
    step_bias, decay_log, skip_scale, mixer_in_weight, mixer_out_weight, query_weight, key_weight,
    value_weight, attend_weight, gate_up_weight, down_weight,
):
    is_first = lax.axis_index("section") == 0
    core = lax.axis_index("core")
    shard = mixer_in_weight.shape[1]
    packed_a = jnp.concatenate(
        [
            mixer_in_weight[0, :, :AT_Q],
            query_weight[0],
            key_weight[0],
            value_weight[0],
            mixer_in_weight[0, :, AT_Q:],
            jnp.zeros((shard, LANES - MH), bf16),
        ],
        axis=1,
    )
    packed_b = jnp.concatenate(
        [mixer_out_weight[0].T, attend_weight[0].T, gate_up_weight[0], down_weight[0].T], axis=1
    )

    layout = row_layout(doc_ids)
    params = core_params(
        conv_weight[0], conv_bias[0], step_bias[0], decay_log[0], skip_scale[0], mixer_gain[0]
    )
    turn = ring_columns(core)

    def own_order(values):
        if values.dtype == bf16:
            return dot_nn(values, turn).astype(bf16)
        return dot_exact(values, turn.astype(f32))

    def whole_order(values):
        if values.dtype == bf16:
            return dot_nt(values, turn).astype(bf16)
        return dot_exact(values, turn.astype(f32).T)

    pre_row = own_order(pre_gain)
    mlp_row = own_order(mlp_gain)
    first_rows = own_order(inputs)

    positions = jnp.arange(TOK, dtype=jnp.int32)
    live = (positions[None, :] < row_live[:, None]).reshape(MB * TOK, 1)
    from_loss = own_order(jnp.where(live, out_grad, jnp.zeros_like(out_grad)))
    first_rows, from_loss = tied(first_rows, from_loss)

    ring_a = RingGather(packed_a)
    ring_b = RingGather(packed_b)
    ring_a.step()
    ring_b.step()
    ring_a.last()
    now_a, now_b = tied(ring_a.operands(), ring_b.operands())
    ring_a.send(*now_a)
    ring_b.send(*now_b)
    own_a = jnp.concatenate(ring_a.slots, axis=0)
    pair_a = (own_a, swapped(own_a))
    now_b, gain_now, pair_a = tied(ring_b.operands(), pre_row, pair_a)
    ring_b.send(*now_b)
    _, projected = project(first_rows, gain_now, *pair_a)
    projected = projected.reshape(MB, TOK, WIDE_A)
    mixed = core_forward(0, projected, layout, params)
    ring_b.hold(mixed)
    now_b, mixed = tied(ring_b.operands(), mixed)
    ring_b.send(*now_b)
    mixed, _, _ = core_forward(1, projected, layout, params, held=mixed)
    ring_b.hold(mixed)
    while ring_b.left:
        ring_b.step()
    pair_b = (
        jnp.concatenate(ring_b.slots, axis=0),
        jnp.concatenate([swapped(slot) for slot in ring_b.slots], axis=0),
    )
    mixed = mixed.reshape(MB * TOK, MIXED)
    handed = feed_forward(first_rows, mixed, mlp_row, *pair_b, keep=False)

    parts = [first_rows[row * TOK : (row + 1) * TOK] for row in range(MB)]
    received = [passed_along(one, "section", 1) for one in handed]
    held, cores = (), ()
    starts = []
    for row in range(MB):
        start = jnp.where(is_first, parts[row], received[row])
        held = project(start, pre_row, *pair_a, row=row, held=held)
        starts.append(start)
        cores = core_forward(row, held[1].reshape(MB, TOK, WIDE_A), layout, params, held=cores)
        if row + 1 < MB:
            received[row + 1], cores, held = tied(received[row + 1], cores, held)
    start_rows = jnp.concatenate(starts, axis=0)
    normed, projected = held
    projected = projected.reshape(MB, TOK, WIDE_A)
    mixed, pre, yns = cores
    mixed = mixed.reshape(MB * TOK, MIXED)
    result, middle, normed_two, gate, up, act = feed_forward(
        start_rows, mixed, mlp_row, *pair_b, keep=True
    )
    their_mixed = swapped(mixed)
    their_act = swapped(act)
    their_normed = swapped(normed[:, SIDE:])
    their_normed_two = swapped(normed_two[:, SIDE:])

    received = jnp.zeros((TOK, D), bf16)
    lefts = []
    rights = []
    rows = []
    picks = jnp.where(is_first, jnp.array([1, 0]), jnp.array([0, 1])).astype(jnp.int32)

    def tick_left(which):
        return [(lefts[1][which], None, 0), (lefts[2][which], None, 0)] + [
            (lefts[1][which + 2], None, 0), (lefts[2][which + 2], None, 0)
        ]

    def tick_right(which):
        return [(rights[tick][which + far], None) for far in (0, 2) for tick in (1, 2)]

    def saved_left(own, their):
        return [(own, 0, 0), (own, 1, 0), (their, 0, 0), (their, 1, 0)]

    def saved_right(own, their):
        return [(own, 0), (own, 1), (their, 0), (their, 1)]

    for tick in range(3):
        row = jnp.where(is_first, (1, 1, 0)[tick], (1, 0, 1)[tick]).astype(jnp.int32).reshape(1)
        if tick == 1:
            row, their_mixed, their_act, their_normed, their_normed_two = tied(
                row, their_mixed, their_act, their_normed, their_normed_two
            )
        if tick == 2:
            row, lefts[1], rights[1], rows[1] = tied(row, lefts[1], rights[1], rows[1])
        loss_row = (1, 0, 1)[tick]
        cotangent = jnp.where(
            is_first, received, from_loss[loss_row * TOK : (loss_row + 1) * TOK]
        )
        d_gate, d_up, d_middle, middle_low, d_mixed, mlp_grad = feed_back(
            row, cotangent, gate, up, middle, mlp_row, *pair_b
        )
        lefts.append(
            (cotangent, middle_low, swapped(cotangent[:, SIDE:]), swapped(middle_low[:, SIDE:]))
        )
        rights.append((d_gate, d_up, swapped(d_gate), swapped(d_up)))
        if tick == 2:
            sum_c = weight_grad(
                picks,
                1024,
                [
                    (tick_left(1), saved_right(mixed, their_mixed)),
                    (tick_left(0), saved_right(act, their_act)),
                ],
            )
            ring_c = RingReduce(sum_c)
            ring_c.step()
            picks_now, now_c, rights[2] = tied(picks, ring_c.operands(), rights[2])
            ring_c.send(*now_c)
            sum_b = weight_grad(
                picks_now,
                1024,
                [
                    (saved_left(normed_two, their_normed_two), tick_right(0)),
                    (saved_left(normed_two, their_normed_two), tick_right(1)),
                ],
            )
            ring_b = RingReduce(sum_b)
            ring_c.hold(sum_b)
            now_b, now_c, row = tied(ring_b.operands(), ring_c.operands(), row)
            ring_c.send(*now_c)
            ring_b.send(*now_b)
        proj_low, small = core_backward(row, projected, pre, yns, d_mixed, layout, params)
        if tick == 2:
            ring_b.hold(proj_low)
            ring_c.hold(proj_low)
            now_b, proj_low, ring_c.ahead, ring_c.back = tied(
                ring_b.operands(), proj_low, ring_c.ahead, ring_c.back
            )
            ring_b.send(*now_b)
        their_low = swapped(proj_low)
        d_rows, d_low, pre_grad = project_back(
            row, proj_low, start_rows, d_middle, pre_row, *pair_a
        )
        if tick == 2:
            (p_one, their_one), (p_two, their_two) = rows[1][1], (proj_low, their_low)
            ring_b.hold(d_rows)
            now_b, d_rows, their_two = tied(ring_b.operands(), d_rows, their_two)
            ring_b.send(*now_b)
            picks_now, d_rows, now_b = tied(picks, d_rows, now_b)
            sum_a = weight_grad(
                picks_now,
                WIDE_A // 3,
                [
                    (
                        saved_left(normed, their_normed),
                        [(p_one, None), (p_two, None), (their_one, None), (their_two, None)],
                    )
                ],
            )
            ring_b.hold(sum_a)
            rings_a = [RingReduce(sum_a[:, :CUT_A]), RingReduce(sum_a[:, CUT_A:])]
            now_a, now_b, d_rows = tied(
                [ring.operands() for ring in rings_a], ring_b.operands(), d_rows
            )
            for ring, now in zip(rings_a, now_a):
                ring.send(*now)
            ring_b.send(*now_b)
        rows.append((d_rows, (proj_low, their_low), pre_grad, mlp_grad, small))
        if tick < 2:
            received = passed_along(d_low, "section", -1)

    start_grad = jnp.concatenate(
        [
            jnp.where(is_first, rows[2][0], rows[1][0]),
            jnp.where(is_first, rows[1][0], rows[2][0]),
        ],
        axis=0,
    )
    pre_sum, mlp_sum, small = (one + two for one, two in zip(rows[1][2:], rows[2][2:]))
    gain_sums = whole_order(jnp.concatenate([pre_sum, mlp_sum], axis=0))
    small = jnp.concatenate([small, jnp.pad(gain_sums, ((0, 6), (0, CH - D)))], axis=0)
    hops = small_hops(lax.axis_size("chip"))
    small = hops.pop(0)(small)
    first_round = True
    while rings_a[0].left:
        for ring in rings_a:
            ring.step()
        if first_round:
            ring_c.step()
            first_round = False
        small = tied(small, rings_a[0].ahead)[0]
        if hops:
            small = hops.pop(0)(small)
    for hop in hops:
        small = hop(small)
    share_c = ring_c.total()
    share_b = ring_b.total()
    share_a = jnp.concatenate([ring.total() for ring in rings_a], axis=1)
    skip_sum = jnp.sum(small[6, :E].reshape(MH, MP), axis=1)
    mixer_in_grad = jnp.concatenate([share_a[:, :AT_Q], share_a[:, AT_DT : AT_DT + MH]], axis=1)
    return (
        whole_order(result)[None],
        whole_order(start_grad)[None],
        small[8:9, :D],
        small[9:10, :D],
        small[5:6, :E],
        small[None, :4],
        small[4:5],
        small[7:8, :MH],
        small[7:8, LANES : LANES + MH],
        skip_sum[None],
        mixer_in_grad[None],
        share_c[:, :E].T[None],
        share_a[:, AT_Q:AT_K][None],
        share_a[:, AT_K:AT_V][None],
        share_a[:, AT_V:AT_DT][None],
        share_c[:, E:MIXED].T[None],
        share_b[None],
        share_c[:, MIXED:].T[None],
    )


def solution(mesh):
    dp = mesh.shape["dp"]
    devices = mesh.devices.reshape(mesh.shape["section"], dp // 2, 2)
    paired = Mesh(devices, ("section", "chip", "core"))
    over = ("chip", "core")
    rows = P(over, None)
    small = P("section", None)
    by_row = P("section", over, None)
    by_col = P("section", None, over)
    small_specs = (small, small, small, P("section", None, None), small, small, small, small)
    big_specs = (by_row, by_col, by_row, by_row, by_row, by_col, by_row, by_col)
    in_specs = (rows, rows, rows, P(over)) + small_specs + big_specs
    out_specs = (by_row, by_row) + small_specs + big_specs
    return jax.shard_map(
        per_device, mesh=paired, in_specs=in_specs, out_specs=out_specs, check_vma=False
    )
```

```python
import functools
import math

import jax
import jax.numpy as jnp
from jax import lax
from jax.experimental import pallas as pl
from jax.experimental.pallas import tpu as pltpu
from jax.sharding import Mesh
from jax.sharding import PartitionSpec as P

D = 1024
FF = 2048
MH = 24
MP = 64
NS = 128
AH = 8
KVH = 2
HD = 64
MB = 2
TOK = 256
E = 1536
CH = 1792
HALF = TOK // 2
PAIRS = MH // 2
LANES = 128
SIDE = D // 2
MIB = 2**20

AT_W = E
AT_Q = E + CH
AT_K = AT_Q + AH * HD
AT_V = AT_K + KVH * HD
AT_DT = AT_V + KVH * HD
WIDE_A = AT_DT + LANES
CUT_A = 16 * LANES
MIXED = E + AH * HD
AT_GU = MIXED
AT_DN = AT_GU + 2 * FF
WIDE_B = AT_DN + FF

highest = lax.Precision.HIGHEST
epsilon = 1e-05
rope_base = 100000000000.0
bf16 = jnp.bfloat16
f32 = jnp.float32


def dot_nn(left, right):
    return lax.dot_general(left, right, (((1,), (0,)), ((), ())), preferred_element_type=f32)


def dot_nt(left, right):
    return lax.dot_general(left, right, (((1,), (1,)), ((), ())), preferred_element_type=f32)


def dot_tn(left, right):
    return lax.dot_general(left, right, (((0,), (0,)), ((), ())), preferred_element_type=f32)


def dot_exact(left, right):
    return lax.dot_general(
        left, right, (((1,), (0,)), ((), ())), precision=highest, preferred_element_type=f32
    )


def softplus(value):
    return jnp.maximum(value, 0.0) + jnp.log1p(jnp.exp(-jnp.abs(value)))


def lane_low(rows):
    return lax.broadcasted_iota(jnp.int32, (rows, LANES), 1) < HD


def rope_halves(rows):
    return (lax.broadcasted_iota(jnp.int32, (rows, LANES), 1) & (HD - 1)) < HD // 2


def rope_turn(tile, cosine, sine):
    swapped = jnp.where(
        rope_halves(tile.shape[0]),
        -pltpu.roll(tile, LANES - HD // 2, 1),
        pltpu.roll(tile, HD // 2, 1),
    )
    return tile * cosine + swapped * sine


def rope_back(tile, cosine, sine):
    swapped = jnp.where(
        rope_halves(tile.shape[0]),
        pltpu.roll(tile, LANES - HD // 2, 1),
        -pltpu.roll(tile, HD // 2, 1),
    )
    return tile * cosine + swapped * sine


def both_halves(tile):
    swapped = pltpu.roll(tile, HD, 1)
    low = lane_low(tile.shape[0])
    return (jnp.where(low, tile, swapped), jnp.where(low, swapped, tile))


def tile_at(index):
    return pl.ds(pl.multiple_of(index * LANES, LANES), LANES)


def tile_from(start, index):
    return pl.ds(pl.multiple_of(start + index * LANES, LANES), LANES)


def allowed_pairs(doc_col_ref, doc_row_ref):
    later = lax.broadcasted_iota(jnp.int32, (TOK, TOK), 0)
    early = lax.broadcasted_iota(jnp.int32, (TOK, TOK), 1)
    same = doc_col_ref[:, 0:1] == doc_row_ref[0:1, :]
    return (later >= early) & same


def core_forward_kernel(
    pa_ref, rope_ref, mask_ref, doc_col_ref, doc_row_ref, taps_ref, head_ref, wide_ref,
    xb_ref, pre_ref, yns_ref,
    conv_s, cb_s, sum_s,
):
    def conv_tile(index, carry):
        rows = pa_ref[:, tile_from(AT_W, index)]
        at = tile_at(index)
        total = taps_ref[4:5, at] + taps_ref[3:4, at] * rows
        for shift in (1, 2, 3):
            moved = mask_ref[:, (shift - 1) * LANES : shift * LANES] * pltpu.roll(rows, shift, 0)
            total = total + taps_ref[3 - shift : 4 - shift, at] * moved
        pre_ref[:, at] = total
        conv_s[:, at] = total * jax.nn.sigmoid(total)
        return carry

    lax.fori_loop(0, CH // LANES, conv_tile, 0)

    allowed = allowed_pairs(doc_col_ref, doc_row_ref)
    steps = softplus(pa_ref[:, AT_DT:] + head_ref[0:1, :])
    rates = -steps * head_ref[1:2, :]
    totals = dot_exact(jnp.where(allowed, 1.0, 0.0), rates)
    totals_t = totals.T
    inward = conv_s[:, E : E + NS].astype(bf16)
    outward = conv_s[:, E + NS :].astype(bf16)
    cb_s[...] = jnp.where(allowed, dot_nt(outward, inward), 0.0)
    low = lane_low(TOK)
    for pair in range(PAIRS):
        lanes = slice(pair * LANES, (pair + 1) * LANES)
        first = 2 * pair
        step_pair = jnp.where(low, steps[:, first : first + 1], steps[:, first + 1 : first + 2])
        scaled = (conv_s[:, lanes] * step_pair).astype(bf16)
        halves = []
        for head in (first, first + 1):
            col = totals[:, head : head + 1]
            row = totals_t[head : head + 1, :]
            top = jnp.exp(jnp.minimum(col[:HALF] - row[:, :HALF], 0.0)) * cb_s[:HALF, :HALF]
            end = jnp.exp(jnp.minimum(col[HALF:] - row, 0.0)) * cb_s[HALF:, :]
            halves.append(
                jnp.concatenate(
                    [dot_nn(top.astype(bf16), scaled[:HALF]), dot_nn(end.astype(bf16), scaled)],
                    axis=0,
                )
            )
        yns_ref[:, lanes] = jnp.where(low, halves[0], halves[1])

    sum_s[...] = jnp.zeros((TOK, LANES), f32)

    def gate_tile(index, carry):
        at = tile_at(index)
        gate = pa_ref[:, at]
        rows = yns_ref[:, at] + wide_ref[0:1, at] * conv_s[:, at]
        gated = rows * (gate * jax.nn.sigmoid(gate))
        sum_s[...] += gated * gated
        conv_s[:, at] = gated
        return carry

    lax.fori_loop(0, E // LANES, gate_tile, 0)
    scale = lax.rsqrt(jnp.sum(sum_s[...], axis=1, keepdims=True) * (1.0 / E) + epsilon)

    def norm_tile(index, carry):
        at = tile_at(index)
        xb_ref[:, at] = (conv_s[:, at] * scale * wide_ref[1:2, at]).astype(bf16)
        return carry

    lax.fori_loop(0, E // LANES, norm_tile, 0)

    cosine = rope_ref[:, :LANES]
    sine = rope_ref[:, LANES:]
    keys = both_halves(rope_turn(pa_ref[:, AT_K:AT_V], cosine, sine))
    values = both_halves(pa_ref[:, AT_V:AT_DT])
    keys = tuple(part.astype(bf16) for part in keys)
    values = tuple(part.astype(bf16) for part in values)
    for pair in range(AH // 2):
        group = pair // (AH // (2 * KVH))
        at = AT_Q + pair * LANES
        turned = rope_turn(pa_ref[:, at : at + LANES], cosine, sine) * (1.0 / math.sqrt(HD))
        halves = []
        for side in range(2):
            chosen = low if side == 0 else jnp.logical_not(low)
            query = jnp.where(chosen, turned, 0.0).astype(bf16)
            parts = []
            for rows, cols in ((slice(0, HALF), HALF), (slice(HALF, TOK), TOK)):
                scores = dot_nt(query[rows], keys[group][:cols])
                scores = jnp.where(allowed[rows, :cols], scores, -1e30)
                top = jnp.max(scores, axis=1, keepdims=True)
                weights = jnp.exp(scores - top)
                share = 1.0 / jnp.sum(weights, axis=1, keepdims=True)
                parts.append(dot_nn(weights.astype(bf16), values[group][:cols]) * share)
            halves.append(jnp.concatenate(parts, axis=0))
        out = jnp.where(low, halves[0], halves[1])
        xb_ref[:, E + pair * LANES : E + (pair + 1) * LANES] = out.astype(bf16)


def silu_slope(value, gate):
    return gate * (1.0 + value * (1.0 - gate))


def core_backward_kernel(
    pick_ref,
    pa_ref, pre_ref, yns_ref, dxb_ref, rope_ref, mask_ref, doc_col_ref, doc_row_ref,
    taps_ref, head_ref, wide_ref,
    pg_ref, small_ref,
    x_s, dx_s, dyb_s, cbt_s, dcbt_s, sum_s, ssum_s,
):
    small_ref[...] = jnp.zeros_like(small_ref)
    sum_s[...] = jnp.zeros((TOK, LANES), f32)
    ssum_s[...] = jnp.zeros((TOK, LANES), f32)

    def start_tile(index, carry):
        at = tile_at(index)
        pre = pre_ref[:, at]
        heads_in = pre * jax.nn.sigmoid(pre)
        x_s[:, at] = heads_in
        gate = pa_ref[:, at]
        rows = yns_ref[:, at] + wide_ref[0:1, at] * heads_in
        gated = rows * (gate * jax.nn.sigmoid(gate))
        sum_s[...] += gated * gated
        ssum_s[...] += dxb_ref[:, at] * wide_ref[1:2, at] * gated
        return carry

    lax.fori_loop(0, E // LANES, start_tile, 0)
    scale = lax.rsqrt(jnp.sum(sum_s[...], axis=1, keepdims=True) * (1.0 / E) + epsilon)
    pull = jnp.sum(ssum_s[...], axis=1, keepdims=True) * (1.0 / E) * scale * scale * scale

    def gate_tile(index, carry):
        at = tile_at(index)
        heads_in = x_s[:, at]
        skip = wide_ref[0:1, at]
        gate = pa_ref[:, at]
        opened = jax.nn.sigmoid(gate)
        rows = yns_ref[:, at] + skip * heads_in
        gated = rows * (gate * opened)
        arrived = dxb_ref[:, at]
        d_gated = scale * (arrived * wide_ref[1:2, at]) - gated * pull
        small_ref[5:6, at] = jnp.sum(arrived * gated * scale, axis=0, keepdims=True)
        d_rows = d_gated * (gate * opened)
        pg_ref[:, at] = (d_gated * rows * silu_slope(gate, opened)).astype(bf16)
        small_ref[6:7, at] = jnp.sum(d_rows * heads_in, axis=0, keepdims=True)
        dyb_s[:, at] = d_rows.astype(bf16)
        dx_s[:, at] = skip * d_rows
        return carry

    lax.fori_loop(0, E // LANES, gate_tile, 0)

    def state_tile(index, carry):
        at = tile_from(E, index)
        pre = pre_ref[:, at]
        x_s[:, at] = pre * jax.nn.sigmoid(pre)
        return carry

    lax.fori_loop(0, 2, state_tile, 0)

    later = lax.broadcasted_iota(jnp.int32, (TOK, TOK), 1)
    early = lax.broadcasted_iota(jnp.int32, (TOK, TOK), 0)
    allowed_t = (later >= early) & (doc_col_ref[:, 0:1] == doc_row_ref[0:1, :])
    allowed = allowed_pairs(doc_col_ref, doc_row_ref)
    raw = pa_ref[:, AT_DT:] + head_ref[0:1, :]
    steps = softplus(raw)
    decay = head_ref[1:2, :]
    rates = -steps * decay
    totals = dot_exact(jnp.where(allowed, 1.0, 0.0), rates)
    totals_t = totals.T
    inward = x_s[:, E : E + NS].astype(bf16)
    outward = x_s[:, E + NS :].astype(bf16)
    cbt_s[...] = jnp.where(allowed_t, dot_nt(inward, outward), 0.0)
    dcbt_s[...] = jnp.zeros((TOK, TOK), f32)
    low = lane_low(TOK)
    spread_row = lax.broadcasted_iota(jnp.int32, (LANES, LANES), 0) >= HD
    spread_col = lax.broadcasted_iota(jnp.int32, (LANES, LANES), 1)
    sum_s[...] = jnp.zeros((TOK, LANES), f32)
    ssum_s[...] = jnp.zeros((TOK, LANES), f32)
    for pair in range(PAIRS):
        lanes = slice(pair * LANES, (pair + 1) * LANES)
        first = 2 * pair
        step_pair = jnp.where(low, steps[:, first : first + 1], steps[:, first + 1 : first + 2])
        heads_in = x_s[:, lanes]
        scaled = (heads_in * step_pair).astype(bf16)
        d_rows = dyb_s[:, lanes]
        halves = []
        for side, head in enumerate((first, first + 1)):
            chosen = low if side == 0 else jnp.logical_not(low)
            own = jnp.where(chosen, scaled, jnp.zeros_like(scaled))
            col = totals[:, head : head + 1]
            row = totals_t[head : head + 1, :]
            top = jnp.exp(jnp.minimum(row - col[:HALF], 0.0))
            end = jnp.exp(jnp.minimum(row[:, HALF:] - col[HALF:], 0.0))
            top_mix = (top * cbt_s[:HALF, :]).astype(bf16)
            end_mix = (end * cbt_s[HALF:, HALF:]).astype(bf16)
            dcbt_s[:HALF, :] += dot_nt(own[:HALF], d_rows) * top
            dcbt_s[HALF:, HALF:] += dot_nt(own[HALF:], d_rows[HALF:]) * end
            halves.append(
                jnp.concatenate(
                    [dot_nn(top_mix, d_rows), dot_nn(end_mix, d_rows[HALF:])], axis=0
                )
            )
        d_scaled = jnp.where(low, halves[0], halves[1])
        dx_s[:, lanes] += d_scaled * step_pair
        spread = (spread_col == jnp.where(spread_row, first + 1, first)).astype(bf16)
        for value, into in (
            (d_scaled * heads_in, sum_s),
            (d_rows.astype(f32) * yns_ref[:, lanes] - scaled.astype(f32) * d_scaled, ssum_s),
        ):
            coarse = value.astype(bf16)
            fine = (value - coarse.astype(f32)).astype(bf16)
            into[...] += dot_nn(coarse, spread) + dot_nn(fine, spread)

    d_rates = dot_exact(jnp.where(allowed_t, 1.0, 0.0), ssum_s[...])
    d_steps = sum_s[...] - decay * d_rates
    d_raw = d_steps * jax.nn.sigmoid(raw)
    pg_ref[:, AT_DT:] = d_raw.astype(bf16)
    small_ref[7:8, :LANES] = jnp.sum(d_raw, axis=0, keepdims=True)
    small_ref[7:8, LANES : 2 * LANES] = jnp.sum(d_rates * rates, axis=0, keepdims=True)
    d_pairs = jnp.where(allowed_t, dcbt_s[...], 0.0).astype(bf16)
    dx_s[:, E : E + NS] = dot_nn(d_pairs, outward)
    dx_s[:, E + NS :] = dot_tn(d_pairs, inward)

    def conv_tile(index, carry):
        at = tile_at(index)
        pre = pre_ref[:, at]
        d_pre = dx_s[:, at] * silu_slope(pre, jax.nn.sigmoid(pre))
        rows = pa_ref[:, tile_from(AT_W, index)]
        small_ref[4:5, at] = jnp.sum(d_pre, axis=0, keepdims=True)
        small_ref[3:4, at] = jnp.sum(d_pre * rows, axis=0, keepdims=True)
        back = taps_ref[3:4, at] * d_pre
        for shift in (1, 2, 3):
            held = mask_ref[:, (shift - 1) * LANES : shift * LANES] * d_pre
            small_ref[3 - shift : 4 - shift, at] = jnp.sum(
                held * pltpu.roll(rows, shift, 0), axis=0, keepdims=True
            )
            back = back + taps_ref[3 - shift : 4 - shift, at] * pltpu.roll(held, TOK - shift, 0)
        pg_ref[:, tile_from(AT_W, index)] = back.astype(bf16)
        return carry

    lax.fori_loop(0, CH // LANES, conv_tile, 0)

    cosine = rope_ref[:, :LANES]
    sine = rope_ref[:, LANES:]
    keys = both_halves(rope_turn(pa_ref[:, AT_K:AT_V], cosine, sine))
    values = both_halves(pa_ref[:, AT_V:AT_DT])
    keys = tuple(part.astype(bf16) for part in keys)
    values = tuple(part.astype(bf16) for part in values)
    root = 1.0 / math.sqrt(HD)
    d_keys = []
    d_values = []
    for group in range(KVH):
        key = keys[group]
        value = values[group]
        d_key = jnp.zeros((TOK, LANES), f32)
        d_value = jnp.zeros((TOK, LANES), f32)
        for pair in range(group * (AH // (2 * KVH)), (group + 1) * (AH // (2 * KVH))):
            at = AT_Q + pair * LANES
            turned = rope_turn(pa_ref[:, at : at + LANES], cosine, sine) * root
            arrived = dxb_ref[:, E + pair * LANES : E + (pair + 1) * LANES]
            halves = []
            for side in range(2):
                chosen = low if side == 0 else jnp.logical_not(low)
                query = jnp.where(chosen, turned, 0.0).astype(bf16)
                d_out = jnp.where(chosen, arrived, 0.0).astype(bf16)
                scores = jnp.where(allowed_t, dot_nt(key, query), -1e30)
                peak = jnp.max(scores, axis=0, keepdims=True)
                weights = jnp.exp(scores - peak)
                weights = weights * (1.0 / jnp.sum(weights, axis=0, keepdims=True))
                d_weights = dot_nt(value, d_out)
                offset = jnp.sum(weights * d_weights, axis=0, keepdims=True)
                d_scores = (weights * (d_weights - offset)).astype(bf16)
                d_value = d_value + dot_nn(weights.astype(bf16), d_out)
                d_key = d_key + dot_nn(d_scores, query)
                halves.append(dot_tn(d_scores, key))
            d_query = rope_back(jnp.where(low, halves[0], halves[1]) * root, cosine, sine)
            pg_ref[:, at : at + LANES] = d_query.astype(bf16)
        d_keys.append(d_key + pltpu.roll(d_key, HD, 1))
        d_values.append(d_value + pltpu.roll(d_value, HD, 1))
    d_key = rope_back(jnp.where(low, d_keys[0], d_keys[1]), cosine, sine)
    pg_ref[:, AT_K:AT_V] = d_key.astype(bf16)
    pg_ref[:, AT_V:AT_DT] = jnp.where(low, d_values[0], d_values[1]).astype(bf16)


def row_block(width):
    return pl.BlockSpec((None, TOK, width), lambda row: (row, 0, 0))


def whole_block(shape):
    return pl.BlockSpec(shape, lambda row: (0,) * len(shape))


def core_forward(row, projected, layout, params, held=()):
    rope, masks, doc_cols, doc_rows = layout
    taps, heads, wide = params

    def block(width, depth=TOK):
        return pl.BlockSpec((None, depth, width), lambda step: (row, 0, 0))

    kernel = core_forward_kernel
    if held:
        def kernel(*refs):
            core_forward_kernel(*refs[:8], *refs[11:])

    return pl.pallas_call(
        kernel,
        grid=(1,),
        in_specs=[
            block(WIDE_A),
            block(2 * LANES),
            block(3 * LANES),
            block(LANES),
            block(TOK, 8),
            whole_block(taps.shape),
            whole_block(heads.shape),
            whole_block(wide.shape),
        ]
        + [pl.BlockSpec(memory_space=pl.ANY)] * len(held),
        out_specs=[block(MIXED), block(CH), block(E)],
        out_shape=[
            jax.ShapeDtypeStruct((MB, TOK, MIXED), bf16),
            jax.ShapeDtypeStruct((MB, TOK, CH), f32),
            jax.ShapeDtypeStruct((MB, TOK, E), f32),
        ],
        scratch_shapes=[
            pltpu.VMEM((TOK, CH), f32),
            pltpu.VMEM((TOK, TOK), f32),
            pltpu.VMEM((TOK, LANES), f32),
        ],
        input_output_aliases={8: 0, 9: 1, 10: 2} if held else {},
        compiler_params=pltpu.CompilerParams(vmem_limit_bytes=26 * MIB),
        cost_estimate=pl.CostEstimate(
            flops=4 * 10**8, bytes_accessed=12 * 2**20, transcendentals=10**6
        ),
        name="core_forward",
    )(projected, rope, masks, doc_cols, doc_rows, taps, heads, wide, *held)


def core_backward(row, projected, pre, yns, d_mixed, layout, params):
    rope, masks, doc_cols, doc_rows = layout
    taps, heads, wide = params

    def picked(width, depth=TOK):
        return pl.BlockSpec((None, depth, width), lambda step, pick: (pick[0], 0, 0))

    def plain(shape):
        return pl.BlockSpec(shape, lambda step, pick: (0,) * len(shape))

    return pl.pallas_call(
        core_backward_kernel,
        grid_spec=pltpu.PrefetchScalarGridSpec(
            num_scalar_prefetch=1,
            grid=(1,),
            in_specs=[
                picked(WIDE_A),
                picked(CH),
                picked(E),
                plain((TOK, MIXED)),
                picked(2 * LANES),
                picked(3 * LANES),
                picked(LANES),
                picked(TOK, 8),
                plain(taps.shape),
                plain(heads.shape),
                plain(wide.shape),
            ],
            out_specs=[plain((TOK, WIDE_A)), plain((8, CH))],
            scratch_shapes=[
                pltpu.VMEM((TOK, CH), f32),
                pltpu.VMEM((TOK, CH), f32),
                pltpu.VMEM((TOK, E), bf16),
                pltpu.VMEM((TOK, TOK), f32),
                pltpu.VMEM((TOK, TOK), f32),
                pltpu.VMEM((TOK, LANES), f32),
                pltpu.VMEM((TOK, LANES), f32),
            ],
        ),
        out_shape=[
            jax.ShapeDtypeStruct((TOK, WIDE_A), bf16),
            jax.ShapeDtypeStruct((8, CH), f32),
        ],
        compiler_params=pltpu.CompilerParams(vmem_limit_bytes=34 * MIB),
        cost_estimate=pl.CostEstimate(
            flops=10**9, bytes_accessed=16 * 2**20, transcendentals=2 * 10**6
        ),
        name="core_backward",
    )(
        row, projected, pre, yns, d_mixed, rope, masks, doc_cols, doc_rows,
        taps, heads, wide,
    )


def passed_along(value, axis, steps):
    count = lax.axis_size(axis)
    leading, last = (max(0, -steps), min(count, count - steps))
    return lax.ppermute(value, axis, [(source, source + steps) for source in range(leading, last)])


def norm_rows(values):
    return lax.rsqrt(jnp.mean(values * values, axis=-1, keepdims=True) + epsilon)


def norm_back(values, gain, arrived):
    scale = norm_rows(values)
    weighted = arrived * gain
    pull = jnp.mean(weighted * values, axis=-1, keepdims=True) * scale * scale * scale
    gain_grad = jnp.sum(arrived * values * scale, axis=0, keepdims=True)
    return (weighted * scale - values * pull, gain_grad)


def project_kernel(rows_ref, gain_ref, own_ref, other_ref, normed_ref, out_ref):
    @pl.when(pl.program_id(0) == 0)
    def _():
        rows = rows_ref[...].astype(f32)
        normed_ref[...] = (rows * norm_rows(rows) * gain_ref[...]).astype(bf16)

    out_ref[...] = dot_nn(normed_ref[:, :SIDE], own_ref[...]) + dot_nn(
        normed_ref[:, SIDE:], other_ref[...]
    )


def project(rows, gain, own, other, row=None, held=()):
    count = rows.shape[0]
    tile = WIDE_A // 3
    weight = pl.BlockSpec((SIDE, tile), lambda step: (0, step))
    at = row or 0
    total = count if row is None else MB * TOK
    kernel = project_kernel
    if held:
        def kernel(rows_ref, gain_ref, own_ref, other_ref, old_normed, old_out, *outs):
            project_kernel(rows_ref, gain_ref, own_ref, other_ref, *outs)

    return pl.pallas_call(
        kernel,
        grid=(3,),
        in_specs=[whole_block((count, D)), whole_block((1, D)), weight, weight]
        + [pl.BlockSpec(memory_space=pl.ANY)] * len(held),
        out_specs=[
            pl.BlockSpec((count, D), lambda step: (at, 0)),
            pl.BlockSpec((count, tile), lambda step: (at, step)),
        ],
        out_shape=[
            jax.ShapeDtypeStruct((total, D), bf16),
            jax.ShapeDtypeStruct((total, WIDE_A), f32),
        ],
        input_output_aliases={4: 0, 5: 1} if held else {},
        compiler_params=pltpu.CompilerParams(vmem_limit_bytes=20 * MIB),
        cost_estimate=pl.CostEstimate(
            flops=2 * count * D * WIDE_A,
            bytes_accessed=2 * D * WIDE_A + 4 * count * WIDE_A,
            transcendentals=0,
        ),
        name="project",
    )(rows, gain, own, other, *held)


def feed_forward_kernel(
    keep, rows_ref, mixed_ref, gain_ref,
    out_own, out_other, gate_own, gate_other, up_own, up_other, down_own, down_other,
    *refs,
):
    if keep:
        low_ref, middle_ref, normed_ref, gate_ref, up_ref, act_ref, total_s = refs
    else:
        *row_refs, middle_ref, normed_ref, total_s = refs
    step = pl.program_id(0)

    @pl.when(step == 0)
    def _():
        middle_ref[...] = rows_ref[...].astype(f32)

    @pl.when(step < 4)
    def _():
        mixed = mixed_ref[...]
        middle_ref[:, :SIDE] += dot_nt(mixed, out_own[...])
        middle_ref[:, SIDE:] += dot_nt(mixed, out_other[...])

    @pl.when(step == 3)
    def _():
        middle = middle_ref[...]
        normed_ref[...] = (middle * norm_rows(middle) * gain_ref[...]).astype(bf16)
        total_s[...] = middle

    @pl.when(step >= 4)
    def _():
        left = normed_ref[:, :SIDE]
        right = normed_ref[:, SIDE:]
        gate = dot_nn(left, gate_own[...]) + dot_nn(right, gate_other[...])
        up = dot_nn(left, up_own[...]) + dot_nn(right, up_other[...])
        act = (gate * jax.nn.sigmoid(gate) * up).astype(bf16)
        if keep:
            gate_ref[...] = gate
            up_ref[...] = up
            act_ref[...] = act
        total_s[:, :SIDE] += dot_nt(act, down_own[...])
        total_s[:, SIDE:] += dot_nt(act, down_other[...])

    @pl.when(step == 7)
    def _():
        if keep:
            low_ref[...] = total_s[...].astype(bf16)
        else:
            for row, row_ref in enumerate(row_refs):
                row_ref[...] = total_s[row * TOK : (row + 1) * TOK, :].astype(bf16)


def b_block(start, skipped):
    return pl.BlockSpec(
        (SIDE, 512), lambda step, *pick: (0, start + jnp.clip(step - skipped, 0, 3))
    )


def b_blocks(parts):
    return [b_block(start, skipped) for start, skipped in parts for _ in range(2)]


def feed_forward(rows, mixed, gain, own, other, keep):
    count = rows.shape[0]
    wide = pl.BlockSpec((count, 512), lambda step: (0, jnp.clip(step - 4, 0, 3)))
    out_specs = [whole_block((count, D))]
    out_shape = [jax.ShapeDtypeStruct((count, D), bf16)]
    scratch = [pltpu.VMEM((count, D), f32)]
    if keep:
        out_specs += [whole_block((count, D)), whole_block((count, D)), wide, wide, wide]
        out_shape += [
            jax.ShapeDtypeStruct((count, D), f32),
            jax.ShapeDtypeStruct((count, D), bf16),
            jax.ShapeDtypeStruct((count, FF), f32),
            jax.ShapeDtypeStruct((count, FF), f32),
            jax.ShapeDtypeStruct((count, FF), bf16),
        ]
    else:
        out_specs = [whole_block((TOK, D))] * MB
        out_shape = [jax.ShapeDtypeStruct((TOK, D), bf16)] * MB
        scratch = [pltpu.VMEM((count, D), f32), pltpu.VMEM((count, D), bf16)] + scratch
    return pl.pallas_call(
        functools.partial(feed_forward_kernel, keep),
        grid=(8,),
        in_specs=[
            whole_block((count, D)),
            pl.BlockSpec((count, 512), lambda step: (0, jnp.clip(step, 0, 3))),
            whole_block((1, D)),
        ]
        + b_blocks(((0, 0), (4, 4), (8, 4), (12, 4))),
        out_specs=out_specs,
        out_shape=out_shape,
        scratch_shapes=scratch,
        compiler_params=pltpu.CompilerParams(vmem_limit_bytes=32 * MIB),
        cost_estimate=pl.CostEstimate(
            flops=2 * count * D * WIDE_B, bytes_accessed=2 * D * WIDE_B, transcendentals=0
        ),
        name="feed_forward",
    )(rows, mixed, gain, *([own, other] * 4))


def feed_back_kernel(
    pick_ref, cot_ref, gate_ref, up_ref, middle_ref, gain_ref,
    down_own, down_other, gate_own, gate_other, up_own, up_other, out_own, out_other,
    d_gate_ref, d_up_ref, d_middle_ref, low_ref, d_mixed_ref, gain_grad_ref,
    total_s,
):
    step = pl.program_id(0)

    @pl.when(step == 0)
    def _():
        total_s[...] = jnp.zeros_like(total_s)

    @pl.when(step < 4)
    def _():
        arrived = dot_nn(cot_ref[:, :SIDE], down_own[...]) + dot_nn(
            cot_ref[:, SIDE:], down_other[...]
        )
        gate = gate_ref[...]
        opened = jax.nn.sigmoid(gate)
        d_gate = (arrived * up_ref[...] * silu_slope(gate, opened)).astype(bf16)
        d_up = (arrived * (gate * opened)).astype(bf16)
        d_gate_ref[...] = d_gate
        d_up_ref[...] = d_up
        total_s[:, :SIDE] += dot_nt(d_gate, gate_own[...]) + dot_nt(d_up, up_own[...])
        total_s[:, SIDE:] += dot_nt(d_gate, gate_other[...]) + dot_nt(d_up, up_other[...])

    @pl.when(step == 3)
    def _():
        d_norm, gain_grad = norm_back(middle_ref[...], gain_ref[...], total_s[...])
        d_middle = cot_ref[...].astype(f32) + d_norm
        d_middle_ref[...] = d_middle
        low_ref[...] = d_middle.astype(bf16)
        gain_grad_ref[...] = gain_grad

    @pl.when(step >= 4)
    def _():
        d_mixed_ref[...] = dot_nn(low_ref[:, :SIDE], out_own[...]) + dot_nn(
            low_ref[:, SIDE:], out_other[...]
        )


def feed_back(row, cotangent, gate, up, middle, gain, own, other):
    saved = pl.BlockSpec((TOK, 512), lambda step, pick: (pick[0], jnp.clip(step, 0, 3)))
    early = pl.BlockSpec((TOK, 512), lambda step, pick: (0, jnp.clip(step, 0, 3)))
    late = pl.BlockSpec((TOK, 512), lambda step, pick: (0, jnp.clip(step - 4, 0, 3)))
    full = pl.BlockSpec((TOK, D), lambda step, pick: (0, 0))
    gain_block = pl.BlockSpec((1, D), lambda step, pick: (0, 0))
    return pl.pallas_call(
        feed_back_kernel,
        grid_spec=pltpu.PrefetchScalarGridSpec(
            num_scalar_prefetch=1,
            grid=(8,),
            in_specs=[
                full,
                saved,
                saved,
                pl.BlockSpec((TOK, D), lambda step, pick: (pick[0], 0)),
                gain_block,
            ]
            + b_blocks(((12, 0), (4, 0), (8, 0), (0, 4))),
            out_specs=[early, early, full, full, late, gain_block],
            scratch_shapes=[pltpu.VMEM((TOK, D), f32)],
        ),
        out_shape=[
            jax.ShapeDtypeStruct((TOK, FF), bf16),
            jax.ShapeDtypeStruct((TOK, FF), bf16),
            jax.ShapeDtypeStruct((TOK, D), f32),
            jax.ShapeDtypeStruct((TOK, D), bf16),
            jax.ShapeDtypeStruct((TOK, MIXED), f32),
            jax.ShapeDtypeStruct((1, D), f32),
        ],
        compiler_params=pltpu.CompilerParams(vmem_limit_bytes=24 * MIB),
        cost_estimate=pl.CostEstimate(
            flops=2 * TOK * D * WIDE_B, bytes_accessed=2 * D * WIDE_B, transcendentals=0
        ),
        name="feed_back",
    )(row, cotangent, gate, up, middle, gain, *([own, other] * 4))


def project_back_kernel(
    pick_ref, grad_ref, rows_ref, d_middle_ref, gain_ref, own_ref, other_ref,
    d_rows_ref, low_ref, gain_grad_ref, total_s,
):
    step = pl.program_id(0)

    @pl.when(step == 0)
    def _():
        total_s[...] = jnp.zeros_like(total_s)

    total_s[:, :SIDE] += dot_nt(grad_ref[...], own_ref[...])
    total_s[:, SIDE:] += dot_nt(grad_ref[...], other_ref[...])

    @pl.when(step == 2)
    def _():
        d_norm, gain_grad = norm_back(rows_ref[...].astype(f32), gain_ref[...], total_s[...])
        d_rows = d_middle_ref[...] + d_norm
        d_rows_ref[...] = d_rows
        low_ref[...] = d_rows.astype(bf16)
        gain_grad_ref[...] = gain_grad


def project_back(row, proj_low, start_rows, d_middle, gain, own, other):
    tile = WIDE_A // 3
    weight = pl.BlockSpec((SIDE, tile), lambda step, pick: (0, step))
    full = pl.BlockSpec((TOK, D), lambda step, pick: (0, 0))
    gain_block = pl.BlockSpec((1, D), lambda step, pick: (0, 0))
    return pl.pallas_call(
        project_back_kernel,
        grid_spec=pltpu.PrefetchScalarGridSpec(
            num_scalar_prefetch=1,
            grid=(3,),
            in_specs=[
                pl.BlockSpec((TOK, tile), lambda step, pick: (0, step)),
                pl.BlockSpec((TOK, D), lambda step, pick: (pick[0], 0)),
                full,
                gain_block,
                weight,
                weight,
            ],
            out_specs=[full, full, gain_block],
            scratch_shapes=[pltpu.VMEM((TOK, D), f32)],
        ),
        out_shape=[
            jax.ShapeDtypeStruct((TOK, D), f32),
            jax.ShapeDtypeStruct((TOK, D), bf16),
            jax.ShapeDtypeStruct((1, D), f32),
        ],
        compiler_params=pltpu.CompilerParams(vmem_limit_bytes=18 * MIB),
        cost_estimate=pl.CostEstimate(
            flops=2 * TOK * D * WIDE_A, bytes_accessed=2 * D * WIDE_A, transcendentals=0
        ),
        name="project_back",
    )(row, proj_low, start_rows, d_middle, gain, own, other)


def weight_grad_kernel(groups, pick_ref, *refs):
    lefts = refs[: 4 * len(groups)]
    rights = refs[4 * len(groups) : 8 * len(groups)]
    sum_ref, left_s = refs[8 * len(groups) :]
    step = pl.program_id(0)
    for index, (start, count) in enumerate(groups):
        four = lefts[4 * index : 4 * index + 4]
        blocks = rights[4 * index : 4 * index + 4]

        @pl.when(step == start)
        def _(four=four):
            for place, ref in enumerate(four):
                left_s[:, place * TOK : (place + 1) * TOK] = ref[...].astype(f32).T.astype(bf16)

        @pl.when((step >= start) & (step < start + count))
        def _(blocks=blocks):
            right = jnp.concatenate([ref[...] for ref in blocks], axis=0)
            sum_ref[...] = dot_nn(left_s[...], right).astype(bf16)


def weight_grad(picks, tile, groups):
    steps = []
    in_left = []
    in_right = []
    operands_left = []
    operands_right = []
    start = 0
    for left, right in groups:
        count = right[0][0].shape[1] // tile
        steps.append((start, count))
        for array, which, column in left:
            in_left.append(
                pl.BlockSpec(
                    (TOK, SIDE),
                    lambda step, pick, which=which, column=column: (
                        0 if which is None else pick[which],
                        column,
                    ),
                )
            )
            operands_left.append(array)
        for array, which in right:
            in_right.append(
                pl.BlockSpec(
                    (TOK, tile),
                    lambda step, pick, which=which, start=start, count=count: (
                        0 if which is None else pick[which],
                        jnp.clip(step - start, 0, count - 1),
                    ),
                )
            )
            operands_right.append(array)
        start += count
    return pl.pallas_call(
        functools.partial(weight_grad_kernel, tuple(steps)),
        grid_spec=pltpu.PrefetchScalarGridSpec(
            num_scalar_prefetch=1,
            grid=(start,),
            in_specs=in_left + in_right,
            out_specs=pl.BlockSpec((SIDE, tile), lambda step, pick: (0, step)),
            scratch_shapes=[pltpu.VMEM((SIDE, 4 * TOK), bf16)],
        ),
        out_shape=jax.ShapeDtypeStruct((SIDE, start * tile), bf16),
        compiler_params=pltpu.CompilerParams(vmem_limit_bytes=30 * MIB),
        cost_estimate=pl.CostEstimate(
            flops=8 * TOK * SIDE * start * tile,
            bytes_accessed=4 * SIDE * start * tile,
            transcendentals=0,
        ),
        name="weight_grad",
    )(picks, *operands_left, *operands_right)


def row_layout(doc_ids):
    rows = doc_ids.shape[0]
    positions = jnp.arange(TOK, dtype=jnp.int32)
    earlier = jnp.sum((doc_ids[:, None, :] < doc_ids[:, :, None]).astype(jnp.int32), axis=2)
    places = positions[None, :] - earlier
    half_dim = HD // 2
    inverse_freq = rope_base ** (-jnp.arange(half_dim, dtype=f32) / half_dim)
    angles = places.astype(f32)[:, :, None] * inverse_freq[None, None, :]
    repeats = LANES // half_dim
    rope = jnp.concatenate([jnp.cos(angles)] * repeats + [jnp.sin(angles)] * repeats, axis=-1)
    masks = jnp.concatenate(
        [
            jnp.broadcast_to((places >= shift).astype(f32)[:, :, None], (rows, TOK, LANES))
            for shift in (1, 2, 3)
        ],
        axis=-1,
    )
    doc_cols = jnp.broadcast_to(doc_ids[:, :, None], (rows, TOK, LANES))
    doc_rows = jnp.broadcast_to(doc_ids[:, None, :], (rows, 8, TOK))
    return (rope, masks, doc_cols, doc_rows)


def core_params(conv_weight, conv_bias, step_bias, decay_log, skip_scale, mixer_gain):
    taps = jnp.concatenate([conv_weight, conv_bias[None], jnp.zeros((3, CH), f32)], axis=0)
    heads = jnp.zeros((8, LANES), f32)
    heads = heads.at[0, :MH].set(step_bias).at[1, :MH].set(jnp.exp(decay_log))
    wide = jnp.concatenate(
        [jnp.repeat(skip_scale, MP)[None], mixer_gain[None], jnp.zeros((6, E), f32)], axis=0
    )
    return (taps, heads, wide)


def swapped(value):
    return lax.ppermute(value, "core", [(0, 1), (1, 0)])


def ring_order(chips):
    return [2 * step for step in range(chips // 2)] + [
        2 * step + 1 for step in reversed(range(chips // 2))
    ]


def ring_place(chip, chips):
    return jnp.where(chip % 2 == 0, chip // 2, chips - 1 - chip // 2)


def onward(value, steps):
    order = ring_order(lax.axis_size("chip"))
    chips = len(order)
    return lax.ppermute(
        value, "chip", [(order[at], order[(at + steps) % chips]) for at in range(chips)]
    )


def slot_offsets(chips):
    offsets = [0]
    for far in range(1, chips // 2):
        offsets += [-far, far]
    return offsets + [chips // 2]


def tied(*values):
    return lax.optimization_barrier(values)


class RingGather:
    def __init__(self, shard):
        self.slots = [shard]
        self.ahead = self.back = shard
        self.left = lax.axis_size("chip") // 2

    def operands(self):
        half = self.ahead.shape[0] // 2
        if self.left == 1:
            return self.ahead[:half], self.back[half:]
        return self.ahead, self.back

    def send(self, ahead, back):
        self.ahead, self.back = tied(onward(ahead, 1), onward(back, -1))
        self.slots += [self.ahead, self.back]
        self.left -= 1
        return self.ahead

    def step(self):
        return self.send(*self.operands())

    def last(self):
        while self.left > 1:
            self.step()

    def hold(self, value):
        self.ahead, self.back, _ = tied(self.ahead, self.back, value)
        self.slots[-2:] = [self.ahead, self.back]


class RingReduce:
    def __init__(self, sums):
        self.sums = sums
        self.chips = lax.axis_size("chip")
        self.size = sums.shape[0] // self.chips
        self.left = self.chips // 2
        self.ahead = self.back = None

    def slot(self, index, start=0, stop=None):
        stop = self.size if stop is None else stop
        return self.sums[index * self.size + start : index * self.size + stop]

    def operands(self):
        half = self.size // 2
        if self.ahead is None:
            last = self.chips - 1
            return self.slot(last, 0, half), self.slot(last, half)
        ahead, back = self.ahead.astype(f32), self.back.astype(f32)
        if self.left == self.chips // 2 - 1:
            ahead = jnp.pad(ahead, ((0, half), (0, 0)))
            back = jnp.pad(back, ((half, 0), (0, 0)))
        return (
            (self.slot(2 * self.left).astype(f32) + ahead).astype(bf16),
            (self.slot(2 * self.left - 1).astype(f32) + back).astype(bf16),
        )

    def send(self, ahead, back):
        self.ahead, self.back = tied(onward(ahead, 1), onward(back, -1))
        self.left -= 1
        return self.ahead

    def step(self):
        return self.send(*self.operands())

    def hold(self, value):
        self.ahead, self.back, _ = tied(self.ahead, self.back, value)

    def total(self):
        while self.left > 0:
            self.step()
        return self.slot(0).astype(f32) + self.ahead.astype(f32) + self.back.astype(f32)


def small_hops(chips):
    if chips & (chips - 1):
        return [lambda value: lax.psum(value, ("chip", "core"))]
    hops = [lambda value: value + swapped(value)]
    for bit in range(chips.bit_length() - 1):
        pairs = [(chip, chip ^ (1 << bit)) for chip in range(chips)]
        hops.append(lambda value, pairs=pairs: value + lax.ppermute(value, "chip", pairs))
    return hops


def ring_columns(core):
    chips = lax.axis_size("chip")
    place = ring_place(lax.axis_index("chip"), chips)
    own = []
    for offset in slot_offsets(chips):
        at = (place + offset) % chips
        own.append(jnp.where(at < chips // 2, 2 * at, 2 * (chips - 1 - at) + 1))
    own = jnp.stack(own)
    width = D // (2 * chips)
    starts = jnp.concatenate([2 * own + core, 2 * own + 1 - core]) * width
    wanted = (starts[:, None] + jnp.arange(width)[None, :]).reshape(D)
    return (jnp.arange(D)[:, None] == wanted[None, :]).astype(bf16)


def per_device(
    inputs, out_grad, doc_ids, row_live, pre_gain, mlp_gain, mixer_gain, conv_weight, conv_bias,
    step_bias, decay_log, skip_scale, mixer_in_weight, mixer_out_weight, query_weight, key_weight,
    value_weight, attend_weight, gate_up_weight, down_weight,
):
    is_first = lax.axis_index("section") == 0
    core = lax.axis_index("core")
    shard = mixer_in_weight.shape[1]
    packed_a = jnp.concatenate(
        [
            mixer_in_weight[0, :, :AT_Q],
            query_weight[0],
            key_weight[0],
            value_weight[0],
            mixer_in_weight[0, :, AT_Q:],
            jnp.zeros((shard, LANES - MH), bf16),
        ],
        axis=1,
    )
    packed_b = jnp.concatenate(
        [mixer_out_weight[0].T, attend_weight[0].T, gate_up_weight[0], down_weight[0].T], axis=1
    )

    layout = row_layout(doc_ids)
    params = core_params(
        conv_weight[0], conv_bias[0], step_bias[0], decay_log[0], skip_scale[0], mixer_gain[0]
    )
    turn = ring_columns(core)

    def own_order(values):
        if values.dtype == bf16:
            return dot_nn(values, turn).astype(bf16)
        return dot_exact(values, turn.astype(f32))

    def whole_order(values):
        if values.dtype == bf16:
            return dot_nt(values, turn).astype(bf16)
        return dot_exact(values, turn.astype(f32).T)

    pre_row = own_order(pre_gain)
    mlp_row = own_order(mlp_gain)
    first_rows = own_order(inputs)

    positions = jnp.arange(TOK, dtype=jnp.int32)
    live = (positions[None, :] < row_live[:, None]).reshape(MB * TOK, 1)
    from_loss = own_order(jnp.where(live, out_grad, jnp.zeros_like(out_grad)))
    first_rows, from_loss = tied(first_rows, from_loss)

    ring_a = RingGather(packed_a)
    ring_b = RingGather(packed_b)
    ring_a.step()
    ring_b.step()
    ring_a.last()
    now_a, now_b = tied(ring_a.operands(), ring_b.operands())
    ring_a.send(*now_a)
    ring_b.send(*now_b)
    own_a = jnp.concatenate(ring_a.slots, axis=0)
    pair_a = (own_a, swapped(own_a))
    now_b, gain_now, pair_a = tied(ring_b.operands(), pre_row, pair_a)
    ring_b.send(*now_b)
    _, projected = project(first_rows, gain_now, *pair_a)
    projected = projected.reshape(MB, TOK, WIDE_A)
    mixed = core_forward(0, projected, layout, params)
    ring_b.hold(mixed)
    now_b, mixed = tied(ring_b.operands(), mixed)
    ring_b.send(*now_b)
    mixed, _, _ = core_forward(1, projected, layout, params, held=mixed)
    ring_b.hold(mixed)
    while ring_b.left:
        ring_b.step()
    pair_b = (
        jnp.concatenate(ring_b.slots, axis=0),
        jnp.concatenate([swapped(slot) for slot in ring_b.slots], axis=0),
    )
    mixed = mixed.reshape(MB * TOK, MIXED)
    handed = feed_forward(first_rows, mixed, mlp_row, *pair_b, keep=False)

    parts = [first_rows[row * TOK : (row + 1) * TOK] for row in range(MB)]
    received = [passed_along(one, "section", 1) for one in handed]
    held, cores = (), ()
    starts = []
    for row in range(MB):
        start = jnp.where(is_first, parts[row], received[row])
        held = project(start, pre_row, *pair_a, row=row, held=held)
        starts.append(start)
        cores = core_forward(row, held[1].reshape(MB, TOK, WIDE_A), layout, params, held=cores)
        if row + 1 < MB:
            received[row + 1], cores, held = tied(received[row + 1], cores, held)
    start_rows = jnp.concatenate(starts, axis=0)
    normed, projected = held
    projected = projected.reshape(MB, TOK, WIDE_A)
    mixed, pre, yns = cores
    mixed = mixed.reshape(MB * TOK, MIXED)
    result, middle, normed_two, gate, up, act = feed_forward(
        start_rows, mixed, mlp_row, *pair_b, keep=True
    )
    their_mixed = swapped(mixed)
    their_act = swapped(act)
    their_normed = swapped(normed[:, SIDE:])
    their_normed_two = swapped(normed_two[:, SIDE:])

    received = jnp.zeros((TOK, D), bf16)
    lefts = []
    rights = []
    rows = []
    picks = jnp.where(is_first, jnp.array([1, 0]), jnp.array([0, 1])).astype(jnp.int32)

    def tick_left(which):
        return [(lefts[1][which], None, 0), (lefts[2][which], None, 0)] + [
            (lefts[1][which + 2], None, 0), (lefts[2][which + 2], None, 0)
        ]

    def tick_right(which):
        return [(rights[tick][which + far], None) for far in (0, 2) for tick in (1, 2)]

    def saved_left(own, their):
        return [(own, 0, 0), (own, 1, 0), (their, 0, 0), (their, 1, 0)]

    def saved_right(own, their):
        return [(own, 0), (own, 1), (their, 0), (their, 1)]

    for tick in range(3):
        row = jnp.where(is_first, (1, 1, 0)[tick], (1, 0, 1)[tick]).astype(jnp.int32).reshape(1)
        if tick == 1:
            row, their_mixed, their_act, their_normed, their_normed_two = tied(
                row, their_mixed, their_act, their_normed, their_normed_two
            )
        if tick == 2:
            row, lefts[1], rights[1], rows[1] = tied(row, lefts[1], rights[1], rows[1])
        loss_row = (1, 0, 1)[tick]
        cotangent = jnp.where(
            is_first, received, from_loss[loss_row * TOK : (loss_row + 1) * TOK]
        )
        d_gate, d_up, d_middle, middle_low, d_mixed, mlp_grad = feed_back(
            row, cotangent, gate, up, middle, mlp_row, *pair_b
        )
        lefts.append(
            (cotangent, middle_low, swapped(cotangent[:, SIDE:]), swapped(middle_low[:, SIDE:]))
        )
        rights.append((d_gate, d_up, swapped(d_gate), swapped(d_up)))
        if tick == 2:
            sum_c = weight_grad(
                picks,
                1024,
                [
                    (tick_left(1), saved_right(mixed, their_mixed)),
                    (tick_left(0), saved_right(act, their_act)),
                ],
            )
            ring_c = RingReduce(sum_c)
            ring_c.step()
            picks_now, now_c, rights[2] = tied(picks, ring_c.operands(), rights[2])
            ring_c.send(*now_c)
            sum_b = weight_grad(
                picks_now,
                1024,
                [
                    (saved_left(normed_two, their_normed_two), tick_right(0)),
                    (saved_left(normed_two, their_normed_two), tick_right(1)),
                ],
            )
            ring_b = RingReduce(sum_b)
            ring_c.hold(sum_b)
            now_b, now_c, row = tied(ring_b.operands(), ring_c.operands(), row)
            ring_c.send(*now_c)
            ring_b.send(*now_b)
        proj_low, small = core_backward(row, projected, pre, yns, d_mixed, layout, params)
        if tick == 2:
            ring_b.hold(proj_low)
            ring_c.hold(proj_low)
            now_b, proj_low, ring_c.ahead, ring_c.back = tied(
                ring_b.operands(), proj_low, ring_c.ahead, ring_c.back
            )
            ring_b.send(*now_b)
        their_low = swapped(proj_low)
        d_rows, d_low, pre_grad = project_back(
            row, proj_low, start_rows, d_middle, pre_row, *pair_a
        )
        if tick == 2:
            (p_one, their_one), (p_two, their_two) = rows[1][1], (proj_low, their_low)
            ring_b.hold(d_rows)
            now_b, d_rows, their_two = tied(ring_b.operands(), d_rows, their_two)
            ring_b.send(*now_b)
            picks_now, d_rows, now_b = tied(picks, d_rows, now_b)
            sum_a = weight_grad(
                picks_now,
                WIDE_A // 3,
                [
                    (
                        saved_left(normed, their_normed),
                        [(p_one, None), (p_two, None), (their_one, None), (their_two, None)],
                    )
                ],
            )
            ring_b.hold(sum_a)
            rings_a = [RingReduce(sum_a[:, :CUT_A]), RingReduce(sum_a[:, CUT_A:])]
            now_a, now_b, d_rows = tied(
                [ring.operands() for ring in rings_a], ring_b.operands(), d_rows
            )
            for ring, now in zip(rings_a, now_a):
                ring.send(*now)
            ring_b.send(*now_b)
        rows.append((d_rows, (proj_low, their_low), pre_grad, mlp_grad, small))
        if tick < 2:
            received = passed_along(d_low, "section", -1)

    start_grad = jnp.concatenate(
        [
            jnp.where(is_first, rows[2][0], rows[1][0]),
            jnp.where(is_first, rows[1][0], rows[2][0]),
        ],
        axis=0,
    )
    pre_sum, mlp_sum, small = (one + two for one, two in zip(rows[1][2:], rows[2][2:]))
    gain_sums = whole_order(jnp.concatenate([pre_sum, mlp_sum], axis=0))
    small = jnp.concatenate([small, jnp.pad(gain_sums, ((0, 6), (0, CH - D)))], axis=0)
    hops = small_hops(lax.axis_size("chip"))
    small = hops.pop(0)(small)
    first_round = True
    while rings_a[0].left:
        for ring in rings_a:
            ring.step()
        if first_round:
            ring_c.step()
            first_round = False
        small = tied(small, rings_a[0].ahead)[0]
        if hops:
            small = hops.pop(0)(small)
    for hop in hops:
        small = hop(small)
    share_c = ring_c.total()
    share_b = ring_b.total()
    share_a = jnp.concatenate([ring.total() for ring in rings_a], axis=1)
    skip_sum = jnp.sum(small[6, :E].reshape(MH, MP), axis=1)
    mixer_in_grad = jnp.concatenate([share_a[:, :AT_Q], share_a[:, AT_DT : AT_DT + MH]], axis=1)
    return (
        whole_order(result)[None],
        whole_order(start_grad)[None],
        small[8:9, :D],
        small[9:10, :D],
        small[5:6, :E],
        small[None, :4],
        small[4:5],
        small[7:8, :MH],
        small[7:8, LANES : LANES + MH],
        skip_sum[None],
        mixer_in_grad[None],
        share_c[:, :E].T[None],
        share_a[:, AT_Q:AT_K][None],
        share_a[:, AT_K:AT_V][None],
        share_a[:, AT_V:AT_DT][None],
        share_c[:, E:MIXED].T[None],
        share_b[None],
        share_c[:, MIXED:].T[None],
    )


def solution(mesh):
    dp = mesh.shape["dp"]
    devices = mesh.devices.reshape(mesh.shape["section"], dp // 2, 2)
    paired = Mesh(devices, ("section", "chip", "core"))
    over = ("chip", "core")
    rows = P(over, None)
    small = P("section", None)
    by_row = P("section", over, None)
    by_col = P("section", None, over)
    small_specs = (small, small, small, P("section", None, None), small, small, small, small)
    big_specs = (by_row, by_col, by_row, by_row, by_row, by_col, by_row, by_col)
    in_specs = (rows, rows, rows, P(over)) + small_specs + big_specs
    out_specs = (by_row, by_row) + small_specs + big_specs
    return jax.shard_map(
        per_device, mesh=paired, in_specs=in_specs, out_specs=out_specs, check_vma=False
    )
```

```python
import functools
import math

import jax
import jax.numpy as jnp
from jax import lax
from jax.experimental import pallas as pl
from jax.experimental.pallas import tpu as pltpu
from jax.sharding import Mesh
from jax.sharding import PartitionSpec as P

D = 1024
FF = 2048
MH = 24
MP = 64
NS = 128
AH = 8
KVH = 2
HD = 64
MB = 2
TOK = 256
E = 1536
CH = 1792
HALF = TOK // 2
PAIRS = MH // 2
LANES = 128
SIDE = D // 2
MIB = 2**20
CORE_VMEM = 18 * MIB
ATTEND_VMEM = 12 * MIB
MIXER_VMEM = 24 * MIB

AT_W = E
AT_Q = E + CH
AT_K = AT_Q + AH * HD
AT_V = AT_K + KVH * HD
AT_DT = AT_V + KVH * HD
WIDE_A = AT_DT + LANES
CUT_A = 16 * LANES
MIXED = E + AH * HD
AT_GU = MIXED
AT_DN = AT_GU + 2 * FF
WIDE_B = AT_DN + FF

highest = lax.Precision.HIGHEST
epsilon = 1e-05
rope_base = 100000000000.0
bf16 = jnp.bfloat16
f32 = jnp.float32


def dot_nn(left, right):
    return lax.dot_general(left, right, (((1,), (0,)), ((), ())), preferred_element_type=f32)


def dot_nt(left, right):
    return lax.dot_general(left, right, (((1,), (1,)), ((), ())), preferred_element_type=f32)


def dot_tn(left, right):
    return lax.dot_general(left, right, (((0,), (0,)), ((), ())), preferred_element_type=f32)


def dot_exact(left, right):
    return lax.dot_general(
        left, right, (((1,), (0,)), ((), ())), precision=highest, preferred_element_type=f32
    )


def softplus(value):
    return jnp.maximum(value, 0.0) + jnp.log1p(jnp.exp(-jnp.abs(value)))


def lane_low(rows):
    return lax.broadcasted_iota(jnp.int32, (rows, LANES), 1) < HD


def rope_halves(rows):
    return (lax.broadcasted_iota(jnp.int32, (rows, LANES), 1) & (HD - 1)) < HD // 2


def rope_turn(tile, cosine, sine):
    swapped = jnp.where(
        rope_halves(tile.shape[0]),
        -pltpu.roll(tile, LANES - HD // 2, 1),
        pltpu.roll(tile, HD // 2, 1),
    )
    return tile * cosine + swapped * sine


def rope_back(tile, cosine, sine):
    swapped = jnp.where(
        rope_halves(tile.shape[0]),
        pltpu.roll(tile, LANES - HD // 2, 1),
        -pltpu.roll(tile, HD // 2, 1),
    )
    return tile * cosine + swapped * sine


def both_halves(tile):
    swapped = pltpu.roll(tile, HD, 1)
    low = lane_low(tile.shape[0])
    return (jnp.where(low, tile, swapped), jnp.where(low, swapped, tile))


def tile_at(index):
    return pl.ds(pl.multiple_of(index * LANES, LANES), LANES)


def tile_from(start, index):
    return pl.ds(pl.multiple_of(start + index * LANES, LANES), LANES)


def allowed_pairs(doc_col_ref, doc_row_ref):
    later = lax.broadcasted_iota(jnp.int32, (TOK, TOK), 0)
    early = lax.broadcasted_iota(jnp.int32, (TOK, TOK), 1)
    same = doc_col_ref[:, 0:1] == doc_row_ref[0:1, :]
    return (later >= early) & same


def pair_rows(tile):
    low = lane_low(tile.shape[0])
    zero = jnp.zeros_like(tile)
    return jnp.concatenate([jnp.where(low, tile, zero), jnp.where(low, zero, tile)], axis=0)


def pair_lanes(rows):
    half = rows.shape[0] // 2
    return jnp.where(lane_low(half), rows[:half], rows[half:])


def core_forward_kernel(
    held, pm_ref, pq_ref, pd_ref, rope_ref, mask_ref, doc_col_ref, doc_row_ref,
    taps_ref, head_ref, wide_ref, *refs,
):
    xb_ref, pre_ref, yns_ref, conv_s, cb_s, bias_s, sum_s = refs[3:] if held else refs

    def conv_tile(index, carry):
        rows = pm_ref[:, tile_from(AT_W, index)].astype(f32)
        at = tile_at(index)
        total = taps_ref[4:5, at] + taps_ref[3:4, at] * rows
        for shift in (1, 2, 3):
            moved = mask_ref[:, (shift - 1) * LANES : shift * LANES] * pltpu.roll(rows, shift, 0)
            total = total + taps_ref[3 - shift : 4 - shift, at] * moved
        total = total.astype(bf16)
        pre_ref[:, at] = total
        total = total.astype(f32)
        conv_s[:, at] = total * jax.nn.sigmoid(total)
        return carry

    lax.fori_loop(0, CH // LANES, conv_tile, 0)

    allowed = allowed_pairs(doc_col_ref, doc_row_ref)
    bias_s[...] = jnp.where(allowed, 0.0, -1e30)
    steps = softplus(pd_ref[...] + head_ref[0:1, :])
    rates = -steps * head_ref[1:2, :]
    totals = dot_exact(jnp.where(allowed, 1.0, 0.0), rates)
    totals_t = totals.T
    inward = conv_s[:, E : E + NS].astype(bf16)
    outward = conv_s[:, E + NS :].astype(bf16)
    cb_s[...] = jnp.where(allowed, dot_nt(outward, inward), 0.0)
    low = lane_low(TOK)
    for pair in range(PAIRS):
        lanes = slice(pair * LANES, (pair + 1) * LANES)
        first = 2 * pair
        step_pair = jnp.where(low, steps[:, first : first + 1], steps[:, first + 1 : first + 2])
        scaled = (conv_s[:, lanes] * step_pair).astype(bf16)
        mixes = []
        for head in (first, first + 1):
            apart = totals[:, head : head + 1] - totals_t[head : head + 1, :]
            mixes.append((jnp.exp(jnp.minimum(apart, 0.0)) * cb_s[...]).astype(bf16))
        yns_ref[:, lanes] = pair_lanes(dot_nn(jnp.concatenate(mixes, axis=0), scaled))

    sum_s[...] = jnp.zeros((TOK, LANES), f32)

    def gate_tile(index, carry):
        at = tile_at(index)
        gate = pm_ref[:, at].astype(f32)
        rows = yns_ref[:, at] + wide_ref[0:1, at] * conv_s[:, at]
        gated = rows * (gate * jax.nn.sigmoid(gate))
        sum_s[...] += gated * gated
        conv_s[:, at] = gated
        return carry

    lax.fori_loop(0, E // LANES, gate_tile, 0)
    scale = lax.rsqrt(jnp.sum(sum_s[...], axis=1, keepdims=True) * (1.0 / E) + epsilon)

    def norm_tile(index, carry):
        at = tile_at(index)
        xb_ref[:, at] = (conv_s[:, at] * scale * wide_ref[1:2, at]).astype(bf16)
        return carry

    lax.fori_loop(0, E // LANES, norm_tile, 0)

    cosine = rope_ref[:, :LANES]
    sine = rope_ref[:, LANES:]
    keys = both_halves(rope_turn(pq_ref[:, AH * HD : AH * HD + LANES].astype(f32), cosine, sine))
    values = both_halves(pq_ref[:, AH * HD + LANES :].astype(f32))
    keys = tuple(part.astype(bf16) for part in keys)
    values = tuple(part.astype(bf16) for part in values)
    for pair in range(AH // 2):
        group = pair // (AH // (2 * KVH))
        at = pair * LANES
        turned = rope_turn(pq_ref[:, at : at + LANES].astype(f32), cosine, sine)
        scores = dot_nt(pair_rows((turned * (1.0 / math.sqrt(HD))).astype(bf16)), keys[group])
        weights = []
        shares = []
        for part in (scores[:TOK], scores[TOK:]):
            part = part + bias_s[...]
            part = jnp.exp(part - jnp.max(part, axis=1, keepdims=True))
            shares.append(1.0 / jnp.sum(part, axis=1, keepdims=True))
            weights.append(part.astype(bf16))
        out = pair_lanes(dot_nn(jnp.concatenate(weights, axis=0), values[group]))
        out = out * jnp.where(low, shares[0], shares[1])
        xb_ref[:, E + pair * LANES : E + (pair + 1) * LANES] = out.astype(bf16)


def silu_slope(value, gate):
    return gate * (1.0 + value * (1.0 - gate))


def attend_back_kernel(
    pick_ref, pq_ref, dxb_ref, rope_ref, doc_col_ref, doc_row_ref, pg_ref, bias_s
):
    later = lax.broadcasted_iota(jnp.int32, (TOK, TOK), 1)
    early = lax.broadcasted_iota(jnp.int32, (TOK, TOK), 0)
    allowed_t = (later >= early) & (doc_col_ref[:, 0:1] == doc_row_ref[0:1, :])
    bias_s[...] = jnp.where(allowed_t, 0.0, -1e30)
    low = lane_low(TOK)
    cosine = rope_ref[:, :LANES]
    sine = rope_ref[:, LANES:]
    keys = both_halves(rope_turn(pq_ref[:, AH * HD : AH * HD + LANES].astype(f32), cosine, sine))
    values = both_halves(pq_ref[:, AH * HD + LANES :].astype(f32))
    root = 1.0 / math.sqrt(HD)
    d_keys = []
    d_values = []
    for group in range(KVH):
        key = keys[group].astype(bf16)
        key_rows = pair_rows(key)
        value_rows = pair_rows(values[group].astype(bf16))
        d_key = jnp.zeros((TOK, LANES), f32)
        d_value = jnp.zeros((TOK, LANES), f32)
        for pair in range(group * (AH // (2 * KVH)), (group + 1) * (AH // (2 * KVH))):
            at = pair * LANES
            turned = rope_turn(pq_ref[:, at : at + LANES].astype(f32), cosine, sine) * root
            query = turned.astype(bf16)
            d_out = dxb_ref[:, E + at : E + at + LANES].astype(bf16)
            scores = dot_nt(key_rows, query)
            d_weights = dot_nt(value_rows, d_out)
            weights = []
            d_scores = []
            for part in (slice(0, TOK), slice(TOK, 2 * TOK)):
                score = scores[part] + bias_s[...]
                weight = jnp.exp(score - jnp.max(score, axis=0, keepdims=True))
                weight = weight * (1.0 / jnp.sum(weight, axis=0, keepdims=True))
                d_weight = d_weights[part]
                offset = jnp.sum(weight * d_weight, axis=0, keepdims=True)
                weights.append(weight.astype(bf16))
                d_scores.append((weight * (d_weight - offset)).astype(bf16))
            d_value = d_value + pair_lanes(dot_nn(jnp.concatenate(weights, axis=0), d_out))
            d_key = d_key + pair_lanes(dot_nn(jnp.concatenate(d_scores, axis=0), query))
            d_query = pair_lanes(dot_tn(jnp.concatenate(d_scores, axis=1), key))
            pg_ref[:, at : at + LANES] = rope_back(d_query * root, cosine, sine).astype(bf16)
        d_keys.append(d_key + pltpu.roll(d_key, HD, 1))
        d_values.append(d_value + pltpu.roll(d_value, HD, 1))
    d_key = rope_back(jnp.where(low, d_keys[0], d_keys[1]), cosine, sine)
    pg_ref[:, AH * HD : AH * HD + LANES] = d_key.astype(bf16)
    pg_ref[:, AH * HD + LANES :] = jnp.where(low, d_values[0], d_values[1]).astype(bf16)


def mixer_back_kernel(
    pick_ref, pm_ref, pd_ref, pre_ref, yns_ref, dxb_ref, attend_ref, mask_ref, doc_col_ref,
    doc_row_ref, taps_ref, head_ref, wide_ref,
    pg_ref, small_ref,
    x_s, dx_s, dyb_s, cbt_s, dcbt_s, sum_s, ssum_s,
):
    small_ref[...] = jnp.zeros_like(small_ref)
    pg_ref[:, AT_Q:AT_DT] = attend_ref[...]
    sum_s[...] = jnp.zeros((TOK, LANES), f32)
    ssum_s[...] = jnp.zeros((TOK, LANES), f32)

    def start_tile(index, carry):
        at = tile_at(index)
        pre = pre_ref[:, at].astype(f32)
        heads_in = pre * jax.nn.sigmoid(pre)
        x_s[:, at] = heads_in
        gate = pm_ref[:, at].astype(f32)
        rows = yns_ref[:, at] + wide_ref[0:1, at] * heads_in
        gated = rows * (gate * jax.nn.sigmoid(gate))
        sum_s[...] += gated * gated
        ssum_s[...] += dxb_ref[:, at] * wide_ref[1:2, at] * gated
        return carry

    lax.fori_loop(0, E // LANES, start_tile, 0)
    scale = lax.rsqrt(jnp.sum(sum_s[...], axis=1, keepdims=True) * (1.0 / E) + epsilon)
    pull = jnp.sum(ssum_s[...], axis=1, keepdims=True) * (1.0 / E) * scale * scale * scale

    def gate_tile(index, carry):
        at = tile_at(index)
        heads_in = x_s[:, at]
        skip = wide_ref[0:1, at]
        gate = pm_ref[:, at].astype(f32)
        opened = jax.nn.sigmoid(gate)
        rows = yns_ref[:, at] + skip * heads_in
        gated = rows * (gate * opened)
        arrived = dxb_ref[:, at]
        d_gated = scale * (arrived * wide_ref[1:2, at]) - gated * pull
        small_ref[5:6, at] = jnp.sum(arrived * gated * scale, axis=0, keepdims=True)
        d_rows = d_gated * (gate * opened)
        pg_ref[:, at] = (d_gated * rows * silu_slope(gate, opened)).astype(bf16)
        small_ref[6:7, at] = jnp.sum(d_rows * heads_in, axis=0, keepdims=True)
        dyb_s[:, at] = d_rows.astype(bf16)
        dx_s[:, at] = skip * d_rows
        return carry

    lax.fori_loop(0, E // LANES, gate_tile, 0)

    def state_tile(index, carry):
        at = tile_from(E, index)
        pre = pre_ref[:, at].astype(f32)
        x_s[:, at] = pre * jax.nn.sigmoid(pre)
        return carry

    lax.fori_loop(0, 2, state_tile, 0)

    later = lax.broadcasted_iota(jnp.int32, (TOK, TOK), 1)
    early = lax.broadcasted_iota(jnp.int32, (TOK, TOK), 0)
    allowed_t = (later >= early) & (doc_col_ref[:, 0:1] == doc_row_ref[0:1, :])
    allowed = allowed_pairs(doc_col_ref, doc_row_ref)
    raw = pd_ref[...] + head_ref[0:1, :]
    steps = softplus(raw)
    decay = head_ref[1:2, :]
    rates = -steps * decay
    totals = dot_exact(jnp.where(allowed, 1.0, 0.0), rates)
    totals_t = totals.T
    inward = x_s[:, E : E + NS].astype(bf16)
    outward = x_s[:, E + NS :].astype(bf16)
    cbt_s[...] = jnp.where(allowed_t, dot_nt(inward, outward), 0.0)
    dcbt_s[...] = jnp.zeros((TOK, TOK), f32)
    low = lane_low(TOK)
    spread_row = lax.broadcasted_iota(jnp.int32, (2 * LANES, LANES), 0) // HD
    spread_col = lax.broadcasted_iota(jnp.int32, (2 * LANES, LANES), 1)
    sum_s[...] = jnp.zeros((TOK, LANES), f32)
    ssum_s[...] = jnp.zeros((TOK, LANES), f32)
    waiting = None
    for pair in range(PAIRS):
        lanes = slice(pair * LANES, (pair + 1) * LANES)
        first = 2 * pair
        step_pair = jnp.where(low, steps[:, first : first + 1], steps[:, first + 1 : first + 2])
        heads_in = x_s[:, lanes]
        scaled = (heads_in * step_pair).astype(bf16)
        d_rows = dyb_s[:, lanes]
        d_mix = dot_nt(pair_rows(scaled), d_rows)
        mixes = []
        d_pairs = None
        for side, head in enumerate((first, first + 1)):
            apart = totals_t[head : head + 1, :] - totals[:, head : head + 1]
            decays = jnp.exp(jnp.minimum(apart, 0.0))
            mixes.append((decays * cbt_s[...]).astype(bf16))
            part = d_mix[side * TOK : (side + 1) * TOK] * decays
            d_pairs = part if d_pairs is None else d_pairs + part
        dcbt_s[...] += d_pairs
        d_scaled = pair_lanes(dot_nn(jnp.concatenate(mixes, axis=0), d_rows))
        dx_s[:, lanes] += d_scaled * step_pair
        value = d_rows.astype(f32) * yns_ref[:, lanes] - scaled.astype(f32) * d_scaled
        coarse = value.astype(bf16)
        fine = (value - coarse.astype(f32)).astype(bf16)
        spread = (spread_col == first + (spread_row & 1)).astype(bf16)
        ssum_s[...] += dot_nn(jnp.concatenate([coarse, fine], axis=1), spread)
        value = (d_scaled * heads_in).astype(bf16)
        if pair % 2 == 0:
            waiting = value
        else:
            spread = (spread_col == first - 2 + spread_row).astype(bf16)
            sum_s[...] += dot_nn(jnp.concatenate([waiting, value], axis=1), spread)

    d_rates = dot_exact(jnp.where(allowed_t, 1.0, 0.0), ssum_s[...])
    d_steps = sum_s[...] - decay * d_rates
    d_raw = d_steps * jax.nn.sigmoid(raw)
    pg_ref[:, AT_DT:] = d_raw.astype(bf16)
    small_ref[7:8, :LANES] = jnp.sum(d_raw, axis=0, keepdims=True)
    small_ref[7:8, LANES : 2 * LANES] = jnp.sum(d_rates * rates, axis=0, keepdims=True)
    d_pairs = jnp.where(allowed_t, dcbt_s[...], 0.0).astype(bf16)
    dx_s[:, E : E + NS] = dot_nn(d_pairs, outward)
    dx_s[:, E + NS :] = dot_tn(d_pairs, inward)

    def conv_tile(index, carry):
        at = tile_at(index)
        pre = pre_ref[:, at].astype(f32)
        d_pre = dx_s[:, at] * silu_slope(pre, jax.nn.sigmoid(pre))
        rows = pm_ref[:, tile_from(AT_W, index)].astype(f32)
        small_ref[4:5, at] = jnp.sum(d_pre, axis=0, keepdims=True)
        small_ref[3:4, at] = jnp.sum(d_pre * rows, axis=0, keepdims=True)
        back = taps_ref[3:4, at] * d_pre
        for shift in (1, 2, 3):
            held = mask_ref[:, (shift - 1) * LANES : shift * LANES] * d_pre
            small_ref[3 - shift : 4 - shift, at] = jnp.sum(
                held * pltpu.roll(rows, shift, 0), axis=0, keepdims=True
            )
            back = back + taps_ref[3 - shift : 4 - shift, at] * pltpu.roll(held, TOK - shift, 0)
        pg_ref[:, tile_from(AT_W, index)] = back.astype(bf16)
        return carry

    lax.fori_loop(0, CH // LANES, conv_tile, 0)


def whole_block(shape):
    return pl.BlockSpec(shape, lambda *steps: (0,) * len(shape))


def once(shape, place):
    return pl.BlockSpec(shape, place, pipeline_mode=pl.Buffered(1))


def core_forward(row, projected, layout, params, held=()):
    operands = (*projected, *layout)

    def block(array):
        return once((None,) + array.shape[1:], lambda step: (row, 0, 0))

    outs = [
        jax.ShapeDtypeStruct((MB, TOK, MIXED), bf16),
        jax.ShapeDtypeStruct((MB, TOK, CH), bf16),
        jax.ShapeDtypeStruct((MB, TOK, E), f32),
    ]
    return pl.pallas_call(
        functools.partial(core_forward_kernel, bool(held)),
        grid=(1,),
        in_specs=[block(array) for array in operands]
        + [once(array.shape, lambda step: (0, 0)) for array in params]
        + [pl.BlockSpec(memory_space=pl.ANY)] * len(held),
        out_specs=[block(array) for array in outs],
        out_shape=outs,
        scratch_shapes=[
            pltpu.VMEM((TOK, CH), f32),
            pltpu.VMEM((TOK, TOK), f32),
            pltpu.VMEM((TOK, TOK), f32),
            pltpu.VMEM((TOK, LANES), f32),
        ],
        input_output_aliases={10: 0, 11: 1, 12: 2} if held else {},
        compiler_params=pltpu.CompilerParams(vmem_limit_bytes=CORE_VMEM),
        cost_estimate=pl.CostEstimate(
            flops=4 * 10**8, bytes_accessed=12 * 2**20, transcendentals=10**6
        ),
        name="core_forward",
    )(*operands, *params, *held)


def core_back_specs(by_row, plain):
    return [
        once((None,) + array.shape[1:], lambda step, pick: (pick[0], 0, 0)) if chosen
        else once(array.shape, lambda step, pick: (0, 0))
        for chosen, arrays in ((True, by_row), (False, plain))
        for array in arrays
    ]


def attend_back(row, projected, d_mixed, layout):
    rope, masks, doc_cols, doc_rows = layout
    return pl.pallas_call(
        attend_back_kernel,
        grid_spec=pltpu.PrefetchScalarGridSpec(
            num_scalar_prefetch=1,
            grid=(1,),
            in_specs=core_back_specs([projected[1]], [d_mixed])
            + core_back_specs([rope, doc_cols, doc_rows], []),
            out_specs=once((TOK, AT_DT - AT_Q), lambda step, pick: (0, 0)),
            scratch_shapes=[pltpu.VMEM((TOK, TOK), f32)],
        ),
        out_shape=jax.ShapeDtypeStruct((TOK, AT_DT - AT_Q), bf16),
        compiler_params=pltpu.CompilerParams(vmem_limit_bytes=ATTEND_VMEM),
        cost_estimate=pl.CostEstimate(
            flops=3 * 10**8, bytes_accessed=4 * 2**20, transcendentals=6 * 10**5
        ),
        name="attend_back",
    )(row, projected[1], d_mixed, rope, doc_cols, doc_rows)


def mixer_back(row, projected, pre, yns, d_mixed, attended, layout, params):
    rope, masks, doc_cols, doc_rows = layout
    return pl.pallas_call(
        mixer_back_kernel,
        grid_spec=pltpu.PrefetchScalarGridSpec(
            num_scalar_prefetch=1,
            grid=(1,),
            in_specs=core_back_specs(
                [projected[0], projected[2], pre, yns], [d_mixed, attended]
            )
            + core_back_specs([masks, doc_cols, doc_rows], params),
            out_specs=[
                once((TOK, WIDE_A), lambda step, pick: (0, 0)),
                once((8, CH), lambda step, pick: (0, 0)),
            ],
            scratch_shapes=[
                pltpu.VMEM((TOK, CH), f32),
                pltpu.VMEM((TOK, CH), f32),
                pltpu.VMEM((TOK, E), bf16),
                pltpu.VMEM((TOK, TOK), f32),
                pltpu.VMEM((TOK, TOK), f32),
                pltpu.VMEM((TOK, LANES), f32),
                pltpu.VMEM((TOK, LANES), f32),
            ],
        ),
        out_shape=[
            jax.ShapeDtypeStruct((TOK, WIDE_A), bf16),
            jax.ShapeDtypeStruct((8, CH), f32),
        ],
        compiler_params=pltpu.CompilerParams(vmem_limit_bytes=MIXER_VMEM),
        cost_estimate=pl.CostEstimate(
            flops=7 * 10**8, bytes_accessed=10 * 2**20, transcendentals=15 * 10**5
        ),
        name="mixer_back",
    )(
        row, projected[0], projected[2], pre, yns, d_mixed, attended, masks, doc_cols, doc_rows,
        *params,
    )


def passed_along(value, axis, steps):
    count = lax.axis_size(axis)
    leading, last = (max(0, -steps), min(count, count - steps))
    return lax.ppermute(value, axis, [(source, source + steps) for source in range(leading, last)])


def norm_rows(values):
    return lax.rsqrt(jnp.mean(values * values, axis=-1, keepdims=True) + epsilon)


def norm_back(values, gain, arrived):
    scale = norm_rows(values)
    weighted = arrived * gain
    pull = jnp.mean(weighted * values, axis=-1, keepdims=True) * scale * scale * scale
    gain_grad = jnp.sum(arrived * values * scale, axis=0, keepdims=True)
    return (weighted * scale - values * pull, gain_grad)


def project_kernel(rows_ref, gain_ref, own_ref, other_ref, *refs):
    normed_ref, pm_ref, pq_ref, pd_ref = refs[-4:]
    step = pl.program_id(0)

    @pl.when(step == 0)
    def _():
        rows = rows_ref[...].astype(f32)
        normed_ref[...] = (rows * norm_rows(rows) * gain_ref[...]).astype(bf16)

    out = dot_nn(normed_ref[:, :SIDE], own_ref[...]) + dot_nn(normed_ref[:, SIDE:], other_ref[...])
    tile = WIDE_A // 3
    for index in range(2):
        @pl.when(step == index)
        def _(index=index):
            pm_ref[:, index * tile : (index + 1) * tile] = out.astype(bf16)

    @pl.when(step == 2)
    def _():
        pm_ref[:, 2 * tile :] = out[:, : AT_Q - 2 * tile].astype(bf16)
        pq_ref[...] = out[:, AT_Q - 2 * tile : AT_DT - 2 * tile].astype(bf16)
        pd_ref[...] = out[:, AT_DT - 2 * tile :]


def project(rows, gain, own, other, row=None, held=()):
    count = rows.shape[0]
    tile = WIDE_A // 3
    weight = pl.BlockSpec((SIDE, tile), lambda step: (0, step))
    at = row or 0
    total = count if row is None else MB * TOK
    widths = ((D, bf16), (AT_Q, bf16), (AT_DT - AT_Q, bf16), (LANES, f32))
    return pl.pallas_call(
        project_kernel,
        grid=(3,),
        in_specs=[whole_block((count, D)), whole_block((1, D)), weight, weight]
        + [pl.BlockSpec(memory_space=pl.ANY)] * len(held),
        out_specs=[pl.BlockSpec((count, width), lambda step: (at, 0)) for width, _ in widths],
        out_shape=[jax.ShapeDtypeStruct((total, width), kind) for width, kind in widths],
        input_output_aliases={4 + index: index for index in range(len(held))},
        compiler_params=pltpu.CompilerParams(vmem_limit_bytes=20 * MIB),
        cost_estimate=pl.CostEstimate(
            flops=2 * count * D * WIDE_A,
            bytes_accessed=2 * D * WIDE_A + 2 * count * WIDE_A,
            transcendentals=0,
        ),
        name="project",
    )(rows, gain, own, other, *held)


def by_row(projected):
    return tuple(array.reshape(MB, TOK, -1) for array in projected[1:])


def feed_forward_kernel(
    keep, rows_ref, mixed_ref, gain_ref,
    out_own, out_other, gate_own, gate_other, up_own, up_other, down_own, down_other,
    *refs,
):
    if keep:
        low_ref, middle_ref, normed_ref, gate_ref, up_ref, act_ref, total_s = refs
    else:
        *row_refs, middle_ref, normed_ref, total_s = refs
    step = pl.program_id(0)

    @pl.when(step == 0)
    def _():
        middle_ref[...] = rows_ref[...].astype(f32)

    @pl.when(step < 4)
    def _():
        mixed = mixed_ref[...]
        middle_ref[:, :SIDE] += dot_nt(mixed, out_own[...])
        middle_ref[:, SIDE:] += dot_nt(mixed, out_other[...])

    @pl.when(step == 3)
    def _():
        middle = middle_ref[...]
        normed_ref[...] = (middle * norm_rows(middle) * gain_ref[...]).astype(bf16)
        total_s[...] = middle

    @pl.when(step >= 4)
    def _():
        left = normed_ref[:, :SIDE]
        right = normed_ref[:, SIDE:]
        gate = dot_nn(left, gate_own[...]) + dot_nn(right, gate_other[...])
        up = dot_nn(left, up_own[...]) + dot_nn(right, up_other[...])
        act = (gate * jax.nn.sigmoid(gate) * up).astype(bf16)
        if keep:
            gate_ref[...] = gate.astype(bf16)
            up_ref[...] = up.astype(bf16)
            act_ref[...] = act
        total_s[:, :SIDE] += dot_nt(act, down_own[...])
        total_s[:, SIDE:] += dot_nt(act, down_other[...])

    @pl.when(step == 7)
    def _():
        if keep:
            low_ref[...] = total_s[...].astype(bf16)
        else:
            for row, row_ref in enumerate(row_refs):
                row_ref[...] = total_s[row * TOK : (row + 1) * TOK, :].astype(bf16)


def b_block(start, skipped):
    return pl.BlockSpec(
        (SIDE, 512), lambda step, *pick: (0, start + jnp.clip(step - skipped, 0, 3))
    )


def b_blocks(parts):
    return [b_block(start, skipped) for start, skipped in parts for _ in range(2)]


def feed_forward(rows, mixed, gain, own, other, keep):
    count = rows.shape[0]
    wide = pl.BlockSpec((count, 512), lambda step: (0, jnp.clip(step - 4, 0, 3)))
    out_specs = [whole_block((count, D))]
    out_shape = [jax.ShapeDtypeStruct((count, D), bf16)]
    scratch = [pltpu.VMEM((count, D), f32)]
    if keep:
        out_specs += [whole_block((count, D)), whole_block((count, D)), wide, wide, wide]
        out_shape += [
            jax.ShapeDtypeStruct((count, D), f32),
            jax.ShapeDtypeStruct((count, D), bf16),
            jax.ShapeDtypeStruct((count, FF), bf16),
            jax.ShapeDtypeStruct((count, FF), bf16),
            jax.ShapeDtypeStruct((count, FF), bf16),
        ]
    else:
        out_specs = [whole_block((TOK, D))] * MB
        out_shape = [jax.ShapeDtypeStruct((TOK, D), bf16)] * MB
        scratch = [pltpu.VMEM((count, D), f32), pltpu.VMEM((count, D), bf16)] + scratch
    return pl.pallas_call(
        functools.partial(feed_forward_kernel, keep),
        grid=(8,),
        in_specs=[
            whole_block((count, D)),
            pl.BlockSpec((count, 512), lambda step: (0, jnp.clip(step, 0, 3))),
            whole_block((1, D)),
        ]
        + b_blocks(((0, 0), (4, 4), (8, 4), (12, 4))),
        out_specs=out_specs,
        out_shape=out_shape,
        scratch_shapes=scratch,
        compiler_params=pltpu.CompilerParams(vmem_limit_bytes=32 * MIB),
        cost_estimate=pl.CostEstimate(
            flops=2 * count * D * WIDE_B, bytes_accessed=2 * D * WIDE_B, transcendentals=0
        ),
        name="feed_forward",
    )(rows, mixed, gain, *([own, other] * 4))


def feed_back_kernel(
    pick_ref, cot_ref, gate_ref, up_ref, middle_ref, gain_ref,
    down_own, down_other, gate_own, gate_other, up_own, up_other, out_own, out_other,
    d_gate_ref, d_up_ref, d_middle_ref, low_ref, d_mixed_ref, gain_grad_ref,
    total_s,
):
    step = pl.program_id(0)

    @pl.when(step == 0)
    def _():
        total_s[...] = jnp.zeros_like(total_s)

    @pl.when(step < 4)
    def _():
        arrived = dot_nn(cot_ref[:, :SIDE], down_own[...]) + dot_nn(
            cot_ref[:, SIDE:], down_other[...]
        )
        gate = gate_ref[...].astype(f32)
        opened = jax.nn.sigmoid(gate)
        d_gate = (arrived * up_ref[...].astype(f32) * silu_slope(gate, opened)).astype(bf16)
        d_up = (arrived * (gate * opened)).astype(bf16)
        d_gate_ref[...] = d_gate
        d_up_ref[...] = d_up
        total_s[:, :SIDE] += dot_nt(d_gate, gate_own[...]) + dot_nt(d_up, up_own[...])
        total_s[:, SIDE:] += dot_nt(d_gate, gate_other[...]) + dot_nt(d_up, up_other[...])

    @pl.when(step == 3)
    def _():
        d_norm, gain_grad = norm_back(middle_ref[...], gain_ref[...], total_s[...])
        d_middle = cot_ref[...].astype(f32) + d_norm
        d_middle_ref[...] = d_middle
        low_ref[...] = d_middle.astype(bf16)
        gain_grad_ref[...] = gain_grad

    @pl.when(step >= 4)
    def _():
        d_mixed_ref[...] = dot_nn(low_ref[:, :SIDE], out_own[...]) + dot_nn(
            low_ref[:, SIDE:], out_other[...]
        )


def feed_back(row, cotangent, gate, up, middle, gain, own, other):
    saved = pl.BlockSpec((TOK, 512), lambda step, pick: (pick[0], jnp.clip(step, 0, 3)))
    early = pl.BlockSpec((TOK, 512), lambda step, pick: (0, jnp.clip(step, 0, 3)))
    late = pl.BlockSpec((TOK, 512), lambda step, pick: (0, jnp.clip(step - 4, 0, 3)))
    full = pl.BlockSpec((TOK, D), lambda step, pick: (0, 0))
    gain_block = pl.BlockSpec((1, D), lambda step, pick: (0, 0))
    return pl.pallas_call(
        feed_back_kernel,
        grid_spec=pltpu.PrefetchScalarGridSpec(
            num_scalar_prefetch=1,
            grid=(8,),
            in_specs=[
                full,
                saved,
                saved,
                pl.BlockSpec((TOK, D), lambda step, pick: (pick[0], 0)),
                gain_block,
            ]
            + b_blocks(((12, 0), (4, 0), (8, 0), (0, 4))),
            out_specs=[early, early, full, full, late, gain_block],
            scratch_shapes=[pltpu.VMEM((TOK, D), f32)],
        ),
        out_shape=[
            jax.ShapeDtypeStruct((TOK, FF), bf16),
            jax.ShapeDtypeStruct((TOK, FF), bf16),
            jax.ShapeDtypeStruct((TOK, D), f32),
            jax.ShapeDtypeStruct((TOK, D), bf16),
            jax.ShapeDtypeStruct((TOK, MIXED), f32),
            jax.ShapeDtypeStruct((1, D), f32),
        ],
        compiler_params=pltpu.CompilerParams(vmem_limit_bytes=24 * MIB),
        cost_estimate=pl.CostEstimate(
            flops=2 * TOK * D * WIDE_B, bytes_accessed=2 * D * WIDE_B, transcendentals=0
        ),
        name="feed_back",
    )(row, cotangent, gate, up, middle, gain, *([own, other] * 4))


def project_back_kernel(
    pick_ref, grad_ref, rows_ref, d_middle_ref, gain_ref, own_ref, other_ref,
    d_rows_ref, low_ref, gain_grad_ref, total_s,
):
    step = pl.program_id(0)

    @pl.when(step == 0)
    def _():
        total_s[...] = jnp.zeros_like(total_s)

    total_s[:, :SIDE] += dot_nt(grad_ref[...], own_ref[...])
    total_s[:, SIDE:] += dot_nt(grad_ref[...], other_ref[...])

    @pl.when(step == 2)
    def _():
        d_norm, gain_grad = norm_back(rows_ref[...].astype(f32), gain_ref[...], total_s[...])
        d_rows = d_middle_ref[...] + d_norm
        d_rows_ref[...] = d_rows
        low_ref[...] = d_rows.astype(bf16)
        gain_grad_ref[...] = gain_grad


def project_back(row, proj_low, start_rows, d_middle, gain, own, other):
    tile = WIDE_A // 3
    weight = pl.BlockSpec((SIDE, tile), lambda step, pick: (0, step))
    full = pl.BlockSpec((TOK, D), lambda step, pick: (0, 0))
    gain_block = pl.BlockSpec((1, D), lambda step, pick: (0, 0))
    return pl.pallas_call(
        project_back_kernel,
        grid_spec=pltpu.PrefetchScalarGridSpec(
            num_scalar_prefetch=1,
            grid=(3,),
            in_specs=[
                pl.BlockSpec((TOK, tile), lambda step, pick: (0, step)),
                pl.BlockSpec((TOK, D), lambda step, pick: (pick[0], 0)),
                full,
                gain_block,
                weight,
                weight,
            ],
            out_specs=[full, full, gain_block],
            scratch_shapes=[pltpu.VMEM((TOK, D), f32)],
        ),
        out_shape=[
            jax.ShapeDtypeStruct((TOK, D), f32),
            jax.ShapeDtypeStruct((TOK, D), bf16),
            jax.ShapeDtypeStruct((1, D), f32),
        ],
        compiler_params=pltpu.CompilerParams(vmem_limit_bytes=18 * MIB),
        cost_estimate=pl.CostEstimate(
            flops=2 * TOK * D * WIDE_A, bytes_accessed=2 * D * WIDE_A, transcendentals=0
        ),
        name="project_back",
    )(row, proj_low, start_rows, d_middle, gain, own, other)


def weight_grad_kernel(groups, pick_ref, *refs):
    lefts = refs[: 4 * len(groups)]
    rights = refs[4 * len(groups) : 8 * len(groups)]
    sum_ref, left_s = refs[8 * len(groups) :]
    step = pl.program_id(0)
    for index, (start, count) in enumerate(groups):
        four = lefts[4 * index : 4 * index + 4]
        blocks = rights[4 * index : 4 * index + 4]

        @pl.when(step == start)
        def _(four=four):
            for place, ref in enumerate(four):
                left_s[:, place * TOK : (place + 1) * TOK] = ref[...].astype(f32).T.astype(bf16)

        @pl.when((step >= start) & (step < start + count))
        def _(blocks=blocks):
            right = jnp.concatenate([ref[...] for ref in blocks], axis=0)
            sum_ref[...] = dot_nn(left_s[...], right).astype(bf16)


def weight_grad(picks, tile, groups):
    steps = []
    in_left = []
    in_right = []
    operands_left = []
    operands_right = []
    start = 0
    for left, right in groups:
        count = right[0][0].shape[1] // tile
        steps.append((start, count))
        for array, which, column in left:
            in_left.append(
                pl.BlockSpec(
                    (TOK, SIDE),
                    lambda step, pick, which=which, column=column: (
                        0 if which is None else pick[which],
                        column,
                    ),
                )
            )
            operands_left.append(array)
        for array, which in right:
            in_right.append(
                pl.BlockSpec(
                    (TOK, tile),
                    lambda step, pick, which=which, start=start, count=count: (
                        0 if which is None else pick[which],
                        jnp.clip(step - start, 0, count - 1),
                    ),
                )
            )
            operands_right.append(array)
        start += count
    return pl.pallas_call(
        functools.partial(weight_grad_kernel, tuple(steps)),
        grid_spec=pltpu.PrefetchScalarGridSpec(
            num_scalar_prefetch=1,
            grid=(start,),
            in_specs=in_left + in_right,
            out_specs=pl.BlockSpec((SIDE, tile), lambda step, pick: (0, step)),
            scratch_shapes=[pltpu.VMEM((SIDE, 4 * TOK), bf16)],
        ),
        out_shape=jax.ShapeDtypeStruct((SIDE, start * tile), bf16),
        compiler_params=pltpu.CompilerParams(vmem_limit_bytes=30 * MIB),
        cost_estimate=pl.CostEstimate(
            flops=8 * TOK * SIDE * start * tile,
            bytes_accessed=4 * SIDE * start * tile,
            transcendentals=0,
        ),
        name="weight_grad",
    )(picks, *operands_left, *operands_right)


def row_layout(doc_ids):
    rows = doc_ids.shape[0]
    positions = jnp.arange(TOK, dtype=jnp.int32)
    earlier = jnp.sum((doc_ids[:, None, :] < doc_ids[:, :, None]).astype(jnp.int32), axis=2)
    places = positions[None, :] - earlier
    half_dim = HD // 2
    inverse_freq = rope_base ** (-jnp.arange(half_dim, dtype=f32) / half_dim)
    angles = places.astype(f32)[:, :, None] * inverse_freq[None, None, :]
    repeats = LANES // half_dim
    rope = jnp.concatenate([jnp.cos(angles)] * repeats + [jnp.sin(angles)] * repeats, axis=-1)
    masks = jnp.concatenate(
        [
            jnp.broadcast_to((places >= shift).astype(f32)[:, :, None], (rows, TOK, LANES))
            for shift in (1, 2, 3)
        ],
        axis=-1,
    )
    doc_cols = jnp.broadcast_to(doc_ids[:, :, None], (rows, TOK, LANES))
    doc_rows = jnp.broadcast_to(doc_ids[:, None, :], (rows, 8, TOK))
    return (rope, masks, doc_cols, doc_rows)


def core_params(conv_weight, conv_bias, step_bias, decay_log, skip_scale, mixer_gain):
    taps = jnp.concatenate([conv_weight, conv_bias[None], jnp.zeros((3, CH), f32)], axis=0)
    heads = jnp.zeros((8, LANES), f32)
    heads = heads.at[0, :MH].set(step_bias).at[1, :MH].set(jnp.exp(decay_log))
    wide = jnp.concatenate(
        [jnp.repeat(skip_scale, MP)[None], mixer_gain[None], jnp.zeros((6, E), f32)], axis=0
    )
    return (taps, heads, wide)


def swapped(value):
    return lax.ppermute(value, "core", [(0, 1), (1, 0)])


def ring_order(chips):
    return [2 * step for step in range(chips // 2)] + [
        2 * step + 1 for step in reversed(range(chips // 2))
    ]


def ring_place(chip, chips):
    return jnp.where(chip % 2 == 0, chip // 2, chips - 1 - chip // 2)


def onward(value, steps):
    order = ring_order(lax.axis_size("chip"))
    chips = len(order)
    return lax.ppermute(
        value, "chip", [(order[at], order[(at + steps) % chips]) for at in range(chips)]
    )


def slot_offsets(chips):
    offsets = [0]
    for far in range(1, chips // 2):
        offsets += [-far, far]
    return offsets + [chips // 2]


def tied(*values):
    return lax.optimization_barrier(values)


class RingGather:
    def __init__(self, shard):
        self.slots = [shard]
        self.ahead = self.back = shard
        self.left = lax.axis_size("chip") // 2

    def operands(self):
        half = self.ahead.shape[0] // 2
        if self.left == 1:
            return self.ahead[:half], self.back[half:]
        return self.ahead, self.back

    def send(self, ahead, back):
        self.ahead, self.back = tied(onward(ahead, 1), onward(back, -1))
        self.slots += [self.ahead, self.back]
        self.left -= 1
        return self.ahead

    def step(self):
        return self.send(*self.operands())

    def last(self):
        while self.left > 1:
            self.step()

    def hold(self, value):
        self.ahead, self.back, _ = tied(self.ahead, self.back, value)
        self.slots[-2:] = [self.ahead, self.back]


class RingReduce:
    def __init__(self, sums):
        self.sums = sums
        self.chips = lax.axis_size("chip")
        self.size = sums.shape[0] // self.chips
        self.left = self.chips // 2
        self.ahead = self.back = None

    def slot(self, index, start=0, stop=None):
        stop = self.size if stop is None else stop
        return self.sums[index * self.size + start : index * self.size + stop]

    def operands(self):
        half = self.size // 2
        if self.ahead is None:
            last = self.chips - 1
            return self.slot(last, 0, half), self.slot(last, half)
        ahead, back = self.ahead.astype(f32), self.back.astype(f32)
        if self.left == self.chips // 2 - 1:
            ahead = jnp.pad(ahead, ((0, half), (0, 0)))
            back = jnp.pad(back, ((half, 0), (0, 0)))
        return (
            (self.slot(2 * self.left).astype(f32) + ahead).astype(bf16),
            (self.slot(2 * self.left - 1).astype(f32) + back).astype(bf16),
        )

    def send(self, ahead, back):
        self.ahead, self.back = tied(onward(ahead, 1), onward(back, -1))
        self.left -= 1
        return self.ahead

    def step(self):
        return self.send(*self.operands())

    def hold(self, value):
        self.ahead, self.back, _ = tied(self.ahead, self.back, value)

    def total(self):
        while self.left > 0:
            self.step()
        return self.slot(0).astype(f32) + self.ahead.astype(f32) + self.back.astype(f32)


def small_hops(chips):
    if chips & (chips - 1):
        return [lambda value: lax.psum(value, ("chip", "core"))]
    hops = [lambda value: value + swapped(value)]
    for bit in range(chips.bit_length() - 1):
        pairs = [(chip, chip ^ (1 << bit)) for chip in range(chips)]
        hops.append(lambda value, pairs=pairs: value + lax.ppermute(value, "chip", pairs))
    return hops


def ring_columns(core):
    chips = lax.axis_size("chip")
    place = ring_place(lax.axis_index("chip"), chips)
    own = []
    for offset in slot_offsets(chips):
        at = (place + offset) % chips
        own.append(jnp.where(at < chips // 2, 2 * at, 2 * (chips - 1 - at) + 1))
    own = jnp.stack(own)
    width = D // (2 * chips)
    starts = jnp.concatenate([2 * own + core, 2 * own + 1 - core]) * width
    wanted = (starts[:, None] + jnp.arange(width)[None, :]).reshape(D)
    return (jnp.arange(D)[:, None] == wanted[None, :]).astype(bf16)


def per_device(
    inputs, out_grad, doc_ids, row_live, pre_gain, mlp_gain, mixer_gain, conv_weight, conv_bias,
    step_bias, decay_log, skip_scale, mixer_in_weight, mixer_out_weight, query_weight, key_weight,
    value_weight, attend_weight, gate_up_weight, down_weight,
):
    is_first = lax.axis_index("section") == 0
    core = lax.axis_index("core")
    shard = mixer_in_weight.shape[1]
    packed_a = jnp.concatenate(
        [
            mixer_in_weight[0, :, :AT_Q],
            query_weight[0],
            key_weight[0],
            value_weight[0],
            mixer_in_weight[0, :, AT_Q:],
            jnp.zeros((shard, LANES - MH), bf16),
        ],
        axis=1,
    )
    packed_b = jnp.concatenate(
        [mixer_out_weight[0].T, attend_weight[0].T, gate_up_weight[0], down_weight[0].T], axis=1
    )

    layout = row_layout(doc_ids)
    params = core_params(
        conv_weight[0], conv_bias[0], step_bias[0], decay_log[0], skip_scale[0], mixer_gain[0]
    )
    turn = ring_columns(core)

    def own_order(values):
        if values.dtype == bf16:
            return dot_nn(values, turn).astype(bf16)
        return dot_exact(values, turn.astype(f32))

    def whole_order(values):
        if values.dtype == bf16:
            return dot_nt(values, turn).astype(bf16)
        return dot_exact(values, turn.astype(f32).T)

    pre_row = own_order(pre_gain)
    mlp_row = own_order(mlp_gain)
    first_rows = own_order(inputs)

    positions = jnp.arange(TOK, dtype=jnp.int32)
    live = (positions[None, :] < row_live[:, None]).reshape(MB * TOK, 1)
    from_loss = own_order(jnp.where(live, out_grad, jnp.zeros_like(out_grad)))
    first_rows, from_loss = tied(first_rows, from_loss)

    ring_a = RingGather(packed_a)
    ring_b = RingGather(packed_b)
    ring_a.step()
    ring_b.step()
    ring_a.last()
    now_a, now_b = tied(ring_a.operands(), ring_b.operands())
    ring_a.send(*now_a)
    ring_b.send(*now_b)
    own_a = jnp.concatenate(ring_a.slots, axis=0)
    pair_a = (own_a, swapped(own_a))
    now_b, gain_now, pair_a = tied(ring_b.operands(), pre_row, pair_a)
    ring_b.send(*now_b)
    projected = by_row(project(first_rows, gain_now, *pair_a))
    mixed = core_forward(0, projected, layout, params)
    ring_b.hold(mixed)
    now_b, mixed = tied(ring_b.operands(), mixed)
    ring_b.send(*now_b)
    mixed, _, _ = core_forward(1, projected, layout, params, held=mixed)
    ring_b.hold(mixed)
    while ring_b.left:
        ring_b.step()
    pair_b = (
        jnp.concatenate(ring_b.slots, axis=0),
        jnp.concatenate([swapped(slot) for slot in ring_b.slots], axis=0),
    )
    mixed = mixed.reshape(MB * TOK, MIXED)
    handed = feed_forward(first_rows, mixed, mlp_row, *pair_b, keep=False)

    parts = [first_rows[row * TOK : (row + 1) * TOK] for row in range(MB)]
    received = [passed_along(one, "section", 1) for one in handed]
    held, cores = (), ()
    starts = []
    for row in range(MB):
        start = jnp.where(is_first, parts[row], received[row])
        held = project(start, pre_row, *pair_a, row=row, held=held)
        starts.append(start)
        cores = core_forward(row, by_row(held), layout, params, held=cores)
        if row + 1 < MB:
            received[row + 1], cores, held = tied(received[row + 1], cores, held)
    start_rows = jnp.concatenate(starts, axis=0)
    normed = held[0]
    projected = by_row(held)
    mixed, pre, yns = cores
    mixed = mixed.reshape(MB * TOK, MIXED)
    result, middle, normed_two, gate, up, act = feed_forward(
        start_rows, mixed, mlp_row, *pair_b, keep=True
    )
    their_mixed = swapped(mixed)
    their_act = swapped(act)
    their_normed = swapped(normed[:, SIDE:])
    their_normed_two = swapped(normed_two[:, SIDE:])

    received = jnp.zeros((TOK, D), bf16)
    lefts = []
    rights = []
    rows = []
    picks = jnp.where(is_first, jnp.array([1, 0]), jnp.array([0, 1])).astype(jnp.int32)

    def tick_left(which):
        return [(lefts[1][which], None, 0), (lefts[2][which], None, 0)] + [
            (lefts[1][which + 2], None, 0), (lefts[2][which + 2], None, 0)
        ]

    def tick_right(which):
        return [(rights[tick][which + far], None) for far in (0, 2) for tick in (1, 2)]

    def saved_left(own, their):
        return [(own, 0, 0), (own, 1, 0), (their, 0, 0), (their, 1, 0)]

    def saved_right(own, their):
        return [(own, 0), (own, 1), (their, 0), (their, 1)]

    for tick in range(3):
        row = jnp.where(is_first, (1, 1, 0)[tick], (1, 0, 1)[tick]).astype(jnp.int32).reshape(1)
        if tick == 1:
            row, their_mixed, their_act, their_normed, their_normed_two = tied(
                row, their_mixed, their_act, their_normed, their_normed_two
            )
        if tick == 2:
            row, lefts[1], rights[1], rows[1] = tied(row, lefts[1], rights[1], rows[1])
        loss_row = (1, 0, 1)[tick]
        cotangent = jnp.where(
            is_first, received, from_loss[loss_row * TOK : (loss_row + 1) * TOK]
        )
        d_gate, d_up, d_middle, middle_low, d_mixed, mlp_grad = feed_back(
            row, cotangent, gate, up, middle, mlp_row, *pair_b
        )
        lefts.append(
            (cotangent, middle_low, swapped(cotangent[:, SIDE:]), swapped(middle_low[:, SIDE:]))
        )
        rights.append((d_gate, d_up, swapped(d_gate), swapped(d_up)))
        if tick < 2:
            attended = attend_back(row, projected, d_mixed, layout)
            proj_low, small = mixer_back(
                row, projected, pre, yns, d_mixed, attended, layout, params
            )
            their_low = swapped(proj_low)
        else:
            sum_c = weight_grad(
                picks,
                1024,
                [
                    (tick_left(1), saved_right(mixed, their_mixed)),
                    (tick_left(0), saved_right(act, their_act)),
                ],
            )
            ring_c = RingReduce(sum_c)
            now_c, row = tied(ring_c.operands(), row)
            ring_c.send(*now_c)
            attended = attend_back(row, projected, d_mixed, layout)
            ring_c.hold(attended)
            picks_now, now_c, rights[2] = tied(picks, ring_c.operands(), rights[2])
            ring_c.send(*now_c)
            sum_b = weight_grad(
                picks_now,
                1024,
                [
                    (saved_left(normed_two, their_normed_two), tick_right(0)),
                    (saved_left(normed_two, their_normed_two), tick_right(1)),
                ],
            )
            ring_b = RingReduce(sum_b)
            ring_c.hold(sum_b)
            now_b, now_c, row, attended = tied(
                ring_b.operands(), ring_c.operands(), row, attended
            )
            ring_c.send(*now_c)
            ring_b.send(*now_b)
            proj_low, small = mixer_back(
                row, projected, pre, yns, d_mixed, attended, layout, params
            )
            their_low = swapped(proj_low)
            ring_b.hold(proj_low)
            ring_c.hold(proj_low)
            now_b, now_c, picks_now = tied(ring_b.operands(), ring_c.operands(), picks)
            ring_b.send(*now_b)
            ring_c.send(*now_c)
            (p_one, their_one), (p_two, their_two) = rows[1][1], (proj_low, their_low)
            sum_a = weight_grad(
                picks_now,
                WIDE_A // 3,
                [
                    (
                        saved_left(normed, their_normed),
                        [(p_one, None), (p_two, None), (their_one, None), (their_two, None)],
                    )
                ],
            )
            ring_b.hold(sum_a)
            rings_a = [RingReduce(sum_a[:, :CUT_A]), RingReduce(sum_a[:, CUT_A:])]
            now_a, now_b, row = tied([ring.operands() for ring in rings_a], ring_b.operands(), row)
            for ring, now in zip(rings_a, now_a):
                ring.send(*now)
            ring_b.send(*now_b)
        d_rows, d_low, pre_grad = project_back(
            row, proj_low, start_rows, d_middle, pre_row, *pair_a
        )
        rows.append((d_rows, (proj_low, their_low), pre_grad, mlp_grad, small))
        if tick < 2:
            received = passed_along(d_low, "section", -1)

    start_grad = jnp.concatenate(
        [
            jnp.where(is_first, rows[2][0], rows[1][0]),
            jnp.where(is_first, rows[1][0], rows[2][0]),
        ],
        axis=0,
    )
    pre_sum, mlp_sum, small = (one + two for one, two in zip(rows[1][2:], rows[2][2:]))
    gain_sums = whole_order(jnp.concatenate([pre_sum, mlp_sum], axis=0))
    small = jnp.concatenate([small, jnp.pad(gain_sums, ((0, 6), (0, CH - D)))], axis=0)
    hops = small_hops(lax.axis_size("chip"))
    small = hops.pop(0)(small)
    first_round = True
    while rings_a[0].left:
        for ring in rings_a:
            ring.step()
        if first_round:
            ring_b.step()
            first_round = False
        small = tied(small, rings_a[0].ahead)[0]
        if hops:
            small = hops.pop(0)(small)
    for hop in hops:
        small = hop(small)
    share_c = ring_c.total()
    share_b = ring_b.total()
    share_a = jnp.concatenate([ring.total() for ring in rings_a], axis=1)
    skip_sum = jnp.sum(small[6, :E].reshape(MH, MP), axis=1)
    mixer_in_grad = jnp.concatenate([share_a[:, :AT_Q], share_a[:, AT_DT : AT_DT + MH]], axis=1)
    return (
        whole_order(result)[None],
        whole_order(start_grad)[None],
        small[8:9, :D],
        small[9:10, :D],
        small[5:6, :E],
        small[None, :4],
        small[4:5],
        small[7:8, :MH],
        small[7:8, LANES : LANES + MH],
        skip_sum[None],
        mixer_in_grad[None],
        share_c[:, :E].T[None],
        share_a[:, AT_Q:AT_K][None],
        share_a[:, AT_K:AT_V][None],
        share_a[:, AT_V:AT_DT][None],
        share_c[:, E:MIXED].T[None],
        share_b[None],
        share_c[:, MIXED:].T[None],
    )


def solution(mesh):
    dp = mesh.shape["dp"]
    devices = mesh.devices.reshape(mesh.shape["section"], dp // 2, 2)
    paired = Mesh(devices, ("section", "chip", "core"))
    over = ("chip", "core")
    rows = P(over, None)
    small = P("section", None)
    by_row = P("section", over, None)
    by_col = P("section", None, over)
    small_specs = (small, small, small, P("section", None, None), small, small, small, small)
    big_specs = (by_row, by_col, by_row, by_row, by_row, by_col, by_row, by_col)
    in_specs = (rows, rows, rows, P(over)) + small_specs + big_specs
    out_specs = (by_row, by_row) + small_specs + big_specs
    return jax.shard_map(
        per_device, mesh=paired, in_specs=in_specs, out_specs=out_specs, check_vma=False
    )
```

```python
import functools
import math

import jax
import jax.numpy as jnp
from jax import lax
from jax.experimental import pallas as pl
from jax.experimental.pallas import tpu as pltpu
from jax.sharding import Mesh
from jax.sharding import PartitionSpec as P

D = 1024
FF = 2048
MH = 24
MP = 64
NS = 128
AH = 8
KVH = 2
HD = 64
MB = 2
TOK = 256
E = 1536
CH = 1792
HALF = TOK // 2
PAIRS = MH // 2
LANES = 128
SIDE = D // 2
MIB = 2**20

AT_W = E
AT_Q = E + CH
AT_K = AT_Q + AH * HD
AT_V = AT_K + KVH * HD
AT_DT = AT_V + KVH * HD
WIDE_A = AT_DT + LANES
CUT_A = 16 * LANES
MIXED = E + AH * HD
AT_GU = MIXED
AT_DN = AT_GU + 2 * FF
WIDE_B = AT_DN + FF

highest = lax.Precision.HIGHEST
epsilon = 1e-05
rope_base = 100000000000.0
bf16 = jnp.bfloat16
f32 = jnp.float32


def dot_nn(left, right):
    return lax.dot_general(left, right, (((1,), (0,)), ((), ())), preferred_element_type=f32)


def dot_nt(left, right):
    return lax.dot_general(left, right, (((1,), (1,)), ((), ())), preferred_element_type=f32)


def dot_tn(left, right):
    return lax.dot_general(left, right, (((0,), (0,)), ((), ())), preferred_element_type=f32)


def dot_exact(left, right):
    return lax.dot_general(
        left, right, (((1,), (0,)), ((), ())), precision=highest, preferred_element_type=f32
    )


def softplus(value):
    return jnp.maximum(value, 0.0) + jnp.log1p(jnp.exp(-jnp.abs(value)))


def lane_low(rows):
    return lax.broadcasted_iota(jnp.int32, (rows, LANES), 1) < HD


def rope_halves(rows):
    return (lax.broadcasted_iota(jnp.int32, (rows, LANES), 1) & (HD - 1)) < HD // 2


def rope_turn(tile, cosine, sine):
    swapped = jnp.where(
        rope_halves(tile.shape[0]),
        -pltpu.roll(tile, LANES - HD // 2, 1),
        pltpu.roll(tile, HD // 2, 1),
    )
    return tile * cosine + swapped * sine


def rope_back(tile, cosine, sine):
    swapped = jnp.where(
        rope_halves(tile.shape[0]),
        pltpu.roll(tile, LANES - HD // 2, 1),
        -pltpu.roll(tile, HD // 2, 1),
    )
    return tile * cosine + swapped * sine


def both_halves(tile):
    swapped = pltpu.roll(tile, HD, 1)
    low = lane_low(tile.shape[0])
    return (jnp.where(low, tile, swapped), jnp.where(low, swapped, tile))


def tile_at(index):
    return pl.ds(pl.multiple_of(index * LANES, LANES), LANES)


def tile_from(start, index):
    return pl.ds(pl.multiple_of(start + index * LANES, LANES), LANES)


def allowed_pairs(doc_col_ref, doc_row_ref):
    later = lax.broadcasted_iota(jnp.int32, (TOK, TOK), 0)
    early = lax.broadcasted_iota(jnp.int32, (TOK, TOK), 1)
    same = doc_col_ref[:, 0:1] == doc_row_ref[0:1, :]
    return (later >= early) & same


def pair_rows(tile):
    low = lane_low(tile.shape[0])
    zero = jnp.zeros_like(tile)
    return jnp.concatenate([jnp.where(low, tile, zero), jnp.where(low, zero, tile)], axis=0)


def pair_lanes(rows):
    half = rows.shape[0] // 2
    return jnp.where(lane_low(half), rows[:half], rows[half:])


def core_forward_kernel(
    held, pm_ref, pq_ref, pd_ref, rope_ref, mask_ref, doc_col_ref, doc_row_ref,
    taps_ref, head_ref, wide_ref, *refs,
):
    xb_ref, pre_ref, yns_ref, conv_s, cb_s, bias_s, sum_s = refs[3:] if held else refs

    def conv_tile(index, carry):
        rows = pm_ref[:, tile_from(AT_W, index)].astype(f32)
        at = tile_at(index)
        total = taps_ref[4:5, at] + taps_ref[3:4, at] * rows
        for shift in (1, 2, 3):
            moved = mask_ref[:, (shift - 1) * LANES : shift * LANES] * pltpu.roll(rows, shift, 0)
            total = total + taps_ref[3 - shift : 4 - shift, at] * moved
        total = total.astype(bf16)
        pre_ref[:, at] = total
        total = total.astype(f32)
        conv_s[:, at] = total * jax.nn.sigmoid(total)
        return carry

    lax.fori_loop(0, CH // LANES, conv_tile, 0)

    allowed = allowed_pairs(doc_col_ref, doc_row_ref)
    bias_s[...] = jnp.where(allowed, 0.0, -1e30)
    steps = softplus(pd_ref[...] + head_ref[0:1, :])
    rates = -steps * head_ref[1:2, :]
    totals = dot_exact(jnp.where(allowed, 1.0, 0.0), rates)
    totals_t = totals.T
    inward = conv_s[:, E : E + NS].astype(bf16)
    outward = conv_s[:, E + NS :].astype(bf16)
    cb_s[...] = jnp.where(allowed, dot_nt(outward, inward), 0.0)
    low = lane_low(TOK)
    for pair in range(PAIRS):
        lanes = slice(pair * LANES, (pair + 1) * LANES)
        first = 2 * pair
        step_pair = jnp.where(low, steps[:, first : first + 1], steps[:, first + 1 : first + 2])
        scaled = (conv_s[:, lanes] * step_pair).astype(bf16)
        mixes = []
        for head in (first, first + 1):
            apart = totals[:, head : head + 1] - totals_t[head : head + 1, :]
            mixes.append((jnp.exp(jnp.minimum(apart, 0.0)) * cb_s[...]).astype(bf16))
        yns_ref[:, lanes] = pair_lanes(dot_nn(jnp.concatenate(mixes, axis=0), scaled))

    sum_s[...] = jnp.zeros((TOK, LANES), f32)

    def gate_tile(index, carry):
        at = tile_at(index)
        gate = pm_ref[:, at].astype(f32)
        rows = yns_ref[:, at] + wide_ref[0:1, at] * conv_s[:, at]
        gated = rows * (gate * jax.nn.sigmoid(gate))
        sum_s[...] += gated * gated
        conv_s[:, at] = gated
        return carry

    lax.fori_loop(0, E // LANES, gate_tile, 0)
    scale = lax.rsqrt(jnp.sum(sum_s[...], axis=1, keepdims=True) * (1.0 / E) + epsilon)

    def norm_tile(index, carry):
        at = tile_at(index)
        xb_ref[:, at] = (conv_s[:, at] * scale * wide_ref[1:2, at]).astype(bf16)
        return carry

    lax.fori_loop(0, E // LANES, norm_tile, 0)

    cosine = rope_ref[:, :LANES]
    sine = rope_ref[:, LANES:]
    keys = both_halves(rope_turn(pq_ref[:, AH * HD : AH * HD + LANES].astype(f32), cosine, sine))
    values = both_halves(pq_ref[:, AH * HD + LANES :].astype(f32))
    keys = tuple(part.astype(bf16) for part in keys)
    values = tuple(part.astype(bf16) for part in values)
    for pair in range(AH // 2):
        group = pair // (AH // (2 * KVH))
        at = pair * LANES
        turned = rope_turn(pq_ref[:, at : at + LANES].astype(f32), cosine, sine)
        scores = dot_nt(pair_rows((turned * (1.0 / math.sqrt(HD))).astype(bf16)), keys[group])
        weights = []
        shares = []
        for part in (scores[:TOK], scores[TOK:]):
            part = part + bias_s[...]
            part = jnp.exp(part - jnp.max(part, axis=1, keepdims=True))
            shares.append(1.0 / jnp.sum(part, axis=1, keepdims=True))
            weights.append(part.astype(bf16))
        out = pair_lanes(dot_nn(jnp.concatenate(weights, axis=0), values[group]))
        out = out * jnp.where(low, shares[0], shares[1])
        xb_ref[:, E + pair * LANES : E + (pair + 1) * LANES] = out.astype(bf16)


def silu_slope(value, gate):
    return gate * (1.0 + value * (1.0 - gate))


def attend_back_kernel(
    pick_ref, pq_ref, dxb_ref, rope_ref, doc_col_ref, doc_row_ref, pg_ref, bias_s
):
    later = lax.broadcasted_iota(jnp.int32, (TOK, TOK), 1)
    early = lax.broadcasted_iota(jnp.int32, (TOK, TOK), 0)
    allowed_t = (later >= early) & (doc_col_ref[:, 0:1] == doc_row_ref[0:1, :])
    bias_s[...] = jnp.where(allowed_t, 0.0, -1e30)
    low = lane_low(TOK)
    cosine = rope_ref[:, :LANES]
    sine = rope_ref[:, LANES:]
    keys = both_halves(rope_turn(pq_ref[:, AH * HD : AH * HD + LANES].astype(f32), cosine, sine))
    values = both_halves(pq_ref[:, AH * HD + LANES :].astype(f32))
    root = 1.0 / math.sqrt(HD)
    d_keys = []
    d_values = []
    for group in range(KVH):
        key = keys[group].astype(bf16)
        key_rows = pair_rows(key)
        value_rows = pair_rows(values[group].astype(bf16))
        d_key = jnp.zeros((TOK, LANES), f32)
        d_value = jnp.zeros((TOK, LANES), f32)
        for pair in range(group * (AH // (2 * KVH)), (group + 1) * (AH // (2 * KVH))):
            at = pair * LANES
            turned = rope_turn(pq_ref[:, at : at + LANES].astype(f32), cosine, sine) * root
            query = turned.astype(bf16)
            d_out = dxb_ref[:, E + at : E + at + LANES].astype(bf16)
            scores = dot_nt(key_rows, query)
            d_weights = dot_nt(value_rows, d_out)
            weights = []
            d_scores = []
            for part in (slice(0, TOK), slice(TOK, 2 * TOK)):
                score = scores[part] + bias_s[...]
                weight = jnp.exp(score - jnp.max(score, axis=0, keepdims=True))
                weight = weight * (1.0 / jnp.sum(weight, axis=0, keepdims=True))
                d_weight = d_weights[part]
                offset = jnp.sum(weight * d_weight, axis=0, keepdims=True)
                weights.append(weight.astype(bf16))
                d_scores.append((weight * (d_weight - offset)).astype(bf16))
            d_value = d_value + pair_lanes(dot_nn(jnp.concatenate(weights, axis=0), d_out))
            d_key = d_key + pair_lanes(dot_nn(jnp.concatenate(d_scores, axis=0), query))
            d_query = pair_lanes(dot_tn(jnp.concatenate(d_scores, axis=1), key))
            pg_ref[:, at : at + LANES] = rope_back(d_query * root, cosine, sine).astype(bf16)
        d_keys.append(d_key + pltpu.roll(d_key, HD, 1))
        d_values.append(d_value + pltpu.roll(d_value, HD, 1))
    d_key = rope_back(jnp.where(low, d_keys[0], d_keys[1]), cosine, sine)
    pg_ref[:, AH * HD : AH * HD + LANES] = d_key.astype(bf16)
    pg_ref[:, AH * HD + LANES :] = jnp.where(low, d_values[0], d_values[1]).astype(bf16)


def mixer_back_kernel(
    pick_ref, pm_ref, pd_ref, pre_ref, yns_ref, dxb_ref, attend_ref, mask_ref, doc_col_ref,
    doc_row_ref, taps_ref, head_ref, wide_ref,
    pg_ref, small_ref,
    x_s, dx_s, dyb_s, cbt_s, dcbt_s, sum_s, ssum_s,
):
    small_ref[...] = jnp.zeros_like(small_ref)
    pg_ref[:, AT_Q:AT_DT] = attend_ref[...]
    sum_s[...] = jnp.zeros((TOK, LANES), f32)
    ssum_s[...] = jnp.zeros((TOK, LANES), f32)

    def start_tile(index, carry):
        at = tile_at(index)
        pre = pre_ref[:, at].astype(f32)
        heads_in = pre * jax.nn.sigmoid(pre)
        x_s[:, at] = heads_in
        gate = pm_ref[:, at].astype(f32)
        rows = yns_ref[:, at] + wide_ref[0:1, at] * heads_in
        gated = rows * (gate * jax.nn.sigmoid(gate))
        sum_s[...] += gated * gated
        ssum_s[...] += dxb_ref[:, at] * wide_ref[1:2, at] * gated
        return carry

    lax.fori_loop(0, E // LANES, start_tile, 0)
    scale = lax.rsqrt(jnp.sum(sum_s[...], axis=1, keepdims=True) * (1.0 / E) + epsilon)
    pull = jnp.sum(ssum_s[...], axis=1, keepdims=True) * (1.0 / E) * scale * scale * scale

    def gate_tile(index, carry):
        at = tile_at(index)
        heads_in = x_s[:, at]
        skip = wide_ref[0:1, at]
        gate = pm_ref[:, at].astype(f32)
        opened = jax.nn.sigmoid(gate)
        rows = yns_ref[:, at] + skip * heads_in
        gated = rows * (gate * opened)
        arrived = dxb_ref[:, at]
        d_gated = scale * (arrived * wide_ref[1:2, at]) - gated * pull
        small_ref[5:6, at] = jnp.sum(arrived * gated * scale, axis=0, keepdims=True)
        d_rows = d_gated * (gate * opened)
        pg_ref[:, at] = (d_gated * rows * silu_slope(gate, opened)).astype(bf16)
        small_ref[6:7, at] = jnp.sum(d_rows * heads_in, axis=0, keepdims=True)
        dyb_s[:, at] = d_rows.astype(bf16)
        dx_s[:, at] = skip * d_rows
        return carry

    lax.fori_loop(0, E // LANES, gate_tile, 0)

    def state_tile(index, carry):
        at = tile_from(E, index)
        pre = pre_ref[:, at].astype(f32)
        x_s[:, at] = pre * jax.nn.sigmoid(pre)
        return carry

    lax.fori_loop(0, 2, state_tile, 0)

    later = lax.broadcasted_iota(jnp.int32, (TOK, TOK), 1)
    early = lax.broadcasted_iota(jnp.int32, (TOK, TOK), 0)
    allowed_t = (later >= early) & (doc_col_ref[:, 0:1] == doc_row_ref[0:1, :])
    allowed = allowed_pairs(doc_col_ref, doc_row_ref)
    raw = pd_ref[...] + head_ref[0:1, :]
    steps = softplus(raw)
    decay = head_ref[1:2, :]
    rates = -steps * decay
    totals = dot_exact(jnp.where(allowed, 1.0, 0.0), rates)
    totals_t = totals.T
    inward = x_s[:, E : E + NS].astype(bf16)
    outward = x_s[:, E + NS :].astype(bf16)
    cbt_s[...] = jnp.where(allowed_t, dot_nt(inward, outward), 0.0)
    dcbt_s[...] = jnp.zeros((TOK, TOK), f32)
    low = lane_low(TOK)
    spread_row = lax.broadcasted_iota(jnp.int32, (2 * LANES, LANES), 0) // HD
    spread_col = lax.broadcasted_iota(jnp.int32, (2 * LANES, LANES), 1)
    sum_s[...] = jnp.zeros((TOK, LANES), f32)
    ssum_s[...] = jnp.zeros((TOK, LANES), f32)
    waiting = None
    for pair in range(PAIRS):
        lanes = slice(pair * LANES, (pair + 1) * LANES)
        first = 2 * pair
        step_pair = jnp.where(low, steps[:, first : first + 1], steps[:, first + 1 : first + 2])
        heads_in = x_s[:, lanes]
        scaled = (heads_in * step_pair).astype(bf16)
        d_rows = dyb_s[:, lanes]
        d_mix = dot_nt(pair_rows(scaled), d_rows)
        mixes = []
        d_pairs = None
        for side, head in enumerate((first, first + 1)):
            apart = totals_t[head : head + 1, :] - totals[:, head : head + 1]
            decays = jnp.exp(jnp.minimum(apart, 0.0))
            mixes.append((decays * cbt_s[...]).astype(bf16))
            part = d_mix[side * TOK : (side + 1) * TOK] * decays
            d_pairs = part if d_pairs is None else d_pairs + part
        dcbt_s[...] += d_pairs
        d_scaled = pair_lanes(dot_nn(jnp.concatenate(mixes, axis=0), d_rows))
        dx_s[:, lanes] += d_scaled * step_pair
        value = d_rows.astype(f32) * yns_ref[:, lanes] - scaled.astype(f32) * d_scaled
        coarse = value.astype(bf16)
        fine = (value - coarse.astype(f32)).astype(bf16)
        spread = (spread_col == first + (spread_row & 1)).astype(bf16)
        ssum_s[...] += dot_nn(jnp.concatenate([coarse, fine], axis=1), spread)
        value = (d_scaled * heads_in).astype(bf16)
        if pair % 2 == 0:
            waiting = value
        else:
            spread = (spread_col == first - 2 + spread_row).astype(bf16)
            sum_s[...] += dot_nn(jnp.concatenate([waiting, value], axis=1), spread)

    d_rates = dot_exact(jnp.where(allowed_t, 1.0, 0.0), ssum_s[...])
    d_steps = sum_s[...] - decay * d_rates
    d_raw = d_steps * jax.nn.sigmoid(raw)
    pg_ref[:, AT_DT:] = d_raw.astype(bf16)
    small_ref[7:8, :LANES] = jnp.sum(d_raw, axis=0, keepdims=True)
    small_ref[7:8, LANES : 2 * LANES] = jnp.sum(d_rates * rates, axis=0, keepdims=True)
    d_pairs = jnp.where(allowed_t, dcbt_s[...], 0.0).astype(bf16)
    dx_s[:, E : E + NS] = dot_nn(d_pairs, outward)
    dx_s[:, E + NS :] = dot_tn(d_pairs, inward)

    def conv_tile(index, carry):
        at = tile_at(index)
        pre = pre_ref[:, at].astype(f32)
        d_pre = dx_s[:, at] * silu_slope(pre, jax.nn.sigmoid(pre))
        rows = pm_ref[:, tile_from(AT_W, index)].astype(f32)
        small_ref[4:5, at] = jnp.sum(d_pre, axis=0, keepdims=True)
        small_ref[3:4, at] = jnp.sum(d_pre * rows, axis=0, keepdims=True)
        back = taps_ref[3:4, at] * d_pre
        for shift in (1, 2, 3):
            held = mask_ref[:, (shift - 1) * LANES : shift * LANES] * d_pre
            small_ref[3 - shift : 4 - shift, at] = jnp.sum(
                held * pltpu.roll(rows, shift, 0), axis=0, keepdims=True
            )
            back = back + taps_ref[3 - shift : 4 - shift, at] * pltpu.roll(held, TOK - shift, 0)
        pg_ref[:, tile_from(AT_W, index)] = back.astype(bf16)
        return carry

    lax.fori_loop(0, CH // LANES, conv_tile, 0)


def whole_block(shape):
    return pl.BlockSpec(shape, lambda *steps: (0,) * len(shape))


def once(shape, place):
    return pl.BlockSpec(shape, place, pipeline_mode=pl.Buffered(1))


def core_forward(row, projected, layout, params, held=()):
    operands = (*projected, *layout)

    def block(array):
        return once((None,) + array.shape[1:], lambda step: (row, 0, 0))

    outs = [
        jax.ShapeDtypeStruct((MB, TOK, MIXED), bf16),
        jax.ShapeDtypeStruct((MB, TOK, CH), bf16),
        jax.ShapeDtypeStruct((MB, TOK, E), f32),
    ]
    return pl.pallas_call(
        functools.partial(core_forward_kernel, bool(held)),
        grid=(1,),
        in_specs=[block(array) for array in operands]
        + [once(array.shape, lambda step: (0, 0)) for array in params]
        + [pl.BlockSpec(memory_space=pl.ANY)] * len(held),
        out_specs=[block(array) for array in outs],
        out_shape=outs,
        scratch_shapes=[
            pltpu.VMEM((TOK, CH), f32),
            pltpu.VMEM((TOK, TOK), f32),
            pltpu.VMEM((TOK, TOK), f32),
            pltpu.VMEM((TOK, LANES), f32),
        ],
        input_output_aliases={10: 0, 11: 1, 12: 2} if held else {},
        compiler_params=pltpu.CompilerParams(vmem_limit_bytes=12 * MIB),
        cost_estimate=pl.CostEstimate(
            flops=4 * 10**8, bytes_accessed=12 * 2**20, transcendentals=10**6
        ),
        name="core_forward",
    )(*operands, *params, *held)


def core_back_specs(by_row, plain):
    return [
        once((None,) + array.shape[1:], lambda step, pick: (pick[0], 0, 0)) if chosen
        else once(array.shape, lambda step, pick: (0, 0))
        for chosen, arrays in ((True, by_row), (False, plain))
        for array in arrays
    ]


def attend_back(row, projected, d_mixed, layout):
    rope, masks, doc_cols, doc_rows = layout
    return pl.pallas_call(
        attend_back_kernel,
        grid_spec=pltpu.PrefetchScalarGridSpec(
            num_scalar_prefetch=1,
            grid=(1,),
            in_specs=core_back_specs([projected[1]], [d_mixed])
            + core_back_specs([rope, doc_cols, doc_rows], []),
            out_specs=once((TOK, AT_DT - AT_Q), lambda step, pick: (0, 0)),
            scratch_shapes=[pltpu.VMEM((TOK, TOK), f32)],
        ),
        out_shape=jax.ShapeDtypeStruct((TOK, AT_DT - AT_Q), bf16),
        compiler_params=pltpu.CompilerParams(vmem_limit_bytes=6 * MIB),
        cost_estimate=pl.CostEstimate(
            flops=3 * 10**8, bytes_accessed=4 * 2**20, transcendentals=6 * 10**5
        ),
        name="attend_back",
    )(row, projected[1], d_mixed, rope, doc_cols, doc_rows)


def mixer_back(row, projected, pre, yns, d_mixed, attended, layout, params):
    rope, masks, doc_cols, doc_rows = layout
    return pl.pallas_call(
        mixer_back_kernel,
        grid_spec=pltpu.PrefetchScalarGridSpec(
            num_scalar_prefetch=1,
            grid=(1,),
            in_specs=core_back_specs(
                [projected[0], projected[2], pre, yns], [d_mixed, attended]
            )
            + core_back_specs([masks, doc_cols, doc_rows], params),
            out_specs=[
                once((TOK, WIDE_A), lambda step, pick: (0, 0)),
                once((8, CH), lambda step, pick: (0, 0)),
            ],
            scratch_shapes=[
                pltpu.VMEM((TOK, CH), f32),
                pltpu.VMEM((TOK, CH), f32),
                pltpu.VMEM((TOK, E), bf16),
                pltpu.VMEM((TOK, TOK), f32),
                pltpu.VMEM((TOK, TOK), f32),
                pltpu.VMEM((TOK, LANES), f32),
                pltpu.VMEM((TOK, LANES), f32),
            ],
        ),
        out_shape=[
            jax.ShapeDtypeStruct((TOK, WIDE_A), bf16),
            jax.ShapeDtypeStruct((8, CH), f32),
        ],
        compiler_params=pltpu.CompilerParams(vmem_limit_bytes=15 * MIB),
        cost_estimate=pl.CostEstimate(
            flops=7 * 10**8, bytes_accessed=10 * 2**20, transcendentals=15 * 10**5
        ),
        name="mixer_back",
    )(
        row, projected[0], projected[2], pre, yns, d_mixed, attended, masks, doc_cols, doc_rows,
        *params,
    )


def passed_along(value, axis, steps):
    count = lax.axis_size(axis)
    leading, last = (max(0, -steps), min(count, count - steps))
    return lax.ppermute(value, axis, [(source, source + steps) for source in range(leading, last)])


def norm_rows(values):
    return lax.rsqrt(jnp.mean(values * values, axis=-1, keepdims=True) + epsilon)


def norm_back(values, gain, arrived):
    scale = norm_rows(values)
    weighted = arrived * gain
    pull = jnp.mean(weighted * values, axis=-1, keepdims=True) * scale * scale * scale
    gain_grad = jnp.sum(arrived * values * scale, axis=0, keepdims=True)
    return (weighted * scale - values * pull, gain_grad)


def project_kernel(rows_ref, gain_ref, own_ref, other_ref, *refs):
    normed_ref, pm_ref, pq_ref, pd_ref = refs[-4:]
    step = pl.program_id(0)

    @pl.when(step == 0)
    def _():
        rows = rows_ref[...].astype(f32)
        normed_ref[...] = (rows * norm_rows(rows) * gain_ref[...]).astype(bf16)

    out = dot_nn(normed_ref[:, :SIDE], own_ref[...]) + dot_nn(normed_ref[:, SIDE:], other_ref[...])
    tile = WIDE_A // 3
    for index in range(2):
        @pl.when(step == index)
        def _(index=index):
            pm_ref[:, index * tile : (index + 1) * tile] = out.astype(bf16)

    @pl.when(step == 2)
    def _():
        pm_ref[:, 2 * tile :] = out[:, : AT_Q - 2 * tile].astype(bf16)
        pq_ref[...] = out[:, AT_Q - 2 * tile : AT_DT - 2 * tile].astype(bf16)
        pd_ref[...] = out[:, AT_DT - 2 * tile :]


def project(rows, gain, own, other, row=None, held=()):
    count = rows.shape[0]
    tile = WIDE_A // 3
    weight = pl.BlockSpec((SIDE, tile), lambda step: (0, step))
    at = row or 0
    total = count if row is None else MB * TOK
    widths = ((D, bf16), (AT_Q, bf16), (AT_DT - AT_Q, bf16), (LANES, f32))
    return pl.pallas_call(
        project_kernel,
        grid=(3,),
        in_specs=[whole_block((count, D)), whole_block((1, D)), weight, weight]
        + [pl.BlockSpec(memory_space=pl.ANY)] * len(held),
        out_specs=[pl.BlockSpec((count, width), lambda step: (at, 0)) for width, _ in widths],
        out_shape=[jax.ShapeDtypeStruct((total, width), kind) for width, kind in widths],
        input_output_aliases={4 + index: index for index in range(len(held))},
        compiler_params=pltpu.CompilerParams(vmem_limit_bytes=15 * MIB),
        cost_estimate=pl.CostEstimate(
            flops=2 * count * D * WIDE_A,
            bytes_accessed=2 * D * WIDE_A + 2 * count * WIDE_A,
            transcendentals=0,
        ),
        name="project",
    )(rows, gain, own, other, *held)


def by_row(projected):
    return tuple(array.reshape(MB, TOK, -1) for array in projected[1:])


def feed_forward_kernel(
    keep, rows_ref, mixed_ref, gain_ref,
    out_own, out_other, gate_own, gate_other, up_own, up_other, down_own, down_other,
    *refs,
):
    if keep:
        low_ref, middle_ref, normed_ref, gate_ref, up_ref, act_ref, total_s = refs
    else:
        *row_refs, middle_ref, normed_ref, total_s = refs
    step = pl.program_id(0)

    @pl.when(step == 0)
    def _():
        middle_ref[...] = rows_ref[...].astype(f32)

    @pl.when(step < 4)
    def _():
        mixed = mixed_ref[...]
        middle_ref[:, :SIDE] += dot_nt(mixed, out_own[...])
        middle_ref[:, SIDE:] += dot_nt(mixed, out_other[...])

    @pl.when(step == 3)
    def _():
        middle = middle_ref[...]
        normed_ref[...] = (middle * norm_rows(middle) * gain_ref[...]).astype(bf16)
        total_s[...] = middle

    @pl.when(step >= 4)
    def _():
        left = normed_ref[:, :SIDE]
        right = normed_ref[:, SIDE:]
        gate = dot_nn(left, gate_own[...]) + dot_nn(right, gate_other[...])
        up = dot_nn(left, up_own[...]) + dot_nn(right, up_other[...])
        act = (gate * jax.nn.sigmoid(gate) * up).astype(bf16)
        if keep:
            gate_ref[...] = gate.astype(bf16)
            up_ref[...] = up.astype(bf16)
            act_ref[...] = act
        total_s[:, :SIDE] += dot_nt(act, down_own[...])
        total_s[:, SIDE:] += dot_nt(act, down_other[...])

    @pl.when(step == 7)
    def _():
        if keep:
            low_ref[...] = total_s[...].astype(bf16)
        else:
            for row, row_ref in enumerate(row_refs):
                row_ref[...] = total_s[row * TOK : (row + 1) * TOK, :].astype(bf16)


def b_block(start, skipped):
    return pl.BlockSpec(
        (SIDE, 512), lambda step, *pick: (0, start + jnp.clip(step - skipped, 0, 3))
    )


def b_blocks(parts):
    return [b_block(start, skipped) for start, skipped in parts for _ in range(2)]


def feed_forward(rows, mixed, gain, own, other, keep):
    count = rows.shape[0]
    wide = pl.BlockSpec((count, 512), lambda step: (0, jnp.clip(step - 4, 0, 3)))
    out_specs = [whole_block((count, D))]
    out_shape = [jax.ShapeDtypeStruct((count, D), bf16)]
    scratch = [pltpu.VMEM((count, D), f32)]
    if keep:
        out_specs += [whole_block((count, D)), whole_block((count, D)), wide, wide, wide]
        out_shape += [
            jax.ShapeDtypeStruct((count, D), f32),
            jax.ShapeDtypeStruct((count, D), bf16),
            jax.ShapeDtypeStruct((count, FF), bf16),
            jax.ShapeDtypeStruct((count, FF), bf16),
            jax.ShapeDtypeStruct((count, FF), bf16),
        ]
    else:
        out_specs = [whole_block((TOK, D))] * MB
        out_shape = [jax.ShapeDtypeStruct((TOK, D), bf16)] * MB
        scratch = [pltpu.VMEM((count, D), f32), pltpu.VMEM((count, D), bf16)] + scratch
    return pl.pallas_call(
        functools.partial(feed_forward_kernel, keep),
        grid=(8,),
        in_specs=[
            whole_block((count, D)),
            pl.BlockSpec((count, 512), lambda step: (0, jnp.clip(step, 0, 3))),
            whole_block((1, D)),
        ]
        + b_blocks(((0, 0), (4, 4), (8, 4), (12, 4))),
        out_specs=out_specs,
        out_shape=out_shape,
        scratch_shapes=scratch,
        compiler_params=pltpu.CompilerParams(vmem_limit_bytes=22 * MIB),
        cost_estimate=pl.CostEstimate(
            flops=2 * count * D * WIDE_B, bytes_accessed=2 * D * WIDE_B, transcendentals=0
        ),
        name="feed_forward",
    )(rows, mixed, gain, *([own, other] * 4))


def feed_back_kernel(
    pick_ref, cot_ref, gate_ref, up_ref, middle_ref, gain_ref,
    down_own, down_other, gate_own, gate_other, up_own, up_other, out_own, out_other,
    d_gate_ref, d_up_ref, d_middle_ref, low_ref, d_mixed_ref, gain_grad_ref,
    total_s,
):
    step = pl.program_id(0)

    @pl.when(step == 0)
    def _():
        total_s[...] = jnp.zeros_like(total_s)

    @pl.when(step < 4)
    def _():
        arrived = dot_nn(cot_ref[:, :SIDE], down_own[...]) + dot_nn(
            cot_ref[:, SIDE:], down_other[...]
        )
        gate = gate_ref[...].astype(f32)
        opened = jax.nn.sigmoid(gate)
        d_gate = (arrived * up_ref[...].astype(f32) * silu_slope(gate, opened)).astype(bf16)
        d_up = (arrived * (gate * opened)).astype(bf16)
        d_gate_ref[...] = d_gate
        d_up_ref[...] = d_up
        total_s[:, :SIDE] += dot_nt(d_gate, gate_own[...]) + dot_nt(d_up, up_own[...])
        total_s[:, SIDE:] += dot_nt(d_gate, gate_other[...]) + dot_nt(d_up, up_other[...])

    @pl.when(step == 3)
    def _():
        d_norm, gain_grad = norm_back(middle_ref[...], gain_ref[...], total_s[...])
        d_middle = cot_ref[...].astype(f32) + d_norm
        d_middle_ref[...] = d_middle
        low_ref[...] = d_middle.astype(bf16)
        gain_grad_ref[...] = gain_grad

    @pl.when(step >= 4)
    def _():
        d_mixed_ref[...] = dot_nn(low_ref[:, :SIDE], out_own[...]) + dot_nn(
            low_ref[:, SIDE:], out_other[...]
        )


def feed_back(row, cotangent, gate, up, middle, gain, own, other):
    saved = pl.BlockSpec((TOK, 512), lambda step, pick: (pick[0], jnp.clip(step, 0, 3)))
    early = pl.BlockSpec((TOK, 512), lambda step, pick: (0, jnp.clip(step, 0, 3)))
    late = pl.BlockSpec((TOK, 512), lambda step, pick: (0, jnp.clip(step - 4, 0, 3)))
    full = pl.BlockSpec((TOK, D), lambda step, pick: (0, 0))
    gain_block = pl.BlockSpec((1, D), lambda step, pick: (0, 0))
    return pl.pallas_call(
        feed_back_kernel,
        grid_spec=pltpu.PrefetchScalarGridSpec(
            num_scalar_prefetch=1,
            grid=(8,),
            in_specs=[
                full,
                saved,
                saved,
                pl.BlockSpec((TOK, D), lambda step, pick: (pick[0], 0)),
                gain_block,
            ]
            + b_blocks(((12, 0), (4, 0), (8, 0), (0, 4))),
            out_specs=[early, early, full, full, late, gain_block],
            scratch_shapes=[pltpu.VMEM((TOK, D), f32)],
        ),
        out_shape=[
            jax.ShapeDtypeStruct((TOK, FF), bf16),
            jax.ShapeDtypeStruct((TOK, FF), bf16),
            jax.ShapeDtypeStruct((TOK, D), f32),
            jax.ShapeDtypeStruct((TOK, D), bf16),
            jax.ShapeDtypeStruct((TOK, MIXED), f32),
            jax.ShapeDtypeStruct((1, D), f32),
        ],
        compiler_params=pltpu.CompilerParams(vmem_limit_bytes=46 * MIB),
        cost_estimate=pl.CostEstimate(
            flops=2 * TOK * D * WIDE_B, bytes_accessed=2 * D * WIDE_B, transcendentals=0
        ),
        name="feed_back",
    )(row, cotangent, gate, up, middle, gain, *([own, other] * 4))


def project_back_kernel(
    pick_ref, grad_ref, rows_ref, d_middle_ref, gain_ref, own_ref, other_ref,
    d_rows_ref, low_ref, gain_grad_ref, total_s,
):
    step = pl.program_id(0)

    @pl.when(step == 0)
    def _():
        total_s[...] = jnp.zeros_like(total_s)

    total_s[:, :SIDE] += dot_nt(grad_ref[...], own_ref[...])
    total_s[:, SIDE:] += dot_nt(grad_ref[...], other_ref[...])

    @pl.when(step == 2)
    def _():
        d_norm, gain_grad = norm_back(rows_ref[...].astype(f32), gain_ref[...], total_s[...])
        d_rows = d_middle_ref[...] + d_norm
        d_rows_ref[...] = d_rows
        low_ref[...] = d_rows.astype(bf16)
        gain_grad_ref[...] = gain_grad


def project_back(row, proj_low, start_rows, d_middle, gain, own, other):
    tile = WIDE_A // 3
    weight = pl.BlockSpec((SIDE, tile), lambda step, pick: (0, step))
    full = pl.BlockSpec((TOK, D), lambda step, pick: (0, 0))
    gain_block = pl.BlockSpec((1, D), lambda step, pick: (0, 0))
    return pl.pallas_call(
        project_back_kernel,
        grid_spec=pltpu.PrefetchScalarGridSpec(
            num_scalar_prefetch=1,
            grid=(3,),
            in_specs=[
                pl.BlockSpec((TOK, tile), lambda step, pick: (0, step)),
                pl.BlockSpec((TOK, D), lambda step, pick: (pick[0], 0)),
                full,
                gain_block,
                weight,
                weight,
            ],
            out_specs=[full, full, gain_block],
            scratch_shapes=[pltpu.VMEM((TOK, D), f32)],
        ),
        out_shape=[
            jax.ShapeDtypeStruct((TOK, D), f32),
            jax.ShapeDtypeStruct((TOK, D), bf16),
            jax.ShapeDtypeStruct((1, D), f32),
        ],
        compiler_params=pltpu.CompilerParams(vmem_limit_bytes=15 * MIB),
        cost_estimate=pl.CostEstimate(
            flops=2 * TOK * D * WIDE_A, bytes_accessed=2 * D * WIDE_A, transcendentals=0
        ),
        name="project_back",
    )(row, proj_low, start_rows, d_middle, gain, own, other)


def weight_grad_kernel(groups, pick_ref, *refs):
    lefts = refs[: 4 * len(groups)]
    rights = refs[4 * len(groups) : 8 * len(groups)]
    sum_ref, left_s = refs[8 * len(groups) :]
    step = pl.program_id(0)
    for index, (start, count) in enumerate(groups):
        four = lefts[4 * index : 4 * index + 4]
        blocks = rights[4 * index : 4 * index + 4]

        @pl.when(step == start)
        def _(four=four):
            for place, ref in enumerate(four):
                left_s[:, place * TOK : (place + 1) * TOK] = ref[...].astype(f32).T.astype(bf16)

        @pl.when((step >= start) & (step < start + count))
        def _(blocks=blocks):
            right = jnp.concatenate([ref[...] for ref in blocks], axis=0)
            sum_ref[...] = dot_nn(left_s[...], right).astype(bf16)


def weight_grad(picks, tile, groups):
    steps = []
    in_left = []
    in_right = []
    operands_left = []
    operands_right = []
    start = 0
    for left, right in groups:
        count = right[0][0].shape[1] // tile
        steps.append((start, count))
        for array, which, column in left:
            in_left.append(
                pl.BlockSpec(
                    (TOK, SIDE),
                    lambda step, pick, which=which, column=column: (
                        0 if which is None else pick[which],
                        column,
                    ),
                )
            )
            operands_left.append(array)
        for array, which in right:
            in_right.append(
                pl.BlockSpec(
                    (TOK, tile),
                    lambda step, pick, which=which, start=start, count=count: (
                        0 if which is None else pick[which],
                        jnp.clip(step - start, 0, count - 1),
                    ),
                )
            )
            operands_right.append(array)
        start += count
    return pl.pallas_call(
        functools.partial(weight_grad_kernel, tuple(steps)),
        grid_spec=pltpu.PrefetchScalarGridSpec(
            num_scalar_prefetch=1,
            grid=(start,),
            in_specs=in_left + in_right,
            out_specs=pl.BlockSpec((SIDE, tile), lambda step, pick: (0, step)),
            scratch_shapes=[pltpu.VMEM((SIDE, 4 * TOK), bf16)],
        ),
        out_shape=jax.ShapeDtypeStruct((SIDE, start * tile), bf16),
        compiler_params=pltpu.CompilerParams(vmem_limit_bytes=16 * MIB),
        cost_estimate=pl.CostEstimate(
            flops=8 * TOK * SIDE * start * tile,
            bytes_accessed=4 * SIDE * start * tile,
            transcendentals=0,
        ),
        name="weight_grad",
    )(picks, *operands_left, *operands_right)


def row_layout(doc_ids):
    rows = doc_ids.shape[0]
    positions = jnp.arange(TOK, dtype=jnp.int32)
    earlier = jnp.sum((doc_ids[:, None, :] < doc_ids[:, :, None]).astype(jnp.int32), axis=2)
    places = positions[None, :] - earlier
    half_dim = HD // 2
    inverse_freq = rope_base ** (-jnp.arange(half_dim, dtype=f32) / half_dim)
    angles = places.astype(f32)[:, :, None] * inverse_freq[None, None, :]
    repeats = LANES // half_dim
    rope = jnp.concatenate([jnp.cos(angles)] * repeats + [jnp.sin(angles)] * repeats, axis=-1)
    masks = jnp.concatenate(
        [
            jnp.broadcast_to((places >= shift).astype(f32)[:, :, None], (rows, TOK, LANES))
            for shift in (1, 2, 3)
        ],
        axis=-1,
    )
    doc_cols = jnp.broadcast_to(doc_ids[:, :, None], (rows, TOK, LANES))
    doc_rows = jnp.broadcast_to(doc_ids[:, None, :], (rows, 8, TOK))
    return (rope, masks, doc_cols, doc_rows)


def core_params(conv_weight, conv_bias, step_bias, decay_log, skip_scale, mixer_gain):
    taps = jnp.concatenate([conv_weight, conv_bias[None], jnp.zeros((3, CH), f32)], axis=0)
    heads = jnp.zeros((8, LANES), f32)
    heads = heads.at[0, :MH].set(step_bias).at[1, :MH].set(jnp.exp(decay_log))
    wide = jnp.concatenate(
        [jnp.repeat(skip_scale, MP)[None], mixer_gain[None], jnp.zeros((6, E), f32)], axis=0
    )
    return (taps, heads, wide)


def swapped(value):
    return lax.ppermute(value, "core", [(0, 1), (1, 0)])


def ring_order(chips):
    return [2 * step for step in range(chips // 2)] + [
        2 * step + 1 for step in reversed(range(chips // 2))
    ]


def ring_place(chip, chips):
    return jnp.where(chip % 2 == 0, chip // 2, chips - 1 - chip // 2)


def onward(value, steps):
    order = ring_order(lax.axis_size("chip"))
    chips = len(order)
    return lax.ppermute(
        value, "chip", [(order[at], order[(at + steps) % chips]) for at in range(chips)]
    )


def slot_offsets(chips):
    offsets = [0]
    for far in range(1, chips // 2):
        offsets += [-far, far]
    return offsets + [chips // 2]


def tied(*values):
    return lax.optimization_barrier(values)


class RingGather:
    def __init__(self, shard):
        self.slots = [shard]
        self.ahead = self.back = shard
        self.left = lax.axis_size("chip") // 2

    def operands(self):
        half = self.ahead.shape[0] // 2
        if self.left == 1:
            return self.ahead[:half], self.back[half:]
        return self.ahead, self.back

    def send(self, ahead, back):
        self.ahead, self.back = tied(onward(ahead, 1), onward(back, -1))
        self.slots += [self.ahead, self.back]
        self.left -= 1
        return self.ahead

    def step(self):
        return self.send(*self.operands())

    def last(self):
        while self.left > 1:
            self.step()

    def hold(self, value):
        self.ahead, self.back, _ = tied(self.ahead, self.back, value)
        self.slots[-2:] = [self.ahead, self.back]


class RingReduce:
    def __init__(self, sums):
        self.sums = sums
        self.chips = lax.axis_size("chip")
        self.size = sums.shape[0] // self.chips
        self.left = self.chips // 2
        self.ahead = self.back = None

    def slot(self, index, start=0, stop=None):
        stop = self.size if stop is None else stop
        return self.sums[index * self.size + start : index * self.size + stop]

    def operands(self):
        half = self.size // 2
        if self.ahead is None:
            last = self.chips - 1
            return self.slot(last, 0, half), self.slot(last, half)
        ahead, back = self.ahead.astype(f32), self.back.astype(f32)
        if self.left == self.chips // 2 - 1:
            ahead = jnp.pad(ahead, ((0, half), (0, 0)))
            back = jnp.pad(back, ((half, 0), (0, 0)))
        return (
            (self.slot(2 * self.left).astype(f32) + ahead).astype(bf16),
            (self.slot(2 * self.left - 1).astype(f32) + back).astype(bf16),
        )

    def send(self, ahead, back):
        self.ahead, self.back = tied(onward(ahead, 1), onward(back, -1))
        self.left -= 1
        return self.ahead

    def step(self):
        return self.send(*self.operands())

    def hold(self, value):
        self.ahead, self.back, _ = tied(self.ahead, self.back, value)

    def columns(self, start, stop):
        part = RingReduce(self.sums[:, start:stop])
        part.left = self.left
        part.ahead, part.back = self.ahead[:, start:stop], self.back[:, start:stop]
        return part

    def total(self):
        while self.left > 0:
            self.step()
        return self.slot(0).astype(f32) + self.ahead.astype(f32) + self.back.astype(f32)


def small_hops(chips):
    if chips & (chips - 1):
        return [lambda value: lax.psum(value, ("chip", "core")) - value]
    hops = [swapped]
    for bit in range(chips.bit_length() - 1):
        pairs = [(chip, chip ^ (1 << bit)) for chip in range(chips)]
        hops.append(lambda value, pairs=pairs: lax.ppermute(value, "chip", pairs))
    return hops


def ring_columns(core):
    chips = lax.axis_size("chip")
    place = ring_place(lax.axis_index("chip"), chips)
    own = []
    for offset in slot_offsets(chips):
        at = (place + offset) % chips
        own.append(jnp.where(at < chips // 2, 2 * at, 2 * (chips - 1 - at) + 1))
    own = jnp.stack(own)
    width = D // (2 * chips)
    starts = jnp.concatenate([2 * own + core, 2 * own + 1 - core]) * width
    wanted = (starts[:, None] + jnp.arange(width)[None, :]).reshape(D)
    return (jnp.arange(D)[:, None] == wanted[None, :]).astype(bf16)


def per_device(
    inputs, out_grad, doc_ids, row_live, pre_gain, mlp_gain, mixer_gain, conv_weight, conv_bias,
    step_bias, decay_log, skip_scale, mixer_in_weight, mixer_out_weight, query_weight, key_weight,
    value_weight, attend_weight, gate_up_weight, down_weight,
):
    is_first = lax.axis_index("section") == 0
    core = lax.axis_index("core")
    shard = mixer_in_weight.shape[1]
    packed_a = jnp.concatenate(
        [
            mixer_in_weight[0, :, :AT_Q],
            query_weight[0],
            key_weight[0],
            value_weight[0],
            mixer_in_weight[0, :, AT_Q:],
            jnp.zeros((shard, LANES - MH), bf16),
        ],
        axis=1,
    )
    packed_b = jnp.concatenate(
        [mixer_out_weight[0].T, attend_weight[0].T, gate_up_weight[0], down_weight[0].T], axis=1
    )

    layout = row_layout(doc_ids)
    params = core_params(
        conv_weight[0], conv_bias[0], step_bias[0], decay_log[0], skip_scale[0], mixer_gain[0]
    )
    turn = ring_columns(core)

    def own_order(values):
        if values.dtype == bf16:
            return dot_nn(values, turn).astype(bf16)
        return dot_exact(values, turn.astype(f32))

    def whole_order(values):
        if values.dtype == bf16:
            return dot_nt(values, turn).astype(bf16)
        return dot_exact(values, turn.astype(f32).T)

    pre_row = own_order(pre_gain)
    mlp_row = own_order(mlp_gain)
    first_rows = own_order(inputs)

    positions = jnp.arange(TOK, dtype=jnp.int32)
    live = (positions[None, :] < row_live[:, None]).reshape(MB * TOK, 1)
    from_loss = own_order(jnp.where(live, out_grad, jnp.zeros_like(out_grad)))
    first_rows, from_loss = tied(first_rows, from_loss)

    ring_a = RingGather(packed_a)
    ring_b = RingGather(packed_b)
    ring_a.step()
    ring_b.step()
    ring_a.last()
    now_a, now_b = tied(ring_a.operands(), ring_b.operands())
    ring_a.send(*now_a)
    ring_b.send(*now_b)
    own_a = jnp.concatenate(ring_a.slots, axis=0)
    pair_a = (own_a, swapped(own_a))
    now_b, gain_now, pair_a = tied(ring_b.operands(), pre_row, pair_a)
    ring_b.send(*now_b)
    projected = by_row(project(first_rows, gain_now, *pair_a))
    mixed = core_forward(0, projected, layout, params)
    ring_b.hold(mixed)
    now_b, mixed = tied(ring_b.operands(), mixed)
    ring_b.send(*now_b)
    mixed, _, _ = core_forward(1, projected, layout, params, held=mixed)
    ring_b.hold(mixed)
    while ring_b.left:
        ring_b.step()
    pair_b = (
        jnp.concatenate(ring_b.slots, axis=0),
        jnp.concatenate([swapped(slot) for slot in ring_b.slots], axis=0),
    )
    mixed = mixed.reshape(MB * TOK, MIXED)
    handed = feed_forward(first_rows, mixed, mlp_row, *pair_b, keep=False)

    parts = [first_rows[row * TOK : (row + 1) * TOK] for row in range(MB)]
    received = [passed_along(one, "section", 1) for one in handed]
    held, cores = (), ()
    starts = []
    for row in range(MB):
        start = jnp.where(is_first, parts[row], received[row])
        held = project(start, pre_row, *pair_a, row=row, held=held)
        starts.append(start)
        cores = core_forward(row, by_row(held), layout, params, held=cores)
        if row + 1 < MB:
            received[row + 1], cores, held = tied(received[row + 1], cores, held)
    start_rows = jnp.concatenate(starts, axis=0)
    normed = held[0]
    projected = by_row(held)
    mixed, pre, yns = cores
    mixed = mixed.reshape(MB * TOK, MIXED)
    result, middle, normed_two, gate, up, act = feed_forward(
        start_rows, mixed, mlp_row, *pair_b, keep=True
    )
    their_mixed = swapped(mixed)
    their_act = swapped(act)
    their_normed = swapped(normed[:, SIDE:])
    their_normed_two = swapped(normed_two[:, SIDE:])

    received = jnp.zeros((TOK, D), bf16)
    lefts = []
    rights = []
    rows = []
    picks = jnp.where(is_first, jnp.array([1, 0]), jnp.array([0, 1])).astype(jnp.int32)

    def tick_left(which):
        return [(lefts[1][which], None, 0), (lefts[2][which], None, 0)] + [
            (lefts[1][which + 2], None, 0), (lefts[2][which + 2], None, 0)
        ]

    def tick_right(which):
        return [(rights[tick][which + far], None) for far in (0, 2) for tick in (1, 2)]

    def saved_left(own, their):
        return [(own, 0, 0), (own, 1, 0), (their, 0, 0), (their, 1, 0)]

    def saved_right(own, their):
        return [(own, 0), (own, 1), (their, 0), (their, 1)]

    for tick in range(3):
        row = jnp.where(is_first, (1, 1, 0)[tick], (1, 0, 1)[tick]).astype(jnp.int32).reshape(1)
        if tick == 1:
            row, their_mixed, their_act, their_normed, their_normed_two = tied(
                row, their_mixed, their_act, their_normed, their_normed_two
            )
        if tick == 2:
            row, lefts[1], rights[1], rows[1] = tied(row, lefts[1], rights[1], rows[1])
        loss_row = (1, 0, 1)[tick]
        cotangent = jnp.where(
            is_first, received, from_loss[loss_row * TOK : (loss_row + 1) * TOK]
        )
        d_gate, d_up, d_middle, middle_low, d_mixed, mlp_grad = feed_back(
            row, cotangent, gate, up, middle, mlp_row, *pair_b
        )
        lefts.append(
            (cotangent, middle_low, swapped(cotangent[:, SIDE:]), swapped(middle_low[:, SIDE:]))
        )
        rights.append((d_gate, d_up, swapped(d_gate), swapped(d_up)))
        if tick < 2:
            attended = attend_back(row, projected, d_mixed, layout)
            proj_low, small = mixer_back(
                row, projected, pre, yns, d_mixed, attended, layout, params
            )
            their_low = swapped(proj_low)
        else:
            sum_c = weight_grad(
                picks,
                1024,
                [
                    (tick_left(1), saved_right(mixed, their_mixed)),
                    (tick_left(0), saved_right(act, their_act)),
                ],
            )
            ring_c = RingReduce(sum_c)
            now_c, row = tied(ring_c.operands(), row)
            ring_c.send(*now_c)
            attended = attend_back(row, projected, d_mixed, layout)
            ring_c.hold(attended)
            picks_now, now_c, rights[2] = tied(picks, ring_c.operands(), rights[2])
            ring_c.send(*now_c)
            sum_b = weight_grad(
                picks_now,
                1024,
                [
                    (saved_left(normed_two, their_normed_two), tick_right(0)),
                    (saved_left(normed_two, their_normed_two), tick_right(1)),
                ],
            )
            ring_b = RingReduce(sum_b)
            ring_c.hold(sum_b)
            now_b, now_c, row, attended = tied(
                ring_b.operands(), ring_c.operands(), row, attended
            )
            ring_c.send(*now_c)
            ring_b.send(*now_b)
            proj_low, small = mixer_back(
                row, projected, pre, yns, d_mixed, attended, layout, params
            )
            proj_low, ring_b.ahead, ring_b.back, ring_c.ahead, ring_c.back = tied(
                proj_low, ring_b.ahead, ring_b.back, ring_c.ahead, ring_c.back
            )
            their_low = swapped(proj_low)
            now_b, row = tied(ring_b.operands(), row)
            ring_b.send(*now_b)
            d_rows, d_low, pre_grad = project_back(
                row, proj_low, start_rows, d_middle, pre_row, *pair_a
            )
            now_c, their_low, d_rows, pre_grad = tied(
                ring_c.operands(), their_low, d_rows, pre_grad
            )
            ring_c.send(*now_c)
            picks_now, now_c = tied(picks, now_c)
            (p_one, their_one), (p_two, their_two) = rows[1][1], (proj_low, their_low)
            sum_a = weight_grad(
                picks_now,
                WIDE_A // 3,
                [
                    (
                        saved_left(normed, their_normed),
                        [(p_one, None), (p_two, None), (their_one, None), (their_two, None)],
                    )
                ],
            )
            ring_b.hold(sum_a)
            ring_a = RingReduce(sum_a)
            ring_c.hold(sum_a)
            now_a, now_b, ring_c.ahead, ring_c.back = tied(
                ring_a.operands(), ring_b.operands(), ring_c.ahead, ring_c.back
            )
            ring_b.send(*now_b)
            ring_a.send(*now_a)
        if tick < 2:
            d_rows, d_low, pre_grad = project_back(
                row, proj_low, start_rows, d_middle, pre_row, *pair_a
            )
        rows.append((d_rows, (proj_low, their_low), pre_grad, mlp_grad, small))
        if tick < 2:
            received = passed_along(d_low, "section", -1)

    pre_sum, mlp_sum, small = (one + two for one, two in zip(rows[1][2:], rows[2][2:]))
    gain_sums = whole_order(jnp.concatenate([pre_sum, mlp_sum], axis=0))
    small = jnp.concatenate([small, jnp.pad(gain_sums, ((0, 6), (0, CH - D)))], axis=0)

    hops = small_hops(lax.axis_size("chip"))

    def hop_beside(small, ring):
        if not hops:
            return small
        small, moved, _ = tied(small, hops.pop(0)(small), ring.ahead)
        return small + moved

    small = hop_beside(small, ring_a)
    ring_b.step()
    ring_a.step()
    small = hop_beside(small, ring_a)
    while ring_a.left > 2:
        ring_a.step()
    rings_a = [ring_a.columns(0, CUT_A), ring_a.columns(CUT_A, WIDE_A)]
    while rings_a[0].left:
        for ring in rings_a:
            ring.step()
        small = hop_beside(small, rings_a[0])
    for hop in hops:
        small = small + hop(small)
    share_c = ring_c.total()
    share_b = ring_b.total()
    share_a = jnp.concatenate([ring.total() for ring in rings_a], axis=1)

    start_grad = jnp.concatenate(
        [
            jnp.where(is_first, rows[2][0], rows[1][0]),
            jnp.where(is_first, rows[1][0], rows[2][0]),
        ],
        axis=0,
    )
    skip_sum = jnp.sum(small[6, :E].reshape(MH, MP), axis=1)
    mixer_in_grad = jnp.concatenate([share_a[:, :AT_Q], share_a[:, AT_DT : AT_DT + MH]], axis=1)
    return (
        whole_order(result)[None],
        whole_order(start_grad)[None],
        small[8:9, :D],
        small[9:10, :D],
        small[5:6, :E],
        small[None, :4],
        small[4:5],
        small[7:8, :MH],
        small[7:8, LANES : LANES + MH],
        skip_sum[None],
        mixer_in_grad[None],
        share_c[:, :E].T[None],
        share_a[:, AT_Q:AT_K][None],
        share_a[:, AT_K:AT_V][None],
        share_a[:, AT_V:AT_DT][None],
        share_c[:, E:MIXED].T[None],
        share_b[None],
        share_c[:, MIXED:].T[None],
    )


def solution(mesh):
    dp = mesh.shape["dp"]
    devices = mesh.devices.reshape(mesh.shape["section"], dp // 2, 2)
    paired = Mesh(devices, ("section", "chip", "core"))
    over = ("chip", "core")
    rows = P(over, None)
    small = P("section", None)
    by_row = P("section", over, None)
    by_col = P("section", None, over)
    small_specs = (small, small, small, P("section", None, None), small, small, small, small)
    big_specs = (by_row, by_col, by_row, by_row, by_row, by_col, by_row, by_col)
    in_specs = (rows, rows, rows, P(over)) + small_specs + big_specs
    out_specs = (by_row, by_row) + small_specs + big_specs
    return jax.shard_map(
        per_device, mesh=paired, in_specs=in_specs, out_specs=out_specs, check_vma=False
    )
```

```python
import functools
import math

import jax
import jax.numpy as jnp
from jax import lax
from jax.experimental import pallas as pl
from jax.experimental.pallas import tpu as pltpu
from jax.sharding import Mesh
from jax.sharding import PartitionSpec as P

D = 1024
FF = 2048
MH = 24
MP = 64
NS = 128
AH = 8
KVH = 2
HD = 64
MB = 2
TOK = 256
E = 1536
CH = 1792
HALF = TOK // 2
PAIRS = MH // 2
LANES = 128
SIDE = D // 2
MIB = 2**20

AT_W = E
AT_Q = E + CH
AT_K = AT_Q + AH * HD
AT_V = AT_K + KVH * HD
AT_DT = AT_V + KVH * HD
WIDE_A = AT_DT + LANES
CUT_A = 16 * LANES
MIXED = E + AH * HD
AT_GU = MIXED
AT_DN = AT_GU + 2 * FF
WIDE_B = AT_DN + FF

highest = lax.Precision.HIGHEST
epsilon = 1e-05
rope_base = 100000000000.0
bf16 = jnp.bfloat16
f32 = jnp.float32


def dot_nn(left, right):
    return lax.dot_general(left, right, (((1,), (0,)), ((), ())), preferred_element_type=f32)


def dot_nt(left, right):
    return lax.dot_general(left, right, (((1,), (1,)), ((), ())), preferred_element_type=f32)


def dot_tn(left, right):
    return lax.dot_general(left, right, (((0,), (0,)), ((), ())), preferred_element_type=f32)


def dot_exact(left, right):
    return lax.dot_general(
        left, right, (((1,), (0,)), ((), ())), precision=highest, preferred_element_type=f32
    )


def softplus(value):
    return jnp.maximum(value, 0.0) + jnp.log1p(jnp.exp(-jnp.abs(value)))


def lane_low(rows):
    return lax.broadcasted_iota(jnp.int32, (rows, LANES), 1) < HD


def rope_halves(rows):
    return (lax.broadcasted_iota(jnp.int32, (rows, LANES), 1) & (HD - 1)) < HD // 2


def rope_turn(tile, cosine, sine):
    swapped = jnp.where(
        rope_halves(tile.shape[0]),
        -pltpu.roll(tile, LANES - HD // 2, 1),
        pltpu.roll(tile, HD // 2, 1),
    )
    return tile * cosine + swapped * sine


def rope_back(tile, cosine, sine):
    swapped = jnp.where(
        rope_halves(tile.shape[0]),
        pltpu.roll(tile, LANES - HD // 2, 1),
        -pltpu.roll(tile, HD // 2, 1),
    )
    return tile * cosine + swapped * sine


def both_halves(tile):
    swapped = pltpu.roll(tile, HD, 1)
    low = lane_low(tile.shape[0])
    return (jnp.where(low, tile, swapped), jnp.where(low, swapped, tile))


def tile_at(index):
    return pl.ds(pl.multiple_of(index * LANES, LANES), LANES)


def tile_from(start, index):
    return pl.ds(pl.multiple_of(start + index * LANES, LANES), LANES)


def allowed_pairs(doc_col_ref, doc_row_ref):
    later = lax.broadcasted_iota(jnp.int32, (TOK, TOK), 0)
    early = lax.broadcasted_iota(jnp.int32, (TOK, TOK), 1)
    same = doc_col_ref[:, 0:1] == doc_row_ref[0:1, :]
    return (later >= early) & same


def pair_rows(tile):
    low = lane_low(tile.shape[0])
    zero = jnp.zeros_like(tile)
    return jnp.concatenate([jnp.where(low, tile, zero), jnp.where(low, zero, tile)], axis=0)


def pair_lanes(rows):
    half = rows.shape[0] // 2
    return jnp.where(lane_low(half), rows[:half], rows[half:])


def core_forward_kernel(
    held, pm_ref, pq_ref, pd_ref, rope_ref, mask_ref, doc_col_ref, doc_row_ref,
    taps_ref, head_ref, wide_ref, *refs,
):
    xb_ref, pre_ref, yns_ref, conv_s, cb_s, bias_s, sum_s = refs[3:] if held else refs

    def conv_tile(index, carry):
        rows = pm_ref[:, tile_from(AT_W, index)].astype(f32)
        at = tile_at(index)
        total = taps_ref[4:5, at] + taps_ref[3:4, at] * rows
        for shift in (1, 2, 3):
            moved = mask_ref[:, (shift - 1) * LANES : shift * LANES] * pltpu.roll(rows, shift, 0)
            total = total + taps_ref[3 - shift : 4 - shift, at] * moved
        total = total.astype(bf16)
        pre_ref[:, at] = total
        total = total.astype(f32)
        conv_s[:, at] = total * jax.nn.sigmoid(total)
        return carry

    lax.fori_loop(0, CH // LANES, conv_tile, 0)

    allowed = allowed_pairs(doc_col_ref, doc_row_ref)
    bias_s[...] = jnp.where(allowed, 0.0, -1e30)
    steps = softplus(pd_ref[...] + head_ref[0:1, :])
    rates = -steps * head_ref[1:2, :]
    totals = dot_exact(jnp.where(allowed, 1.0, 0.0), rates)
    totals_t = totals.T
    inward = conv_s[:, E : E + NS].astype(bf16)
    outward = conv_s[:, E + NS :].astype(bf16)
    cb_s[...] = jnp.where(allowed, dot_nt(outward, inward), 0.0)
    low = lane_low(TOK)
    for pair in range(PAIRS):
        lanes = slice(pair * LANES, (pair + 1) * LANES)
        first = 2 * pair
        step_pair = jnp.where(low, steps[:, first : first + 1], steps[:, first + 1 : first + 2])
        scaled = (conv_s[:, lanes] * step_pair).astype(bf16)
        mixes = []
        for head in (first, first + 1):
            apart = totals[:, head : head + 1] - totals_t[head : head + 1, :]
            mixes.append((jnp.exp(jnp.minimum(apart, 0.0)) * cb_s[...]).astype(bf16))
        yns_ref[:, lanes] = pair_lanes(dot_nn(jnp.concatenate(mixes, axis=0), scaled))

    sum_s[...] = jnp.zeros((TOK, LANES), f32)

    def gate_tile(index, carry):
        at = tile_at(index)
        gate = pm_ref[:, at].astype(f32)
        rows = yns_ref[:, at] + wide_ref[0:1, at] * conv_s[:, at]
        gated = rows * (gate * jax.nn.sigmoid(gate))
        sum_s[...] += gated * gated
        conv_s[:, at] = gated
        return carry

    lax.fori_loop(0, E // LANES, gate_tile, 0)
    scale = lax.rsqrt(jnp.sum(sum_s[...], axis=1, keepdims=True) * (1.0 / E) + epsilon)

    def norm_tile(index, carry):
        at = tile_at(index)
        xb_ref[:, at] = (conv_s[:, at] * scale * wide_ref[1:2, at]).astype(bf16)
        return carry

    lax.fori_loop(0, E // LANES, norm_tile, 0)

    cosine = rope_ref[:, :LANES]
    sine = rope_ref[:, LANES:]
    keys = both_halves(rope_turn(pq_ref[:, AH * HD : AH * HD + LANES].astype(f32), cosine, sine))
    values = both_halves(pq_ref[:, AH * HD + LANES :].astype(f32))
    keys = tuple(part.astype(bf16) for part in keys)
    values = tuple(part.astype(bf16) for part in values)
    for pair in range(AH // 2):
        group = pair // (AH // (2 * KVH))
        at = pair * LANES
        turned = rope_turn(pq_ref[:, at : at + LANES].astype(f32), cosine, sine)
        scores = dot_nt(pair_rows((turned * (1.0 / math.sqrt(HD))).astype(bf16)), keys[group])
        weights = []
        shares = []
        for part in (scores[:TOK], scores[TOK:]):
            part = part + bias_s[...]
            part = jnp.exp(part - jnp.max(part, axis=1, keepdims=True))
            shares.append(1.0 / jnp.sum(part, axis=1, keepdims=True))
            weights.append(part.astype(bf16))
        out = pair_lanes(dot_nn(jnp.concatenate(weights, axis=0), values[group]))
        out = out * jnp.where(low, shares[0], shares[1])
        xb_ref[:, E + pair * LANES : E + (pair + 1) * LANES] = out.astype(bf16)


def silu_slope(value, gate):
    return gate * (1.0 + value * (1.0 - gate))


def attend_back_kernel(
    pick_ref, pq_ref, dxb_ref, rope_ref, doc_col_ref, doc_row_ref, pg_ref, bias_s
):
    later = lax.broadcasted_iota(jnp.int32, (TOK, TOK), 1)
    early = lax.broadcasted_iota(jnp.int32, (TOK, TOK), 0)
    allowed_t = (later >= early) & (doc_col_ref[:, 0:1] == doc_row_ref[0:1, :])
    bias_s[...] = jnp.where(allowed_t, 0.0, -1e30)
    low = lane_low(TOK)
    cosine = rope_ref[:, :LANES]
    sine = rope_ref[:, LANES:]
    keys = both_halves(rope_turn(pq_ref[:, AH * HD : AH * HD + LANES].astype(f32), cosine, sine))
    values = both_halves(pq_ref[:, AH * HD + LANES :].astype(f32))
    root = 1.0 / math.sqrt(HD)
    d_keys = []
    d_values = []
    for group in range(KVH):
        key = keys[group].astype(bf16)
        key_rows = pair_rows(key)
        value_rows = pair_rows(values[group].astype(bf16))
        d_key = jnp.zeros((TOK, LANES), f32)
        d_value = jnp.zeros((TOK, LANES), f32)
        for pair in range(group * (AH // (2 * KVH)), (group + 1) * (AH // (2 * KVH))):
            at = pair * LANES
            turned = rope_turn(pq_ref[:, at : at + LANES].astype(f32), cosine, sine) * root
            query = turned.astype(bf16)
            d_out = dxb_ref[:, E + at : E + at + LANES].astype(bf16)
            scores = dot_nt(key_rows, query)
            d_weights = dot_nt(value_rows, d_out)
            weights = []
            d_scores = []
            for part in (slice(0, TOK), slice(TOK, 2 * TOK)):
                score = scores[part] + bias_s[...]
                weight = jnp.exp(score - jnp.max(score, axis=0, keepdims=True))
                weight = weight * (1.0 / jnp.sum(weight, axis=0, keepdims=True))
                d_weight = d_weights[part]
                offset = jnp.sum(weight * d_weight, axis=0, keepdims=True)
                weights.append(weight.astype(bf16))
                d_scores.append((weight * (d_weight - offset)).astype(bf16))
            d_value = d_value + pair_lanes(dot_nn(jnp.concatenate(weights, axis=0), d_out))
            d_key = d_key + pair_lanes(dot_nn(jnp.concatenate(d_scores, axis=0), query))
            d_query = pair_lanes(dot_tn(jnp.concatenate(d_scores, axis=1), key))
            pg_ref[:, at : at + LANES] = rope_back(d_query * root, cosine, sine).astype(bf16)
        d_keys.append(d_key + pltpu.roll(d_key, HD, 1))
        d_values.append(d_value + pltpu.roll(d_value, HD, 1))
    d_key = rope_back(jnp.where(low, d_keys[0], d_keys[1]), cosine, sine)
    pg_ref[:, AH * HD : AH * HD + LANES] = d_key.astype(bf16)
    pg_ref[:, AH * HD + LANES :] = jnp.where(low, d_values[0], d_values[1]).astype(bf16)


def mixer_back_kernel(
    pick_ref, pm_ref, pd_ref, pre_ref, yns_ref, dxb_ref, attend_ref, mask_ref, doc_col_ref,
    doc_row_ref, taps_ref, head_ref, wide_ref,
    pg_ref, small_ref,
    x_s, dx_s, dyb_s, cbt_s, dcbt_s, sum_s, ssum_s,
):
    small_ref[...] = jnp.zeros_like(small_ref)
    pg_ref[:, AT_Q:AT_DT] = attend_ref[...]
    sum_s[...] = jnp.zeros((TOK, LANES), f32)
    ssum_s[...] = jnp.zeros((TOK, LANES), f32)

    def start_tile(index, carry):
        at = tile_at(index)
        pre = pre_ref[:, at].astype(f32)
        heads_in = pre * jax.nn.sigmoid(pre)
        x_s[:, at] = heads_in
        gate = pm_ref[:, at].astype(f32)
        rows = yns_ref[:, at] + wide_ref[0:1, at] * heads_in
        gated = rows * (gate * jax.nn.sigmoid(gate))
        sum_s[...] += gated * gated
        ssum_s[...] += dxb_ref[:, at] * wide_ref[1:2, at] * gated
        return carry

    lax.fori_loop(0, E // LANES, start_tile, 0)
    scale = lax.rsqrt(jnp.sum(sum_s[...], axis=1, keepdims=True) * (1.0 / E) + epsilon)
    pull = jnp.sum(ssum_s[...], axis=1, keepdims=True) * (1.0 / E) * scale * scale * scale

    def gate_tile(index, carry):
        at = tile_at(index)
        heads_in = x_s[:, at]
        skip = wide_ref[0:1, at]
        gate = pm_ref[:, at].astype(f32)
        opened = jax.nn.sigmoid(gate)
        rows = yns_ref[:, at] + skip * heads_in
        gated = rows * (gate * opened)
        arrived = dxb_ref[:, at]
        d_gated = scale * (arrived * wide_ref[1:2, at]) - gated * pull
        small_ref[5:6, at] = jnp.sum(arrived * gated * scale, axis=0, keepdims=True)
        d_rows = d_gated * (gate * opened)
        pg_ref[:, at] = (d_gated * rows * silu_slope(gate, opened)).astype(bf16)
        small_ref[6:7, at] = jnp.sum(d_rows * heads_in, axis=0, keepdims=True)
        dyb_s[:, at] = d_rows.astype(bf16)
        dx_s[:, at] = skip * d_rows
        return carry

    lax.fori_loop(0, E // LANES, gate_tile, 0)

    def state_tile(index, carry):
        at = tile_from(E, index)
        pre = pre_ref[:, at].astype(f32)
        x_s[:, at] = pre * jax.nn.sigmoid(pre)
        return carry

    lax.fori_loop(0, 2, state_tile, 0)

    later = lax.broadcasted_iota(jnp.int32, (TOK, TOK), 1)
    early = lax.broadcasted_iota(jnp.int32, (TOK, TOK), 0)
    allowed_t = (later >= early) & (doc_col_ref[:, 0:1] == doc_row_ref[0:1, :])
    allowed = allowed_pairs(doc_col_ref, doc_row_ref)
    raw = pd_ref[...] + head_ref[0:1, :]
    steps = softplus(raw)
    decay = head_ref[1:2, :]
    rates = -steps * decay
    totals = dot_exact(jnp.where(allowed, 1.0, 0.0), rates)
    totals_t = totals.T
    inward = x_s[:, E : E + NS].astype(bf16)
    outward = x_s[:, E + NS :].astype(bf16)
    cbt_s[...] = jnp.where(allowed_t, dot_nt(inward, outward), 0.0)
    dcbt_s[...] = jnp.zeros((TOK, TOK), f32)
    low = lane_low(TOK)
    spread_row = lax.broadcasted_iota(jnp.int32, (2 * LANES, LANES), 0) // HD
    spread_col = lax.broadcasted_iota(jnp.int32, (2 * LANES, LANES), 1)
    sum_s[...] = jnp.zeros((TOK, LANES), f32)
    ssum_s[...] = jnp.zeros((TOK, LANES), f32)
    waiting = None
    for pair in range(PAIRS):
        lanes = slice(pair * LANES, (pair + 1) * LANES)
        first = 2 * pair
        step_pair = jnp.where(low, steps[:, first : first + 1], steps[:, first + 1 : first + 2])
        heads_in = x_s[:, lanes]
        scaled = (heads_in * step_pair).astype(bf16)
        d_rows = dyb_s[:, lanes]
        d_mix = dot_nt(pair_rows(scaled), d_rows)
        mixes = []
        d_pairs = None
        for side, head in enumerate((first, first + 1)):
            apart = totals_t[head : head + 1, :] - totals[:, head : head + 1]
            decays = jnp.exp(jnp.minimum(apart, 0.0))
            mixes.append((decays * cbt_s[...]).astype(bf16))
            part = d_mix[side * TOK : (side + 1) * TOK] * decays
            d_pairs = part if d_pairs is None else d_pairs + part
        dcbt_s[...] += d_pairs
        d_scaled = pair_lanes(dot_nn(jnp.concatenate(mixes, axis=0), d_rows))
        dx_s[:, lanes] += d_scaled * step_pair
        value = d_rows.astype(f32) * yns_ref[:, lanes] - scaled.astype(f32) * d_scaled
        coarse = value.astype(bf16)
        fine = (value - coarse.astype(f32)).astype(bf16)
        spread = (spread_col == first + (spread_row & 1)).astype(bf16)
        ssum_s[...] += dot_nn(jnp.concatenate([coarse, fine], axis=1), spread)
        value = (d_scaled * heads_in).astype(bf16)
        if pair % 2 == 0:
            waiting = value
        else:
            spread = (spread_col == first - 2 + spread_row).astype(bf16)
            sum_s[...] += dot_nn(jnp.concatenate([waiting, value], axis=1), spread)

    d_rates = dot_exact(jnp.where(allowed_t, 1.0, 0.0), ssum_s[...])
    d_steps = sum_s[...] - decay * d_rates
    d_raw = d_steps * jax.nn.sigmoid(raw)
    pg_ref[:, AT_DT:] = d_raw.astype(bf16)
    small_ref[7:8, :LANES] = jnp.sum(d_raw, axis=0, keepdims=True)
    small_ref[7:8, LANES : 2 * LANES] = jnp.sum(d_rates * rates, axis=0, keepdims=True)
    d_pairs = jnp.where(allowed_t, dcbt_s[...], 0.0).astype(bf16)
    dx_s[:, E : E + NS] = dot_nn(d_pairs, outward)
    dx_s[:, E + NS :] = dot_tn(d_pairs, inward)

    def conv_tile(index, carry):
        at = tile_at(index)
        pre = pre_ref[:, at].astype(f32)
        d_pre = dx_s[:, at] * silu_slope(pre, jax.nn.sigmoid(pre))
        rows = pm_ref[:, tile_from(AT_W, index)].astype(f32)
        small_ref[4:5, at] = jnp.sum(d_pre, axis=0, keepdims=True)
        small_ref[3:4, at] = jnp.sum(d_pre * rows, axis=0, keepdims=True)
        back = taps_ref[3:4, at] * d_pre
        for shift in (1, 2, 3):
            held = mask_ref[:, (shift - 1) * LANES : shift * LANES] * d_pre
            small_ref[3 - shift : 4 - shift, at] = jnp.sum(
                held * pltpu.roll(rows, shift, 0), axis=0, keepdims=True
            )
            back = back + taps_ref[3 - shift : 4 - shift, at] * pltpu.roll(held, TOK - shift, 0)
        pg_ref[:, tile_from(AT_W, index)] = back.astype(bf16)
        return carry

    lax.fori_loop(0, CH // LANES, conv_tile, 0)


def whole_block(shape):
    return pl.BlockSpec(shape, lambda *steps: (0,) * len(shape))


def once(shape, place):
    return pl.BlockSpec(shape, place, pipeline_mode=pl.Buffered(1))


def core_forward(row, projected, layout, params, held=()):
    operands = (*projected, *layout)

    def block(array):
        return once((None,) + array.shape[1:], lambda step: (row, 0, 0))

    outs = [
        jax.ShapeDtypeStruct((MB, TOK, MIXED), bf16),
        jax.ShapeDtypeStruct((MB, TOK, CH), bf16),
        jax.ShapeDtypeStruct((MB, TOK, E), f32),
    ]
    return pl.pallas_call(
        functools.partial(core_forward_kernel, bool(held)),
        grid=(1,),
        in_specs=[block(array) for array in operands]
        + [once(array.shape, lambda step: (0, 0)) for array in params]
        + [pl.BlockSpec(memory_space=pl.ANY)] * len(held),
        out_specs=[block(array) for array in outs],
        out_shape=outs,
        scratch_shapes=[
            pltpu.VMEM((TOK, CH), f32),
            pltpu.VMEM((TOK, TOK), f32),
            pltpu.VMEM((TOK, TOK), f32),
            pltpu.VMEM((TOK, LANES), f32),
        ],
        input_output_aliases={10: 0, 11: 1, 12: 2} if held else {},
        compiler_params=pltpu.CompilerParams(vmem_limit_bytes=12 * MIB),
        cost_estimate=pl.CostEstimate(
            flops=4 * 10**8, bytes_accessed=12 * 2**20, transcendentals=10**6
        ),
        name="core_forward",
    )(*operands, *params, *held)


def core_back_specs(by_row, plain):
    return [
        once((None,) + array.shape[1:], lambda step, pick: (pick[0], 0, 0)) if chosen
        else once(array.shape, lambda step, pick: (0, 0))
        for chosen, arrays in ((True, by_row), (False, plain))
        for array in arrays
    ]


def attend_back(row, projected, d_mixed, layout):
    rope, masks, doc_cols, doc_rows = layout
    return pl.pallas_call(
        attend_back_kernel,
        grid_spec=pltpu.PrefetchScalarGridSpec(
            num_scalar_prefetch=1,
            grid=(1,),
            in_specs=core_back_specs([projected[1]], [d_mixed])
            + core_back_specs([rope, doc_cols, doc_rows], []),
            out_specs=once((TOK, AT_DT - AT_Q), lambda step, pick: (0, 0)),
            scratch_shapes=[pltpu.VMEM((TOK, TOK), f32)],
        ),
        out_shape=jax.ShapeDtypeStruct((TOK, AT_DT - AT_Q), bf16),
        compiler_params=pltpu.CompilerParams(vmem_limit_bytes=6 * MIB),
        cost_estimate=pl.CostEstimate(
            flops=3 * 10**8, bytes_accessed=4 * 2**20, transcendentals=6 * 10**5
        ),
        name="attend_back",
    )(row, projected[1], d_mixed, rope, doc_cols, doc_rows)


def mixer_back(row, projected, pre, yns, d_mixed, attended, layout, params):
    rope, masks, doc_cols, doc_rows = layout
    return pl.pallas_call(
        mixer_back_kernel,
        grid_spec=pltpu.PrefetchScalarGridSpec(
            num_scalar_prefetch=1,
            grid=(1,),
            in_specs=core_back_specs(
                [projected[0], projected[2], pre, yns], [d_mixed, attended]
            )
            + core_back_specs([masks, doc_cols, doc_rows], params),
            out_specs=[
                once((TOK, WIDE_A), lambda step, pick: (0, 0)),
                once((8, CH), lambda step, pick: (0, 0)),
            ],
            scratch_shapes=[
                pltpu.VMEM((TOK, CH), f32),
                pltpu.VMEM((TOK, CH), f32),
                pltpu.VMEM((TOK, E), bf16),
                pltpu.VMEM((TOK, TOK), f32),
                pltpu.VMEM((TOK, TOK), f32),
                pltpu.VMEM((TOK, LANES), f32),
                pltpu.VMEM((TOK, LANES), f32),
            ],
        ),
        out_shape=[
            jax.ShapeDtypeStruct((TOK, WIDE_A), bf16),
            jax.ShapeDtypeStruct((8, CH), f32),
        ],
        compiler_params=pltpu.CompilerParams(vmem_limit_bytes=15 * MIB),
        cost_estimate=pl.CostEstimate(
            flops=7 * 10**8, bytes_accessed=10 * 2**20, transcendentals=15 * 10**5
        ),
        name="mixer_back",
    )(
        row, projected[0], projected[2], pre, yns, d_mixed, attended, masks, doc_cols, doc_rows,
        *params,
    )


def passed_along(value, axis, steps):
    count = lax.axis_size(axis)
    leading, last = (max(0, -steps), min(count, count - steps))
    return lax.ppermute(value, axis, [(source, source + steps) for source in range(leading, last)])


def norm_rows(values):
    return lax.rsqrt(jnp.mean(values * values, axis=-1, keepdims=True) + epsilon)


def norm_back(values, gain, arrived):
    scale = norm_rows(values)
    weighted = arrived * gain
    pull = jnp.mean(weighted * values, axis=-1, keepdims=True) * scale * scale * scale
    gain_grad = jnp.sum(arrived * values * scale, axis=0, keepdims=True)
    return (weighted * scale - values * pull, gain_grad)


def project_kernel(rows_ref, gain_ref, own_ref, other_ref, *refs):
    normed_ref, pm_ref, pq_ref, pd_ref = refs[-4:]
    step = pl.program_id(0)

    @pl.when(step == 0)
    def _():
        rows = rows_ref[...].astype(f32)
        normed_ref[...] = (rows * norm_rows(rows) * gain_ref[...]).astype(bf16)

    out = dot_nn(normed_ref[:, :SIDE], own_ref[...]) + dot_nn(normed_ref[:, SIDE:], other_ref[...])
    tile = WIDE_A // 3
    for index in range(2):
        @pl.when(step == index)
        def _(index=index):
            pm_ref[:, index * tile : (index + 1) * tile] = out.astype(bf16)

    @pl.when(step == 2)
    def _():
        pm_ref[:, 2 * tile :] = out[:, : AT_Q - 2 * tile].astype(bf16)
        pq_ref[...] = out[:, AT_Q - 2 * tile : AT_DT - 2 * tile].astype(bf16)
        pd_ref[...] = out[:, AT_DT - 2 * tile :]


def project(rows, gain, own, other, row=None, held=()):
    count = rows.shape[0]
    tile = WIDE_A // 3
    weight = pl.BlockSpec((SIDE, tile), lambda step: (0, step))
    at = row or 0
    total = count if row is None else MB * TOK
    widths = ((D, bf16), (AT_Q, bf16), (AT_DT - AT_Q, bf16), (LANES, f32))
    return pl.pallas_call(
        project_kernel,
        grid=(3,),
        in_specs=[whole_block((count, D)), whole_block((1, D)), weight, weight]
        + [pl.BlockSpec(memory_space=pl.ANY)] * len(held),
        out_specs=[pl.BlockSpec((count, width), lambda step: (at, 0)) for width, _ in widths],
        out_shape=[jax.ShapeDtypeStruct((total, width), kind) for width, kind in widths],
        input_output_aliases={4 + index: index for index in range(len(held))},
        compiler_params=pltpu.CompilerParams(vmem_limit_bytes=15 * MIB),
        cost_estimate=pl.CostEstimate(
            flops=2 * count * D * WIDE_A,
            bytes_accessed=2 * D * WIDE_A + 2 * count * WIDE_A,
            transcendentals=0,
        ),
        name="project",
    )(rows, gain, own, other, *held)


def by_row(projected):
    return tuple(array.reshape(MB, TOK, -1) for array in projected[1:])


def feed_forward_kernel(
    keep, rows_ref, mixed_ref, gain_ref,
    out_own, out_other, gate_own, gate_other, up_own, up_other, down_own, down_other,
    *refs,
):
    if keep:
        low_ref, middle_ref, normed_ref, gate_ref, up_ref, act_ref, total_s = refs[-7:]
    else:
        low_ref, middle_ref, normed_ref, total_s = refs
    step = pl.program_id(0)

    @pl.when(step == 0)
    def _():
        middle_ref[...] = rows_ref[...].astype(f32)

    @pl.when(step < 4)
    def _():
        mixed = mixed_ref[...]
        middle_ref[:, :SIDE] += dot_nt(mixed, out_own[...])
        middle_ref[:, SIDE:] += dot_nt(mixed, out_other[...])

    @pl.when(step == 3)
    def _():
        middle = middle_ref[...]
        normed_ref[...] = (middle * norm_rows(middle) * gain_ref[...]).astype(bf16)
        total_s[...] = middle

    @pl.when(step >= 4)
    def _():
        left = normed_ref[:, :SIDE]
        right = normed_ref[:, SIDE:]
        gate = dot_nn(left, gate_own[...]) + dot_nn(right, gate_other[...])
        up = dot_nn(left, up_own[...]) + dot_nn(right, up_other[...])
        act = (gate * jax.nn.sigmoid(gate) * up).astype(bf16)
        if keep:
            gate_ref[...] = gate.astype(bf16)
            up_ref[...] = up.astype(bf16)
            act_ref[...] = act
        total_s[:, :SIDE] += dot_nt(act, down_own[...])
        total_s[:, SIDE:] += dot_nt(act, down_other[...])

    @pl.when(step == 7)
    def _():
        low_ref[...] = total_s[...].astype(bf16)


def b_block(start, skipped):
    return pl.BlockSpec(
        (SIDE, 512), lambda step, *pick: (0, start + jnp.clip(step - skipped, 0, 3))
    )


def b_blocks(parts):
    return [b_block(start, skipped) for start, skipped in parts for _ in range(2)]


def feed_forward(row, rows, mixed, gain, own, other, held=None):
    keep = held is not None
    at = row if rows.shape[0] > TOK else 0

    def late(step):
        return (row, jnp.clip(step - 4, 0, 3))

    wide = pl.BlockSpec((TOK, 512), late)
    full = pl.BlockSpec((TOK, D), lambda step: (row, 0))
    scratch = [pltpu.VMEM((TOK, D), f32)]
    if keep:
        out_specs = [full, full, full, wide, wide, wide]
        out_shape = [
            jax.ShapeDtypeStruct((MB * TOK, width), kind)
            for width, kind in ((D, bf16), (D, f32), (D, bf16), (FF, bf16), (FF, bf16), (FF, bf16))
        ]
    else:
        out_specs = [whole_block((TOK, D))]
        out_shape = [jax.ShapeDtypeStruct((TOK, D), bf16)]
        scratch = [pltpu.VMEM((TOK, D), f32), pltpu.VMEM((TOK, D), bf16)] + scratch
    held = tuple(held or ())
    return pl.pallas_call(
        functools.partial(feed_forward_kernel, keep),
        grid=(8,),
        in_specs=[
            pl.BlockSpec((TOK, D), lambda step: (at, 0)),
            pl.BlockSpec((TOK, 512), lambda step: (row, jnp.clip(step, 0, 3))),
            whole_block((1, D)),
        ]
        + b_blocks(((0, 0), (4, 4), (8, 4), (12, 4)))
        + [pl.BlockSpec(memory_space=pl.ANY)] * len(held),
        out_specs=out_specs,
        out_shape=out_shape,
        scratch_shapes=scratch,
        input_output_aliases={11 + index: index for index in range(len(held))},
        compiler_params=pltpu.CompilerParams(vmem_limit_bytes=(18 if not keep else 46) * MIB),
        cost_estimate=pl.CostEstimate(
            flops=2 * TOK * D * WIDE_B, bytes_accessed=2 * D * WIDE_B, transcendentals=0
        ),
        name="feed_forward",
    )(rows, mixed, gain, *([own, other] * 4), *held)


def feed_back_kernel(
    pick_ref, cot_ref, gate_ref, up_ref, middle_ref, gain_ref,
    down_own, down_other, gate_own, gate_other, up_own, up_other, out_own, out_other,
    d_gate_ref, d_up_ref, d_middle_ref, low_ref, d_mixed_ref, gain_grad_ref,
    total_s,
):
    step = pl.program_id(0)

    @pl.when(step == 0)
    def _():
        total_s[...] = jnp.zeros_like(total_s)

    @pl.when(step < 4)
    def _():
        arrived = dot_nn(cot_ref[:, :SIDE], down_own[...]) + dot_nn(
            cot_ref[:, SIDE:], down_other[...]
        )
        gate = gate_ref[...].astype(f32)
        opened = jax.nn.sigmoid(gate)
        d_gate = (arrived * up_ref[...].astype(f32) * silu_slope(gate, opened)).astype(bf16)
        d_up = (arrived * (gate * opened)).astype(bf16)
        d_gate_ref[...] = d_gate
        d_up_ref[...] = d_up
        total_s[:, :SIDE] += dot_nt(d_gate, gate_own[...]) + dot_nt(d_up, up_own[...])
        total_s[:, SIDE:] += dot_nt(d_gate, gate_other[...]) + dot_nt(d_up, up_other[...])

    @pl.when(step == 3)
    def _():
        d_norm, gain_grad = norm_back(middle_ref[...], gain_ref[...], total_s[...])
        d_middle = cot_ref[...].astype(f32) + d_norm
        d_middle_ref[...] = d_middle
        low_ref[...] = d_middle.astype(bf16)
        gain_grad_ref[...] = gain_grad

    @pl.when(step >= 4)
    def _():
        d_mixed_ref[...] = dot_nn(low_ref[:, :SIDE], out_own[...]) + dot_nn(
            low_ref[:, SIDE:], out_other[...]
        )


def feed_back(row, cotangent, gate, up, middle, gain, own, other):
    saved = pl.BlockSpec((TOK, 512), lambda step, pick: (pick[0], jnp.clip(step, 0, 3)))
    early = pl.BlockSpec((TOK, 512), lambda step, pick: (0, jnp.clip(step, 0, 3)))
    late = pl.BlockSpec((TOK, 512), lambda step, pick: (0, jnp.clip(step - 4, 0, 3)))
    full = pl.BlockSpec((TOK, D), lambda step, pick: (0, 0))
    gain_block = pl.BlockSpec((1, D), lambda step, pick: (0, 0))
    return pl.pallas_call(
        feed_back_kernel,
        grid_spec=pltpu.PrefetchScalarGridSpec(
            num_scalar_prefetch=1,
            grid=(8,),
            in_specs=[
                full,
                saved,
                saved,
                pl.BlockSpec((TOK, D), lambda step, pick: (pick[0], 0)),
                gain_block,
            ]
            + b_blocks(((12, 0), (4, 0), (8, 0), (0, 4))),
            out_specs=[early, early, full, full, late, gain_block],
            scratch_shapes=[pltpu.VMEM((TOK, D), f32)],
        ),
        out_shape=[
            jax.ShapeDtypeStruct((TOK, FF), bf16),
            jax.ShapeDtypeStruct((TOK, FF), bf16),
            jax.ShapeDtypeStruct((TOK, D), f32),
            jax.ShapeDtypeStruct((TOK, D), bf16),
            jax.ShapeDtypeStruct((TOK, MIXED), f32),
            jax.ShapeDtypeStruct((1, D), f32),
        ],
        compiler_params=pltpu.CompilerParams(vmem_limit_bytes=46 * MIB),
        cost_estimate=pl.CostEstimate(
            flops=2 * TOK * D * WIDE_B, bytes_accessed=2 * D * WIDE_B, transcendentals=0
        ),
        name="feed_back",
    )(row, cotangent, gate, up, middle, gain, *([own, other] * 4))


def project_back_kernel(
    pick_ref, grad_ref, rows_ref, d_middle_ref, gain_ref, own_ref, other_ref,
    d_rows_ref, low_ref, gain_grad_ref, total_s,
):
    step = pl.program_id(0)

    @pl.when(step == 0)
    def _():
        total_s[...] = jnp.zeros_like(total_s)

    total_s[:, :SIDE] += dot_nt(grad_ref[...], own_ref[...])
    total_s[:, SIDE:] += dot_nt(grad_ref[...], other_ref[...])

    @pl.when(step == 2)
    def _():
        d_norm, gain_grad = norm_back(rows_ref[...].astype(f32), gain_ref[...], total_s[...])
        d_rows = d_middle_ref[...] + d_norm
        d_rows_ref[...] = d_rows
        low_ref[...] = d_rows.astype(bf16)
        gain_grad_ref[...] = gain_grad


def project_back(row, proj_low, start_rows, d_middle, gain, own, other):
    tile = WIDE_A // 3
    weight = pl.BlockSpec((SIDE, tile), lambda step, pick: (0, step))
    full = pl.BlockSpec((TOK, D), lambda step, pick: (0, 0))
    gain_block = pl.BlockSpec((1, D), lambda step, pick: (0, 0))
    return pl.pallas_call(
        project_back_kernel,
        grid_spec=pltpu.PrefetchScalarGridSpec(
            num_scalar_prefetch=1,
            grid=(3,),
            in_specs=[
                pl.BlockSpec((TOK, tile), lambda step, pick: (0, step)),
                pl.BlockSpec((TOK, D), lambda step, pick: (pick[0], 0)),
                full,
                gain_block,
                weight,
                weight,
            ],
            out_specs=[full, full, gain_block],
            scratch_shapes=[pltpu.VMEM((TOK, D), f32)],
        ),
        out_shape=[
            jax.ShapeDtypeStruct((TOK, D), f32),
            jax.ShapeDtypeStruct((TOK, D), bf16),
            jax.ShapeDtypeStruct((1, D), f32),
        ],
        compiler_params=pltpu.CompilerParams(vmem_limit_bytes=15 * MIB),
        cost_estimate=pl.CostEstimate(
            flops=2 * TOK * D * WIDE_A, bytes_accessed=2 * D * WIDE_A, transcendentals=0
        ),
        name="project_back",
    )(row, proj_low, start_rows, d_middle, gain, own, other)


def weight_grad_kernel(groups, pick_ref, *refs):
    lefts = refs[: 4 * len(groups)]
    rights = refs[4 * len(groups) : 8 * len(groups)]
    sum_ref, left_s = refs[8 * len(groups) :]
    step = pl.program_id(0)
    for index, (start, count) in enumerate(groups):
        four = lefts[4 * index : 4 * index + 4]
        blocks = rights[4 * index : 4 * index + 4]

        @pl.when(step == start)
        def _(four=four):
            for place, ref in enumerate(four):
                left_s[:, place * TOK : (place + 1) * TOK] = ref[...].astype(f32).T.astype(bf16)

        @pl.when((step >= start) & (step < start + count))
        def _(blocks=blocks):
            right = jnp.concatenate([ref[...] for ref in blocks], axis=0)
            sum_ref[...] = dot_nn(left_s[...], right).astype(bf16)


def weight_grad(picks, tile, groups):
    steps = []
    in_left = []
    in_right = []
    operands_left = []
    operands_right = []
    start = 0
    for left, right in groups:
        count = right[0][0].shape[1] // tile
        steps.append((start, count))
        for array, which, column in left:
            in_left.append(
                pl.BlockSpec(
                    (TOK, SIDE),
                    lambda step, pick, which=which, column=column: (
                        0 if which is None else pick[which],
                        column,
                    ),
                )
            )
            operands_left.append(array)
        for array, which in right:
            in_right.append(
                pl.BlockSpec(
                    (TOK, tile),
                    lambda step, pick, which=which, start=start, count=count: (
                        0 if which is None else pick[which],
                        jnp.clip(step - start, 0, count - 1),
                    ),
                )
            )
            operands_right.append(array)
        start += count
    return pl.pallas_call(
        functools.partial(weight_grad_kernel, tuple(steps)),
        grid_spec=pltpu.PrefetchScalarGridSpec(
            num_scalar_prefetch=1,
            grid=(start,),
            in_specs=in_left + in_right,
            out_specs=pl.BlockSpec((SIDE, tile), lambda step, pick: (0, step)),
            scratch_shapes=[pltpu.VMEM((SIDE, 4 * TOK), bf16)],
        ),
        out_shape=jax.ShapeDtypeStruct((SIDE, start * tile), bf16),
        compiler_params=pltpu.CompilerParams(vmem_limit_bytes=16 * MIB),
        cost_estimate=pl.CostEstimate(
            flops=8 * TOK * SIDE * start * tile,
            bytes_accessed=4 * SIDE * start * tile,
            transcendentals=0,
        ),
        name="weight_grad",
    )(picks, *operands_left, *operands_right)


def row_layout(doc_ids):
    rows = doc_ids.shape[0]
    positions = jnp.arange(TOK, dtype=jnp.int32)
    earlier = jnp.sum((doc_ids[:, None, :] < doc_ids[:, :, None]).astype(jnp.int32), axis=2)
    places = positions[None, :] - earlier
    half_dim = HD // 2
    inverse_freq = rope_base ** (-jnp.arange(half_dim, dtype=f32) / half_dim)
    angles = places.astype(f32)[:, :, None] * inverse_freq[None, None, :]
    repeats = LANES // half_dim
    rope = jnp.concatenate([jnp.cos(angles)] * repeats + [jnp.sin(angles)] * repeats, axis=-1)
    masks = jnp.concatenate(
        [
            jnp.broadcast_to((places >= shift).astype(f32)[:, :, None], (rows, TOK, LANES))
            for shift in (1, 2, 3)
        ],
        axis=-1,
    )
    doc_cols = jnp.broadcast_to(doc_ids[:, :, None], (rows, TOK, LANES))
    doc_rows = jnp.broadcast_to(doc_ids[:, None, :], (rows, 8, TOK))
    return (rope, masks, doc_cols, doc_rows)


def core_params(conv_weight, conv_bias, step_bias, decay_log, skip_scale, mixer_gain):
    taps = jnp.concatenate([conv_weight, conv_bias[None], jnp.zeros((3, CH), f32)], axis=0)
    heads = jnp.zeros((8, LANES), f32)
    heads = heads.at[0, :MH].set(step_bias).at[1, :MH].set(jnp.exp(decay_log))
    wide = jnp.concatenate(
        [jnp.repeat(skip_scale, MP)[None], mixer_gain[None], jnp.zeros((6, E), f32)], axis=0
    )
    return (taps, heads, wide)


def swapped(value):
    return lax.ppermute(value, "core", [(0, 1), (1, 0)])


def ring_order(chips):
    return [2 * step for step in range(chips // 2)] + [
        2 * step + 1 for step in reversed(range(chips // 2))
    ]


def ring_place(chip, chips):
    return jnp.where(chip % 2 == 0, chip // 2, chips - 1 - chip // 2)


def onward(value, steps):
    order = ring_order(lax.axis_size("chip"))
    chips = len(order)
    return lax.ppermute(
        value, "chip", [(order[at], order[(at + steps) % chips]) for at in range(chips)]
    )


def slot_offsets(chips):
    offsets = [0]
    for far in range(1, chips // 2):
        offsets += [-far, far]
    return offsets + [chips // 2]


def tied(*values):
    return lax.optimization_barrier(values)


class RingGather:
    def __init__(self, shard):
        self.slots = [shard]
        self.ahead = self.back = shard
        self.left = lax.axis_size("chip") // 2

    def operands(self):
        half = self.ahead.shape[0] // 2
        if self.left == 1:
            return self.ahead[:half], self.back[half:]
        return self.ahead, self.back

    def send(self, ahead, back):
        self.ahead, self.back = tied(onward(ahead, 1), onward(back, -1))
        self.slots += [self.ahead, self.back]
        self.left -= 1
        return self.ahead

    def step(self):
        return self.send(*self.operands())

    def last(self):
        while self.left > 1:
            self.step()

    def hold(self, value):
        self.ahead, self.back, _ = tied(self.ahead, self.back, value)
        self.slots[-2:] = [self.ahead, self.back]


class RingReduce:
    def __init__(self, sums):
        self.sums = sums
        self.chips = lax.axis_size("chip")
        self.size = sums.shape[0] // self.chips
        self.left = self.chips // 2
        self.ahead = self.back = None

    def slot(self, index, start=0, stop=None):
        stop = self.size if stop is None else stop
        return self.sums[index * self.size + start : index * self.size + stop]

    def operands(self):
        half = self.size // 2
        if self.ahead is None:
            last = self.chips - 1
            return self.slot(last, 0, half), self.slot(last, half)
        ahead, back = self.ahead.astype(f32), self.back.astype(f32)
        if self.left == self.chips // 2 - 1:
            ahead = jnp.pad(ahead, ((0, half), (0, 0)))
            back = jnp.pad(back, ((half, 0), (0, 0)))
        return (
            (self.slot(2 * self.left).astype(f32) + ahead).astype(bf16),
            (self.slot(2 * self.left - 1).astype(f32) + back).astype(bf16),
        )

    def send(self, ahead, back):
        self.ahead, self.back = tied(onward(ahead, 1), onward(back, -1))
        self.left -= 1
        return self.ahead

    def step(self):
        return self.send(*self.operands())

    def hold(self, value):
        self.ahead, self.back, _ = tied(self.ahead, self.back, value)

    def columns(self, start, stop):
        part = RingReduce(self.sums[:, start:stop])
        part.left = self.left
        part.ahead, part.back = self.ahead[:, start:stop], self.back[:, start:stop]
        return part

    def total(self):
        while self.left > 0:
            self.step()
        return self.slot(0).astype(f32) + self.ahead.astype(f32) + self.back.astype(f32)


def small_hops(chips):
    if chips & (chips - 1):
        return [lambda value: lax.psum(value, ("chip", "core")) - value]
    hops = [swapped]
    for bit in range(chips.bit_length() - 1):
        pairs = [(chip, chip ^ (1 << bit)) for chip in range(chips)]
        hops.append(lambda value, pairs=pairs: lax.ppermute(value, "chip", pairs))
    return hops


def ring_columns(core):
    chips = lax.axis_size("chip")
    place = ring_place(lax.axis_index("chip"), chips)
    own = []
    for offset in slot_offsets(chips):
        at = (place + offset) % chips
        own.append(jnp.where(at < chips // 2, 2 * at, 2 * (chips - 1 - at) + 1))
    own = jnp.stack(own)
    width = D // (2 * chips)
    starts = jnp.concatenate([2 * own + core, 2 * own + 1 - core]) * width
    wanted = (starts[:, None] + jnp.arange(width)[None, :]).reshape(D)
    return (jnp.arange(D)[:, None] == wanted[None, :]).astype(bf16)


def per_device(
    inputs, out_grad, doc_ids, row_live, pre_gain, mlp_gain, mixer_gain, conv_weight, conv_bias,
    step_bias, decay_log, skip_scale, mixer_in_weight, mixer_out_weight, query_weight, key_weight,
    value_weight, attend_weight, gate_up_weight, down_weight,
):
    is_first = lax.axis_index("section") == 0
    core = lax.axis_index("core")
    shard = mixer_in_weight.shape[1]
    packed_a = jnp.concatenate(
        [
            mixer_in_weight[0, :, :AT_Q],
            query_weight[0],
            key_weight[0],
            value_weight[0],
            mixer_in_weight[0, :, AT_Q:],
            jnp.zeros((shard, LANES - MH), bf16),
        ],
        axis=1,
    )
    packed_b = jnp.concatenate(
        [mixer_out_weight[0].T, attend_weight[0].T, gate_up_weight[0], down_weight[0].T], axis=1
    )

    layout = row_layout(doc_ids)
    params = core_params(
        conv_weight[0], conv_bias[0], step_bias[0], decay_log[0], skip_scale[0], mixer_gain[0]
    )
    turn = ring_columns(core)

    def own_order(values):
        if values.dtype == bf16:
            return dot_nn(values, turn).astype(bf16)
        return dot_exact(values, turn.astype(f32))

    def whole_order(values):
        if values.dtype == bf16:
            return dot_nt(values, turn).astype(bf16)
        return dot_exact(values, turn.astype(f32).T)

    pre_row = own_order(pre_gain)
    mlp_row = own_order(mlp_gain)
    first_rows = own_order(inputs)

    positions = jnp.arange(TOK, dtype=jnp.int32)
    live = (positions[None, :] < row_live[:, None]).reshape(MB * TOK, 1)
    from_loss = own_order(jnp.where(live, out_grad, jnp.zeros_like(out_grad)))
    first_rows, from_loss = tied(first_rows, from_loss)

    ring_a = RingGather(packed_a)
    ring_b = RingGather(packed_b)
    ring_a.step()
    ring_b.step()
    ring_a.last()
    now_a, now_b = tied(ring_a.operands(), ring_b.operands())
    ring_a.send(*now_a)
    ring_b.send(*now_b)
    own_a = jnp.concatenate(ring_a.slots, axis=0)
    pair_a = (own_a, swapped(own_a))
    now_b, gain_now, pair_a = tied(ring_b.operands(), pre_row, pair_a)
    ring_b.send(*now_b)
    projected = by_row(project(first_rows, gain_now, *pair_a))
    mixed = core_forward(0, projected, layout, params)
    ring_b.hold(mixed)
    now_b, mixed = tied(ring_b.operands(), mixed)
    ring_b.send(*now_b)
    mixed, _, _ = core_forward(1, projected, layout, params, held=mixed)
    ring_b.hold(mixed)
    while ring_b.left:
        ring_b.step()
    pair_b = (
        jnp.concatenate(ring_b.slots, axis=0),
        jnp.concatenate([swapped(slot) for slot in ring_b.slots], axis=0),
    )
    mixed = mixed.reshape(MB * TOK, MIXED)
    received = {}
    for row in (1, 0):
        (handed,) = feed_forward(row, first_rows, mixed, mlp_row, *pair_b)
        received[row] = passed_along(handed, "section", 1)

    def second_pass(row, projects=(), cores=(), forwards=()):
        start = jnp.where(is_first, first_rows[row * TOK : (row + 1) * TOK], received[row])
        projects = project(start, pre_row, *pair_a, row=row, held=projects)
        cores = core_forward(row, by_row(projects), layout, params, held=cores)
        mixed = cores[0].reshape(MB * TOK, MIXED)
        forwards = feed_forward(row, start, mixed, mlp_row, *pair_b, held=forwards)
        return start, projects, cores, forwards

    arrived = jnp.zeros((TOK, D), bf16)
    lefts = []
    rights = []
    rows = []
    picks = jnp.where(is_first, jnp.array([1, 0]), jnp.array([0, 1])).astype(jnp.int32)

    def tick_left(which):
        return [(lefts[1][which], None, 0), (lefts[2][which], None, 0)] + [
            (lefts[1][which + 2], None, 0), (lefts[2][which + 2], None, 0)
        ]

    def tick_right(which):
        return [(rights[tick][which + far], None) for far in (0, 2) for tick in (1, 2)]

    def saved_left(own, their):
        return [(own, 0, 0), (own, 1, 0), (their, 0, 0), (their, 1, 0)]

    def saved_right(own, their):
        return [(own, 0), (own, 1), (their, 0), (their, 1)]

    start, projects, cores, forwards = second_pass(1)
    starts = {1: start}
    start_rows = jnp.concatenate([start, start], axis=0)
    for tick in range(3):
        if tick == 1:
            (projects, cores, forwards), received[0], _ = tied(
                (projects, cores, forwards), received[0], d_low
            )
            starts[0], projects, cores, forwards = second_pass(0, projects, cores, forwards)
            start_rows = jnp.concatenate([starts[0], starts[1]], axis=0)
            arrived, forwards = tied(arrived, forwards)
        normed, projected = projects[0], by_row(projects)
        mixed, pre, yns = cores[0].reshape(MB * TOK, MIXED), cores[1], cores[2]
        result, middle, normed_two, gate, up, act = forwards
        row = jnp.where(is_first, (1, 1, 0)[tick], (1, 0, 1)[tick]).astype(jnp.int32).reshape(1)
        if tick == 2:
            row, lefts[1], rights[1], rows[1] = tied(row, lefts[1], rights[1], rows[1])
        loss_row = (1, 0, 1)[tick]
        cotangent = jnp.where(
            is_first, arrived, from_loss[loss_row * TOK : (loss_row + 1) * TOK]
        )
        if tick == 1:
            cotangent, swaps = tied(
                cotangent, (mixed, act, normed[:, SIDE:], normed_two[:, SIDE:])
            )
            their_mixed, their_act, their_normed, their_normed_two = map(swapped, swaps)
        d_gate, d_up, d_middle, middle_low, d_mixed, mlp_grad = feed_back(
            row, cotangent, gate, up, middle, mlp_row, *pair_b
        )
        lefts.append(
            (cotangent, middle_low, swapped(cotangent[:, SIDE:]), swapped(middle_low[:, SIDE:]))
        )
        rights.append((d_gate, d_up, swapped(d_gate), swapped(d_up)))
        if tick < 2:
            attended = attend_back(row, projected, d_mixed, layout)
            if tick == 1:
                row, their_mixed, their_act, their_normed, their_normed_two = tied(
                    row, their_mixed, their_act, their_normed, their_normed_two
                )
            proj_low, small = mixer_back(
                row, projected, pre, yns, d_mixed, attended, layout, params
            )
            their_low = swapped(proj_low)
        else:
            sum_c = weight_grad(
                picks,
                1024,
                [
                    (tick_left(1), saved_right(mixed, their_mixed)),
                    (tick_left(0), saved_right(act, their_act)),
                ],
            )
            ring_c = RingReduce(sum_c)
            now_c, row = tied(ring_c.operands(), row)
            ring_c.send(*now_c)
            attended = attend_back(row, projected, d_mixed, layout)
            ring_c.hold(attended)
            picks_now, now_c, rights[2] = tied(picks, ring_c.operands(), rights[2])
            ring_c.send(*now_c)
            sum_b = weight_grad(
                picks_now,
                1024,
                [
                    (saved_left(normed_two, their_normed_two), tick_right(0)),
                    (saved_left(normed_two, their_normed_two), tick_right(1)),
                ],
            )
            ring_b = RingReduce(sum_b)
            ring_c.hold(sum_b)
            now_b, now_c, row, attended = tied(
                ring_b.operands(), ring_c.operands(), row, attended
            )
            ring_c.send(*now_c)
            ring_b.send(*now_b)
            proj_low, small = mixer_back(
                row, projected, pre, yns, d_mixed, attended, layout, params
            )
            proj_low, ring_b.ahead, ring_b.back, ring_c.ahead, ring_c.back = tied(
                proj_low, ring_b.ahead, ring_b.back, ring_c.ahead, ring_c.back
            )
            their_low = swapped(proj_low)
            now_b, row = tied(ring_b.operands(), row)
            ring_b.send(*now_b)
            d_rows, d_low, pre_grad = project_back(
                row, proj_low, start_rows, d_middle, pre_row, *pair_a
            )
            now_c, their_low, d_rows, pre_grad = tied(
                ring_c.operands(), their_low, d_rows, pre_grad
            )
            ring_c.send(*now_c)
            picks_now, now_c = tied(picks, now_c)
            (p_one, their_one), (p_two, their_two) = rows[1][1], (proj_low, their_low)
            sum_a = weight_grad(
                picks_now,
                WIDE_A // 3,
                [
                    (
                        saved_left(normed, their_normed),
                        [(p_one, None), (p_two, None), (their_one, None), (their_two, None)],
                    )
                ],
            )
            ring_b.hold(sum_a)
            ring_a = RingReduce(sum_a)
            ring_c.hold(sum_a)
            now_a, now_b, ring_c.ahead, ring_c.back = tied(
                ring_a.operands(), ring_b.operands(), ring_c.ahead, ring_c.back
            )
            ring_b.send(*now_b)
            ring_a.send(*now_a)
        if tick < 2:
            d_rows, d_low, pre_grad = project_back(
                row, proj_low, start_rows, d_middle, pre_row, *pair_a
            )
        rows.append((d_rows, (proj_low, their_low), pre_grad, mlp_grad, small))
        if tick < 2:
            arrived = passed_along(d_low, "section", -1)

    pre_sum, mlp_sum, small = (one + two for one, two in zip(rows[1][2:], rows[2][2:]))
    gain_sums = whole_order(jnp.concatenate([pre_sum, mlp_sum], axis=0))
    small = jnp.concatenate([small, jnp.pad(gain_sums, ((0, 6), (0, CH - D)))], axis=0)

    hops = small_hops(lax.axis_size("chip"))

    def hop_beside(small, ring):
        if not hops:
            return small
        small, moved, _ = tied(small, hops.pop(0)(small), ring.ahead)
        return small + moved

    small = hop_beside(small, ring_a)
    ring_b.step()
    ring_a.step()
    small = hop_beside(small, ring_a)
    while ring_a.left > 2:
        ring_a.step()
    d_last = tied(rows[2][0], ring_a.ahead)[0]
    rings_a = [ring_a.columns(0, CUT_A), ring_a.columns(CUT_A, WIDE_A)]
    while rings_a[0].left:
        for ring in rings_a:
            ring.step()
        small = hop_beside(small, rings_a[0])
    for hop in hops:
        small = small + hop(small)
    share_c = ring_c.total()
    share_b = ring_b.total()
    share_a = jnp.concatenate([ring.total() for ring in rings_a], axis=1)

    start_grad = jnp.concatenate(
        [
            jnp.where(is_first, d_last, rows[1][0]),
            jnp.where(is_first, rows[1][0], d_last),
        ],
        axis=0,
    )
    skip_sum = jnp.sum(small[6, :E].reshape(MH, MP), axis=1)
    mixer_in_grad = jnp.concatenate([share_a[:, :AT_Q], share_a[:, AT_DT : AT_DT + MH]], axis=1)
    return (
        whole_order(result)[None],
        whole_order(start_grad)[None],
        small[8:9, :D],
        small[9:10, :D],
        small[5:6, :E],
        small[None, :4],
        small[4:5],
        small[7:8, :MH],
        small[7:8, LANES : LANES + MH],
        skip_sum[None],
        mixer_in_grad[None],
        share_c[:, :E].T[None],
        share_a[:, AT_Q:AT_K][None],
        share_a[:, AT_K:AT_V][None],
        share_a[:, AT_V:AT_DT][None],
        share_c[:, E:MIXED].T[None],
        share_b[None],
        share_c[:, MIXED:].T[None],
    )


def solution(mesh):
    dp = mesh.shape["dp"]
    devices = mesh.devices.reshape(mesh.shape["section"], dp // 2, 2)
    paired = Mesh(devices, ("section", "chip", "core"))
    over = ("chip", "core")
    rows = P(over, None)
    small = P("section", None)
    by_row = P("section", over, None)
    by_col = P("section", None, over)
    small_specs = (small, small, small, P("section", None, None), small, small, small, small)
    big_specs = (by_row, by_col, by_row, by_row, by_row, by_col, by_row, by_col)
    in_specs = (rows, rows, rows, P(over)) + small_specs + big_specs
    out_specs = (by_row, by_row) + small_specs + big_specs
    return jax.shard_map(
        per_device, mesh=paired, in_specs=in_specs, out_specs=out_specs, check_vma=False
    )
```

```python
import functools
import math

import jax
import jax.numpy as jnp
from jax import lax
from jax.experimental import pallas as pl
from jax.experimental.pallas import tpu as pltpu
from jax.sharding import Mesh
from jax.sharding import PartitionSpec as P

D = 1024
FF = 2048
MH = 24
MP = 64
NS = 128
AH = 8
KVH = 2
HD = 64
MB = 2
TOK = 256
E = 1536
CH = 1792
HALF = TOK // 2
PAIRS = MH // 2
LANES = 128
SIDE = D // 2
MIB = 2**20

AT_W = E
AT_Q = E + CH
AT_K = AT_Q + AH * HD
AT_V = AT_K + KVH * HD
AT_DT = AT_V + KVH * HD
WIDE_A = AT_DT + LANES
CUT_A = 16 * LANES
BLOCK = 512
MIXED = E + AH * HD
AT_GU = MIXED
AT_DN = AT_GU + 2 * FF
WIDE_B = AT_DN + FF

highest = lax.Precision.HIGHEST
epsilon = 1e-05
rope_base = 100000000000.0
bf16 = jnp.bfloat16
f32 = jnp.float32


def dot_nn(left, right):
    return lax.dot_general(left, right, (((1,), (0,)), ((), ())), preferred_element_type=f32)


def dot_nt(left, right):
    return lax.dot_general(left, right, (((1,), (1,)), ((), ())), preferred_element_type=f32)


def dot_tn(left, right):
    return lax.dot_general(left, right, (((0,), (0,)), ((), ())), preferred_element_type=f32)


def dot_exact(left, right):
    return lax.dot_general(
        left, right, (((1,), (0,)), ((), ())), precision=highest, preferred_element_type=f32
    )


def softplus(value):
    return jnp.maximum(value, 0.0) + jnp.log1p(jnp.exp(-jnp.abs(value)))


def lane_low(rows):
    return lax.broadcasted_iota(jnp.int32, (rows, LANES), 1) < HD


def rope_halves(rows):
    return (lax.broadcasted_iota(jnp.int32, (rows, LANES), 1) & (HD - 1)) < HD // 2


def rope_turn(tile, cosine, sine):
    swapped = jnp.where(
        rope_halves(tile.shape[0]),
        -pltpu.roll(tile, LANES - HD // 2, 1),
        pltpu.roll(tile, HD // 2, 1),
    )
    return tile * cosine + swapped * sine


def rope_back(tile, cosine, sine):
    swapped = jnp.where(
        rope_halves(tile.shape[0]),
        pltpu.roll(tile, LANES - HD // 2, 1),
        -pltpu.roll(tile, HD // 2, 1),
    )
    return tile * cosine + swapped * sine


def both_halves(tile):
    swapped = pltpu.roll(tile, HD, 1)
    low = lane_low(tile.shape[0])
    return (jnp.where(low, tile, swapped), jnp.where(low, swapped, tile))


def tile_at(index):
    return pl.ds(pl.multiple_of(index * LANES, LANES), LANES)


def tile_from(start, index):
    return pl.ds(pl.multiple_of(start + index * LANES, LANES), LANES)


def allowed_pairs(doc_col_ref, doc_row_ref):
    later = lax.broadcasted_iota(jnp.int32, (TOK, TOK), 0)
    early = lax.broadcasted_iota(jnp.int32, (TOK, TOK), 1)
    same = doc_col_ref[:, 0:1] == doc_row_ref[0:1, :]
    return (later >= early) & same


def pair_rows(tile):
    low = lane_low(tile.shape[0])
    zero = jnp.zeros_like(tile)
    return jnp.concatenate([jnp.where(low, tile, zero), jnp.where(low, zero, tile)], axis=0)


def pair_lanes(rows):
    half = rows.shape[0] // 2
    return jnp.where(lane_low(half), rows[:half], rows[half:])


def core_forward_kernel(
    held, pm_ref, pq_ref, pd_ref, rope_ref, mask_ref, doc_col_ref, doc_row_ref,
    taps_ref, head_ref, wide_ref, *refs,
):
    xb_ref, pre_ref, yns_ref, conv_s, cb_s, bias_s, sum_s = refs[3:] if held else refs

    def conv_tile(index, carry):
        rows = pm_ref[:, tile_from(AT_W, index)].astype(f32)
        at = tile_at(index)
        total = taps_ref[4:5, at] + taps_ref[3:4, at] * rows
        for shift in (1, 2, 3):
            moved = mask_ref[:, (shift - 1) * LANES : shift * LANES] * pltpu.roll(rows, shift, 0)
            total = total + taps_ref[3 - shift : 4 - shift, at] * moved
        total = total.astype(bf16)
        pre_ref[:, at] = total
        total = total.astype(f32)
        conv_s[:, at] = total * jax.nn.sigmoid(total)
        return carry

    lax.fori_loop(0, CH // LANES, conv_tile, 0)

    allowed = allowed_pairs(doc_col_ref, doc_row_ref)
    bias_s[...] = jnp.where(allowed, 0.0, -1e30)
    steps = softplus(pd_ref[...] + head_ref[0:1, :])
    rates = -steps * head_ref[1:2, :]
    totals = dot_exact(jnp.where(allowed, 1.0, 0.0), rates)
    totals_t = totals.T
    inward = conv_s[:, E : E + NS].astype(bf16)
    outward = conv_s[:, E + NS :].astype(bf16)
    cb_s[...] = jnp.where(allowed, dot_nt(outward, inward), 0.0)
    low = lane_low(TOK)
    for pair in range(PAIRS):
        lanes = slice(pair * LANES, (pair + 1) * LANES)
        first = 2 * pair
        step_pair = jnp.where(low, steps[:, first : first + 1], steps[:, first + 1 : first + 2])
        scaled = (conv_s[:, lanes] * step_pair).astype(bf16)
        mixes = []
        for head in (first, first + 1):
            apart = totals[:, head : head + 1] - totals_t[head : head + 1, :]
            mixes.append((jnp.exp(jnp.minimum(apart, 0.0)) * cb_s[...]).astype(bf16))
        yns_ref[:, lanes] = pair_lanes(dot_nn(jnp.concatenate(mixes, axis=0), scaled))

    sum_s[...] = jnp.zeros((TOK, LANES), f32)

    def gate_tile(index, carry):
        at = tile_at(index)
        gate = pm_ref[:, at].astype(f32)
        rows = yns_ref[:, at] + wide_ref[0:1, at] * conv_s[:, at]
        gated = rows * (gate * jax.nn.sigmoid(gate))
        sum_s[...] += gated * gated
        conv_s[:, at] = gated
        return carry

    lax.fori_loop(0, E // LANES, gate_tile, 0)
    scale = lax.rsqrt(jnp.sum(sum_s[...], axis=1, keepdims=True) * (1.0 / E) + epsilon)

    def norm_tile(index, carry):
        at = tile_at(index)
        xb_ref[:, at] = (conv_s[:, at] * scale * wide_ref[1:2, at]).astype(bf16)
        return carry

    lax.fori_loop(0, E // LANES, norm_tile, 0)

    cosine = rope_ref[:, :LANES]
    sine = rope_ref[:, LANES:]
    keys = both_halves(rope_turn(pq_ref[:, AH * HD : AH * HD + LANES].astype(f32), cosine, sine))
    values = both_halves(pq_ref[:, AH * HD + LANES :].astype(f32))
    keys = tuple(part.astype(bf16) for part in keys)
    values = tuple(part.astype(bf16) for part in values)
    for pair in range(AH // 2):
        group = pair // (AH // (2 * KVH))
        at = pair * LANES
        turned = rope_turn(pq_ref[:, at : at + LANES].astype(f32), cosine, sine)
        scores = dot_nt(pair_rows((turned * (1.0 / math.sqrt(HD))).astype(bf16)), keys[group])
        weights = []
        shares = []
        for part in (scores[:TOK], scores[TOK:]):
            part = part + bias_s[...]
            part = jnp.exp(part - jnp.max(part, axis=1, keepdims=True))
            shares.append(1.0 / jnp.sum(part, axis=1, keepdims=True))
            weights.append(part.astype(bf16))
        out = pair_lanes(dot_nn(jnp.concatenate(weights, axis=0), values[group]))
        out = out * jnp.where(low, shares[0], shares[1])
        xb_ref[:, E + pair * LANES : E + (pair + 1) * LANES] = out.astype(bf16)


def silu_slope(value, gate):
    return gate * (1.0 + value * (1.0 - gate))


def attend_back_kernel(
    pick_ref, pq_ref, dxb_ref, rope_ref, doc_col_ref, doc_row_ref, pg_ref, bias_s
):
    later = lax.broadcasted_iota(jnp.int32, (TOK, TOK), 1)
    early = lax.broadcasted_iota(jnp.int32, (TOK, TOK), 0)
    allowed_t = (later >= early) & (doc_col_ref[:, 0:1] == doc_row_ref[0:1, :])
    bias_s[...] = jnp.where(allowed_t, 0.0, -1e30)
    low = lane_low(TOK)
    cosine = rope_ref[:, :LANES]
    sine = rope_ref[:, LANES:]
    keys = both_halves(rope_turn(pq_ref[:, AH * HD : AH * HD + LANES].astype(f32), cosine, sine))
    values = both_halves(pq_ref[:, AH * HD + LANES :].astype(f32))
    root = 1.0 / math.sqrt(HD)
    d_keys = []
    d_values = []
    for group in range(KVH):
        key = keys[group].astype(bf16)
        key_rows = pair_rows(key)
        value_rows = pair_rows(values[group].astype(bf16))
        d_key = jnp.zeros((TOK, LANES), f32)
        d_value = jnp.zeros((TOK, LANES), f32)
        for pair in range(group * (AH // (2 * KVH)), (group + 1) * (AH // (2 * KVH))):
            at = pair * LANES
            turned = rope_turn(pq_ref[:, at : at + LANES].astype(f32), cosine, sine) * root
            query = turned.astype(bf16)
            d_out = dxb_ref[:, E + at : E + at + LANES].astype(bf16)
            scores = dot_nt(key_rows, query)
            d_weights = dot_nt(value_rows, d_out)
            weights = []
            d_scores = []
            for part in (slice(0, TOK), slice(TOK, 2 * TOK)):
                score = scores[part] + bias_s[...]
                weight = jnp.exp(score - jnp.max(score, axis=0, keepdims=True))
                weight = weight * (1.0 / jnp.sum(weight, axis=0, keepdims=True))
                d_weight = d_weights[part]
                offset = jnp.sum(weight * d_weight, axis=0, keepdims=True)
                weights.append(weight.astype(bf16))
                d_scores.append((weight * (d_weight - offset)).astype(bf16))
            d_value = d_value + pair_lanes(dot_nn(jnp.concatenate(weights, axis=0), d_out))
            d_key = d_key + pair_lanes(dot_nn(jnp.concatenate(d_scores, axis=0), query))
            d_query = pair_lanes(dot_tn(jnp.concatenate(d_scores, axis=1), key))
            pg_ref[:, at : at + LANES] = rope_back(d_query * root, cosine, sine).astype(bf16)
        d_keys.append(d_key + pltpu.roll(d_key, HD, 1))
        d_values.append(d_value + pltpu.roll(d_value, HD, 1))
    d_key = rope_back(jnp.where(low, d_keys[0], d_keys[1]), cosine, sine)
    pg_ref[:, AH * HD : AH * HD + LANES] = d_key.astype(bf16)
    pg_ref[:, AH * HD + LANES :] = jnp.where(low, d_values[0], d_values[1]).astype(bf16)


def mixer_back_kernel(
    pick_ref, pm_ref, pd_ref, pre_ref, yns_ref, dxb_ref, attend_ref, mask_ref, doc_col_ref,
    doc_row_ref, taps_ref, head_ref, wide_ref,
    pg_ref, small_ref,
    x_s, dx_s, dyb_s, cbt_s, dcbt_s, sum_s, ssum_s,
):
    small_ref[...] = jnp.zeros_like(small_ref)
    pg_ref[:, AT_Q:AT_DT] = attend_ref[...]
    sum_s[...] = jnp.zeros((TOK, LANES), f32)
    ssum_s[...] = jnp.zeros((TOK, LANES), f32)

    def start_tile(index, carry):
        at = tile_at(index)
        pre = pre_ref[:, at].astype(f32)
        heads_in = pre * jax.nn.sigmoid(pre)
        x_s[:, at] = heads_in
        gate = pm_ref[:, at].astype(f32)
        rows = yns_ref[:, at] + wide_ref[0:1, at] * heads_in
        gated = rows * (gate * jax.nn.sigmoid(gate))
        sum_s[...] += gated * gated
        ssum_s[...] += dxb_ref[:, at] * wide_ref[1:2, at] * gated
        return carry

    lax.fori_loop(0, E // LANES, start_tile, 0)
    scale = lax.rsqrt(jnp.sum(sum_s[...], axis=1, keepdims=True) * (1.0 / E) + epsilon)
    pull = jnp.sum(ssum_s[...], axis=1, keepdims=True) * (1.0 / E) * scale * scale * scale

    def gate_tile(index, carry):
        at = tile_at(index)
        heads_in = x_s[:, at]
        skip = wide_ref[0:1, at]
        gate = pm_ref[:, at].astype(f32)
        opened = jax.nn.sigmoid(gate)
        rows = yns_ref[:, at] + skip * heads_in
        gated = rows * (gate * opened)
        arrived = dxb_ref[:, at]
        d_gated = scale * (arrived * wide_ref[1:2, at]) - gated * pull
        small_ref[5:6, at] = jnp.sum(arrived * gated * scale, axis=0, keepdims=True)
        d_rows = d_gated * (gate * opened)
        pg_ref[:, at] = (d_gated * rows * silu_slope(gate, opened)).astype(bf16)
        small_ref[6:7, at] = jnp.sum(d_rows * heads_in, axis=0, keepdims=True)
        dyb_s[:, at] = d_rows.astype(bf16)
        dx_s[:, at] = skip * d_rows
        return carry

    lax.fori_loop(0, E // LANES, gate_tile, 0)

    def state_tile(index, carry):
        at = tile_from(E, index)
        pre = pre_ref[:, at].astype(f32)
        x_s[:, at] = pre * jax.nn.sigmoid(pre)
        return carry

    lax.fori_loop(0, 2, state_tile, 0)

    later = lax.broadcasted_iota(jnp.int32, (TOK, TOK), 1)
    early = lax.broadcasted_iota(jnp.int32, (TOK, TOK), 0)
    allowed_t = (later >= early) & (doc_col_ref[:, 0:1] == doc_row_ref[0:1, :])
    allowed = allowed_pairs(doc_col_ref, doc_row_ref)
    raw = pd_ref[...] + head_ref[0:1, :]
    steps = softplus(raw)
    decay = head_ref[1:2, :]
    rates = -steps * decay
    totals = dot_exact(jnp.where(allowed, 1.0, 0.0), rates)
    totals_t = totals.T
    inward = x_s[:, E : E + NS].astype(bf16)
    outward = x_s[:, E + NS :].astype(bf16)
    cbt_s[...] = jnp.where(allowed_t, dot_nt(inward, outward), 0.0)
    dcbt_s[...] = jnp.zeros((TOK, TOK), f32)
    low = lane_low(TOK)
    spread_row = lax.broadcasted_iota(jnp.int32, (2 * LANES, LANES), 0) // HD
    spread_col = lax.broadcasted_iota(jnp.int32, (2 * LANES, LANES), 1)
    sum_s[...] = jnp.zeros((TOK, LANES), f32)
    ssum_s[...] = jnp.zeros((TOK, LANES), f32)
    waiting = None
    for pair in range(PAIRS):
        lanes = slice(pair * LANES, (pair + 1) * LANES)
        first = 2 * pair
        step_pair = jnp.where(low, steps[:, first : first + 1], steps[:, first + 1 : first + 2])
        heads_in = x_s[:, lanes]
        scaled = (heads_in * step_pair).astype(bf16)
        d_rows = dyb_s[:, lanes]
        d_mix = dot_nt(pair_rows(scaled), d_rows)
        mixes = []
        d_pairs = None
        for side, head in enumerate((first, first + 1)):
            apart = totals_t[head : head + 1, :] - totals[:, head : head + 1]
            decays = jnp.exp(jnp.minimum(apart, 0.0))
            mixes.append((decays * cbt_s[...]).astype(bf16))
            part = d_mix[side * TOK : (side + 1) * TOK] * decays
            d_pairs = part if d_pairs is None else d_pairs + part
        dcbt_s[...] += d_pairs
        d_scaled = pair_lanes(dot_nn(jnp.concatenate(mixes, axis=0), d_rows))
        dx_s[:, lanes] += d_scaled * step_pair
        value = d_rows.astype(f32) * yns_ref[:, lanes] - scaled.astype(f32) * d_scaled
        coarse = value.astype(bf16)
        fine = (value - coarse.astype(f32)).astype(bf16)
        spread = (spread_col == first + (spread_row & 1)).astype(bf16)
        ssum_s[...] += dot_nn(jnp.concatenate([coarse, fine], axis=1), spread)
        value = (d_scaled * heads_in).astype(bf16)
        if pair % 2 == 0:
            waiting = value
        else:
            spread = (spread_col == first - 2 + spread_row).astype(bf16)
            sum_s[...] += dot_nn(jnp.concatenate([waiting, value], axis=1), spread)

    d_rates = dot_exact(jnp.where(allowed_t, 1.0, 0.0), ssum_s[...])
    d_steps = sum_s[...] - decay * d_rates
    d_raw = d_steps * jax.nn.sigmoid(raw)
    pg_ref[:, AT_DT:] = d_raw.astype(bf16)
    small_ref[7:8, :LANES] = jnp.sum(d_raw, axis=0, keepdims=True)
    small_ref[7:8, LANES : 2 * LANES] = jnp.sum(d_rates * rates, axis=0, keepdims=True)
    d_pairs = jnp.where(allowed_t, dcbt_s[...], 0.0).astype(bf16)
    dx_s[:, E : E + NS] = dot_nn(d_pairs, outward)
    dx_s[:, E + NS :] = dot_tn(d_pairs, inward)

    def conv_tile(index, carry):
        at = tile_at(index)
        pre = pre_ref[:, at].astype(f32)
        d_pre = dx_s[:, at] * silu_slope(pre, jax.nn.sigmoid(pre))
        rows = pm_ref[:, tile_from(AT_W, index)].astype(f32)
        small_ref[4:5, at] = jnp.sum(d_pre, axis=0, keepdims=True)
        small_ref[3:4, at] = jnp.sum(d_pre * rows, axis=0, keepdims=True)
        back = taps_ref[3:4, at] * d_pre
        for shift in (1, 2, 3):
            held = mask_ref[:, (shift - 1) * LANES : shift * LANES] * d_pre
            small_ref[3 - shift : 4 - shift, at] = jnp.sum(
                held * pltpu.roll(rows, shift, 0), axis=0, keepdims=True
            )
            back = back + taps_ref[3 - shift : 4 - shift, at] * pltpu.roll(held, TOK - shift, 0)
        pg_ref[:, tile_from(AT_W, index)] = back.astype(bf16)
        return carry

    lax.fori_loop(0, CH // LANES, conv_tile, 0)


def whole_block(shape):
    return pl.BlockSpec(shape, lambda *steps: (0,) * len(shape))


def once(shape, place):
    return pl.BlockSpec(shape, place, pipeline_mode=pl.Buffered(1))


def core_forward(row, projected, layout, params, held=()):
    operands = (*projected, *layout)

    def block(array):
        return once((None,) + array.shape[1:], lambda step: (row, 0, 0))

    outs = [
        jax.ShapeDtypeStruct((MB, TOK, MIXED), bf16),
        jax.ShapeDtypeStruct((MB, TOK, CH), bf16),
        jax.ShapeDtypeStruct((MB, TOK, E), f32),
    ]
    return pl.pallas_call(
        functools.partial(core_forward_kernel, bool(held)),
        grid=(1,),
        in_specs=[block(array) for array in operands]
        + [once(array.shape, lambda step: (0, 0)) for array in params]
        + [pl.BlockSpec(memory_space=pl.ANY)] * len(held),
        out_specs=[block(array) for array in outs],
        out_shape=outs,
        scratch_shapes=[
            pltpu.VMEM((TOK, CH), f32),
            pltpu.VMEM((TOK, TOK), f32),
            pltpu.VMEM((TOK, TOK), f32),
            pltpu.VMEM((TOK, LANES), f32),
        ],
        input_output_aliases={10: 0, 11: 1, 12: 2} if held else {},
        compiler_params=pltpu.CompilerParams(vmem_limit_bytes=12 * MIB),
        cost_estimate=pl.CostEstimate(
            flops=4 * 10**8, bytes_accessed=12 * 2**20, transcendentals=10**6
        ),
        name="core_forward",
    )(*operands, *params, *held)


def core_back_specs(by_row, plain):
    return [
        once((None,) + array.shape[1:], lambda step, pick: (pick[0], 0, 0)) if chosen
        else once(array.shape, lambda step, pick: (0, 0))
        for chosen, arrays in ((True, by_row), (False, plain))
        for array in arrays
    ]


def attend_back(row, projected, d_mixed, layout):
    rope, masks, doc_cols, doc_rows = layout
    return pl.pallas_call(
        attend_back_kernel,
        grid_spec=pltpu.PrefetchScalarGridSpec(
            num_scalar_prefetch=1,
            grid=(1,),
            in_specs=core_back_specs([projected[1]], [d_mixed])
            + core_back_specs([rope, doc_cols, doc_rows], []),
            out_specs=once((TOK, AT_DT - AT_Q), lambda step, pick: (0, 0)),
            scratch_shapes=[pltpu.VMEM((TOK, TOK), f32)],
        ),
        out_shape=jax.ShapeDtypeStruct((TOK, AT_DT - AT_Q), bf16),
        compiler_params=pltpu.CompilerParams(vmem_limit_bytes=6 * MIB),
        cost_estimate=pl.CostEstimate(
            flops=3 * 10**8, bytes_accessed=4 * 2**20, transcendentals=6 * 10**5
        ),
        name="attend_back",
    )(row, projected[1], d_mixed, rope, doc_cols, doc_rows)


def mixer_back(row, projected, pre, yns, d_mixed, attended, layout, params):
    rope, masks, doc_cols, doc_rows = layout
    return pl.pallas_call(
        mixer_back_kernel,
        grid_spec=pltpu.PrefetchScalarGridSpec(
            num_scalar_prefetch=1,
            grid=(1,),
            in_specs=core_back_specs(
                [projected[0], projected[2], pre, yns], [d_mixed, attended]
            )
            + core_back_specs([masks, doc_cols, doc_rows], params),
            out_specs=[
                once((TOK, WIDE_A), lambda step, pick: (0, 0)),
                once((8, CH), lambda step, pick: (0, 0)),
            ],
            scratch_shapes=[
                pltpu.VMEM((TOK, CH), f32),
                pltpu.VMEM((TOK, CH), f32),
                pltpu.VMEM((TOK, E), bf16),
                pltpu.VMEM((TOK, TOK), f32),
                pltpu.VMEM((TOK, TOK), f32),
                pltpu.VMEM((TOK, LANES), f32),
                pltpu.VMEM((TOK, LANES), f32),
            ],
        ),
        out_shape=[
            jax.ShapeDtypeStruct((TOK, WIDE_A), bf16),
            jax.ShapeDtypeStruct((8, CH), f32),
        ],
        compiler_params=pltpu.CompilerParams(vmem_limit_bytes=15 * MIB),
        cost_estimate=pl.CostEstimate(
            flops=7 * 10**8, bytes_accessed=10 * 2**20, transcendentals=15 * 10**5
        ),
        name="mixer_back",
    )(
        row, projected[0], projected[2], pre, yns, d_mixed, attended, masks, doc_cols, doc_rows,
        *params,
    )


def passed_along(value, axis, steps):
    count = lax.axis_size(axis)
    leading, last = (max(0, -steps), min(count, count - steps))
    return lax.ppermute(value, axis, [(source, source + steps) for source in range(leading, last)])


def norm_rows(values):
    return lax.rsqrt(jnp.mean(values * values, axis=-1, keepdims=True) + epsilon)


def norm_back(values, gain, arrived):
    scale = norm_rows(values)
    weighted = arrived * gain
    pull = jnp.mean(weighted * values, axis=-1, keepdims=True) * scale * scale * scale
    gain_grad = jnp.sum(arrived * values * scale, axis=0, keepdims=True)
    return (weighted * scale - values * pull, gain_grad)


def project_kernel(rows_ref, gain_ref, own_ref, other_ref, *refs):
    normed_ref, pm_ref, pq_ref, pd_ref = refs[-4:]
    step = pl.program_id(0)

    @pl.when(step == 0)
    def _():
        rows = rows_ref[...].astype(f32)
        normed_ref[...] = (rows * norm_rows(rows) * gain_ref[...]).astype(bf16)

    out = dot_nn(normed_ref[:, :SIDE], own_ref[...]) + dot_nn(normed_ref[:, SIDE:], other_ref[...])
    tile = WIDE_A // 3
    for index in range(2):
        @pl.when(step == index)
        def _(index=index):
            pm_ref[:, index * tile : (index + 1) * tile] = out.astype(bf16)

    @pl.when(step == 2)
    def _():
        pm_ref[:, 2 * tile :] = out[:, : AT_Q - 2 * tile].astype(bf16)
        pq_ref[...] = out[:, AT_Q - 2 * tile : AT_DT - 2 * tile].astype(bf16)
        pd_ref[...] = out[:, AT_DT - 2 * tile :]


def project(rows, gain, own, other, row=None, held=()):
    count = rows.shape[0]
    tile = WIDE_A // 3
    weight = pl.BlockSpec((SIDE, tile), lambda step: (0, step))
    at = row or 0
    total = count if row is None else MB * TOK
    widths = ((D, bf16), (AT_Q, bf16), (AT_DT - AT_Q, bf16), (LANES, f32))
    return pl.pallas_call(
        project_kernel,
        grid=(3,),
        in_specs=[whole_block((count, D)), whole_block((1, D)), weight, weight]
        + [pl.BlockSpec(memory_space=pl.ANY)] * len(held),
        out_specs=[pl.BlockSpec((count, width), lambda step: (at, 0)) for width, _ in widths],
        out_shape=[jax.ShapeDtypeStruct((total, width), kind) for width, kind in widths],
        input_output_aliases={4 + index: index for index in range(len(held))},
        compiler_params=pltpu.CompilerParams(vmem_limit_bytes=15 * MIB),
        cost_estimate=pl.CostEstimate(
            flops=2 * count * D * WIDE_A,
            bytes_accessed=2 * D * WIDE_A + 2 * count * WIDE_A,
            transcendentals=0,
        ),
        name="project",
    )(rows, gain, own, other, *held)


def by_row(projected):
    return tuple(array.reshape(MB, TOK, -1) for array in projected[1:])


def feed_forward_kernel(
    keep, rows_ref, mixed_ref, gain_ref,
    out_own, out_other, gate_own, gate_other, up_own, up_other, down_own, down_other,
    *refs,
):
    if keep:
        low_ref, middle_ref, normed_ref, gate_ref, up_ref, act_ref, total_s = refs[-7:]
    else:
        low_ref, middle_ref, normed_ref, total_s = refs
    step = pl.program_id(0)

    @pl.when(step == 0)
    def _():
        middle_ref[...] = rows_ref[...].astype(f32)

    @pl.when(step < 4)
    def _():
        mixed = mixed_ref[...]
        middle_ref[:, :SIDE] += dot_nt(mixed, out_own[...])
        middle_ref[:, SIDE:] += dot_nt(mixed, out_other[...])

    @pl.when(step == 3)
    def _():
        middle = middle_ref[...]
        normed_ref[...] = (middle * norm_rows(middle) * gain_ref[...]).astype(bf16)
        total_s[...] = middle

    @pl.when(step >= 4)
    def _():
        left = normed_ref[:, :SIDE]
        right = normed_ref[:, SIDE:]
        gate = dot_nn(left, gate_own[...]) + dot_nn(right, gate_other[...])
        up = dot_nn(left, up_own[...]) + dot_nn(right, up_other[...])
        act = (gate * jax.nn.sigmoid(gate) * up).astype(bf16)
        if keep:
            gate_ref[...] = gate.astype(bf16)
            up_ref[...] = up.astype(bf16)
            act_ref[...] = act
        total_s[:, :SIDE] += dot_nt(act, down_own[...])
        total_s[:, SIDE:] += dot_nt(act, down_other[...])

    @pl.when(step == 7)
    def _():
        low_ref[...] = total_s[...].astype(bf16)


def b_block(start, skipped):
    return pl.BlockSpec(
        (None, SIDE, BLOCK), lambda step, *pick: (start + jnp.clip(step - skipped, 0, 3), 0, 0)
    )


def b_blocks(parts):
    return [b_block(start, skipped) for start, skipped in parts for _ in range(2)]


def feed_forward(row, rows, mixed, gain, own, other, held=None):
    keep = held is not None
    at = row if rows.shape[0] > TOK else 0

    def late(step):
        return (row, jnp.clip(step - 4, 0, 3))

    wide = pl.BlockSpec((TOK, 512), late)
    full = pl.BlockSpec((TOK, D), lambda step: (row, 0))
    scratch = [pltpu.VMEM((TOK, D), f32)]
    if keep:
        out_specs = [full, full, full, wide, wide, wide]
        out_shape = [
            jax.ShapeDtypeStruct((MB * TOK, width), kind)
            for width, kind in ((D, bf16), (D, f32), (D, bf16), (FF, bf16), (FF, bf16), (FF, bf16))
        ]
    else:
        out_specs = [whole_block((TOK, D))]
        out_shape = [jax.ShapeDtypeStruct((TOK, D), bf16)]
        scratch = [pltpu.VMEM((TOK, D), f32), pltpu.VMEM((TOK, D), bf16)] + scratch
    held = tuple(held or ())
    return pl.pallas_call(
        functools.partial(feed_forward_kernel, keep),
        grid=(8,),
        in_specs=[
            pl.BlockSpec((TOK, D), lambda step: (at, 0)),
            pl.BlockSpec((TOK, 512), lambda step: (row, jnp.clip(step, 0, 3))),
            whole_block((1, D)),
        ]
        + b_blocks(((0, 0), (4, 4), (8, 4), (12, 4)))
        + [pl.BlockSpec(memory_space=pl.ANY)] * len(held),
        out_specs=out_specs,
        out_shape=out_shape,
        scratch_shapes=scratch,
        input_output_aliases={11 + index: index for index in range(len(held))},
        compiler_params=pltpu.CompilerParams(vmem_limit_bytes=(46 if keep else 18) * MIB),
        cost_estimate=pl.CostEstimate(
            flops=2 * TOK * D * WIDE_B, bytes_accessed=2 * D * WIDE_B, transcendentals=0
        ),
        name="feed_forward",
    )(rows, mixed, gain, *([own, other] * 4), *held)


def feed_back_kernel(
    pick_ref, cot_ref, gate_ref, up_ref, middle_ref, gain_ref,
    down_own, down_other, gate_own, gate_other, up_own, up_other, out_own, out_other,
    d_gate_ref, d_up_ref, d_middle_ref, low_ref, d_mixed_ref, gain_grad_ref,
    total_s,
):
    step = pl.program_id(0)

    @pl.when(step == 0)
    def _():
        total_s[...] = jnp.zeros_like(total_s)

    @pl.when(step < 4)
    def _():
        arrived = dot_nn(cot_ref[:, :SIDE], down_own[...]) + dot_nn(
            cot_ref[:, SIDE:], down_other[...]
        )
        gate = gate_ref[...].astype(f32)
        opened = jax.nn.sigmoid(gate)
        d_gate = (arrived * up_ref[...].astype(f32) * silu_slope(gate, opened)).astype(bf16)
        d_up = (arrived * (gate * opened)).astype(bf16)
        d_gate_ref[...] = d_gate
        d_up_ref[...] = d_up
        total_s[:, :SIDE] += dot_nt(d_gate, gate_own[...]) + dot_nt(d_up, up_own[...])
        total_s[:, SIDE:] += dot_nt(d_gate, gate_other[...]) + dot_nt(d_up, up_other[...])

    @pl.when(step == 3)
    def _():
        d_norm, gain_grad = norm_back(middle_ref[...], gain_ref[...], total_s[...])
        d_middle = cot_ref[...].astype(f32) + d_norm
        d_middle_ref[...] = d_middle
        low_ref[...] = d_middle.astype(bf16)
        gain_grad_ref[...] = gain_grad

    @pl.when(step >= 4)
    def _():
        d_mixed_ref[...] = dot_nn(low_ref[:, :SIDE], out_own[...]) + dot_nn(
            low_ref[:, SIDE:], out_other[...]
        )


def feed_back(row, cotangent, gate, up, middle, gain, own, other):
    saved = pl.BlockSpec((TOK, 512), lambda step, pick: (pick[0], jnp.clip(step, 0, 3)))
    early = pl.BlockSpec((TOK, 512), lambda step, pick: (0, jnp.clip(step, 0, 3)))
    late = pl.BlockSpec((TOK, 512), lambda step, pick: (0, jnp.clip(step - 4, 0, 3)))
    full = pl.BlockSpec((TOK, D), lambda step, pick: (0, 0))
    gain_block = pl.BlockSpec((1, D), lambda step, pick: (0, 0))
    return pl.pallas_call(
        feed_back_kernel,
        grid_spec=pltpu.PrefetchScalarGridSpec(
            num_scalar_prefetch=1,
            grid=(8,),
            in_specs=[
                full,
                saved,
                saved,
                pl.BlockSpec((TOK, D), lambda step, pick: (pick[0], 0)),
                gain_block,
            ]
            + b_blocks(((12, 0), (4, 0), (8, 0), (0, 4))),
            out_specs=[early, early, full, full, late, gain_block],
            scratch_shapes=[pltpu.VMEM((TOK, D), f32)],
        ),
        out_shape=[
            jax.ShapeDtypeStruct((TOK, FF), bf16),
            jax.ShapeDtypeStruct((TOK, FF), bf16),
            jax.ShapeDtypeStruct((TOK, D), f32),
            jax.ShapeDtypeStruct((TOK, D), bf16),
            jax.ShapeDtypeStruct((TOK, MIXED), f32),
            jax.ShapeDtypeStruct((1, D), f32),
        ],
        compiler_params=pltpu.CompilerParams(vmem_limit_bytes=46 * MIB),
        cost_estimate=pl.CostEstimate(
            flops=2 * TOK * D * WIDE_B, bytes_accessed=2 * D * WIDE_B, transcendentals=0
        ),
        name="feed_back",
    )(row, cotangent, gate, up, middle, gain, *([own, other] * 4))


def project_back_kernel(
    pick_ref, grad_ref, rows_ref, d_middle_ref, gain_ref, own_ref, other_ref,
    d_rows_ref, low_ref, gain_grad_ref, total_s,
):
    step = pl.program_id(0)

    @pl.when(step == 0)
    def _():
        total_s[...] = jnp.zeros_like(total_s)

    total_s[:, :SIDE] += dot_nt(grad_ref[...], own_ref[...])
    total_s[:, SIDE:] += dot_nt(grad_ref[...], other_ref[...])

    @pl.when(step == 2)
    def _():
        d_norm, gain_grad = norm_back(rows_ref[...].astype(f32), gain_ref[...], total_s[...])
        d_rows = d_middle_ref[...] + d_norm
        d_rows_ref[...] = d_rows
        low_ref[...] = d_rows.astype(bf16)
        gain_grad_ref[...] = gain_grad


def project_back(row, proj_low, start_rows, d_middle, gain, own, other):
    tile = WIDE_A // 3
    weight = pl.BlockSpec((SIDE, tile), lambda step, pick: (0, step))
    full = pl.BlockSpec((TOK, D), lambda step, pick: (0, 0))
    gain_block = pl.BlockSpec((1, D), lambda step, pick: (0, 0))
    return pl.pallas_call(
        project_back_kernel,
        grid_spec=pltpu.PrefetchScalarGridSpec(
            num_scalar_prefetch=1,
            grid=(3,),
            in_specs=[
                pl.BlockSpec((TOK, tile), lambda step, pick: (0, step)),
                pl.BlockSpec((TOK, D), lambda step, pick: (pick[0], 0)),
                full,
                gain_block,
                weight,
                weight,
            ],
            out_specs=[full, full, gain_block],
            scratch_shapes=[pltpu.VMEM((TOK, D), f32)],
        ),
        out_shape=[
            jax.ShapeDtypeStruct((TOK, D), f32),
            jax.ShapeDtypeStruct((TOK, D), bf16),
            jax.ShapeDtypeStruct((1, D), f32),
        ],
        compiler_params=pltpu.CompilerParams(vmem_limit_bytes=15 * MIB),
        cost_estimate=pl.CostEstimate(
            flops=2 * TOK * D * WIDE_A, bytes_accessed=2 * D * WIDE_A, transcendentals=0
        ),
        name="project_back",
    )(row, proj_low, start_rows, d_middle, gain, own, other)


def weight_grad_kernel(groups, pick_ref, *refs):
    lefts = refs[: 4 * len(groups)]
    rights = refs[4 * len(groups) : 8 * len(groups)]
    sum_ref, left_s = refs[8 * len(groups) :]
    step = pl.program_id(0)
    for index, (start, count) in enumerate(groups):
        four = lefts[4 * index : 4 * index + 4]
        blocks = rights[4 * index : 4 * index + 4]

        @pl.when(step == start)
        def _(four=four):
            for place, ref in enumerate(four):
                left_s[:, place * TOK : (place + 1) * TOK] = ref[...].astype(f32).T.astype(bf16)

        @pl.when((step >= start) & (step < start + count))
        def _(blocks=blocks):
            right = jnp.concatenate([ref[...] for ref in blocks], axis=0)
            sum_ref[...] = dot_nn(left_s[...], right).astype(bf16)


def weight_grad(picks, tile, groups):
    steps = []
    in_left = []
    in_right = []
    operands_left = []
    operands_right = []
    start = 0
    for left, right in groups:
        count = right[0][0].shape[1] // tile
        steps.append((start, count))
        for array, which, column in left:
            in_left.append(
                pl.BlockSpec(
                    (TOK, SIDE),
                    lambda step, pick, which=which, column=column: (
                        0 if which is None else pick[which],
                        column,
                    ),
                )
            )
            operands_left.append(array)
        for array, which in right:
            in_right.append(
                pl.BlockSpec(
                    (TOK, tile),
                    lambda step, pick, which=which, start=start, count=count: (
                        0 if which is None else pick[which],
                        jnp.clip(step - start, 0, count - 1),
                    ),
                )
            )
            operands_right.append(array)
        start += count
    return pl.pallas_call(
        functools.partial(weight_grad_kernel, tuple(steps)),
        grid_spec=pltpu.PrefetchScalarGridSpec(
            num_scalar_prefetch=1,
            grid=(start,),
            in_specs=in_left + in_right,
            out_specs=pl.BlockSpec((SIDE, tile), lambda step, pick: (0, step)),
            scratch_shapes=[pltpu.VMEM((SIDE, 4 * TOK), bf16)],
        ),
        out_shape=jax.ShapeDtypeStruct((SIDE, start * tile), bf16),
        compiler_params=pltpu.CompilerParams(vmem_limit_bytes=16 * MIB),
        cost_estimate=pl.CostEstimate(
            flops=8 * TOK * SIDE * start * tile,
            bytes_accessed=4 * SIDE * start * tile,
            transcendentals=0,
        ),
        name="weight_grad",
    )(picks, *operands_left, *operands_right)


def row_layout(doc_ids):
    rows = doc_ids.shape[0]
    positions = jnp.arange(TOK, dtype=jnp.int32)
    earlier = jnp.sum((doc_ids[:, None, :] < doc_ids[:, :, None]).astype(jnp.int32), axis=2)
    places = positions[None, :] - earlier
    half_dim = HD // 2
    inverse_freq = rope_base ** (-jnp.arange(half_dim, dtype=f32) / half_dim)
    angles = places.astype(f32)[:, :, None] * inverse_freq[None, None, :]
    repeats = LANES // half_dim
    rope = jnp.concatenate([jnp.cos(angles)] * repeats + [jnp.sin(angles)] * repeats, axis=-1)
    masks = jnp.concatenate(
        [
            jnp.broadcast_to((places >= shift).astype(f32)[:, :, None], (rows, TOK, LANES))
            for shift in (1, 2, 3)
        ],
        axis=-1,
    )
    doc_cols = jnp.broadcast_to(doc_ids[:, :, None], (rows, TOK, LANES))
    doc_rows = jnp.broadcast_to(doc_ids[:, None, :], (rows, 8, TOK))
    return (rope, masks, doc_cols, doc_rows)


def core_params(conv_weight, conv_bias, step_bias, decay_log, skip_scale, mixer_gain):
    taps = jnp.concatenate([conv_weight, conv_bias[None], jnp.zeros((3, CH), f32)], axis=0)
    heads = jnp.zeros((8, LANES), f32)
    heads = heads.at[0, :MH].set(step_bias).at[1, :MH].set(jnp.exp(decay_log))
    wide = jnp.concatenate(
        [jnp.repeat(skip_scale, MP)[None], mixer_gain[None], jnp.zeros((6, E), f32)], axis=0
    )
    return (taps, heads, wide)


def swapped(value):
    return lax.ppermute(value, "core", [(0, 1), (1, 0)])


def ring_order(chips):
    return [2 * step for step in range(chips // 2)] + [
        2 * step + 1 for step in reversed(range(chips // 2))
    ]


def ring_place(chip, chips):
    return jnp.where(chip % 2 == 0, chip // 2, chips - 1 - chip // 2)


def onward(value, steps):
    order = ring_order(lax.axis_size("chip"))
    chips = len(order)
    return lax.ppermute(
        value, "chip", [(order[at], order[(at + steps) % chips]) for at in range(chips)]
    )


def slot_offsets(chips):
    offsets = [0]
    for far in range(1, chips // 2):
        offsets += [-far, far]
    return offsets + [chips // 2]


def tied(*values):
    return lax.optimization_barrier(values)


class RingGather:
    def __init__(self, shard, axis=0):
        self.axis = axis
        self.half = shard.shape[axis] // 2
        self.steps = []
        self.shard = self.ahead = self.back = shard
        self.left = lax.axis_size("chip") // 2

    def operands(self):
        if self.left == 1:
            return (
                lax.slice_in_dim(self.ahead, 0, self.half, axis=self.axis),
                lax.slice_in_dim(self.back, self.half, 2 * self.half, axis=self.axis),
            )
        return self.ahead, self.back

    def send(self, ahead, back):
        self.ahead, self.back = tied(onward(ahead, 1), onward(back, -1))
        self.steps.append((self.ahead, self.back))
        self.left -= 1

    def step(self):
        self.send(*self.operands())

    def hold(self, value):
        self.ahead, self.back, _ = tied(self.ahead, self.back, value)
        self.steps[-1] = (self.ahead, self.back)

    def own(self):
        parts = [self.shard] + [one for step in self.steps for one in step]
        return jnp.concatenate(parts, axis=self.axis)

    def other(self):
        parts = [self.shard] + [one for step in self.steps for one in step]
        return jnp.concatenate([swapped(part) for part in parts], axis=self.axis)


class RingReduce:
    def __init__(self, sums):
        self.sums = sums
        self.chips = lax.axis_size("chip")
        self.size = sums.shape[0] // self.chips
        self.left = self.chips // 2
        self.ahead = self.back = None

    def slot(self, index, start=0, stop=None):
        stop = self.size if stop is None else stop
        return self.sums[index * self.size + start : index * self.size + stop]

    def operands(self):
        half = self.size // 2
        if self.ahead is None:
            last = self.chips - 1
            return self.slot(last, 0, half), self.slot(last, half)
        ahead, back = self.ahead.astype(f32), self.back.astype(f32)
        if self.left == self.chips // 2 - 1:
            ahead = jnp.pad(ahead, ((0, half), (0, 0)))
            back = jnp.pad(back, ((half, 0), (0, 0)))
        return (
            (self.slot(2 * self.left).astype(f32) + ahead).astype(bf16),
            (self.slot(2 * self.left - 1).astype(f32) + back).astype(bf16),
        )

    def send(self, ahead, back):
        self.ahead, self.back = tied(onward(ahead, 1), onward(back, -1))
        self.left -= 1
        return self.ahead

    def step(self):
        return self.send(*self.operands())

    def hold(self, value):
        self.ahead, self.back, _ = tied(self.ahead, self.back, value)

    def columns(self, start, stop):
        part = RingReduce(self.sums[:, start:stop])
        part.left = self.left
        part.ahead, part.back = self.ahead[:, start:stop], self.back[:, start:stop]
        return part

    def total(self):
        while self.left > 0:
            self.step()
        return self.slot(0).astype(f32) + self.ahead.astype(f32) + self.back.astype(f32)


def small_hops(chips):
    if chips & (chips - 1):
        return [lambda value: lax.psum(value, ("chip", "core")) - value]
    hops = [swapped]
    for bit in range(chips.bit_length() - 1):
        pairs = [(chip, chip ^ (1 << bit)) for chip in range(chips)]
        hops.append(lambda value, pairs=pairs: lax.ppermute(value, "chip", pairs))
    return hops


def ring_columns(core):
    chips = lax.axis_size("chip")
    place = ring_place(lax.axis_index("chip"), chips)
    own = []
    for offset in slot_offsets(chips):
        at = (place + offset) % chips
        own.append(jnp.where(at < chips // 2, 2 * at, 2 * (chips - 1 - at) + 1))
    own = jnp.stack(own)
    width = D // (2 * chips)
    starts = jnp.concatenate([2 * own + core, 2 * own + 1 - core]) * width
    wanted = (starts[:, None] + jnp.arange(width)[None, :]).reshape(D)
    return (jnp.arange(D)[:, None] == wanted[None, :]).astype(bf16)


def per_device(
    inputs, out_grad, doc_ids, row_live, pre_gain, mlp_gain, mixer_gain, conv_weight, conv_bias,
    step_bias, decay_log, skip_scale, mixer_in_weight, mixer_out_weight, query_weight, key_weight,
    value_weight, attend_weight, gate_up_weight, down_weight,
):
    is_first = lax.axis_index("section") == 0
    core = lax.axis_index("core")
    shard = mixer_in_weight.shape[1]
    packed_a = jnp.concatenate(
        [
            mixer_in_weight[0, :, :AT_Q],
            query_weight[0],
            key_weight[0],
            value_weight[0],
            mixer_in_weight[0, :, AT_Q:],
            jnp.zeros((shard, LANES - MH), bf16),
        ],
        axis=1,
    )
    packed_b = jnp.concatenate(
        [mixer_out_weight[0].T, attend_weight[0].T, gate_up_weight[0], down_weight[0].T], axis=1
    )
    packed_b = packed_b.reshape(shard, WIDE_B // BLOCK, BLOCK).swapaxes(0, 1)

    layout = row_layout(doc_ids)
    params = core_params(
        conv_weight[0], conv_bias[0], step_bias[0], decay_log[0], skip_scale[0], mixer_gain[0]
    )
    turn = ring_columns(core)

    def own_order(values):
        if values.dtype == bf16:
            return dot_nn(values, turn).astype(bf16)
        return dot_exact(values, turn.astype(f32))

    def whole_order(values):
        if values.dtype == bf16:
            return dot_nt(values, turn).astype(bf16)
        return dot_exact(values, turn.astype(f32).T)

    pre_row = own_order(pre_gain)
    mlp_row = own_order(mlp_gain)
    first_rows = own_order(inputs)

    positions = jnp.arange(TOK, dtype=jnp.int32)
    live = (positions[None, :] < row_live[:, None]).reshape(MB * TOK, 1)
    from_loss = own_order(jnp.where(live, out_grad, jnp.zeros_like(out_grad)))
    first_rows, from_loss = tied(first_rows, from_loss)

    ring_a = RingGather(packed_a)
    ring_b = RingGather(packed_b, 1)
    ring_b.step()
    ring_a.step()
    ring_a.hold((first_rows, from_loss, layout, params, pre_row, mlp_row))
    while ring_a.left > 1:
        ring_a.step()
    now_b, now_a = tied(ring_b.operands(), ring_a.operands())
    ring_b.send(*now_b)
    ring_a.send(*now_a)
    own_a = ring_a.own()
    pair_a = (own_a, swapped(own_a))
    now_b, gain_now, pair_a = tied(ring_b.operands(), pre_row, pair_a)
    ring_b.send(*now_b)
    projected = by_row(project(first_rows, gain_now, *pair_a))
    mixed = core_forward(0, projected, layout, params)
    ring_b.hold(mixed)
    now_b, mixed = tied(ring_b.operands(), mixed)
    ring_b.send(*now_b)
    mixed, _, _ = core_forward(1, projected, layout, params, held=mixed)
    ring_b.hold(mixed)
    while ring_b.left:
        ring_b.step()
    pair_b = (ring_b.own(), ring_b.other())
    mixed = mixed.reshape(MB * TOK, MIXED)

    received = {}
    for row in (1, 0):
        (handed,) = feed_forward(row, first_rows, mixed, mlp_row, *pair_b)
        received[row] = passed_along(handed, "section", 1)

    def second_pass(row, projects=(), cores=(), forwards=()):
        start = jnp.where(is_first, first_rows[row * TOK : (row + 1) * TOK], received[row])
        projects = project(start, pre_row, *pair_a, row=row, held=projects)
        cores = core_forward(row, by_row(projects), layout, params, held=cores)
        mixed = cores[0].reshape(MB * TOK, MIXED)
        forwards = feed_forward(row, start, mixed, mlp_row, *pair_b, held=forwards)
        return start, projects, cores, forwards

    arrived = jnp.zeros((TOK, D), bf16)
    lefts = []
    rights = []
    rows = []
    picks = jnp.where(is_first, jnp.array([1, 0]), jnp.array([0, 1])).astype(jnp.int32)

    def tick_left(which):
        return [(lefts[1][which], None, 0), (lefts[2][which], None, 0)] + [
            (lefts[1][which + 2], None, 0), (lefts[2][which + 2], None, 0)
        ]

    def tick_right(which):
        return [(rights[tick][which + far], None) for far in (0, 2) for tick in (1, 2)]

    def saved_left(own, their):
        return [(own, 0, 0), (own, 1, 0), (their, 0, 0), (their, 1, 0)]

    def saved_right(own, their):
        return [(own, 0), (own, 1), (their, 0), (their, 1)]

    start, projects, cores, forwards = second_pass(1)
    starts = {1: start}
    start_rows = jnp.concatenate([start, start], axis=0)
    for tick in range(3):
        if tick == 1:
            (projects, cores, forwards), received[0], _ = tied(
                (projects, cores, forwards), received[0], d_low
            )
            starts[0], projects, cores, forwards = second_pass(0, projects, cores, forwards)
            start_rows = jnp.concatenate([starts[0], starts[1]], axis=0)
            arrived, forwards = tied(arrived, forwards)
        normed, projected = projects[0], by_row(projects)
        mixed, pre, yns = cores[0].reshape(MB * TOK, MIXED), cores[1], cores[2]
        result, middle, normed_two, gate, up, act = forwards
        row = jnp.where(is_first, (1, 1, 0)[tick], (1, 0, 1)[tick]).astype(jnp.int32).reshape(1)
        if tick == 2:
            row, lefts[1], rights[1], rows[1] = tied(row, lefts[1], rights[1], rows[1])
        loss_row = (1, 0, 1)[tick]
        cotangent = jnp.where(
            is_first, arrived, from_loss[loss_row * TOK : (loss_row + 1) * TOK]
        )
        if tick == 1:
            cotangent, swaps = tied(
                cotangent, (mixed, act, normed[:, SIDE:], normed_two[:, SIDE:])
            )
            their_mixed, their_act, their_normed, their_normed_two = map(swapped, swaps)
        d_gate, d_up, d_middle, middle_low, d_mixed, mlp_grad = feed_back(
            row, cotangent, gate, up, middle, mlp_row, *pair_b
        )
        lefts.append(
            (cotangent, middle_low, swapped(cotangent[:, SIDE:]), swapped(middle_low[:, SIDE:]))
        )
        rights.append((d_gate, d_up, swapped(d_gate), swapped(d_up)))
        if tick < 2:
            attended = attend_back(row, projected, d_mixed, layout)
            if tick == 1:
                row, their_mixed, their_act, their_normed, their_normed_two = tied(
                    row, their_mixed, their_act, their_normed, their_normed_two
                )
            proj_low, small = mixer_back(
                row, projected, pre, yns, d_mixed, attended, layout, params
            )
            their_low = swapped(proj_low)
        else:
            sum_c = weight_grad(
                picks,
                1024,
                [
                    (tick_left(1), saved_right(mixed, their_mixed)),
                    (tick_left(0), saved_right(act, their_act)),
                ],
            )
            ring_c = RingReduce(sum_c)
            now_c, row = tied(ring_c.operands(), row)
            ring_c.send(*now_c)
            attended = attend_back(row, projected, d_mixed, layout)
            ring_c.hold(attended)
            picks_now, now_c, rights[2] = tied(picks, ring_c.operands(), rights[2])
            ring_c.send(*now_c)
            sum_b = weight_grad(
                picks_now,
                1024,
                [
                    (saved_left(normed_two, their_normed_two), tick_right(0)),
                    (saved_left(normed_two, their_normed_two), tick_right(1)),
                ],
            )
            ring_b = RingReduce(sum_b)
            ring_c.hold(sum_b)
            now_b, now_c, row, attended = tied(
                ring_b.operands(), ring_c.operands(), row, attended
            )
            ring_c.send(*now_c)
            ring_b.send(*now_b)
            proj_low, small = mixer_back(
                row, projected, pre, yns, d_mixed, attended, layout, params
            )
            proj_low, ring_b.ahead, ring_b.back, ring_c.ahead, ring_c.back = tied(
                proj_low, ring_b.ahead, ring_b.back, ring_c.ahead, ring_c.back
            )
            their_low = swapped(proj_low)
            now_b, row = tied(ring_b.operands(), row)
            ring_b.send(*now_b)
            d_rows, d_low, pre_grad = project_back(
                row, proj_low, start_rows, d_middle, pre_row, *pair_a
            )
            now_c, their_low, d_rows, pre_grad = tied(
                ring_c.operands(), their_low, d_rows, pre_grad
            )
            ring_c.send(*now_c)
            picks_now, now_c = tied(picks, now_c)
            (p_one, their_one), (p_two, their_two) = rows[1][1], (proj_low, their_low)
            sum_a = weight_grad(
                picks_now,
                WIDE_A // 3,
                [
                    (
                        saved_left(normed, their_normed),
                        [(p_one, None), (p_two, None), (their_one, None), (their_two, None)],
                    )
                ],
            )
            ring_b.hold(sum_a)
            ring_a = RingReduce(sum_a)
            ring_c.hold(sum_a)
            now_a, now_b, ring_c.ahead, ring_c.back = tied(
                ring_a.operands(), ring_b.operands(), ring_c.ahead, ring_c.back
            )
            ring_b.send(*now_b)
            ring_a.send(*now_a)
        if tick < 2:
            d_rows, d_low, pre_grad = project_back(
                row, proj_low, start_rows, d_middle, pre_row, *pair_a
            )
        rows.append((d_rows, (proj_low, their_low), pre_grad, mlp_grad, small))
        if tick < 2:
            arrived = passed_along(d_low, "section", -1)

    pre_sum, mlp_sum, small = (one + two for one, two in zip(rows[1][2:], rows[2][2:]))
    gain_sums = whole_order(jnp.concatenate([pre_sum, mlp_sum], axis=0))
    small = jnp.concatenate([small, jnp.pad(gain_sums, ((0, 6), (0, CH - D)))], axis=0)

    hops = small_hops(lax.axis_size("chip"))

    def hop_beside(small, ring):
        if not hops:
            return small
        small, moved, _ = tied(small, hops.pop(0)(small), ring.ahead)
        return small + moved

    small = hop_beside(small, ring_a)
    ring_b.step()
    ring_a.step()
    small = hop_beside(small, ring_a)
    while ring_a.left > 2:
        ring_a.step()
    d_last = tied(rows[2][0], ring_a.ahead)[0]
    rings_a = [ring_a.columns(0, CUT_A), ring_a.columns(CUT_A, WIDE_A)]
    while rings_a[0].left:
        for ring in rings_a:
            ring.step()
        small = hop_beside(small, rings_a[0])
    for hop in hops:
        small = small + hop(small)
    share_c = ring_c.total()
    share_b = ring_b.total()
    share_a = jnp.concatenate([ring.total() for ring in rings_a], axis=1)

    start_grad = jnp.concatenate(
        [
            jnp.where(is_first, d_last, rows[1][0]),
            jnp.where(is_first, rows[1][0], d_last),
        ],
        axis=0,
    )
    skip_sum = jnp.sum(small[6, :E].reshape(MH, MP), axis=1)
    mixer_in_grad = jnp.concatenate([share_a[:, :AT_Q], share_a[:, AT_DT : AT_DT + MH]], axis=1)
    return (
        whole_order(result)[None],
        whole_order(start_grad)[None],
        small[8:9, :D],
        small[9:10, :D],
        small[5:6, :E],
        small[None, :4],
        small[4:5],
        small[7:8, :MH],
        small[7:8, LANES : LANES + MH],
        skip_sum[None],
        mixer_in_grad[None],
        share_c[:, :E].T[None],
        share_a[:, AT_Q:AT_K][None],
        share_a[:, AT_K:AT_V][None],
        share_a[:, AT_V:AT_DT][None],
        share_c[:, E:MIXED].T[None],
        share_b[None],
        share_c[:, MIXED:].T[None],
    )


def solution(mesh):
    dp = mesh.shape["dp"]
    devices = mesh.devices.reshape(mesh.shape["section"], dp // 2, 2)
    paired = Mesh(devices, ("section", "chip", "core"))
    over = ("chip", "core")
    rows = P(over, None)
    small = P("section", None)
    by_row = P("section", over, None)
    by_col = P("section", None, over)
    small_specs = (small, small, small, P("section", None, None), small, small, small, small)
    big_specs = (by_row, by_col, by_row, by_row, by_row, by_col, by_row, by_col)
    in_specs = (rows, rows, rows, P(over)) + small_specs + big_specs
    out_specs = (by_row, by_row) + small_specs + big_specs
    return jax.shard_map(
        per_device, mesh=paired, in_specs=in_specs, out_specs=out_specs, check_vma=False
    )
```

```python
import functools
import math

import jax
import jax.numpy as jnp
from jax import lax
from jax.experimental import pallas as pl
from jax.experimental.pallas import tpu as pltpu
from jax.sharding import Mesh
from jax.sharding import PartitionSpec as P

D = 1024
FF = 2048
MH = 24
MP = 64
NS = 128
AH = 8
KVH = 2
HD = 64
MB = 2
TOK = 256
E = 1536
CH = 1792
HALF = TOK // 2
PAIRS = MH // 2
LANES = 128
SIDE = D // 2
MIB = 2**20
FF_VMEM = 22
FB_VMEM = 20

AT_W = E
AT_Q = E + CH
AT_K = AT_Q + AH * HD
AT_V = AT_K + KVH * HD
AT_DT = AT_V + KVH * HD
WIDE_A = AT_DT + LANES
CUT_A = 16 * LANES
MIXED = E + AH * HD
AT_GU = MIXED
AT_DN = AT_GU + 2 * FF
WIDE_B = AT_DN + FF

highest = lax.Precision.HIGHEST
epsilon = 1e-05
rope_base = 100000000000.0
bf16 = jnp.bfloat16
f32 = jnp.float32


def dot_nn(left, right):
    return lax.dot_general(left, right, (((1,), (0,)), ((), ())), preferred_element_type=f32)


def dot_nt(left, right):
    return lax.dot_general(left, right, (((1,), (1,)), ((), ())), preferred_element_type=f32)


def dot_tn(left, right):
    return lax.dot_general(left, right, (((0,), (0,)), ((), ())), preferred_element_type=f32)


def dot_exact(left, right):
    return lax.dot_general(
        left, right, (((1,), (0,)), ((), ())), precision=highest, preferred_element_type=f32
    )


def softplus(value):
    return jnp.maximum(value, 0.0) + jnp.log1p(jnp.exp(-jnp.abs(value)))


def lane_low(rows):
    return lax.broadcasted_iota(jnp.int32, (rows, LANES), 1) < HD


def rope_halves(rows):
    return (lax.broadcasted_iota(jnp.int32, (rows, LANES), 1) & (HD - 1)) < HD // 2


def rope_turn(tile, cosine, sine):
    swapped = jnp.where(
        rope_halves(tile.shape[0]),
        -pltpu.roll(tile, LANES - HD // 2, 1),
        pltpu.roll(tile, HD // 2, 1),
    )
    return tile * cosine + swapped * sine


def rope_back(tile, cosine, sine):
    swapped = jnp.where(
        rope_halves(tile.shape[0]),
        pltpu.roll(tile, LANES - HD // 2, 1),
        -pltpu.roll(tile, HD // 2, 1),
    )
    return tile * cosine + swapped * sine


def both_halves(tile):
    swapped = pltpu.roll(tile, HD, 1)
    low = lane_low(tile.shape[0])
    return (jnp.where(low, tile, swapped), jnp.where(low, swapped, tile))


def tile_at(index):
    return pl.ds(pl.multiple_of(index * LANES, LANES), LANES)


def tile_from(start, index):
    return pl.ds(pl.multiple_of(start + index * LANES, LANES), LANES)


def allowed_pairs(doc_col_ref, doc_row_ref):
    later = lax.broadcasted_iota(jnp.int32, (TOK, TOK), 0)
    early = lax.broadcasted_iota(jnp.int32, (TOK, TOK), 1)
    same = doc_col_ref[:, 0:1] == doc_row_ref[0:1, :]
    return (later >= early) & same


def pair_rows(tile):
    low = lane_low(tile.shape[0])
    zero = jnp.zeros_like(tile)
    return jnp.concatenate([jnp.where(low, tile, zero), jnp.where(low, zero, tile)], axis=0)


def pair_lanes(rows):
    half = rows.shape[0] // 2
    return jnp.where(lane_low(half), rows[:half], rows[half:])


def core_forward_kernel(
    held, pm_ref, pq_ref, pd_ref, rope_ref, mask_ref, doc_col_ref, doc_row_ref,
    taps_ref, head_ref, wide_ref, *refs,
):
    xb_ref, pre_ref, yns_ref, conv_s, cb_s, bias_s, sum_s = refs[3:] if held else refs

    def conv_tile(index, carry):
        rows = pm_ref[:, tile_from(AT_W, index)].astype(f32)
        at = tile_at(index)
        total = taps_ref[4:5, at] + taps_ref[3:4, at] * rows
        for shift in (1, 2, 3):
            moved = mask_ref[:, (shift - 1) * LANES : shift * LANES] * pltpu.roll(rows, shift, 0)
            total = total + taps_ref[3 - shift : 4 - shift, at] * moved
        total = total.astype(bf16)
        pre_ref[:, at] = total
        total = total.astype(f32)
        conv_s[:, at] = total * jax.nn.sigmoid(total)
        return carry

    lax.fori_loop(0, CH // LANES, conv_tile, 0)

    allowed = allowed_pairs(doc_col_ref, doc_row_ref)
    bias_s[...] = jnp.where(allowed, 0.0, -1e30)
    steps = softplus(pd_ref[...] + head_ref[0:1, :])
    rates = -steps * head_ref[1:2, :]
    totals = dot_exact(jnp.where(allowed, 1.0, 0.0), rates)
    totals_t = totals.T
    inward = conv_s[:, E : E + NS].astype(bf16)
    outward = conv_s[:, E + NS :].astype(bf16)
    cb_s[...] = jnp.where(allowed, dot_nt(outward, inward), 0.0)
    low = lane_low(TOK)
    for pair in range(PAIRS):
        lanes = slice(pair * LANES, (pair + 1) * LANES)
        first = 2 * pair
        step_pair = jnp.where(low, steps[:, first : first + 1], steps[:, first + 1 : first + 2])
        scaled = (conv_s[:, lanes] * step_pair).astype(bf16)
        mixes = []
        for head in (first, first + 1):
            apart = totals[:, head : head + 1] - totals_t[head : head + 1, :]
            mixes.append((jnp.exp(jnp.minimum(apart, 0.0)) * cb_s[...]).astype(bf16))
        yns_ref[:, lanes] = pair_lanes(dot_nn(jnp.concatenate(mixes, axis=0), scaled))

    sum_s[...] = jnp.zeros((TOK, LANES), f32)

    def gate_tile(index, carry):
        at = tile_at(index)
        gate = pm_ref[:, at].astype(f32)
        rows = yns_ref[:, at] + wide_ref[0:1, at] * conv_s[:, at]
        gated = rows * (gate * jax.nn.sigmoid(gate))
        sum_s[...] += gated * gated
        conv_s[:, at] = gated
        return carry

    lax.fori_loop(0, E // LANES, gate_tile, 0)
    scale = lax.rsqrt(jnp.sum(sum_s[...], axis=1, keepdims=True) * (1.0 / E) + epsilon)

    def norm_tile(index, carry):
        at = tile_at(index)
        xb_ref[:, at] = (conv_s[:, at] * scale * wide_ref[1:2, at]).astype(bf16)
        return carry

    lax.fori_loop(0, E // LANES, norm_tile, 0)

    cosine = rope_ref[:, :LANES]
    sine = rope_ref[:, LANES:]
    keys = both_halves(rope_turn(pq_ref[:, AH * HD : AH * HD + LANES].astype(f32), cosine, sine))
    values = both_halves(pq_ref[:, AH * HD + LANES :].astype(f32))
    keys = tuple(part.astype(bf16) for part in keys)
    values = tuple(part.astype(bf16) for part in values)
    for pair in range(AH // 2):
        group = pair // (AH // (2 * KVH))
        at = pair * LANES
        turned = rope_turn(pq_ref[:, at : at + LANES].astype(f32), cosine, sine)
        scores = dot_nt(pair_rows((turned * (1.0 / math.sqrt(HD))).astype(bf16)), keys[group])
        weights = []
        shares = []
        for part in (scores[:TOK], scores[TOK:]):
            part = part + bias_s[...]
            part = jnp.exp(part - jnp.max(part, axis=1, keepdims=True))
            shares.append(1.0 / jnp.sum(part, axis=1, keepdims=True))
            weights.append(part.astype(bf16))
        out = pair_lanes(dot_nn(jnp.concatenate(weights, axis=0), values[group]))
        out = out * jnp.where(low, shares[0], shares[1])
        xb_ref[:, E + pair * LANES : E + (pair + 1) * LANES] = out.astype(bf16)


def silu_slope(value, gate):
    return gate * (1.0 + value * (1.0 - gate))


def attend_back_kernel(
    pick_ref, pq_ref, dxb_ref, rope_ref, doc_col_ref, doc_row_ref, pg_ref, bias_s
):
    later = lax.broadcasted_iota(jnp.int32, (TOK, TOK), 1)
    early = lax.broadcasted_iota(jnp.int32, (TOK, TOK), 0)
    allowed_t = (later >= early) & (doc_col_ref[:, 0:1] == doc_row_ref[0:1, :])
    bias_s[...] = jnp.where(allowed_t, 0.0, -1e30)
    low = lane_low(TOK)
    cosine = rope_ref[:, :LANES]
    sine = rope_ref[:, LANES:]
    keys = both_halves(rope_turn(pq_ref[:, AH * HD : AH * HD + LANES].astype(f32), cosine, sine))
    values = both_halves(pq_ref[:, AH * HD + LANES :].astype(f32))
    root = 1.0 / math.sqrt(HD)
    d_keys = []
    d_values = []
    for group in range(KVH):
        key = keys[group].astype(bf16)
        key_rows = pair_rows(key)
        value_rows = pair_rows(values[group].astype(bf16))
        d_key = jnp.zeros((TOK, LANES), f32)
        d_value = jnp.zeros((TOK, LANES), f32)
        for pair in range(group * (AH // (2 * KVH)), (group + 1) * (AH // (2 * KVH))):
            at = pair * LANES
            turned = rope_turn(pq_ref[:, at : at + LANES].astype(f32), cosine, sine) * root
            query = turned.astype(bf16)
            d_out = dxb_ref[:, E + at : E + at + LANES].astype(bf16)
            scores = dot_nt(key_rows, query)
            d_weights = dot_nt(value_rows, d_out)
            weights = []
            d_scores = []
            for part in (slice(0, TOK), slice(TOK, 2 * TOK)):
                score = scores[part] + bias_s[...]
                weight = jnp.exp(score - jnp.max(score, axis=0, keepdims=True))
                weight = weight * (1.0 / jnp.sum(weight, axis=0, keepdims=True))
                d_weight = d_weights[part]
                offset = jnp.sum(weight * d_weight, axis=0, keepdims=True)
                weights.append(weight.astype(bf16))
                d_scores.append((weight * (d_weight - offset)).astype(bf16))
            d_value = d_value + pair_lanes(dot_nn(jnp.concatenate(weights, axis=0), d_out))
            d_key = d_key + pair_lanes(dot_nn(jnp.concatenate(d_scores, axis=0), query))
            d_query = pair_lanes(dot_tn(jnp.concatenate(d_scores, axis=1), key))
            pg_ref[:, at : at + LANES] = rope_back(d_query * root, cosine, sine).astype(bf16)
        d_keys.append(d_key + pltpu.roll(d_key, HD, 1))
        d_values.append(d_value + pltpu.roll(d_value, HD, 1))
    d_key = rope_back(jnp.where(low, d_keys[0], d_keys[1]), cosine, sine)
    pg_ref[:, AH * HD : AH * HD + LANES] = d_key.astype(bf16)
    pg_ref[:, AH * HD + LANES :] = jnp.where(low, d_values[0], d_values[1]).astype(bf16)


def mixer_back_kernel(
    pick_ref, pm_ref, pd_ref, pre_ref, yns_ref, dxb_ref, attend_ref, mask_ref, doc_col_ref,
    doc_row_ref, taps_ref, head_ref, wide_ref,
    pg_ref, small_ref,
    x_s, dx_s, dyb_s, cbt_s, dcbt_s, sum_s, ssum_s,
):
    small_ref[...] = jnp.zeros_like(small_ref)
    pg_ref[:, AT_Q:AT_DT] = attend_ref[...]
    sum_s[...] = jnp.zeros((TOK, LANES), f32)
    ssum_s[...] = jnp.zeros((TOK, LANES), f32)

    def start_tile(index, carry):
        at = tile_at(index)
        pre = pre_ref[:, at].astype(f32)
        heads_in = pre * jax.nn.sigmoid(pre)
        x_s[:, at] = heads_in
        gate = pm_ref[:, at].astype(f32)
        rows = yns_ref[:, at] + wide_ref[0:1, at] * heads_in
        gated = rows * (gate * jax.nn.sigmoid(gate))
        sum_s[...] += gated * gated
        ssum_s[...] += dxb_ref[:, at] * wide_ref[1:2, at] * gated
        return carry

    lax.fori_loop(0, E // LANES, start_tile, 0)
    scale = lax.rsqrt(jnp.sum(sum_s[...], axis=1, keepdims=True) * (1.0 / E) + epsilon)
    pull = jnp.sum(ssum_s[...], axis=1, keepdims=True) * (1.0 / E) * scale * scale * scale

    def gate_tile(index, carry):
        at = tile_at(index)
        heads_in = x_s[:, at]
        skip = wide_ref[0:1, at]
        gate = pm_ref[:, at].astype(f32)
        opened = jax.nn.sigmoid(gate)
        rows = yns_ref[:, at] + skip * heads_in
        gated = rows * (gate * opened)
        arrived = dxb_ref[:, at]
        d_gated = scale * (arrived * wide_ref[1:2, at]) - gated * pull
        small_ref[5:6, at] = jnp.sum(arrived * gated * scale, axis=0, keepdims=True)
        d_rows = d_gated * (gate * opened)
        pg_ref[:, at] = (d_gated * rows * silu_slope(gate, opened)).astype(bf16)
        small_ref[6:7, at] = jnp.sum(d_rows * heads_in, axis=0, keepdims=True)
        dyb_s[:, at] = d_rows.astype(bf16)
        dx_s[:, at] = skip * d_rows
        return carry

    lax.fori_loop(0, E // LANES, gate_tile, 0)

    def state_tile(index, carry):
        at = tile_from(E, index)
        pre = pre_ref[:, at].astype(f32)
        x_s[:, at] = pre * jax.nn.sigmoid(pre)
        return carry

    lax.fori_loop(0, 2, state_tile, 0)

    later = lax.broadcasted_iota(jnp.int32, (TOK, TOK), 1)
    early = lax.broadcasted_iota(jnp.int32, (TOK, TOK), 0)
    allowed_t = (later >= early) & (doc_col_ref[:, 0:1] == doc_row_ref[0:1, :])
    allowed = allowed_pairs(doc_col_ref, doc_row_ref)
    raw = pd_ref[...] + head_ref[0:1, :]
    steps = softplus(raw)
    decay = head_ref[1:2, :]
    rates = -steps * decay
    totals = dot_exact(jnp.where(allowed, 1.0, 0.0), rates)
    totals_t = totals.T
    inward = x_s[:, E : E + NS].astype(bf16)
    outward = x_s[:, E + NS :].astype(bf16)
    cbt_s[...] = jnp.where(allowed_t, dot_nt(inward, outward), 0.0)
    dcbt_s[...] = jnp.zeros((TOK, TOK), f32)
    low = lane_low(TOK)
    spread_row = lax.broadcasted_iota(jnp.int32, (2 * LANES, LANES), 0) // HD
    spread_col = lax.broadcasted_iota(jnp.int32, (2 * LANES, LANES), 1)
    sum_s[...] = jnp.zeros((TOK, LANES), f32)
    ssum_s[...] = jnp.zeros((TOK, LANES), f32)
    waiting = None
    for pair in range(PAIRS):
        lanes = slice(pair * LANES, (pair + 1) * LANES)
        first = 2 * pair
        step_pair = jnp.where(low, steps[:, first : first + 1], steps[:, first + 1 : first + 2])
        heads_in = x_s[:, lanes]
        scaled = (heads_in * step_pair).astype(bf16)
        d_rows = dyb_s[:, lanes]
        d_mix = dot_nt(pair_rows(scaled), d_rows)
        mixes = []
        d_pairs = None
        for side, head in enumerate((first, first + 1)):
            apart = totals_t[head : head + 1, :] - totals[:, head : head + 1]
            decays = jnp.exp(jnp.minimum(apart, 0.0))
            mixes.append((decays * cbt_s[...]).astype(bf16))
            part = d_mix[side * TOK : (side + 1) * TOK] * decays
            d_pairs = part if d_pairs is None else d_pairs + part
        dcbt_s[...] += d_pairs
        d_scaled = pair_lanes(dot_nn(jnp.concatenate(mixes, axis=0), d_rows))
        dx_s[:, lanes] += d_scaled * step_pair
        value = d_rows.astype(f32) * yns_ref[:, lanes] - scaled.astype(f32) * d_scaled
        coarse = value.astype(bf16)
        fine = (value - coarse.astype(f32)).astype(bf16)
        spread = (spread_col == first + (spread_row & 1)).astype(bf16)
        ssum_s[...] += dot_nn(jnp.concatenate([coarse, fine], axis=1), spread)
        value = (d_scaled * heads_in).astype(bf16)
        if pair % 2 == 0:
            waiting = value
        else:
            spread = (spread_col == first - 2 + spread_row).astype(bf16)
            sum_s[...] += dot_nn(jnp.concatenate([waiting, value], axis=1), spread)

    d_rates = dot_exact(jnp.where(allowed_t, 1.0, 0.0), ssum_s[...])
    d_steps = sum_s[...] - decay * d_rates
    d_raw = d_steps * jax.nn.sigmoid(raw)
    pg_ref[:, AT_DT:] = d_raw.astype(bf16)
    small_ref[7:8, :LANES] = jnp.sum(d_raw, axis=0, keepdims=True)
    small_ref[7:8, LANES : 2 * LANES] = jnp.sum(d_rates * rates, axis=0, keepdims=True)
    d_pairs = jnp.where(allowed_t, dcbt_s[...], 0.0).astype(bf16)
    dx_s[:, E : E + NS] = dot_nn(d_pairs, outward)
    dx_s[:, E + NS :] = dot_tn(d_pairs, inward)

    def conv_tile(index, carry):
        at = tile_at(index)
        pre = pre_ref[:, at].astype(f32)
        d_pre = dx_s[:, at] * silu_slope(pre, jax.nn.sigmoid(pre))
        rows = pm_ref[:, tile_from(AT_W, index)].astype(f32)
        small_ref[4:5, at] = jnp.sum(d_pre, axis=0, keepdims=True)
        small_ref[3:4, at] = jnp.sum(d_pre * rows, axis=0, keepdims=True)
        back = taps_ref[3:4, at] * d_pre
        for shift in (1, 2, 3):
            held = mask_ref[:, (shift - 1) * LANES : shift * LANES] * d_pre
            small_ref[3 - shift : 4 - shift, at] = jnp.sum(
                held * pltpu.roll(rows, shift, 0), axis=0, keepdims=True
            )
            back = back + taps_ref[3 - shift : 4 - shift, at] * pltpu.roll(held, TOK - shift, 0)
        pg_ref[:, tile_from(AT_W, index)] = back.astype(bf16)
        return carry

    lax.fori_loop(0, CH // LANES, conv_tile, 0)


def whole_block(shape):
    return pl.BlockSpec(shape, lambda *steps: (0,) * len(shape))


def once(shape, place):
    return pl.BlockSpec(shape, place, pipeline_mode=pl.Buffered(1))


def core_forward(row, projected, layout, params, held=()):
    operands = (*projected, *layout)

    def block(array):
        return once((None,) + array.shape[1:], lambda step: (row, 0, 0))

    outs = [
        jax.ShapeDtypeStruct((MB, TOK, MIXED), bf16),
        jax.ShapeDtypeStruct((MB, TOK, CH), bf16),
        jax.ShapeDtypeStruct((MB, TOK, E), f32),
    ]
    return pl.pallas_call(
        functools.partial(core_forward_kernel, bool(held)),
        grid=(1,),
        in_specs=[block(array) for array in operands]
        + [once(array.shape, lambda step: (0, 0)) for array in params]
        + [pl.BlockSpec(memory_space=pl.ANY)] * len(held),
        out_specs=[block(array) for array in outs],
        out_shape=outs,
        scratch_shapes=[
            pltpu.VMEM((TOK, CH), f32),
            pltpu.VMEM((TOK, TOK), f32),
            pltpu.VMEM((TOK, TOK), f32),
            pltpu.VMEM((TOK, LANES), f32),
        ],
        input_output_aliases={10: 0, 11: 1, 12: 2} if held else {},
        compiler_params=pltpu.CompilerParams(vmem_limit_bytes=12 * MIB),
        cost_estimate=pl.CostEstimate(
            flops=4 * 10**8, bytes_accessed=12 * 2**20, transcendentals=10**6
        ),
        name="core_forward",
    )(*operands, *params, *held)


def core_back_specs(by_row, plain):
    return [
        once((None,) + array.shape[1:], lambda step, pick: (pick[0], 0, 0)) if chosen
        else once(array.shape, lambda step, pick: (0, 0))
        for chosen, arrays in ((True, by_row), (False, plain))
        for array in arrays
    ]


def attend_back(row, projected, d_mixed, layout):
    rope, masks, doc_cols, doc_rows = layout
    return pl.pallas_call(
        attend_back_kernel,
        grid_spec=pltpu.PrefetchScalarGridSpec(
            num_scalar_prefetch=1,
            grid=(1,),
            in_specs=core_back_specs([projected[1]], [d_mixed])
            + core_back_specs([rope, doc_cols, doc_rows], []),
            out_specs=once((TOK, AT_DT - AT_Q), lambda step, pick: (0, 0)),
            scratch_shapes=[pltpu.VMEM((TOK, TOK), f32)],
        ),
        out_shape=jax.ShapeDtypeStruct((TOK, AT_DT - AT_Q), bf16),
        compiler_params=pltpu.CompilerParams(vmem_limit_bytes=6 * MIB),
        cost_estimate=pl.CostEstimate(
            flops=3 * 10**8, bytes_accessed=4 * 2**20, transcendentals=6 * 10**5
        ),
        name="attend_back",
    )(row, projected[1], d_mixed, rope, doc_cols, doc_rows)


def mixer_back(row, projected, pre, yns, d_mixed, attended, layout, params):
    rope, masks, doc_cols, doc_rows = layout
    return pl.pallas_call(
        mixer_back_kernel,
        grid_spec=pltpu.PrefetchScalarGridSpec(
            num_scalar_prefetch=1,
            grid=(1,),
            in_specs=core_back_specs(
                [projected[0], projected[2], pre, yns], [d_mixed, attended]
            )
            + core_back_specs([masks, doc_cols, doc_rows], params),
            out_specs=[
                once((TOK, WIDE_A), lambda step, pick: (0, 0)),
                once((8, CH), lambda step, pick: (0, 0)),
            ],
            scratch_shapes=[
                pltpu.VMEM((TOK, CH), f32),
                pltpu.VMEM((TOK, CH), f32),
                pltpu.VMEM((TOK, E), bf16),
                pltpu.VMEM((TOK, TOK), f32),
                pltpu.VMEM((TOK, TOK), f32),
                pltpu.VMEM((TOK, LANES), f32),
                pltpu.VMEM((TOK, LANES), f32),
            ],
        ),
        out_shape=[
            jax.ShapeDtypeStruct((TOK, WIDE_A), bf16),
            jax.ShapeDtypeStruct((8, CH), f32),
        ],
        compiler_params=pltpu.CompilerParams(vmem_limit_bytes=15 * MIB),
        cost_estimate=pl.CostEstimate(
            flops=7 * 10**8, bytes_accessed=10 * 2**20, transcendentals=15 * 10**5
        ),
        name="mixer_back",
    )(
        row, projected[0], projected[2], pre, yns, d_mixed, attended, masks, doc_cols, doc_rows,
        *params,
    )


def passed_along(value, axis, steps):
    count = lax.axis_size(axis)
    leading, last = (max(0, -steps), min(count, count - steps))
    return lax.ppermute(value, axis, [(source, source + steps) for source in range(leading, last)])


def norm_rows(values):
    return lax.rsqrt(jnp.mean(values * values, axis=-1, keepdims=True) + epsilon)


def norm_back(values, gain, arrived):
    scale = norm_rows(values)
    weighted = arrived * gain
    pull = jnp.mean(weighted * values, axis=-1, keepdims=True) * scale * scale * scale
    gain_grad = jnp.sum(arrived * values * scale, axis=0, keepdims=True)
    return (weighted * scale - values * pull, gain_grad)


def project_kernel(rows_ref, gain_ref, own_ref, other_ref, *refs):
    normed_ref, pm_ref, pq_ref, pd_ref = refs[-4:]
    step = pl.program_id(0)

    @pl.when(step == 0)
    def _():
        rows = rows_ref[...].astype(f32)
        normed_ref[...] = (rows * norm_rows(rows) * gain_ref[...]).astype(bf16)

    out = dot_nn(normed_ref[:, :SIDE], own_ref[...]) + dot_nn(normed_ref[:, SIDE:], other_ref[...])
    tile = WIDE_A // 3
    for index in range(2):
        @pl.when(step == index)
        def _(index=index):
            pm_ref[:, index * tile : (index + 1) * tile] = out.astype(bf16)

    @pl.when(step == 2)
    def _():
        pm_ref[:, 2 * tile :] = out[:, : AT_Q - 2 * tile].astype(bf16)
        pq_ref[...] = out[:, AT_Q - 2 * tile : AT_DT - 2 * tile].astype(bf16)
        pd_ref[...] = out[:, AT_DT - 2 * tile :]


def project(rows, gain, own, other, row=None, held=()):
    count = rows.shape[0]
    tile = WIDE_A // 3
    weight = pl.BlockSpec((SIDE, tile), lambda step: (0, step))
    at = row or 0
    total = count if row is None else MB * TOK
    widths = ((D, bf16), (AT_Q, bf16), (AT_DT - AT_Q, bf16), (LANES, f32))
    return pl.pallas_call(
        project_kernel,
        grid=(3,),
        in_specs=[whole_block((count, D)), whole_block((1, D)), weight, weight]
        + [pl.BlockSpec(memory_space=pl.ANY)] * len(held),
        out_specs=[pl.BlockSpec((count, width), lambda step: (at, 0)) for width, _ in widths],
        out_shape=[jax.ShapeDtypeStruct((total, width), kind) for width, kind in widths],
        input_output_aliases={4 + index: index for index in range(len(held))},
        compiler_params=pltpu.CompilerParams(vmem_limit_bytes=15 * MIB),
        cost_estimate=pl.CostEstimate(
            flops=2 * count * D * WIDE_A,
            bytes_accessed=2 * D * WIDE_A + 2 * count * WIDE_A,
            transcendentals=0,
        ),
        name="project",
    )(rows, gain, own, other, *held)


def by_row(projected):
    return tuple(array.reshape(MB, TOK, -1) for array in projected[1:])


def feed_forward_kernel(
    keep, rows_ref, mixed_ref, gain_ref,
    out_own, out_other, gate_own, gate_other, up_own, up_other, down_own, down_other,
    *refs,
):
    if keep:
        low_ref, middle_ref, normed_ref, gate_ref, up_ref, act_ref, total_s = refs[-7:]
    else:
        low_ref, middle_ref, normed_ref, total_s = refs
    step = pl.program_id(0)

    @pl.when(step == 0)
    def _():
        middle_ref[...] = rows_ref[...].astype(f32)

    @pl.when(step < 4)
    def _():
        mixed = mixed_ref[...]
        middle_ref[:, :SIDE] += dot_nt(mixed, out_own[...])
        middle_ref[:, SIDE:] += dot_nt(mixed, out_other[...])

    @pl.when(step == 3)
    def _():
        middle = middle_ref[...]
        normed_ref[...] = (middle * norm_rows(middle) * gain_ref[...]).astype(bf16)
        total_s[...] = middle

    @pl.when(step >= 4)
    def _():
        left = normed_ref[:, :SIDE]
        right = normed_ref[:, SIDE:]
        gate = dot_nn(left, gate_own[...]) + dot_nn(right, gate_other[...])
        up = dot_nn(left, up_own[...]) + dot_nn(right, up_other[...])
        act = (gate * jax.nn.sigmoid(gate) * up).astype(bf16)
        if keep:
            gate_ref[...] = gate.astype(bf16)
            up_ref[...] = up.astype(bf16)
            act_ref[...] = act
        total_s[:, :SIDE] += dot_nt(act, down_own[...])
        total_s[:, SIDE:] += dot_nt(act, down_other[...])

    @pl.when(step == 7)
    def _():
        low_ref[...] = total_s[...].astype(bf16)


def pinned(own, other):
    return [
        pltpu.with_memory_space_constraint(own, pltpu.VMEM),
        pltpu.with_memory_space_constraint(other, pltpu.HBM),
    ]


def b_block(start, skipped):
    return pl.BlockSpec(
        (SIDE, 512), lambda step, *pick: (0, start + jnp.clip(step - skipped, 0, 3))
    )


def b_blocks(parts):
    return [b_block(start, skipped) for start, skipped in parts for _ in range(2)]


def feed_forward(row, rows, mixed, gain, own, other, held=None):
    keep = held is not None
    at = row if rows.shape[0] > TOK else 0

    def late(step):
        return (row, jnp.clip(step - 4, 0, 3))

    wide = pl.BlockSpec((TOK, 512), late)
    full = pl.BlockSpec((TOK, D), lambda step: (row, 0))
    scratch = [pltpu.VMEM((TOK, D), f32)]
    if keep:
        out_specs = [full, full, full, wide, wide, wide]
        out_shape = [
            jax.ShapeDtypeStruct((MB * TOK, width), kind)
            for width, kind in ((D, bf16), (D, f32), (D, bf16), (FF, bf16), (FF, bf16), (FF, bf16))
        ]
    else:
        out_specs = [whole_block((TOK, D))]
        out_shape = [jax.ShapeDtypeStruct((TOK, D), bf16)]
        scratch = [pltpu.VMEM((TOK, D), f32), pltpu.VMEM((TOK, D), bf16)] + scratch
    held = tuple(held or ())
    return pl.pallas_call(
        functools.partial(feed_forward_kernel, keep),
        grid=(8,),
        in_specs=[
            pl.BlockSpec((TOK, D), lambda step: (at, 0)),
            pl.BlockSpec((TOK, 512), lambda step: (row, jnp.clip(step, 0, 3))),
            whole_block((1, D)),
        ]
        + b_blocks(((0, 0), (4, 4), (8, 4), (12, 4)))
        + [pl.BlockSpec(memory_space=pl.ANY)] * len(held),
        out_specs=out_specs,
        out_shape=out_shape,
        scratch_shapes=scratch,
        input_output_aliases={11 + index: index for index in range(len(held))},
        compiler_params=pltpu.CompilerParams(vmem_limit_bytes=(FF_VMEM if keep else 18) * MIB),
        cost_estimate=pl.CostEstimate(
            flops=2 * TOK * D * WIDE_B, bytes_accessed=2 * D * WIDE_B, transcendentals=0
        ),
        name="feed_forward",
    )(rows, mixed, gain, *((pinned(own, other) if keep else [own, other]) * 4), *held)


def feed_back_kernel(
    pick_ref, cot_ref, gate_ref, up_ref, middle_ref, gain_ref,
    down_own, down_other, gate_own, gate_other, up_own, up_other, out_own, out_other,
    d_gate_ref, d_up_ref, d_middle_ref, low_ref, d_mixed_ref, gain_grad_ref,
    total_s,
):
    step = pl.program_id(0)

    @pl.when(step == 0)
    def _():
        total_s[...] = jnp.zeros_like(total_s)

    @pl.when(step < 4)
    def _():
        arrived = dot_nn(cot_ref[:, :SIDE], down_own[...]) + dot_nn(
            cot_ref[:, SIDE:], down_other[...]
        )
        gate = gate_ref[...].astype(f32)
        opened = jax.nn.sigmoid(gate)
        d_gate = (arrived * up_ref[...].astype(f32) * silu_slope(gate, opened)).astype(bf16)
        d_up = (arrived * (gate * opened)).astype(bf16)
        d_gate_ref[...] = d_gate
        d_up_ref[...] = d_up
        total_s[:, :SIDE] += dot_nt(d_gate, gate_own[...]) + dot_nt(d_up, up_own[...])
        total_s[:, SIDE:] += dot_nt(d_gate, gate_other[...]) + dot_nt(d_up, up_other[...])

    @pl.when(step == 3)
    def _():
        d_norm, gain_grad = norm_back(middle_ref[...], gain_ref[...], total_s[...])
        d_middle = cot_ref[...].astype(f32) + d_norm
        d_middle_ref[...] = d_middle
        low_ref[...] = d_middle.astype(bf16)
        gain_grad_ref[...] = gain_grad

    @pl.when(step >= 4)
    def _():
        d_mixed_ref[...] = dot_nn(low_ref[:, :SIDE], out_own[...]) + dot_nn(
            low_ref[:, SIDE:], out_other[...]
        )


def feed_back(row, cotangent, gate, up, middle, gain, own, other):
    saved = pl.BlockSpec((TOK, 512), lambda step, pick: (pick[0], jnp.clip(step, 0, 3)))
    early = pl.BlockSpec((TOK, 512), lambda step, pick: (0, jnp.clip(step, 0, 3)))
    late = pl.BlockSpec((TOK, 512), lambda step, pick: (0, jnp.clip(step - 4, 0, 3)))
    full = pl.BlockSpec((TOK, D), lambda step, pick: (0, 0))
    gain_block = pl.BlockSpec((1, D), lambda step, pick: (0, 0))
    return pl.pallas_call(
        feed_back_kernel,
        grid_spec=pltpu.PrefetchScalarGridSpec(
            num_scalar_prefetch=1,
            grid=(8,),
            in_specs=[
                full,
                saved,
                saved,
                pl.BlockSpec((TOK, D), lambda step, pick: (pick[0], 0)),
                gain_block,
            ]
            + b_blocks(((12, 0), (4, 0), (8, 0), (0, 4))),
            out_specs=[early, early, full, full, late, gain_block],
            scratch_shapes=[pltpu.VMEM((TOK, D), f32)],
        ),
        out_shape=[
            jax.ShapeDtypeStruct((TOK, FF), bf16),
            jax.ShapeDtypeStruct((TOK, FF), bf16),
            jax.ShapeDtypeStruct((TOK, D), f32),
            jax.ShapeDtypeStruct((TOK, D), bf16),
            jax.ShapeDtypeStruct((TOK, MIXED), f32),
            jax.ShapeDtypeStruct((1, D), f32),
        ],
        compiler_params=pltpu.CompilerParams(vmem_limit_bytes=FB_VMEM * MIB),
        cost_estimate=pl.CostEstimate(
            flops=2 * TOK * D * WIDE_B, bytes_accessed=2 * D * WIDE_B, transcendentals=0
        ),
        name="feed_back",
    )(
        row, cotangent, *(pltpu.with_memory_space_constraint(one, pltpu.HBM) for one in (gate, up)),
        middle, gain, *(pinned(own, other) * 4),
    )


def project_back_kernel(
    pick_ref, grad_ref, rows_ref, d_middle_ref, gain_ref, own_ref, other_ref,
    d_rows_ref, low_ref, gain_grad_ref, total_s,
):
    step = pl.program_id(0)

    @pl.when(step == 0)
    def _():
        total_s[...] = jnp.zeros_like(total_s)

    total_s[:, :SIDE] += dot_nt(grad_ref[...], own_ref[...])
    total_s[:, SIDE:] += dot_nt(grad_ref[...], other_ref[...])

    @pl.when(step == 2)
    def _():
        d_norm, gain_grad = norm_back(rows_ref[...].astype(f32), gain_ref[...], total_s[...])
        d_rows = d_middle_ref[...] + d_norm
        d_rows_ref[...] = d_rows
        low_ref[...] = d_rows.astype(bf16)
        gain_grad_ref[...] = gain_grad


def project_back(row, proj_low, start_rows, d_middle, gain, own, other):
    tile = WIDE_A // 3
    weight = pl.BlockSpec((SIDE, tile), lambda step, pick: (0, step))
    full = pl.BlockSpec((TOK, D), lambda step, pick: (0, 0))
    gain_block = pl.BlockSpec((1, D), lambda step, pick: (0, 0))
    return pl.pallas_call(
        project_back_kernel,
        grid_spec=pltpu.PrefetchScalarGridSpec(
            num_scalar_prefetch=1,
            grid=(3,),
            in_specs=[
                pl.BlockSpec((TOK, tile), lambda step, pick: (0, step)),
                pl.BlockSpec((TOK, D), lambda step, pick: (pick[0], 0)),
                full,
                gain_block,
                weight,
                weight,
            ],
            out_specs=[full, full, gain_block],
            scratch_shapes=[pltpu.VMEM((TOK, D), f32)],
        ),
        out_shape=[
            jax.ShapeDtypeStruct((TOK, D), f32),
            jax.ShapeDtypeStruct((TOK, D), bf16),
            jax.ShapeDtypeStruct((1, D), f32),
        ],
        compiler_params=pltpu.CompilerParams(vmem_limit_bytes=15 * MIB),
        cost_estimate=pl.CostEstimate(
            flops=2 * TOK * D * WIDE_A, bytes_accessed=2 * D * WIDE_A, transcendentals=0
        ),
        name="project_back",
    )(row, proj_low, start_rows, d_middle, gain, own, other)


def weight_grad_kernel(groups, pick_ref, *refs):
    lefts = refs[: 4 * len(groups)]
    rights = refs[4 * len(groups) : 8 * len(groups)]
    sum_ref, left_s = refs[8 * len(groups) :]
    step = pl.program_id(0)
    for index, (start, count) in enumerate(groups):
        four = lefts[4 * index : 4 * index + 4]
        blocks = rights[4 * index : 4 * index + 4]

        @pl.when(step == start)
        def _(four=four):
            for place, ref in enumerate(four):
                left_s[:, place * TOK : (place + 1) * TOK] = ref[...].astype(f32).T.astype(bf16)

        @pl.when((step >= start) & (step < start + count))
        def _(blocks=blocks):
            right = jnp.concatenate([ref[...] for ref in blocks], axis=0)
            sum_ref[...] = dot_nn(left_s[...], right).astype(bf16)


def weight_grad(picks, tile, groups):
    steps = []
    in_left = []
    in_right = []
    operands_left = []
    operands_right = []
    start = 0
    for left, right in groups:
        count = right[0][0].shape[1] // tile
        steps.append((start, count))
        for array, which, column in left:
            in_left.append(
                pl.BlockSpec(
                    (TOK, SIDE),
                    lambda step, pick, which=which, column=column: (
                        0 if which is None else pick[which],
                        column,
                    ),
                )
            )
            operands_left.append(array)
        for array, which in right:
            in_right.append(
                pl.BlockSpec(
                    (TOK, tile),
                    lambda step, pick, which=which, start=start, count=count: (
                        0 if which is None else pick[which],
                        jnp.clip(step - start, 0, count - 1),
                    ),
                )
            )
            operands_right.append(array)
        start += count
    return pl.pallas_call(
        functools.partial(weight_grad_kernel, tuple(steps)),
        grid_spec=pltpu.PrefetchScalarGridSpec(
            num_scalar_prefetch=1,
            grid=(start,),
            in_specs=in_left + in_right,
            out_specs=pl.BlockSpec((SIDE, tile), lambda step, pick: (0, step)),
            scratch_shapes=[pltpu.VMEM((SIDE, 4 * TOK), bf16)],
        ),
        out_shape=jax.ShapeDtypeStruct((SIDE, start * tile), bf16),
        compiler_params=pltpu.CompilerParams(vmem_limit_bytes=16 * MIB),
        cost_estimate=pl.CostEstimate(
            flops=8 * TOK * SIDE * start * tile,
            bytes_accessed=4 * SIDE * start * tile,
            transcendentals=0,
        ),
        name="weight_grad",
    )(picks, *operands_left, *operands_right)


def row_layout(doc_ids):
    rows = doc_ids.shape[0]
    positions = jnp.arange(TOK, dtype=jnp.int32)
    earlier = jnp.sum((doc_ids[:, None, :] < doc_ids[:, :, None]).astype(jnp.int32), axis=2)
    places = positions[None, :] - earlier
    half_dim = HD // 2
    inverse_freq = rope_base ** (-jnp.arange(half_dim, dtype=f32) / half_dim)
    angles = places.astype(f32)[:, :, None] * inverse_freq[None, None, :]
    repeats = LANES // half_dim
    rope = jnp.concatenate([jnp.cos(angles)] * repeats + [jnp.sin(angles)] * repeats, axis=-1)
    masks = jnp.concatenate(
        [
            jnp.broadcast_to((places >= shift).astype(f32)[:, :, None], (rows, TOK, LANES))
            for shift in (1, 2, 3)
        ],
        axis=-1,
    )
    doc_cols = jnp.broadcast_to(doc_ids[:, :, None], (rows, TOK, LANES))
    doc_rows = jnp.broadcast_to(doc_ids[:, None, :], (rows, 8, TOK))
    return (rope, masks, doc_cols, doc_rows)


def core_params(conv_weight, conv_bias, step_bias, decay_log, skip_scale, mixer_gain):
    taps = jnp.concatenate([conv_weight, conv_bias[None], jnp.zeros((3, CH), f32)], axis=0)
    heads = jnp.zeros((8, LANES), f32)
    heads = heads.at[0, :MH].set(step_bias).at[1, :MH].set(jnp.exp(decay_log))
    wide = jnp.concatenate(
        [jnp.repeat(skip_scale, MP)[None], mixer_gain[None], jnp.zeros((6, E), f32)], axis=0
    )
    return (taps, heads, wide)


def swapped(value):
    return lax.ppermute(value, "core", [(0, 1), (1, 0)])


def ring_order(chips):
    return [2 * step for step in range(chips // 2)] + [
        2 * step + 1 for step in reversed(range(chips // 2))
    ]


def ring_place(chip, chips):
    return jnp.where(chip % 2 == 0, chip // 2, chips - 1 - chip // 2)


def onward(value, steps):
    order = ring_order(lax.axis_size("chip"))
    chips = len(order)
    return lax.ppermute(
        value, "chip", [(order[at], order[(at + steps) % chips]) for at in range(chips)]
    )


def slot_offsets(chips):
    offsets = [0]
    for far in range(1, chips // 2):
        offsets += [-far, far]
    return offsets + [chips // 2]


def tied(*values):
    return lax.optimization_barrier(values)


class RingGather:
    def __init__(self, shard):
        self.slots = [shard]
        self.ahead = self.back = shard
        self.left = lax.axis_size("chip") // 2

    def operands(self):
        half = self.ahead.shape[0] // 2
        if self.left == 1:
            return self.ahead[:half], self.back[half:]
        return self.ahead, self.back

    def send(self, ahead, back):
        self.ahead, self.back = tied(onward(ahead, 1), onward(back, -1))
        self.slots += [self.ahead, self.back]
        self.left -= 1
        return self.ahead

    def step(self):
        return self.send(*self.operands())

    def last(self):
        while self.left > 1:
            self.step()

    def hold(self, value):
        self.ahead, self.back, _ = tied(self.ahead, self.back, value)
        self.slots[-2:] = [self.ahead, self.back]


class RingReduce:
    def __init__(self, sums):
        self.sums = sums
        self.chips = lax.axis_size("chip")
        self.size = sums.shape[0] // self.chips
        self.left = self.chips // 2
        self.ahead = self.back = None

    def slot(self, index, start=0, stop=None):
        stop = self.size if stop is None else stop
        return self.sums[index * self.size + start : index * self.size + stop]

    def operands(self):
        half = self.size // 2
        if self.ahead is None:
            last = self.chips - 1
            return self.slot(last, 0, half), self.slot(last, half)
        ahead, back = self.ahead.astype(f32), self.back.astype(f32)
        if self.left == self.chips // 2 - 1:
            ahead = jnp.pad(ahead, ((0, half), (0, 0)))
            back = jnp.pad(back, ((half, 0), (0, 0)))
        return (
            (self.slot(2 * self.left).astype(f32) + ahead).astype(bf16),
            (self.slot(2 * self.left - 1).astype(f32) + back).astype(bf16),
        )

    def send(self, ahead, back):
        self.ahead, self.back = tied(onward(ahead, 1), onward(back, -1))
        self.left -= 1
        return self.ahead

    def step(self):
        return self.send(*self.operands())

    def hold(self, value):
        self.ahead, self.back, _ = tied(self.ahead, self.back, value)

    def columns(self, start, stop):
        part = RingReduce(self.sums[:, start:stop])
        part.left = self.left
        part.ahead, part.back = self.ahead[:, start:stop], self.back[:, start:stop]
        return part

    def total(self):
        while self.left > 0:
            self.step()
        return self.slot(0).astype(f32) + self.ahead.astype(f32) + self.back.astype(f32)


def small_hops(chips):
    if chips & (chips - 1):
        return [lambda value: lax.psum(value, ("chip", "core")) - value]
    hops = [swapped]
    for bit in range(chips.bit_length() - 1):
        pairs = [(chip, chip ^ (1 << bit)) for chip in range(chips)]
        hops.append(lambda value, pairs=pairs: lax.ppermute(value, "chip", pairs))
    return hops


def ring_columns(core):
    chips = lax.axis_size("chip")
    place = ring_place(lax.axis_index("chip"), chips)
    own = []
    for offset in slot_offsets(chips):
        at = (place + offset) % chips
        own.append(jnp.where(at < chips // 2, 2 * at, 2 * (chips - 1 - at) + 1))
    own = jnp.stack(own)
    width = D // (2 * chips)
    starts = jnp.concatenate([2 * own + core, 2 * own + 1 - core]) * width
    wanted = (starts[:, None] + jnp.arange(width)[None, :]).reshape(D)
    return (jnp.arange(D)[:, None] == wanted[None, :]).astype(bf16)


def per_device(
    inputs, out_grad, doc_ids, row_live, pre_gain, mlp_gain, mixer_gain, conv_weight, conv_bias,
    step_bias, decay_log, skip_scale, mixer_in_weight, mixer_out_weight, query_weight, key_weight,
    value_weight, attend_weight, gate_up_weight, down_weight,
):
    is_first = lax.axis_index("section") == 0
    core = lax.axis_index("core")
    shard = mixer_in_weight.shape[1]
    packed_a = jnp.concatenate(
        [
            mixer_in_weight[0, :, :AT_Q],
            query_weight[0],
            key_weight[0],
            value_weight[0],
            mixer_in_weight[0, :, AT_Q:],
            jnp.zeros((shard, LANES - MH), bf16),
        ],
        axis=1,
    )
    packed_b = jnp.concatenate(
        [mixer_out_weight[0].T, attend_weight[0].T, gate_up_weight[0], down_weight[0].T], axis=1
    )

    layout = row_layout(doc_ids)
    params = core_params(
        conv_weight[0], conv_bias[0], step_bias[0], decay_log[0], skip_scale[0], mixer_gain[0]
    )
    turn = ring_columns(core)

    def own_order(values):
        if values.dtype == bf16:
            return dot_nn(values, turn).astype(bf16)
        return dot_exact(values, turn.astype(f32))

    def whole_order(values):
        if values.dtype == bf16:
            return dot_nt(values, turn).astype(bf16)
        return dot_exact(values, turn.astype(f32).T)

    pre_row = own_order(pre_gain)
    mlp_row = own_order(mlp_gain)
    first_rows = own_order(inputs)

    positions = jnp.arange(TOK, dtype=jnp.int32)
    live = (positions[None, :] < row_live[:, None]).reshape(MB * TOK, 1)
    from_loss = own_order(jnp.where(live, out_grad, jnp.zeros_like(out_grad)))
    first_rows, from_loss = tied(first_rows, from_loss)

    ring_a = RingGather(packed_a)
    ring_b = RingGather(packed_b)
    ring_a.step()
    ring_b.step()
    ring_a.last()
    now_a, now_b = tied(ring_a.operands(), ring_b.operands())
    ring_a.send(*now_a)
    ring_b.send(*now_b)
    own_a = jnp.concatenate(ring_a.slots, axis=0)
    pair_a = (own_a, swapped(own_a))
    now_b, gain_now, pair_a = tied(ring_b.operands(), pre_row, pair_a)
    ring_b.send(*now_b)
    projected = by_row(project(first_rows, gain_now, *pair_a))
    mixed = core_forward(0, projected, layout, params)
    ring_b.hold(mixed)
    now_b, mixed = tied(ring_b.operands(), mixed)
    ring_b.send(*now_b)
    mixed, _, _ = core_forward(1, projected, layout, params, held=mixed)
    ring_b.hold(mixed)
    while ring_b.left:
        ring_b.step()
    pair_b = (
        jnp.concatenate(ring_b.slots, axis=0),
        jnp.concatenate([swapped(slot) for slot in ring_b.slots], axis=0),
    )
    mixed = mixed.reshape(MB * TOK, MIXED)
    received = {}
    for row in (1, 0):
        (handed,) = feed_forward(row, first_rows, mixed, mlp_row, *pair_b)
        received[row] = passed_along(handed, "section", 1)

    def second_pass(row, projects=(), cores=(), forwards=()):
        start = jnp.where(is_first, first_rows[row * TOK : (row + 1) * TOK], received[row])
        projects = project(start, pre_row, *pair_a, row=row, held=projects)
        cores = core_forward(row, by_row(projects), layout, params, held=cores)
        mixed = cores[0].reshape(MB * TOK, MIXED)
        forwards = feed_forward(row, start, mixed, mlp_row, *pair_b, held=forwards)
        return start, projects, cores, forwards

    arrived = jnp.zeros((TOK, D), bf16)
    lefts = []
    rights = []
    rows = []
    picks = jnp.where(is_first, jnp.array([1, 0]), jnp.array([0, 1])).astype(jnp.int32)

    def tick_left(which):
        return [(lefts[1][which], None, 0), (lefts[2][which], None, 0)] + [
            (lefts[1][which + 2], None, 0), (lefts[2][which + 2], None, 0)
        ]

    def tick_right(which):
        return [(rights[tick][which + far], None) for far in (0, 2) for tick in (1, 2)]

    def saved_left(own, their):
        return [(own, 0, 0), (own, 1, 0), (their, 0, 0), (their, 1, 0)]

    def saved_right(own, their):
        return [(own, 0), (own, 1), (their, 0), (their, 1)]

    start, projects, cores, forwards = second_pass(1)
    starts = {1: start}
    start_rows = jnp.concatenate([start, start], axis=0)
    for tick in range(3):
        if tick == 1:
            (projects, cores, forwards), received[0], _ = tied(
                (projects, cores, forwards), received[0], d_low
            )
            starts[0], projects, cores, forwards = second_pass(0, projects, cores, forwards)
            start_rows = jnp.concatenate([starts[0], starts[1]], axis=0)
            arrived, forwards = tied(arrived, forwards)
        normed, projected = projects[0], by_row(projects)
        mixed, pre, yns = cores[0].reshape(MB * TOK, MIXED), cores[1], cores[2]
        result, middle, normed_two, gate, up, act = forwards
        row = jnp.where(is_first, (1, 1, 0)[tick], (1, 0, 1)[tick]).astype(jnp.int32).reshape(1)
        if tick == 2:
            row, lefts[1], rights[1], rows[1] = tied(row, lefts[1], rights[1], rows[1])
        loss_row = (1, 0, 1)[tick]
        cotangent = jnp.where(
            is_first, arrived, from_loss[loss_row * TOK : (loss_row + 1) * TOK]
        )
        if tick == 1:
            cotangent, swaps = tied(
                cotangent, (mixed, act, normed[:, SIDE:], normed_two[:, SIDE:])
            )
            their_mixed, their_act, their_normed, their_normed_two = map(swapped, swaps)
        d_gate, d_up, d_middle, middle_low, d_mixed, mlp_grad = feed_back(
            row, cotangent, gate, up, middle, mlp_row, *pair_b
        )
        lefts.append(
            (cotangent, middle_low, swapped(cotangent[:, SIDE:]), swapped(middle_low[:, SIDE:]))
        )
        rights.append((d_gate, d_up, swapped(d_gate), swapped(d_up)))
        if tick < 2:
            attended = attend_back(row, projected, d_mixed, layout)
            if tick == 1:
                row, their_mixed, their_act, their_normed, their_normed_two = tied(
                    row, their_mixed, their_act, their_normed, their_normed_two
                )
            proj_low, small = mixer_back(
                row, projected, pre, yns, d_mixed, attended, layout, params
            )
            their_low = swapped(proj_low)
        else:
            sum_c = weight_grad(
                picks,
                1024,
                [
                    (tick_left(1), saved_right(mixed, their_mixed)),
                    (tick_left(0), saved_right(act, their_act)),
                ],
            )
            ring_c = RingReduce(sum_c)
            now_c, row = tied(ring_c.operands(), row)
            ring_c.send(*now_c)
            attended = attend_back(row, projected, d_mixed, layout)
            ring_c.hold(attended)
            picks_now, now_c, rights[2] = tied(picks, ring_c.operands(), rights[2])
            ring_c.send(*now_c)
            sum_b = weight_grad(
                picks_now,
                1024,
                [
                    (saved_left(normed_two, their_normed_two), tick_right(0)),
                    (saved_left(normed_two, their_normed_two), tick_right(1)),
                ],
            )
            ring_b = RingReduce(sum_b)
            ring_c.hold(sum_b)
            now_b, now_c, row, attended = tied(
                ring_b.operands(), ring_c.operands(), row, attended
            )
            ring_c.send(*now_c)
            ring_b.send(*now_b)
            proj_low, small = mixer_back(
                row, projected, pre, yns, d_mixed, attended, layout, params
            )
            proj_low, ring_b.ahead, ring_b.back, ring_c.ahead, ring_c.back = tied(
                proj_low, ring_b.ahead, ring_b.back, ring_c.ahead, ring_c.back
            )
            their_low = swapped(proj_low)
            now_b, row = tied(ring_b.operands(), row)
            ring_b.send(*now_b)
            d_rows, d_low, pre_grad = project_back(
                row, proj_low, start_rows, d_middle, pre_row, *pair_a
            )
            now_c, their_low, d_rows, pre_grad = tied(
                ring_c.operands(), their_low, d_rows, pre_grad
            )
            ring_c.send(*now_c)
            picks_now, now_c = tied(picks, now_c)
            (p_one, their_one), (p_two, their_two) = rows[1][1], (proj_low, their_low)
            sum_a = weight_grad(
                picks_now,
                WIDE_A // 3,
                [
                    (
                        saved_left(normed, their_normed),
                        [(p_one, None), (p_two, None), (their_one, None), (their_two, None)],
                    )
                ],
            )
            ring_b.hold(sum_a)
            ring_a = RingReduce(sum_a)
            ring_c.hold(sum_a)
            now_a, now_b, ring_c.ahead, ring_c.back = tied(
                ring_a.operands(), ring_b.operands(), ring_c.ahead, ring_c.back
            )
            ring_b.send(*now_b)
            ring_a.send(*now_a)
        if tick < 2:
            d_rows, d_low, pre_grad = project_back(
                row, proj_low, start_rows, d_middle, pre_row, *pair_a
            )
        rows.append((d_rows, (proj_low, their_low), pre_grad, mlp_grad, small))
        if tick < 2:
            arrived = passed_along(d_low, "section", -1)

    pre_sum, mlp_sum, small = (one + two for one, two in zip(rows[1][2:], rows[2][2:]))
    gain_sums = whole_order(jnp.concatenate([pre_sum, mlp_sum], axis=0))
    small = jnp.concatenate([small, jnp.pad(gain_sums, ((0, 6), (0, CH - D)))], axis=0)

    hops = small_hops(lax.axis_size("chip"))

    def hop_beside(small, ring):
        if not hops:
            return small
        small, moved, _ = tied(small, hops.pop(0)(small), ring.ahead)
        return small + moved

    small = hop_beside(small, ring_a)
    ring_b.step()
    ring_a.step()
    small = hop_beside(small, ring_a)
    while ring_a.left > 2:
        ring_a.step()
    d_last = tied(rows[2][0], ring_a.ahead)[0]
    rings_a = [ring_a.columns(0, CUT_A), ring_a.columns(CUT_A, WIDE_A)]
    while rings_a[0].left:
        for ring in rings_a:
            ring.step()
        small = hop_beside(small, rings_a[0])
    for hop in hops:
        small = small + hop(small)
    share_c = ring_c.total()
    share_b = ring_b.total()
    share_a = jnp.concatenate([ring.total() for ring in rings_a], axis=1)

    start_grad = jnp.concatenate(
        [
            jnp.where(is_first, d_last, rows[1][0]),
            jnp.where(is_first, rows[1][0], d_last),
        ],
        axis=0,
    )
    skip_sum = jnp.sum(small[6, :E].reshape(MH, MP), axis=1)
    mixer_in_grad = jnp.concatenate([share_a[:, :AT_Q], share_a[:, AT_DT : AT_DT + MH]], axis=1)
    return (
        whole_order(result)[None],
        whole_order(start_grad)[None],
        small[8:9, :D],
        small[9:10, :D],
        small[5:6, :E],
        small[None, :4],
        small[4:5],
        small[7:8, :MH],
        small[7:8, LANES : LANES + MH],
        skip_sum[None],
        mixer_in_grad[None],
        share_c[:, :E].T[None],
        share_a[:, AT_Q:AT_K][None],
        share_a[:, AT_K:AT_V][None],
        share_a[:, AT_V:AT_DT][None],
        share_c[:, E:MIXED].T[None],
        share_b[None],
        share_c[:, MIXED:].T[None],
    )


def solution(mesh):
    dp = mesh.shape["dp"]
    devices = mesh.devices.reshape(mesh.shape["section"], dp // 2, 2)
    paired = Mesh(devices, ("section", "chip", "core"))
    over = ("chip", "core")
    rows = P(over, None)
    small = P("section", None)
    by_row = P("section", over, None)
    by_col = P("section", None, over)
    small_specs = (small, small, small, P("section", None, None), small, small, small, small)
    big_specs = (by_row, by_col, by_row, by_row, by_row, by_col, by_row, by_col)
    in_specs = (rows, rows, rows, P(over)) + small_specs + big_specs
    out_specs = (by_row, by_row) + small_specs + big_specs
    return jax.shard_map(
        per_device, mesh=paired, in_specs=in_specs, out_specs=out_specs, check_vma=False
    )
```

```python
import functools
import math

import jax
import jax.numpy as jnp
from jax import lax
from jax.experimental import pallas as pl
from jax.experimental.pallas import tpu as pltpu
from jax.sharding import Mesh
from jax.sharding import PartitionSpec as P

D = 1024
FF = 2048
MH = 24
MP = 64
NS = 128
AH = 8
KVH = 2
HD = 64
MB = 2
TOK = 256
E = 1536
CH = 1792
HALF = TOK // 2
PAIRS = MH // 2
LANES = 128
SIDE = D // 2
MIB = 2**20
FF_VMEM = 22
FB_VMEM = 20

AT_W = E
AT_Q = E + CH
AT_K = AT_Q + AH * HD
AT_V = AT_K + KVH * HD
AT_DT = AT_V + KVH * HD
WIDE_A = AT_DT + LANES
CUT_A = 16 * LANES
MIXED = E + AH * HD
AT_GU = MIXED
AT_DN = AT_GU + 2 * FF
WIDE_B = AT_DN + FF

highest = lax.Precision.HIGHEST
epsilon = 1e-05
rope_base = 100000000000.0
bf16 = jnp.bfloat16
f32 = jnp.float32


def dot_nn(left, right):
    return lax.dot_general(left, right, (((1,), (0,)), ((), ())), preferred_element_type=f32)


def dot_nt(left, right):
    return lax.dot_general(left, right, (((1,), (1,)), ((), ())), preferred_element_type=f32)


def dot_tn(left, right):
    return lax.dot_general(left, right, (((0,), (0,)), ((), ())), preferred_element_type=f32)


def dot_exact(left, right):
    return lax.dot_general(
        left, right, (((1,), (0,)), ((), ())), precision=highest, preferred_element_type=f32
    )


def softplus(value):
    return jnp.maximum(value, 0.0) + jnp.log1p(jnp.exp(-jnp.abs(value)))


def lane_low(rows):
    return lax.broadcasted_iota(jnp.int32, (rows, LANES), 1) < HD


def rope_halves(rows):
    return (lax.broadcasted_iota(jnp.int32, (rows, LANES), 1) & (HD - 1)) < HD // 2


def rope_turn(tile, cosine, sine):
    swapped = jnp.where(
        rope_halves(tile.shape[0]),
        -pltpu.roll(tile, LANES - HD // 2, 1),
        pltpu.roll(tile, HD // 2, 1),
    )
    return tile * cosine + swapped * sine


def rope_back(tile, cosine, sine):
    swapped = jnp.where(
        rope_halves(tile.shape[0]),
        pltpu.roll(tile, LANES - HD // 2, 1),
        -pltpu.roll(tile, HD // 2, 1),
    )
    return tile * cosine + swapped * sine


def both_halves(tile):
    swapped = pltpu.roll(tile, HD, 1)
    low = lane_low(tile.shape[0])
    return (jnp.where(low, tile, swapped), jnp.where(low, swapped, tile))


def tile_at(index):
    return pl.ds(pl.multiple_of(index * LANES, LANES), LANES)


def tile_from(start, index):
    return pl.ds(pl.multiple_of(start + index * LANES, LANES), LANES)


def allowed_pairs(doc_col_ref, doc_row_ref):
    later = lax.broadcasted_iota(jnp.int32, (TOK, TOK), 0)
    early = lax.broadcasted_iota(jnp.int32, (TOK, TOK), 1)
    same = doc_col_ref[:, 0:1] == doc_row_ref[0:1, :]
    return (later >= early) & same


def pair_rows(tile):
    low = lane_low(tile.shape[0])
    zero = jnp.zeros_like(tile)
    return jnp.concatenate([jnp.where(low, tile, zero), jnp.where(low, zero, tile)], axis=0)


def pair_lanes(rows):
    half = rows.shape[0] // 2
    return jnp.where(lane_low(half), rows[:half], rows[half:])


def core_forward_kernel(
    held, pm_ref, pq_ref, pd_ref, rope_ref, mask_ref, doc_col_ref, doc_row_ref,
    taps_ref, head_ref, wide_ref, *refs,
):
    xb_ref, pre_ref, yns_ref, conv_s, cb_s, bias_s, sum_s = refs[3:] if held else refs

    def conv_tile(index, carry):
        rows = pm_ref[:, tile_from(AT_W, index)].astype(f32)
        at = tile_at(index)
        total = taps_ref[4:5, at] + taps_ref[3:4, at] * rows
        for shift in (1, 2, 3):
            moved = mask_ref[:, (shift - 1) * LANES : shift * LANES] * pltpu.roll(rows, shift, 0)
            total = total + taps_ref[3 - shift : 4 - shift, at] * moved
        total = total.astype(bf16)
        pre_ref[:, at] = total
        total = total.astype(f32)
        conv_s[:, at] = total * jax.nn.sigmoid(total)
        return carry

    lax.fori_loop(0, CH // LANES, conv_tile, 0)

    allowed = allowed_pairs(doc_col_ref, doc_row_ref)
    bias_s[...] = jnp.where(allowed, 0.0, -1e30)
    steps = softplus(pd_ref[...] + head_ref[0:1, :])
    rates = -steps * head_ref[1:2, :]
    totals = dot_exact(jnp.where(allowed, 1.0, 0.0), rates)
    totals_t = totals.T
    inward = conv_s[:, E : E + NS].astype(bf16)
    outward = conv_s[:, E + NS :].astype(bf16)
    cb_s[...] = jnp.where(allowed, dot_nt(outward, inward), 0.0)
    low = lane_low(TOK)
    for pair in range(PAIRS):
        lanes = slice(pair * LANES, (pair + 1) * LANES)
        first = 2 * pair
        step_pair = jnp.where(low, steps[:, first : first + 1], steps[:, first + 1 : first + 2])
        scaled = (conv_s[:, lanes] * step_pair).astype(bf16)
        mixes = []
        for head in (first, first + 1):
            apart = totals[:, head : head + 1] - totals_t[head : head + 1, :]
            mixes.append((jnp.exp(jnp.minimum(apart, 0.0)) * cb_s[...]).astype(bf16))
        yns_ref[:, lanes] = pair_lanes(dot_nn(jnp.concatenate(mixes, axis=0), scaled))

    sum_s[...] = jnp.zeros((TOK, LANES), f32)

    def gate_tile(index, carry):
        at = tile_at(index)
        gate = pm_ref[:, at].astype(f32)
        rows = yns_ref[:, at] + wide_ref[0:1, at] * conv_s[:, at]
        gated = rows * (gate * jax.nn.sigmoid(gate))
        sum_s[...] += gated * gated
        conv_s[:, at] = gated
        return carry

    lax.fori_loop(0, E // LANES, gate_tile, 0)
    scale = lax.rsqrt(jnp.sum(sum_s[...], axis=1, keepdims=True) * (1.0 / E) + epsilon)

    def norm_tile(index, carry):
        at = tile_at(index)
        xb_ref[:, at] = (conv_s[:, at] * scale * wide_ref[1:2, at]).astype(bf16)
        return carry

    lax.fori_loop(0, E // LANES, norm_tile, 0)

    cosine = rope_ref[:, :LANES]
    sine = rope_ref[:, LANES:]
    keys = both_halves(rope_turn(pq_ref[:, AH * HD : AH * HD + LANES].astype(f32), cosine, sine))
    values = both_halves(pq_ref[:, AH * HD + LANES :].astype(f32))
    keys = tuple(part.astype(bf16) for part in keys)
    values = tuple(part.astype(bf16) for part in values)
    for pair in range(AH // 2):
        group = pair // (AH // (2 * KVH))
        at = pair * LANES
        turned = rope_turn(pq_ref[:, at : at + LANES].astype(f32), cosine, sine)
        scores = dot_nt(pair_rows((turned * (1.0 / math.sqrt(HD))).astype(bf16)), keys[group])
        weights = []
        shares = []
        for part in (scores[:TOK], scores[TOK:]):
            part = part + bias_s[...]
            part = jnp.exp(part - jnp.max(part, axis=1, keepdims=True))
            shares.append(1.0 / jnp.sum(part, axis=1, keepdims=True))
            weights.append(part.astype(bf16))
        out = pair_lanes(dot_nn(jnp.concatenate(weights, axis=0), values[group]))
        out = out * jnp.where(low, shares[0], shares[1])
        xb_ref[:, E + pair * LANES : E + (pair + 1) * LANES] = out.astype(bf16)


def silu_slope(value, gate):
    return gate * (1.0 + value * (1.0 - gate))


def attend_back_kernel(
    pick_ref, pq_ref, dxb_ref, rope_ref, doc_col_ref, doc_row_ref, pg_ref, bias_s
):
    later = lax.broadcasted_iota(jnp.int32, (TOK, TOK), 1)
    early = lax.broadcasted_iota(jnp.int32, (TOK, TOK), 0)
    allowed_t = (later >= early) & (doc_col_ref[:, 0:1] == doc_row_ref[0:1, :])
    bias_s[...] = jnp.where(allowed_t, 0.0, -1e30)
    low = lane_low(TOK)
    cosine = rope_ref[:, :LANES]
    sine = rope_ref[:, LANES:]
    keys = both_halves(rope_turn(pq_ref[:, AH * HD : AH * HD + LANES].astype(f32), cosine, sine))
    values = both_halves(pq_ref[:, AH * HD + LANES :].astype(f32))
    root = 1.0 / math.sqrt(HD)
    d_keys = []
    d_values = []
    for group in range(KVH):
        key = keys[group].astype(bf16)
        key_rows = pair_rows(key)
        value_rows = pair_rows(values[group].astype(bf16))
        d_key = jnp.zeros((TOK, LANES), f32)
        d_value = jnp.zeros((TOK, LANES), f32)
        for pair in range(group * (AH // (2 * KVH)), (group + 1) * (AH // (2 * KVH))):
            at = pair * LANES
            turned = rope_turn(pq_ref[:, at : at + LANES].astype(f32), cosine, sine) * root
            query = turned.astype(bf16)
            d_out = dxb_ref[:, E + at : E + at + LANES].astype(bf16)
            scores = dot_nt(key_rows, query)
            d_weights = dot_nt(value_rows, d_out)
            weights = []
            d_scores = []
            for part in (slice(0, TOK), slice(TOK, 2 * TOK)):
                score = scores[part] + bias_s[...]
                weight = jnp.exp(score - jnp.max(score, axis=0, keepdims=True))
                weight = weight * (1.0 / jnp.sum(weight, axis=0, keepdims=True))
                d_weight = d_weights[part]
                offset = jnp.sum(weight * d_weight, axis=0, keepdims=True)
                weights.append(weight.astype(bf16))
                d_scores.append((weight * (d_weight - offset)).astype(bf16))
            d_value = d_value + pair_lanes(dot_nn(jnp.concatenate(weights, axis=0), d_out))
            d_key = d_key + pair_lanes(dot_nn(jnp.concatenate(d_scores, axis=0), query))
            d_query = pair_lanes(dot_tn(jnp.concatenate(d_scores, axis=1), key))
            pg_ref[:, at : at + LANES] = rope_back(d_query * root, cosine, sine).astype(bf16)
        d_keys.append(d_key + pltpu.roll(d_key, HD, 1))
        d_values.append(d_value + pltpu.roll(d_value, HD, 1))
    d_key = rope_back(jnp.where(low, d_keys[0], d_keys[1]), cosine, sine)
    pg_ref[:, AH * HD : AH * HD + LANES] = d_key.astype(bf16)
    pg_ref[:, AH * HD + LANES :] = jnp.where(low, d_values[0], d_values[1]).astype(bf16)


def mixer_back_kernel(
    pick_ref, pm_ref, pd_ref, pre_ref, yns_ref, dxb_ref, attend_ref, mask_ref, doc_col_ref,
    doc_row_ref, taps_ref, head_ref, wide_ref,
    pg_ref, small_ref,
    x_s, dx_s, dyb_s, cbt_s, dcbt_s, sum_s, ssum_s,
):
    small_ref[...] = jnp.zeros_like(small_ref)
    pg_ref[:, AT_Q:AT_DT] = attend_ref[...]
    sum_s[...] = jnp.zeros((TOK, LANES), f32)
    ssum_s[...] = jnp.zeros((TOK, LANES), f32)

    def start_tile(index, carry):
        at = tile_at(index)
        pre = pre_ref[:, at].astype(f32)
        heads_in = pre * jax.nn.sigmoid(pre)
        x_s[:, at] = heads_in
        gate = pm_ref[:, at].astype(f32)
        rows = yns_ref[:, at] + wide_ref[0:1, at] * heads_in
        gated = rows * (gate * jax.nn.sigmoid(gate))
        sum_s[...] += gated * gated
        ssum_s[...] += dxb_ref[:, at] * wide_ref[1:2, at] * gated
        return carry

    lax.fori_loop(0, E // LANES, start_tile, 0)
    scale = lax.rsqrt(jnp.sum(sum_s[...], axis=1, keepdims=True) * (1.0 / E) + epsilon)
    pull = jnp.sum(ssum_s[...], axis=1, keepdims=True) * (1.0 / E) * scale * scale * scale

    def gate_tile(index, carry):
        at = tile_at(index)
        heads_in = x_s[:, at]
        skip = wide_ref[0:1, at]
        gate = pm_ref[:, at].astype(f32)
        opened = jax.nn.sigmoid(gate)
        rows = yns_ref[:, at] + skip * heads_in
        gated = rows * (gate * opened)
        arrived = dxb_ref[:, at]
        d_gated = scale * (arrived * wide_ref[1:2, at]) - gated * pull
        small_ref[5:6, at] = jnp.sum(arrived * gated * scale, axis=0, keepdims=True)
        d_rows = d_gated * (gate * opened)
        pg_ref[:, at] = (d_gated * rows * silu_slope(gate, opened)).astype(bf16)
        small_ref[6:7, at] = jnp.sum(d_rows * heads_in, axis=0, keepdims=True)
        dyb_s[:, at] = d_rows.astype(bf16)
        dx_s[:, at] = skip * d_rows
        return carry

    lax.fori_loop(0, E // LANES, gate_tile, 0)

    def state_tile(index, carry):
        at = tile_from(E, index)
        pre = pre_ref[:, at].astype(f32)
        x_s[:, at] = pre * jax.nn.sigmoid(pre)
        return carry

    lax.fori_loop(0, 2, state_tile, 0)

    later = lax.broadcasted_iota(jnp.int32, (TOK, TOK), 1)
    early = lax.broadcasted_iota(jnp.int32, (TOK, TOK), 0)
    allowed_t = (later >= early) & (doc_col_ref[:, 0:1] == doc_row_ref[0:1, :])
    allowed = allowed_pairs(doc_col_ref, doc_row_ref)
    raw = pd_ref[...] + head_ref[0:1, :]
    steps = softplus(raw)
    decay = head_ref[1:2, :]
    rates = -steps * decay
    totals = dot_exact(jnp.where(allowed, 1.0, 0.0), rates)
    totals_t = totals.T
    inward = x_s[:, E : E + NS].astype(bf16)
    outward = x_s[:, E + NS :].astype(bf16)
    cbt_s[...] = jnp.where(allowed_t, dot_nt(inward, outward), 0.0)
    dcbt_s[...] = jnp.zeros((TOK, TOK), f32)
    low = lane_low(TOK)
    spread_row = lax.broadcasted_iota(jnp.int32, (2 * LANES, LANES), 0) // HD
    spread_col = lax.broadcasted_iota(jnp.int32, (2 * LANES, LANES), 1)
    sum_s[...] = jnp.zeros((TOK, LANES), f32)
    ssum_s[...] = jnp.zeros((TOK, LANES), f32)
    waiting = None
    for pair in range(PAIRS):
        lanes = slice(pair * LANES, (pair + 1) * LANES)
        first = 2 * pair
        step_pair = jnp.where(low, steps[:, first : first + 1], steps[:, first + 1 : first + 2])
        heads_in = x_s[:, lanes]
        scaled = (heads_in * step_pair).astype(bf16)
        d_rows = dyb_s[:, lanes]
        d_mix = dot_nt(pair_rows(scaled), d_rows)
        mixes = []
        d_pairs = None
        for side, head in enumerate((first, first + 1)):
            apart = totals_t[head : head + 1, :] - totals[:, head : head + 1]
            decays = jnp.exp(jnp.minimum(apart, 0.0))
            mixes.append((decays * cbt_s[...]).astype(bf16))
            part = d_mix[side * TOK : (side + 1) * TOK] * decays
            d_pairs = part if d_pairs is None else d_pairs + part
        dcbt_s[...] += d_pairs
        d_scaled = pair_lanes(dot_nn(jnp.concatenate(mixes, axis=0), d_rows))
        dx_s[:, lanes] += d_scaled * step_pair
        value = d_rows.astype(f32) * yns_ref[:, lanes] - scaled.astype(f32) * d_scaled
        coarse = value.astype(bf16)
        fine = (value - coarse.astype(f32)).astype(bf16)
        spread = (spread_col == first + (spread_row & 1)).astype(bf16)
        ssum_s[...] += dot_nn(jnp.concatenate([coarse, fine], axis=1), spread)
        value = (d_scaled * heads_in).astype(bf16)
        if pair % 2 == 0:
            waiting = value
        else:
            spread = (spread_col == first - 2 + spread_row).astype(bf16)
            sum_s[...] += dot_nn(jnp.concatenate([waiting, value], axis=1), spread)

    d_rates = dot_exact(jnp.where(allowed_t, 1.0, 0.0), ssum_s[...])
    d_steps = sum_s[...] - decay * d_rates
    d_raw = d_steps * jax.nn.sigmoid(raw)
    pg_ref[:, AT_DT:] = d_raw.astype(bf16)
    small_ref[7:8, :LANES] = jnp.sum(d_raw, axis=0, keepdims=True)
    small_ref[7:8, LANES : 2 * LANES] = jnp.sum(d_rates * rates, axis=0, keepdims=True)
    d_pairs = jnp.where(allowed_t, dcbt_s[...], 0.0).astype(bf16)
    dx_s[:, E : E + NS] = dot_nn(d_pairs, outward)
    dx_s[:, E + NS :] = dot_tn(d_pairs, inward)

    def conv_tile(index, carry):
        at = tile_at(index)
        pre = pre_ref[:, at].astype(f32)
        d_pre = dx_s[:, at] * silu_slope(pre, jax.nn.sigmoid(pre))
        rows = pm_ref[:, tile_from(AT_W, index)].astype(f32)
        small_ref[4:5, at] = jnp.sum(d_pre, axis=0, keepdims=True)
        small_ref[3:4, at] = jnp.sum(d_pre * rows, axis=0, keepdims=True)
        back = taps_ref[3:4, at] * d_pre
        for shift in (1, 2, 3):
            held = mask_ref[:, (shift - 1) * LANES : shift * LANES] * d_pre
            small_ref[3 - shift : 4 - shift, at] = jnp.sum(
                held * pltpu.roll(rows, shift, 0), axis=0, keepdims=True
            )
            back = back + taps_ref[3 - shift : 4 - shift, at] * pltpu.roll(held, TOK - shift, 0)
        pg_ref[:, tile_from(AT_W, index)] = back.astype(bf16)
        return carry

    lax.fori_loop(0, CH // LANES, conv_tile, 0)


def whole_block(shape):
    return pl.BlockSpec(shape, lambda *steps: (0,) * len(shape))


def once(shape, place):
    return pl.BlockSpec(shape, place, pipeline_mode=pl.Buffered(1))


def core_forward(row, projected, layout, params, held=()):
    operands = (*projected, *layout)

    def block(array):
        return once((None,) + array.shape[1:], lambda step: (row, 0, 0))

    outs = [
        jax.ShapeDtypeStruct((MB, TOK, MIXED), bf16),
        jax.ShapeDtypeStruct((MB, TOK, CH), bf16),
        jax.ShapeDtypeStruct((MB, TOK, E), f32),
    ]
    return pl.pallas_call(
        functools.partial(core_forward_kernel, bool(held)),
        grid=(1,),
        in_specs=[block(array) for array in operands]
        + [once(array.shape, lambda step: (0, 0)) for array in params]
        + [pl.BlockSpec(memory_space=pl.ANY)] * len(held),
        out_specs=[block(array) for array in outs],
        out_shape=outs,
        scratch_shapes=[
            pltpu.VMEM((TOK, CH), f32),
            pltpu.VMEM((TOK, TOK), f32),
            pltpu.VMEM((TOK, TOK), f32),
            pltpu.VMEM((TOK, LANES), f32),
        ],
        input_output_aliases={10: 0, 11: 1, 12: 2} if held else {},
        compiler_params=pltpu.CompilerParams(vmem_limit_bytes=12 * MIB),
        cost_estimate=pl.CostEstimate(
            flops=4 * 10**8, bytes_accessed=12 * 2**20, transcendentals=10**6
        ),
        name="core_forward",
    )(*operands, *params, *held)


def core_back_specs(by_row, plain):
    return [
        once((None,) + array.shape[1:], lambda step, pick: (pick[0], 0, 0)) if chosen
        else once(array.shape, lambda step, pick: (0, 0))
        for chosen, arrays in ((True, by_row), (False, plain))
        for array in arrays
    ]


def attend_back(row, projected, d_mixed, layout):
    rope, masks, doc_cols, doc_rows = layout
    return pl.pallas_call(
        attend_back_kernel,
        grid_spec=pltpu.PrefetchScalarGridSpec(
            num_scalar_prefetch=1,
            grid=(1,),
            in_specs=core_back_specs([projected[1]], [d_mixed])
            + core_back_specs([rope, doc_cols, doc_rows], []),
            out_specs=once((TOK, AT_DT - AT_Q), lambda step, pick: (0, 0)),
            scratch_shapes=[pltpu.VMEM((TOK, TOK), f32)],
        ),
        out_shape=jax.ShapeDtypeStruct((TOK, AT_DT - AT_Q), bf16),
        compiler_params=pltpu.CompilerParams(vmem_limit_bytes=6 * MIB),
        cost_estimate=pl.CostEstimate(
            flops=3 * 10**8, bytes_accessed=4 * 2**20, transcendentals=6 * 10**5
        ),
        name="attend_back",
    )(row, projected[1], d_mixed, rope, doc_cols, doc_rows)


def mixer_back(row, projected, pre, yns, d_mixed, attended, layout, params):
    rope, masks, doc_cols, doc_rows = layout
    return pl.pallas_call(
        mixer_back_kernel,
        grid_spec=pltpu.PrefetchScalarGridSpec(
            num_scalar_prefetch=1,
            grid=(1,),
            in_specs=core_back_specs(
                [projected[0], projected[2], pre, yns], [d_mixed, attended]
            )
            + core_back_specs([masks, doc_cols, doc_rows], params),
            out_specs=[
                once((TOK, WIDE_A), lambda step, pick: (0, 0)),
                once((8, CH), lambda step, pick: (0, 0)),
            ],
            scratch_shapes=[
                pltpu.VMEM((TOK, CH), f32),
                pltpu.VMEM((TOK, CH), f32),
                pltpu.VMEM((TOK, E), bf16),
                pltpu.VMEM((TOK, TOK), f32),
                pltpu.VMEM((TOK, TOK), f32),
                pltpu.VMEM((TOK, LANES), f32),
                pltpu.VMEM((TOK, LANES), f32),
            ],
        ),
        out_shape=[
            jax.ShapeDtypeStruct((TOK, WIDE_A), bf16),
            jax.ShapeDtypeStruct((8, CH), f32),
        ],
        compiler_params=pltpu.CompilerParams(vmem_limit_bytes=15 * MIB),
        cost_estimate=pl.CostEstimate(
            flops=7 * 10**8, bytes_accessed=10 * 2**20, transcendentals=15 * 10**5
        ),
        name="mixer_back",
    )(
        row, projected[0], projected[2], pre, yns, d_mixed, attended, masks, doc_cols, doc_rows,
        *params,
    )


def passed_along(value, axis, steps):
    count = lax.axis_size(axis)
    leading, last = (max(0, -steps), min(count, count - steps))
    return lax.ppermute(value, axis, [(source, source + steps) for source in range(leading, last)])


def norm_rows(values):
    return lax.rsqrt(jnp.mean(values * values, axis=-1, keepdims=True) + epsilon)


def norm_back(values, gain, arrived):
    scale = norm_rows(values)
    weighted = arrived * gain
    pull = jnp.mean(weighted * values, axis=-1, keepdims=True) * scale * scale * scale
    gain_grad = jnp.sum(arrived * values * scale, axis=0, keepdims=True)
    return (weighted * scale - values * pull, gain_grad)


def project_kernel(rows_ref, gain_ref, own_ref, other_ref, *refs):
    normed_ref, pm_ref, pq_ref, pd_ref = refs[-4:]
    step = pl.program_id(0)

    @pl.when(step == 0)
    def _():
        rows = rows_ref[...].astype(f32)
        normed_ref[...] = (rows * norm_rows(rows) * gain_ref[...]).astype(bf16)

    out = dot_nn(normed_ref[:, :SIDE], own_ref[...]) + dot_nn(normed_ref[:, SIDE:], other_ref[...])
    tile = WIDE_A // 3
    for index in range(2):
        @pl.when(step == index)
        def _(index=index):
            pm_ref[:, index * tile : (index + 1) * tile] = out.astype(bf16)

    @pl.when(step == 2)
    def _():
        pm_ref[:, 2 * tile :] = out[:, : AT_Q - 2 * tile].astype(bf16)
        pq_ref[...] = out[:, AT_Q - 2 * tile : AT_DT - 2 * tile].astype(bf16)
        pd_ref[...] = out[:, AT_DT - 2 * tile :]


def project(rows, gain, own, other, row=None, held=()):
    count = rows.shape[0]
    tile = WIDE_A // 3
    weight = pl.BlockSpec((SIDE, tile), lambda step: (0, step))
    at = row or 0
    total = count if row is None else MB * TOK
    widths = ((D, bf16), (AT_Q, bf16), (AT_DT - AT_Q, bf16), (LANES, f32))
    return pl.pallas_call(
        project_kernel,
        grid=(3,),
        in_specs=[whole_block((count, D)), whole_block((1, D)), weight, weight]
        + [pl.BlockSpec(memory_space=pl.ANY)] * len(held),
        out_specs=[pl.BlockSpec((count, width), lambda step: (at, 0)) for width, _ in widths],
        out_shape=[jax.ShapeDtypeStruct((total, width), kind) for width, kind in widths],
        input_output_aliases={4 + index: index for index in range(len(held))},
        compiler_params=pltpu.CompilerParams(vmem_limit_bytes=15 * MIB),
        cost_estimate=pl.CostEstimate(
            flops=2 * count * D * WIDE_A,
            bytes_accessed=2 * D * WIDE_A + 2 * count * WIDE_A,
            transcendentals=0,
        ),
        name="project",
    )(rows, gain, own, other, *held)


def by_row(projected):
    return tuple(array.reshape(MB, TOK, -1) for array in projected[1:])


def feed_forward_kernel(
    keep, rows_ref, mixed_ref, gain_ref,
    out_own, out_other, gate_own, gate_other, up_own, up_other, down_own, down_other,
    *refs,
):
    if keep:
        low_ref, middle_ref, normed_ref, gate_ref, up_ref, act_ref, total_s = refs[-7:]
    else:
        low_ref, middle_ref, normed_ref, total_s = refs
    step = pl.program_id(0)

    @pl.when(step == 0)
    def _():
        middle_ref[...] = rows_ref[...].astype(f32)

    @pl.when(step < 4)
    def _():
        mixed = mixed_ref[...]
        middle_ref[:, :SIDE] += dot_nt(mixed, out_own[...])
        middle_ref[:, SIDE:] += dot_nt(mixed, out_other[...])

    @pl.when(step == 3)
    def _():
        middle = middle_ref[...]
        normed_ref[...] = (middle * norm_rows(middle) * gain_ref[...]).astype(bf16)
        total_s[...] = middle

    @pl.when(step >= 4)
    def _():
        left = normed_ref[:, :SIDE]
        right = normed_ref[:, SIDE:]
        gate = dot_nn(left, gate_own[...]) + dot_nn(right, gate_other[...])
        up = dot_nn(left, up_own[...]) + dot_nn(right, up_other[...])
        act = (gate * jax.nn.sigmoid(gate) * up).astype(bf16)
        if keep:
            gate_ref[...] = gate.astype(bf16)
            up_ref[...] = up.astype(bf16)
            act_ref[...] = act
        total_s[:, :SIDE] += dot_nt(act, down_own[...])
        total_s[:, SIDE:] += dot_nt(act, down_other[...])

    @pl.when(step == 7)
    def _():
        low_ref[...] = total_s[...].astype(bf16)


def pinned(own, other):
    return [
        pltpu.with_memory_space_constraint(own, pltpu.VMEM),
        pltpu.with_memory_space_constraint(other, pltpu.HBM),
    ]


def b_block(start, skipped):
    return pl.BlockSpec(
        (SIDE, 512), lambda step, *pick: (0, start + jnp.clip(step - skipped, 0, 3))
    )


def b_blocks(parts):
    return [b_block(start, skipped) for start, skipped in parts for _ in range(2)]


def feed_forward(row, rows, mixed, gain, own, other, held=None):
    keep = held is not None
    at = row if rows.shape[0] > TOK else 0

    def late(step):
        return (row, jnp.clip(step - 4, 0, 3))

    wide = pl.BlockSpec((TOK, 512), late)
    full = pl.BlockSpec((TOK, D), lambda step: (row, 0))
    scratch = [pltpu.VMEM((TOK, D), f32)]
    if keep:
        out_specs = [full, full, full, wide, wide, wide]
        out_shape = [
            pltpu.HBM((MB * TOK, width), kind)
            for width, kind in ((D, bf16), (D, f32), (D, bf16), (FF, bf16), (FF, bf16), (FF, bf16))
        ]
    else:
        out_specs = [whole_block((TOK, D))]
        out_shape = [jax.ShapeDtypeStruct((TOK, D), bf16)]
        scratch = [pltpu.VMEM((TOK, D), f32), pltpu.VMEM((TOK, D), bf16)] + scratch
    held = tuple(pltpu.with_memory_space_constraint(one, pltpu.HBM) for one in held or ())
    return pl.pallas_call(
        functools.partial(feed_forward_kernel, keep),
        grid=(8,),
        in_specs=[
            pl.BlockSpec((TOK, D), lambda step: (at, 0)),
            pl.BlockSpec((TOK, 512), lambda step: (row, jnp.clip(step, 0, 3))),
            whole_block((1, D)),
        ]
        + b_blocks(((0, 0), (4, 4), (8, 4), (12, 4)))
        + [pl.BlockSpec(memory_space=pl.ANY)] * len(held),
        out_specs=out_specs,
        out_shape=out_shape,
        scratch_shapes=scratch,
        input_output_aliases={11 + index: index for index in range(len(held))},
        compiler_params=pltpu.CompilerParams(vmem_limit_bytes=(FF_VMEM if keep else 18) * MIB),
        cost_estimate=pl.CostEstimate(
            flops=2 * TOK * D * WIDE_B, bytes_accessed=2 * D * WIDE_B, transcendentals=0
        ),
        name="feed_forward",
    )(rows, mixed, gain, *((pinned(own, other) if keep else [own, other]) * 4), *held)


def feed_back_kernel(
    pick_ref, cot_ref, gate_ref, up_ref, middle_ref, gain_ref,
    down_own, down_other, gate_own, gate_other, up_own, up_other, out_own, out_other,
    d_gate_ref, d_up_ref, d_middle_ref, low_ref, d_mixed_ref, gain_grad_ref,
    total_s,
):
    step = pl.program_id(0)

    @pl.when(step == 0)
    def _():
        total_s[...] = jnp.zeros_like(total_s)

    @pl.when(step < 4)
    def _():
        arrived = dot_nn(cot_ref[:, :SIDE], down_own[...]) + dot_nn(
            cot_ref[:, SIDE:], down_other[...]
        )
        gate = gate_ref[...].astype(f32)
        opened = jax.nn.sigmoid(gate)
        d_gate = (arrived * up_ref[...].astype(f32) * silu_slope(gate, opened)).astype(bf16)
        d_up = (arrived * (gate * opened)).astype(bf16)
        d_gate_ref[...] = d_gate
        d_up_ref[...] = d_up
        total_s[:, :SIDE] += dot_nt(d_gate, gate_own[...]) + dot_nt(d_up, up_own[...])
        total_s[:, SIDE:] += dot_nt(d_gate, gate_other[...]) + dot_nt(d_up, up_other[...])

    @pl.when(step == 3)
    def _():
        d_norm, gain_grad = norm_back(middle_ref[...], gain_ref[...], total_s[...])
        d_middle = cot_ref[...].astype(f32) + d_norm
        d_middle_ref[...] = d_middle
        low_ref[...] = d_middle.astype(bf16)
        gain_grad_ref[...] = gain_grad

    @pl.when(step >= 4)
    def _():
        d_mixed_ref[...] = dot_nn(low_ref[:, :SIDE], out_own[...]) + dot_nn(
            low_ref[:, SIDE:], out_other[...]
        )


def feed_back(row, cotangent, gate, up, middle, gain, own, other):
    saved = pl.BlockSpec((TOK, 512), lambda step, pick: (pick[0], jnp.clip(step, 0, 3)))
    early = pl.BlockSpec((TOK, 512), lambda step, pick: (0, jnp.clip(step, 0, 3)))
    late = pl.BlockSpec((TOK, 512), lambda step, pick: (0, jnp.clip(step - 4, 0, 3)))
    full = pl.BlockSpec((TOK, D), lambda step, pick: (0, 0))
    gain_block = pl.BlockSpec((1, D), lambda step, pick: (0, 0))
    return pl.pallas_call(
        feed_back_kernel,
        grid_spec=pltpu.PrefetchScalarGridSpec(
            num_scalar_prefetch=1,
            grid=(8,),
            in_specs=[
                full,
                saved,
                saved,
                pl.BlockSpec((TOK, D), lambda step, pick: (pick[0], 0)),
                gain_block,
            ]
            + b_blocks(((12, 0), (4, 0), (8, 0), (0, 4))),
            out_specs=[early, early, full, full, late, gain_block],
            scratch_shapes=[pltpu.VMEM((TOK, D), f32)],
        ),
        out_shape=[
            jax.ShapeDtypeStruct((TOK, FF), bf16),
            jax.ShapeDtypeStruct((TOK, FF), bf16),
            jax.ShapeDtypeStruct((TOK, D), f32),
            jax.ShapeDtypeStruct((TOK, D), bf16),
            jax.ShapeDtypeStruct((TOK, MIXED), f32),
            jax.ShapeDtypeStruct((1, D), f32),
        ],
        compiler_params=pltpu.CompilerParams(vmem_limit_bytes=FB_VMEM * MIB),
        cost_estimate=pl.CostEstimate(
            flops=2 * TOK * D * WIDE_B, bytes_accessed=2 * D * WIDE_B, transcendentals=0
        ),
        name="feed_back",
    )(
        row, cotangent, *(pltpu.with_memory_space_constraint(one, pltpu.HBM) for one in (gate, up)),
        pltpu.with_memory_space_constraint(middle, pltpu.HBM), gain, *(pinned(own, other) * 4),
    )


def project_back_kernel(
    pick_ref, grad_ref, rows_ref, d_middle_ref, gain_ref, own_ref, other_ref,
    d_rows_ref, low_ref, gain_grad_ref, total_s,
):
    step = pl.program_id(0)

    @pl.when(step == 0)
    def _():
        total_s[...] = jnp.zeros_like(total_s)

    total_s[:, :SIDE] += dot_nt(grad_ref[...], own_ref[...])
    total_s[:, SIDE:] += dot_nt(grad_ref[...], other_ref[...])

    @pl.when(step == 2)
    def _():
        d_norm, gain_grad = norm_back(rows_ref[...].astype(f32), gain_ref[...], total_s[...])
        d_rows = d_middle_ref[...] + d_norm
        d_rows_ref[...] = d_rows
        low_ref[...] = d_rows.astype(bf16)
        gain_grad_ref[...] = gain_grad


def project_back(row, proj_low, start_rows, d_middle, gain, own, other):
    tile = WIDE_A // 3
    weight = pl.BlockSpec((SIDE, tile), lambda step, pick: (0, step))
    full = pl.BlockSpec((TOK, D), lambda step, pick: (0, 0))
    gain_block = pl.BlockSpec((1, D), lambda step, pick: (0, 0))
    return pl.pallas_call(
        project_back_kernel,
        grid_spec=pltpu.PrefetchScalarGridSpec(
            num_scalar_prefetch=1,
            grid=(3,),
            in_specs=[
                pl.BlockSpec((TOK, tile), lambda step, pick: (0, step)),
                pl.BlockSpec((TOK, D), lambda step, pick: (pick[0], 0)),
                full,
                gain_block,
                weight,
                weight,
            ],
            out_specs=[full, full, gain_block],
            scratch_shapes=[pltpu.VMEM((TOK, D), f32)],
        ),
        out_shape=[
            jax.ShapeDtypeStruct((TOK, D), f32),
            jax.ShapeDtypeStruct((TOK, D), bf16),
            jax.ShapeDtypeStruct((1, D), f32),
        ],
        compiler_params=pltpu.CompilerParams(vmem_limit_bytes=15 * MIB),
        cost_estimate=pl.CostEstimate(
            flops=2 * TOK * D * WIDE_A, bytes_accessed=2 * D * WIDE_A, transcendentals=0
        ),
        name="project_back",
    )(row, proj_low, start_rows, d_middle, gain, own, other)


def weight_grad_kernel(groups, pick_ref, *refs):
    lefts = refs[: 4 * len(groups)]
    rights = refs[4 * len(groups) : 8 * len(groups)]
    sum_ref, left_s = refs[8 * len(groups) :]
    step = pl.program_id(0)
    for index, (start, count) in enumerate(groups):
        four = lefts[4 * index : 4 * index + 4]
        blocks = rights[4 * index : 4 * index + 4]

        @pl.when(step == start)
        def _(four=four):
            for place, ref in enumerate(four):
                left_s[:, place * TOK : (place + 1) * TOK] = ref[...].astype(f32).T.astype(bf16)

        @pl.when((step >= start) & (step < start + count))
        def _(blocks=blocks):
            right = jnp.concatenate([ref[...] for ref in blocks], axis=0)
            sum_ref[...] = dot_nn(left_s[...], right).astype(bf16)


def weight_grad(picks, tile, groups):
    steps = []
    in_left = []
    in_right = []
    operands_left = []
    operands_right = []
    start = 0
    for left, right in groups:
        count = right[0][0].shape[1] // tile
        steps.append((start, count))
        for array, which, column in left:
            in_left.append(
                pl.BlockSpec(
                    (TOK, SIDE),
                    lambda step, pick, which=which, column=column: (
                        0 if which is None else pick[which],
                        column,
                    ),
                )
            )
            operands_left.append(array)
        for array, which in right:
            in_right.append(
                pl.BlockSpec(
                    (TOK, tile),
                    lambda step, pick, which=which, start=start, count=count: (
                        0 if which is None else pick[which],
                        jnp.clip(step - start, 0, count - 1),
                    ),
                )
            )
            operands_right.append(array)
        start += count
    return pl.pallas_call(
        functools.partial(weight_grad_kernel, tuple(steps)),
        grid_spec=pltpu.PrefetchScalarGridSpec(
            num_scalar_prefetch=1,
            grid=(start,),
            in_specs=in_left + in_right,
            out_specs=pl.BlockSpec((SIDE, tile), lambda step, pick: (0, step)),
            scratch_shapes=[pltpu.VMEM((SIDE, 4 * TOK), bf16)],
        ),
        out_shape=jax.ShapeDtypeStruct((SIDE, start * tile), bf16),
        compiler_params=pltpu.CompilerParams(vmem_limit_bytes=16 * MIB),
        cost_estimate=pl.CostEstimate(
            flops=8 * TOK * SIDE * start * tile,
            bytes_accessed=4 * SIDE * start * tile,
            transcendentals=0,
        ),
        name="weight_grad",
    )(picks, *operands_left, *operands_right)


def row_layout(doc_ids):
    rows = doc_ids.shape[0]
    positions = jnp.arange(TOK, dtype=jnp.int32)
    earlier = jnp.sum((doc_ids[:, None, :] < doc_ids[:, :, None]).astype(jnp.int32), axis=2)
    places = positions[None, :] - earlier
    half_dim = HD // 2
    inverse_freq = rope_base ** (-jnp.arange(half_dim, dtype=f32) / half_dim)
    angles = places.astype(f32)[:, :, None] * inverse_freq[None, None, :]
    repeats = LANES // half_dim
    rope = jnp.concatenate([jnp.cos(angles)] * repeats + [jnp.sin(angles)] * repeats, axis=-1)
    masks = jnp.concatenate(
        [
            jnp.broadcast_to((places >= shift).astype(f32)[:, :, None], (rows, TOK, LANES))
            for shift in (1, 2, 3)
        ],
        axis=-1,
    )
    doc_cols = jnp.broadcast_to(doc_ids[:, :, None], (rows, TOK, LANES))
    doc_rows = jnp.broadcast_to(doc_ids[:, None, :], (rows, 8, TOK))
    return (rope, masks, doc_cols, doc_rows)


def core_params(conv_weight, conv_bias, step_bias, decay_log, skip_scale, mixer_gain):
    taps = jnp.concatenate([conv_weight, conv_bias[None], jnp.zeros((3, CH), f32)], axis=0)
    heads = jnp.zeros((8, LANES), f32)
    heads = heads.at[0, :MH].set(step_bias).at[1, :MH].set(jnp.exp(decay_log))
    wide = jnp.concatenate(
        [jnp.repeat(skip_scale, MP)[None], mixer_gain[None], jnp.zeros((6, E), f32)], axis=0
    )
    return (taps, heads, wide)


def swapped(value):
    return lax.ppermute(value, "core", [(0, 1), (1, 0)])


def ring_order(chips):
    return [2 * step for step in range(chips // 2)] + [
        2 * step + 1 for step in reversed(range(chips // 2))
    ]


def ring_place(chip, chips):
    return jnp.where(chip % 2 == 0, chip // 2, chips - 1 - chip // 2)


def onward(value, steps):
    order = ring_order(lax.axis_size("chip"))
    chips = len(order)
    return lax.ppermute(
        value, "chip", [(order[at], order[(at + steps) % chips]) for at in range(chips)]
    )


def slot_offsets(chips):
    offsets = [0]
    for far in range(1, chips // 2):
        offsets += [-far, far]
    return offsets + [chips // 2]


def tied(*values):
    return lax.optimization_barrier(values)


class RingGather:
    def __init__(self, shard):
        self.slots = [shard]
        self.ahead = self.back = shard
        self.left = lax.axis_size("chip") // 2

    def operands(self):
        half = self.ahead.shape[0] // 2
        if self.left == 1:
            return self.ahead[:half], self.back[half:]
        return self.ahead, self.back

    def send(self, ahead, back):
        self.ahead, self.back = tied(onward(ahead, 1), onward(back, -1))
        self.slots += [self.ahead, self.back]
        self.left -= 1
        return self.ahead

    def step(self):
        return self.send(*self.operands())

    def last(self):
        while self.left > 1:
            self.step()

    def hold(self, value):
        self.ahead, self.back, _ = tied(self.ahead, self.back, value)
        self.slots[-2:] = [self.ahead, self.back]


class RingReduce:
    def __init__(self, sums):
        self.sums = sums
        self.chips = lax.axis_size("chip")
        self.size = sums.shape[0] // self.chips
        self.left = self.chips // 2
        self.ahead = self.back = None

    def slot(self, index, start=0, stop=None):
        stop = self.size if stop is None else stop
        return self.sums[index * self.size + start : index * self.size + stop]

    def operands(self):
        half = self.size // 2
        if self.ahead is None:
            last = self.chips - 1
            return self.slot(last, 0, half), self.slot(last, half)
        ahead, back = self.ahead.astype(f32), self.back.astype(f32)
        if self.left == self.chips // 2 - 1:
            ahead = jnp.pad(ahead, ((0, half), (0, 0)))
            back = jnp.pad(back, ((half, 0), (0, 0)))
        return (
            (self.slot(2 * self.left).astype(f32) + ahead).astype(bf16),
            (self.slot(2 * self.left - 1).astype(f32) + back).astype(bf16),
        )

    def send(self, ahead, back):
        self.ahead, self.back = tied(onward(ahead, 1), onward(back, -1))
        self.left -= 1
        return self.ahead

    def step(self):
        return self.send(*self.operands())

    def hold(self, value):
        self.ahead, self.back, _ = tied(self.ahead, self.back, value)

    def columns(self, start, stop):
        part = RingReduce(self.sums[:, start:stop])
        part.left = self.left
        part.ahead, part.back = self.ahead[:, start:stop], self.back[:, start:stop]
        return part

    def total(self):
        while self.left > 0:
            self.step()
        return self.slot(0).astype(f32) + self.ahead.astype(f32) + self.back.astype(f32)


def small_hops(chips):
    if chips & (chips - 1):
        return [lambda value: lax.psum(value, ("chip", "core")) - value]
    hops = [swapped]
    for bit in range(chips.bit_length() - 1):
        pairs = [(chip, chip ^ (1 << bit)) for chip in range(chips)]
        hops.append(lambda value, pairs=pairs: lax.ppermute(value, "chip", pairs))
    return hops


def ring_columns(core):
    chips = lax.axis_size("chip")
    place = ring_place(lax.axis_index("chip"), chips)
    own = []
    for offset in slot_offsets(chips):
        at = (place + offset) % chips
        own.append(jnp.where(at < chips // 2, 2 * at, 2 * (chips - 1 - at) + 1))
    own = jnp.stack(own)
    width = D // (2 * chips)
    starts = jnp.concatenate([2 * own + core, 2 * own + 1 - core]) * width
    wanted = (starts[:, None] + jnp.arange(width)[None, :]).reshape(D)
    return (jnp.arange(D)[:, None] == wanted[None, :]).astype(bf16)


def per_device(
    inputs, out_grad, doc_ids, row_live, pre_gain, mlp_gain, mixer_gain, conv_weight, conv_bias,
    step_bias, decay_log, skip_scale, mixer_in_weight, mixer_out_weight, query_weight, key_weight,
    value_weight, attend_weight, gate_up_weight, down_weight,
):
    is_first = lax.axis_index("section") == 0
    core = lax.axis_index("core")
    shard = mixer_in_weight.shape[1]
    packed_a = jnp.concatenate(
        [
            mixer_in_weight[0, :, :AT_Q],
            query_weight[0],
            key_weight[0],
            value_weight[0],
            mixer_in_weight[0, :, AT_Q:],
            jnp.zeros((shard, LANES - MH), bf16),
        ],
        axis=1,
    )
    packed_b = jnp.concatenate(
        [mixer_out_weight[0].T, attend_weight[0].T, gate_up_weight[0], down_weight[0].T], axis=1
    )

    layout = row_layout(doc_ids)
    params = core_params(
        conv_weight[0], conv_bias[0], step_bias[0], decay_log[0], skip_scale[0], mixer_gain[0]
    )
    turn = ring_columns(core)

    def own_order(values):
        if values.dtype == bf16:
            return dot_nn(values, turn).astype(bf16)
        return dot_exact(values, turn.astype(f32))

    def whole_order(values):
        if values.dtype == bf16:
            return dot_nt(values, turn).astype(bf16)
        return dot_exact(values, turn.astype(f32).T)

    pre_row = own_order(pre_gain)
    mlp_row = own_order(mlp_gain)
    first_rows = own_order(inputs)

    positions = jnp.arange(TOK, dtype=jnp.int32)
    live = (positions[None, :] < row_live[:, None]).reshape(MB * TOK, 1)
    from_loss = own_order(jnp.where(live, out_grad, jnp.zeros_like(out_grad)))
    first_rows, from_loss = tied(first_rows, from_loss)

    ring_a = RingGather(packed_a)
    ring_b = RingGather(packed_b)
    ring_a.step()
    ring_b.step()
    ring_a.last()
    now_a, now_b = tied(ring_a.operands(), ring_b.operands())
    ring_a.send(*now_a)
    ring_b.send(*now_b)
    own_a = jnp.concatenate(ring_a.slots, axis=0)
    pair_a = (own_a, swapped(own_a))
    now_b, gain_now, pair_a = tied(ring_b.operands(), pre_row, pair_a)
    ring_b.send(*now_b)
    projected = by_row(project(first_rows, gain_now, *pair_a))
    mixed = core_forward(0, projected, layout, params)
    ring_b.hold(mixed)
    now_b, mixed = tied(ring_b.operands(), mixed)
    ring_b.send(*now_b)
    mixed, _, _ = core_forward(1, projected, layout, params, held=mixed)
    ring_b.hold(mixed)
    while ring_b.left:
        ring_b.step()
    pair_b = (
        jnp.concatenate(ring_b.slots, axis=0),
        jnp.concatenate([swapped(slot) for slot in ring_b.slots], axis=0),
    )
    mixed = mixed.reshape(MB * TOK, MIXED)
    received = {}
    for row in (1, 0):
        (handed,) = feed_forward(row, first_rows, mixed, mlp_row, *pair_b)
        received[row] = passed_along(handed, "section", 1)

    def second_pass(row, projects=(), cores=(), forwards=()):
        start = jnp.where(is_first, first_rows[row * TOK : (row + 1) * TOK], received[row])
        projects = project(start, pre_row, *pair_a, row=row, held=projects)
        cores = core_forward(row, by_row(projects), layout, params, held=cores)
        mixed = cores[0].reshape(MB * TOK, MIXED)
        forwards = feed_forward(row, start, mixed, mlp_row, *pair_b, held=forwards)
        return start, projects, cores, forwards

    arrived = jnp.zeros((TOK, D), bf16)
    lefts = []
    rights = []
    rows = []
    picks = jnp.where(is_first, jnp.array([1, 0]), jnp.array([0, 1])).astype(jnp.int32)

    def tick_left(which):
        return [(lefts[1][which], None, 0), (lefts[2][which], None, 0)] + [
            (lefts[1][which + 2], None, 0), (lefts[2][which + 2], None, 0)
        ]

    def tick_right(which):
        return [(rights[tick][which + far], None) for far in (0, 2) for tick in (1, 2)]

    def saved_left(own, their):
        return [(own, 0, 0), (own, 1, 0), (their, 0, 0), (their, 1, 0)]

    def saved_right(own, their):
        return [(own, 0), (own, 1), (their, 0), (their, 1)]

    start, projects, cores, forwards = second_pass(1)
    starts = {1: start}
    start_rows = jnp.concatenate([start, start], axis=0)
    for tick in range(3):
        if tick == 1:
            (projects, cores, forwards), received[0], _ = tied(
                (projects, cores, forwards), received[0], d_low
            )
            starts[0], projects, cores, forwards = second_pass(0, projects, cores, forwards)
            start_rows = jnp.concatenate([starts[0], starts[1]], axis=0)
            arrived, forwards = tied(arrived, forwards)
        normed, projected = projects[0], by_row(projects)
        mixed, pre, yns = cores[0].reshape(MB * TOK, MIXED), cores[1], cores[2]
        result, middle, normed_two, gate, up, act = forwards
        row = jnp.where(is_first, (1, 1, 0)[tick], (1, 0, 1)[tick]).astype(jnp.int32).reshape(1)
        if tick == 2:
            row, lefts[1], rights[1], rows[1] = tied(row, lefts[1], rights[1], rows[1])
            section_out = whole_order(result)
            row, section_out = tied(row, section_out)
        loss_row = (1, 0, 1)[tick]
        cotangent = jnp.where(
            is_first, arrived, from_loss[loss_row * TOK : (loss_row + 1) * TOK]
        )
        if tick == 1:
            cotangent, swaps = tied(
                cotangent, (mixed, act, normed[:, SIDE:], normed_two[:, SIDE:])
            )
            their_mixed, their_act, their_normed, their_normed_two = map(swapped, swaps)
        d_gate, d_up, d_middle, middle_low, d_mixed, mlp_grad = feed_back(
            row, cotangent, gate, up, middle, mlp_row, *pair_b
        )
        lefts.append(
            (cotangent, middle_low, swapped(cotangent[:, SIDE:]), swapped(middle_low[:, SIDE:]))
        )
        rights.append((d_gate, d_up, swapped(d_gate), swapped(d_up)))
        if tick < 2:
            attended = attend_back(row, projected, d_mixed, layout)
            if tick == 1:
                row, their_mixed, their_act, their_normed, their_normed_two = tied(
                    row, their_mixed, their_act, their_normed, their_normed_two
                )
            proj_low, small = mixer_back(
                row, projected, pre, yns, d_mixed, attended, layout, params
            )
            their_low = swapped(proj_low)
        else:
            sum_c = weight_grad(
                picks,
                1024,
                [
                    (tick_left(1), saved_right(mixed, their_mixed)),
                    (tick_left(0), saved_right(act, their_act)),
                ],
            )
            ring_c = RingReduce(sum_c)
            now_c, row = tied(ring_c.operands(), row)
            ring_c.send(*now_c)
            attended = attend_back(row, projected, d_mixed, layout)
            ring_c.hold(attended)
            picks_now, now_c, rights[2] = tied(picks, ring_c.operands(), rights[2])
            ring_c.send(*now_c)
            sum_b = weight_grad(
                picks_now,
                1024,
                [
                    (saved_left(normed_two, their_normed_two), tick_right(0)),
                    (saved_left(normed_two, their_normed_two), tick_right(1)),
                ],
            )
            ring_b = RingReduce(sum_b)
            ring_c.hold(sum_b)
            now_b, now_c, row, attended = tied(
                ring_b.operands(), ring_c.operands(), row, attended
            )
            ring_c.send(*now_c)
            ring_b.send(*now_b)
            proj_low, small = mixer_back(
                row, projected, pre, yns, d_mixed, attended, layout, params
            )
            proj_low, ring_b.ahead, ring_b.back, ring_c.ahead, ring_c.back = tied(
                proj_low, ring_b.ahead, ring_b.back, ring_c.ahead, ring_c.back
            )
            their_low = swapped(proj_low)
            now_b, row = tied(ring_b.operands(), row)
            ring_b.send(*now_b)
            d_rows, d_low, pre_grad = project_back(
                row, proj_low, start_rows, d_middle, pre_row, *pair_a
            )
            now_c, their_low, d_rows, pre_grad = tied(
                ring_c.operands(), their_low, d_rows, pre_grad
            )
            ring_c.send(*now_c)
            small_two = (pre_grad, mlp_grad, small)
            pre_sum, mlp_sum, small_sum = (one + two for one, two in zip(rows[1][2:], small_two))
            gain_sums = whole_order(jnp.concatenate([pre_sum, mlp_sum], axis=0))
            small_sum = jnp.concatenate(
                [small_sum, jnp.pad(gain_sums, ((0, 6), (0, CH - D)))], axis=0
            )
            picks_now, now_c, small_sum = tied(picks, now_c, small_sum)
            (p_one, their_one), (p_two, their_two) = rows[1][1], (proj_low, their_low)
            sum_a = weight_grad(
                picks_now,
                WIDE_A // 3,
                [
                    (
                        saved_left(normed, their_normed),
                        [(p_one, None), (p_two, None), (their_one, None), (their_two, None)],
                    )
                ],
            )
            ring_b.hold(sum_a)
            ring_a = RingReduce(sum_a)
            ring_c.hold(sum_a)
            now_a, now_b, ring_c.ahead, ring_c.back = tied(
                ring_a.operands(), ring_b.operands(), ring_c.ahead, ring_c.back
            )
            ring_b.send(*now_b)
            ring_a.send(*now_a)
        if tick < 2:
            d_rows, d_low, pre_grad = project_back(
                row, proj_low, start_rows, d_middle, pre_row, *pair_a
            )
        rows.append((d_rows, (proj_low, their_low), pre_grad, mlp_grad, small))
        if tick < 2:
            arrived = passed_along(d_low, "section", -1)

    hops = small_hops(lax.axis_size("chip"))

    def hop_beside(small, ring):
        if not hops:
            return small
        small, moved, _ = tied(small, hops.pop(0)(small), ring.ahead)
        return small + moved

    small = hop_beside(small_sum, ring_a)
    ring_b.step()
    ring_a.step()
    ring_c.hold(ring_a.ahead)
    small = hop_beside(small, ring_a)
    while ring_a.left > 2:
        ring_a.step()
    d_last = tied(rows[2][0], ring_a.ahead)[0]
    rings_a = [ring_a.columns(0, CUT_A), ring_a.columns(CUT_A, WIDE_A)]
    while rings_a[0].left:
        for ring in rings_a:
            ring.step()
        small = hop_beside(small, rings_a[0])
    for hop in hops:
        small = small + hop(small)
    share_c = ring_c.total()
    share_b = ring_b.total()
    share_a = jnp.concatenate([ring.total() for ring in rings_a], axis=1)

    start_grad = jnp.concatenate(
        [
            jnp.where(is_first, d_last, rows[1][0]),
            jnp.where(is_first, rows[1][0], d_last),
        ],
        axis=0,
    )
    skip_sum = jnp.sum(small[6, :E].reshape(MH, MP), axis=1)
    mixer_in_grad = jnp.concatenate([share_a[:, :AT_Q], share_a[:, AT_DT : AT_DT + MH]], axis=1)
    return (
        section_out[None],
        whole_order(start_grad)[None],
        small[8:9, :D],
        small[9:10, :D],
        small[5:6, :E],
        small[None, :4],
        small[4:5],
        small[7:8, :MH],
        small[7:8, LANES : LANES + MH],
        skip_sum[None],
        mixer_in_grad[None],
        share_c[:, :E].T[None],
        share_a[:, AT_Q:AT_K][None],
        share_a[:, AT_K:AT_V][None],
        share_a[:, AT_V:AT_DT][None],
        share_c[:, E:MIXED].T[None],
        share_b[None],
        share_c[:, MIXED:].T[None],
    )


def solution(mesh):
    dp = mesh.shape["dp"]
    devices = mesh.devices.reshape(mesh.shape["section"], dp // 2, 2)
    paired = Mesh(devices, ("section", "chip", "core"))
    over = ("chip", "core")
    rows = P(over, None)
    small = P("section", None)
    by_row = P("section", over, None)
    by_col = P("section", None, over)
    small_specs = (small, small, small, P("section", None, None), small, small, small, small)
    big_specs = (by_row, by_col, by_row, by_row, by_row, by_col, by_row, by_col)
    in_specs = (rows, rows, rows, P(over)) + small_specs + big_specs
    out_specs = (by_row, by_row) + small_specs + big_specs
    return jax.shard_map(
        per_device, mesh=paired, in_specs=in_specs, out_specs=out_specs, check_vma=False
    )
```

```python
import functools
import math

import jax
import jax.numpy as jnp
from jax import lax
from jax.experimental import pallas as pl
from jax.experimental.pallas import tpu as pltpu
from jax.sharding import Mesh
from jax.sharding import PartitionSpec as P

D = 1024
FF = 2048
MH = 24
MP = 64
NS = 128
AH = 8
KVH = 2
HD = 64
MB = 2
TOK = 256
E = 1536
CH = 1792
HALF = TOK // 2
PAIRS = MH // 2
LANES = 128
SIDE = D // 2
MIB = 2**20
FF_VMEM = 19
FB_VMEM = 17

AT_W = E
AT_Q = E + CH
AT_K = AT_Q + AH * HD
AT_V = AT_K + KVH * HD
AT_DT = AT_V + KVH * HD
WIDE_A = AT_DT + LANES
CUT_A = 16 * LANES
MIXED = E + AH * HD
AT_GU = MIXED
AT_DN = AT_GU + 2 * FF
WIDE_B = AT_DN + FF

highest = lax.Precision.HIGHEST
epsilon = 1e-05
rope_base = 100000000000.0
bf16 = jnp.bfloat16
f32 = jnp.float32


def dot_nn(left, right):
    return lax.dot_general(left, right, (((1,), (0,)), ((), ())), preferred_element_type=f32)


def dot_nt(left, right):
    return lax.dot_general(left, right, (((1,), (1,)), ((), ())), preferred_element_type=f32)


def dot_tn(left, right):
    return lax.dot_general(left, right, (((0,), (0,)), ((), ())), preferred_element_type=f32)


def dot_exact(left, right):
    return lax.dot_general(
        left, right, (((1,), (0,)), ((), ())), precision=highest, preferred_element_type=f32
    )


def softplus(value):
    return jnp.maximum(value, 0.0) + jnp.log1p(jnp.exp(-jnp.abs(value)))


def lane_low(rows):
    return lax.broadcasted_iota(jnp.int32, (rows, LANES), 1) < HD


def rope_halves(rows):
    return (lax.broadcasted_iota(jnp.int32, (rows, LANES), 1) & (HD - 1)) < HD // 2


def rope_turn(tile, cosine, sine):
    swapped = jnp.where(
        rope_halves(tile.shape[0]),
        -pltpu.roll(tile, LANES - HD // 2, 1),
        pltpu.roll(tile, HD // 2, 1),
    )
    return tile * cosine + swapped * sine


def rope_back(tile, cosine, sine):
    swapped = jnp.where(
        rope_halves(tile.shape[0]),
        pltpu.roll(tile, LANES - HD // 2, 1),
        -pltpu.roll(tile, HD // 2, 1),
    )
    return tile * cosine + swapped * sine


def both_halves(tile):
    swapped = pltpu.roll(tile, HD, 1)
    low = lane_low(tile.shape[0])
    return (jnp.where(low, tile, swapped), jnp.where(low, swapped, tile))


def tile_at(index):
    return pl.ds(pl.multiple_of(index * LANES, LANES), LANES)


def tile_from(start, index):
    return pl.ds(pl.multiple_of(start + index * LANES, LANES), LANES)


def allowed_pairs(doc_col_ref, doc_row_ref):
    later = lax.broadcasted_iota(jnp.int32, (TOK, TOK), 0)
    early = lax.broadcasted_iota(jnp.int32, (TOK, TOK), 1)
    same = doc_col_ref[:, 0:1] == doc_row_ref[0:1, :]
    return (later >= early) & same


def pair_rows(tile):
    low = lane_low(tile.shape[0])
    zero = jnp.zeros_like(tile)
    return jnp.concatenate([jnp.where(low, tile, zero), jnp.where(low, zero, tile)], axis=0)


def pair_lanes(rows):
    half = rows.shape[0] // 2
    return jnp.where(lane_low(half), rows[:half], rows[half:])


def core_forward_kernel(
    held, pm_ref, pq_ref, pd_ref, rope_ref, mask_ref, doc_col_ref, doc_row_ref,
    taps_ref, head_ref, wide_ref, *refs,
):
    xb_ref, pre_ref, yns_ref, conv_s, cb_s, bias_s, sum_s = refs[3:] if held else refs

    def conv_tile(index, carry):
        rows = pm_ref[:, tile_from(AT_W, index)].astype(f32)
        at = tile_at(index)
        total = taps_ref[4:5, at] + taps_ref[3:4, at] * rows
        for shift in (1, 2, 3):
            moved = mask_ref[:, (shift - 1) * LANES : shift * LANES] * pltpu.roll(rows, shift, 0)
            total = total + taps_ref[3 - shift : 4 - shift, at] * moved
        total = total.astype(bf16)
        pre_ref[:, at] = total
        total = total.astype(f32)
        conv_s[:, at] = total * jax.nn.sigmoid(total)
        return carry

    lax.fori_loop(0, CH // LANES, conv_tile, 0)

    allowed = allowed_pairs(doc_col_ref, doc_row_ref)
    bias_s[...] = jnp.where(allowed, 0.0, -1e30)
    steps = softplus(pd_ref[...] + head_ref[0:1, :])
    rates = -steps * head_ref[1:2, :]
    totals = dot_exact(jnp.where(allowed, 1.0, 0.0), rates)
    totals_t = totals.T
    inward = conv_s[:, E : E + NS].astype(bf16)
    outward = conv_s[:, E + NS :].astype(bf16)
    cb_s[...] = jnp.where(allowed, dot_nt(outward, inward), 0.0)
    low = lane_low(TOK)
    for pair in range(PAIRS):
        lanes = slice(pair * LANES, (pair + 1) * LANES)
        first = 2 * pair
        step_pair = jnp.where(low, steps[:, first : first + 1], steps[:, first + 1 : first + 2])
        scaled = (conv_s[:, lanes] * step_pair).astype(bf16)
        mixes = []
        for head in (first, first + 1):
            apart = totals[:, head : head + 1] - totals_t[head : head + 1, :]
            mixes.append((jnp.exp(jnp.minimum(apart, 0.0)) * cb_s[...]).astype(bf16))
        yns_ref[:, lanes] = pair_lanes(dot_nn(jnp.concatenate(mixes, axis=0), scaled))

    sum_s[...] = jnp.zeros((TOK, LANES), f32)

    def gate_tile(index, carry):
        at = tile_at(index)
        gate = pm_ref[:, at].astype(f32)
        rows = yns_ref[:, at] + wide_ref[0:1, at] * conv_s[:, at]
        gated = rows * (gate * jax.nn.sigmoid(gate))
        sum_s[...] += gated * gated
        conv_s[:, at] = gated
        return carry

    lax.fori_loop(0, E // LANES, gate_tile, 0)
    scale = lax.rsqrt(jnp.sum(sum_s[...], axis=1, keepdims=True) * (1.0 / E) + epsilon)

    def norm_tile(index, carry):
        at = tile_at(index)
        xb_ref[:, at] = (conv_s[:, at] * scale * wide_ref[1:2, at]).astype(bf16)
        return carry

    lax.fori_loop(0, E // LANES, norm_tile, 0)

    cosine = rope_ref[:, :LANES]
    sine = rope_ref[:, LANES:]
    keys = both_halves(rope_turn(pq_ref[:, AH * HD : AH * HD + LANES].astype(f32), cosine, sine))
    values = both_halves(pq_ref[:, AH * HD + LANES :].astype(f32))
    keys = tuple(part.astype(bf16) for part in keys)
    values = tuple(part.astype(bf16) for part in values)
    for pair in range(AH // 2):
        group = pair // (AH // (2 * KVH))
        at = pair * LANES
        turned = rope_turn(pq_ref[:, at : at + LANES].astype(f32), cosine, sine)
        scores = dot_nt(pair_rows((turned * (1.0 / math.sqrt(HD))).astype(bf16)), keys[group])
        weights = []
        shares = []
        for part in (scores[:TOK], scores[TOK:]):
            part = part + bias_s[...]
            part = jnp.exp(part - jnp.max(part, axis=1, keepdims=True))
            shares.append(1.0 / jnp.sum(part, axis=1, keepdims=True))
            weights.append(part.astype(bf16))
        out = pair_lanes(dot_nn(jnp.concatenate(weights, axis=0), values[group]))
        out = out * jnp.where(low, shares[0], shares[1])
        xb_ref[:, E + pair * LANES : E + (pair + 1) * LANES] = out.astype(bf16)


def silu_slope(value, gate):
    return gate * (1.0 + value * (1.0 - gate))


def attend_back_kernel(
    pick_ref, pq_ref, dxb_ref, rope_ref, doc_col_ref, doc_row_ref, pg_ref, bias_s
):
    later = lax.broadcasted_iota(jnp.int32, (TOK, TOK), 1)
    early = lax.broadcasted_iota(jnp.int32, (TOK, TOK), 0)
    allowed_t = (later >= early) & (doc_col_ref[:, 0:1] == doc_row_ref[0:1, :])
    bias_s[...] = jnp.where(allowed_t, 0.0, -1e30)
    low = lane_low(TOK)
    cosine = rope_ref[:, :LANES]
    sine = rope_ref[:, LANES:]
    keys = both_halves(rope_turn(pq_ref[:, AH * HD : AH * HD + LANES].astype(f32), cosine, sine))
    values = both_halves(pq_ref[:, AH * HD + LANES :].astype(f32))
    root = 1.0 / math.sqrt(HD)
    d_keys = []
    d_values = []
    for group in range(KVH):
        key = keys[group].astype(bf16)
        key_rows = pair_rows(key)
        value_rows = pair_rows(values[group].astype(bf16))
        d_key = jnp.zeros((TOK, LANES), f32)
        d_value = jnp.zeros((TOK, LANES), f32)
        for pair in range(group * (AH // (2 * KVH)), (group + 1) * (AH // (2 * KVH))):
            at = pair * LANES
            turned = rope_turn(pq_ref[:, at : at + LANES].astype(f32), cosine, sine) * root
            query = turned.astype(bf16)
            d_out = dxb_ref[:, E + at : E + at + LANES].astype(bf16)
            scores = dot_nt(key_rows, query)
            d_weights = dot_nt(value_rows, d_out)
            weights = []
            d_scores = []
            for part in (slice(0, TOK), slice(TOK, 2 * TOK)):
                score = scores[part] + bias_s[...]
                weight = jnp.exp(score - jnp.max(score, axis=0, keepdims=True))
                weight = weight * (1.0 / jnp.sum(weight, axis=0, keepdims=True))
                d_weight = d_weights[part]
                offset = jnp.sum(weight * d_weight, axis=0, keepdims=True)
                weights.append(weight.astype(bf16))
                d_scores.append((weight * (d_weight - offset)).astype(bf16))
            d_value = d_value + pair_lanes(dot_nn(jnp.concatenate(weights, axis=0), d_out))
            d_key = d_key + pair_lanes(dot_nn(jnp.concatenate(d_scores, axis=0), query))
            d_query = pair_lanes(dot_tn(jnp.concatenate(d_scores, axis=1), key))
            pg_ref[:, at : at + LANES] = rope_back(d_query * root, cosine, sine).astype(bf16)
        d_keys.append(d_key + pltpu.roll(d_key, HD, 1))
        d_values.append(d_value + pltpu.roll(d_value, HD, 1))
    d_key = rope_back(jnp.where(low, d_keys[0], d_keys[1]), cosine, sine)
    pg_ref[:, AH * HD : AH * HD + LANES] = d_key.astype(bf16)
    pg_ref[:, AH * HD + LANES :] = jnp.where(low, d_values[0], d_values[1]).astype(bf16)


def mixer_back_kernel(
    pick_ref, pm_ref, pd_ref, pre_ref, yns_ref, dxb_ref, attend_ref, mask_ref, doc_col_ref,
    doc_row_ref, taps_ref, head_ref, wide_ref,
    pg_ref, small_ref,
    x_s, dx_s, dyb_s, cbt_s, dcbt_s, sum_s, ssum_s,
):
    small_ref[...] = jnp.zeros_like(small_ref)
    pg_ref[:, AT_Q:AT_DT] = attend_ref[...]
    sum_s[...] = jnp.zeros((TOK, LANES), f32)
    ssum_s[...] = jnp.zeros((TOK, LANES), f32)

    def start_tile(index, carry):
        at = tile_at(index)
        pre = pre_ref[:, at].astype(f32)
        heads_in = pre * jax.nn.sigmoid(pre)
        x_s[:, at] = heads_in
        gate = pm_ref[:, at].astype(f32)
        rows = yns_ref[:, at] + wide_ref[0:1, at] * heads_in
        gated = rows * (gate * jax.nn.sigmoid(gate))
        sum_s[...] += gated * gated
        ssum_s[...] += dxb_ref[:, at] * wide_ref[1:2, at] * gated
        return carry

    lax.fori_loop(0, E // LANES, start_tile, 0)
    scale = lax.rsqrt(jnp.sum(sum_s[...], axis=1, keepdims=True) * (1.0 / E) + epsilon)
    pull = jnp.sum(ssum_s[...], axis=1, keepdims=True) * (1.0 / E) * scale * scale * scale

    def gate_tile(index, carry):
        at = tile_at(index)
        heads_in = x_s[:, at]
        skip = wide_ref[0:1, at]
        gate = pm_ref[:, at].astype(f32)
        opened = jax.nn.sigmoid(gate)
        rows = yns_ref[:, at] + skip * heads_in
        gated = rows * (gate * opened)
        arrived = dxb_ref[:, at]
        d_gated = scale * (arrived * wide_ref[1:2, at]) - gated * pull
        small_ref[5:6, at] = jnp.sum(arrived * gated * scale, axis=0, keepdims=True)
        d_rows = d_gated * (gate * opened)
        pg_ref[:, at] = (d_gated * rows * silu_slope(gate, opened)).astype(bf16)
        small_ref[6:7, at] = jnp.sum(d_rows * heads_in, axis=0, keepdims=True)
        dyb_s[:, at] = d_rows.astype(bf16)
        dx_s[:, at] = skip * d_rows
        return carry

    lax.fori_loop(0, E // LANES, gate_tile, 0)

    def state_tile(index, carry):
        at = tile_from(E, index)
        pre = pre_ref[:, at].astype(f32)
        x_s[:, at] = pre * jax.nn.sigmoid(pre)
        return carry

    lax.fori_loop(0, 2, state_tile, 0)

    later = lax.broadcasted_iota(jnp.int32, (TOK, TOK), 1)
    early = lax.broadcasted_iota(jnp.int32, (TOK, TOK), 0)
    allowed_t = (later >= early) & (doc_col_ref[:, 0:1] == doc_row_ref[0:1, :])
    allowed = allowed_pairs(doc_col_ref, doc_row_ref)
    raw = pd_ref[...] + head_ref[0:1, :]
    steps = softplus(raw)
    decay = head_ref[1:2, :]
    rates = -steps * decay
    totals = dot_exact(jnp.where(allowed, 1.0, 0.0), rates)
    totals_t = totals.T
    inward = x_s[:, E : E + NS].astype(bf16)
    outward = x_s[:, E + NS :].astype(bf16)
    cbt_s[...] = jnp.where(allowed_t, dot_nt(inward, outward), 0.0)
    dcbt_s[...] = jnp.zeros((TOK, TOK), f32)
    low = lane_low(TOK)
    spread_row = lax.broadcasted_iota(jnp.int32, (2 * LANES, LANES), 0) // HD
    spread_col = lax.broadcasted_iota(jnp.int32, (2 * LANES, LANES), 1)
    sum_s[...] = jnp.zeros((TOK, LANES), f32)
    ssum_s[...] = jnp.zeros((TOK, LANES), f32)
    waiting = None
    for pair in range(PAIRS):
        lanes = slice(pair * LANES, (pair + 1) * LANES)
        first = 2 * pair
        step_pair = jnp.where(low, steps[:, first : first + 1], steps[:, first + 1 : first + 2])
        heads_in = x_s[:, lanes]
        scaled = (heads_in * step_pair).astype(bf16)
        d_rows = dyb_s[:, lanes]
        d_mix = dot_nt(pair_rows(scaled), d_rows)
        mixes = []
        d_pairs = None
        for side, head in enumerate((first, first + 1)):
            apart = totals_t[head : head + 1, :] - totals[:, head : head + 1]
            decays = jnp.exp(jnp.minimum(apart, 0.0))
            mixes.append((decays * cbt_s[...]).astype(bf16))
            part = d_mix[side * TOK : (side + 1) * TOK] * decays
            d_pairs = part if d_pairs is None else d_pairs + part
        dcbt_s[...] += d_pairs
        d_scaled = pair_lanes(dot_nn(jnp.concatenate(mixes, axis=0), d_rows))
        dx_s[:, lanes] += d_scaled * step_pair
        value = d_rows.astype(f32) * yns_ref[:, lanes] - scaled.astype(f32) * d_scaled
        coarse = value.astype(bf16)
        fine = (value - coarse.astype(f32)).astype(bf16)
        spread = (spread_col == first + (spread_row & 1)).astype(bf16)
        ssum_s[...] += dot_nn(jnp.concatenate([coarse, fine], axis=1), spread)
        value = (d_scaled * heads_in).astype(bf16)
        if pair % 2 == 0:
            waiting = value
        else:
            spread = (spread_col == first - 2 + spread_row).astype(bf16)
            sum_s[...] += dot_nn(jnp.concatenate([waiting, value], axis=1), spread)

    d_rates = dot_exact(jnp.where(allowed_t, 1.0, 0.0), ssum_s[...])
    d_steps = sum_s[...] - decay * d_rates
    d_raw = d_steps * jax.nn.sigmoid(raw)
    pg_ref[:, AT_DT:] = d_raw.astype(bf16)
    small_ref[7:8, :LANES] = jnp.sum(d_raw, axis=0, keepdims=True)
    small_ref[7:8, LANES : 2 * LANES] = jnp.sum(d_rates * rates, axis=0, keepdims=True)
    d_pairs = jnp.where(allowed_t, dcbt_s[...], 0.0).astype(bf16)
    dx_s[:, E : E + NS] = dot_nn(d_pairs, outward)
    dx_s[:, E + NS :] = dot_tn(d_pairs, inward)

    def conv_tile(index, carry):
        at = tile_at(index)
        pre = pre_ref[:, at].astype(f32)
        d_pre = dx_s[:, at] * silu_slope(pre, jax.nn.sigmoid(pre))
        rows = pm_ref[:, tile_from(AT_W, index)].astype(f32)
        small_ref[4:5, at] = jnp.sum(d_pre, axis=0, keepdims=True)
        small_ref[3:4, at] = jnp.sum(d_pre * rows, axis=0, keepdims=True)
        back = taps_ref[3:4, at] * d_pre
        for shift in (1, 2, 3):
            held = mask_ref[:, (shift - 1) * LANES : shift * LANES] * d_pre
            small_ref[3 - shift : 4 - shift, at] = jnp.sum(
                held * pltpu.roll(rows, shift, 0), axis=0, keepdims=True
            )
            back = back + taps_ref[3 - shift : 4 - shift, at] * pltpu.roll(held, TOK - shift, 0)
        pg_ref[:, tile_from(AT_W, index)] = back.astype(bf16)
        return carry

    lax.fori_loop(0, CH // LANES, conv_tile, 0)


def whole_block(shape):
    return pl.BlockSpec(shape, lambda *steps: (0,) * len(shape))


def once(shape, place):
    return pl.BlockSpec(shape, place, pipeline_mode=pl.Buffered(1))


def core_forward(row, projected, layout, params, held=()):
    operands = (*projected, *layout)
    held = tuple(held)
    if held:
        held = (pltpu.with_memory_space_constraint(held[0], pltpu.HBM),) + held[1:]

    def block(array):
        return once((None,) + array.shape[1:], lambda step: (row, 0, 0))

    outs = [
        pltpu.HBM((MB, TOK, MIXED), bf16),
        jax.ShapeDtypeStruct((MB, TOK, CH), bf16),
        jax.ShapeDtypeStruct((MB, TOK, E), f32),
    ]
    return pl.pallas_call(
        functools.partial(core_forward_kernel, bool(held)),
        grid=(1,),
        in_specs=[block(array) for array in operands]
        + [once(array.shape, lambda step: (0, 0)) for array in params]
        + [pl.BlockSpec(memory_space=pl.ANY)] * len(held),
        out_specs=[block(array) for array in outs],
        out_shape=outs,
        scratch_shapes=[
            pltpu.VMEM((TOK, CH), f32),
            pltpu.VMEM((TOK, TOK), f32),
            pltpu.VMEM((TOK, TOK), f32),
            pltpu.VMEM((TOK, LANES), f32),
        ],
        input_output_aliases={10: 0, 11: 1, 12: 2} if held else {},
        compiler_params=pltpu.CompilerParams(vmem_limit_bytes=12 * MIB),
        cost_estimate=pl.CostEstimate(
            flops=4 * 10**8, bytes_accessed=12 * 2**20, transcendentals=10**6
        ),
        name="core_forward",
    )(*operands, *params, *held)


def core_back_specs(by_row, plain):
    return [
        once((None,) + array.shape[1:], lambda step, pick: (pick[0], 0, 0)) if chosen
        else once(array.shape, lambda step, pick: (0, 0))
        for chosen, arrays in ((True, by_row), (False, plain))
        for array in arrays
    ]


def attend_back(row, projected, d_mixed, layout):
    rope, masks, doc_cols, doc_rows = layout
    return pl.pallas_call(
        attend_back_kernel,
        grid_spec=pltpu.PrefetchScalarGridSpec(
            num_scalar_prefetch=1,
            grid=(1,),
            in_specs=core_back_specs([projected[1]], [d_mixed])
            + core_back_specs([rope, doc_cols, doc_rows], []),
            out_specs=once((TOK, AT_DT - AT_Q), lambda step, pick: (0, 0)),
            scratch_shapes=[pltpu.VMEM((TOK, TOK), f32)],
        ),
        out_shape=jax.ShapeDtypeStruct((TOK, AT_DT - AT_Q), bf16),
        compiler_params=pltpu.CompilerParams(vmem_limit_bytes=6 * MIB),
        cost_estimate=pl.CostEstimate(
            flops=3 * 10**8, bytes_accessed=4 * 2**20, transcendentals=6 * 10**5
        ),
        name="attend_back",
    )(row, projected[1], d_mixed, rope, doc_cols, doc_rows)


def mixer_back(row, projected, pre, yns, d_mixed, attended, layout, params):
    rope, masks, doc_cols, doc_rows = layout
    return pl.pallas_call(
        mixer_back_kernel,
        grid_spec=pltpu.PrefetchScalarGridSpec(
            num_scalar_prefetch=1,
            grid=(1,),
            in_specs=core_back_specs(
                [projected[0], projected[2], pre, yns], [d_mixed, attended]
            )
            + core_back_specs([masks, doc_cols, doc_rows], params),
            out_specs=[
                once((TOK, WIDE_A), lambda step, pick: (0, 0)),
                once((8, CH), lambda step, pick: (0, 0)),
            ],
            scratch_shapes=[
                pltpu.VMEM((TOK, CH), f32),
                pltpu.VMEM((TOK, CH), f32),
                pltpu.VMEM((TOK, E), bf16),
                pltpu.VMEM((TOK, TOK), f32),
                pltpu.VMEM((TOK, TOK), f32),
                pltpu.VMEM((TOK, LANES), f32),
                pltpu.VMEM((TOK, LANES), f32),
            ],
        ),
        out_shape=[
            jax.ShapeDtypeStruct((TOK, WIDE_A), bf16),
            jax.ShapeDtypeStruct((8, CH), f32),
        ],
        compiler_params=pltpu.CompilerParams(vmem_limit_bytes=15 * MIB),
        cost_estimate=pl.CostEstimate(
            flops=7 * 10**8, bytes_accessed=10 * 2**20, transcendentals=15 * 10**5
        ),
        name="mixer_back",
    )(
        row, projected[0], projected[2], pre, yns, d_mixed, attended, masks, doc_cols, doc_rows,
        *params,
    )


def passed_along(value, axis, steps):
    count = lax.axis_size(axis)
    leading, last = (max(0, -steps), min(count, count - steps))
    return lax.ppermute(value, axis, [(source, source + steps) for source in range(leading, last)])


def norm_rows(values):
    return lax.rsqrt(jnp.mean(values * values, axis=-1, keepdims=True) + epsilon)


def norm_back(values, gain, arrived):
    scale = norm_rows(values)
    weighted = arrived * gain
    pull = jnp.mean(weighted * values, axis=-1, keepdims=True) * scale * scale * scale
    gain_grad = jnp.sum(arrived * values * scale, axis=0, keepdims=True)
    return (weighted * scale - values * pull, gain_grad)


def project_kernel(rows_ref, gain_ref, own_ref, other_ref, *refs):
    normed_ref, pm_ref, pq_ref, pd_ref = refs[-4:]
    step = pl.program_id(0)

    @pl.when(step == 0)
    def _():
        rows = rows_ref[...].astype(f32)
        normed_ref[...] = (rows * norm_rows(rows) * gain_ref[...]).astype(bf16)

    out = dot_nn(normed_ref[:, :SIDE], own_ref[...]) + dot_nn(normed_ref[:, SIDE:], other_ref[...])
    tile = WIDE_A // 3
    for index in range(2):
        @pl.when(step == index)
        def _(index=index):
            pm_ref[:, index * tile : (index + 1) * tile] = out.astype(bf16)

    @pl.when(step == 2)
    def _():
        pm_ref[:, 2 * tile :] = out[:, : AT_Q - 2 * tile].astype(bf16)
        pq_ref[...] = out[:, AT_Q - 2 * tile : AT_DT - 2 * tile].astype(bf16)
        pd_ref[...] = out[:, AT_DT - 2 * tile :]


def project(rows, gain, own, other, row=None, held=()):
    count = rows.shape[0]
    tile = WIDE_A // 3
    weight = pl.BlockSpec((SIDE, tile), lambda step: (0, step))
    at = row or 0
    total = count if row is None else MB * TOK
    held = tuple(held)
    if held:
        held = (pltpu.with_memory_space_constraint(held[0], pltpu.HBM),) + held[1:]
    widths = ((D, bf16), (AT_Q, bf16), (AT_DT - AT_Q, bf16), (LANES, f32))
    return pl.pallas_call(
        project_kernel,
        grid=(3,),
        in_specs=[whole_block((count, D)), whole_block((1, D)), weight, weight]
        + [pl.BlockSpec(memory_space=pl.ANY)] * len(held),
        out_specs=[pl.BlockSpec((count, width), lambda step: (at, 0)) for width, _ in widths],
        out_shape=[pltpu.HBM((total, D), bf16)]
        + [jax.ShapeDtypeStruct((total, width), kind) for width, kind in widths[1:]],
        input_output_aliases={4 + index: index for index in range(len(held))},
        compiler_params=pltpu.CompilerParams(vmem_limit_bytes=15 * MIB),
        cost_estimate=pl.CostEstimate(
            flops=2 * count * D * WIDE_A,
            bytes_accessed=2 * D * WIDE_A + 2 * count * WIDE_A,
            transcendentals=0,
        ),
        name="project",
    )(rows, gain, own, other, *held)


def by_row(projected):
    return tuple(array.reshape(MB, TOK, -1) for array in projected[1:])


def feed_forward_kernel(
    keep, rows_ref, mixed_ref, gain_ref,
    out_own, out_other, gate_own, gate_other, up_own, up_other, down_own, down_other,
    *refs,
):
    if keep:
        low_ref, middle_ref, normed_ref, gate_ref, up_ref, act_ref, total_s = refs[-7:]
    else:
        low_ref, middle_ref, normed_ref, total_s = refs
    step = pl.program_id(0)

    @pl.when(step == 0)
    def _():
        middle_ref[...] = rows_ref[...].astype(f32)

    @pl.when(step < 4)
    def _():
        mixed = mixed_ref[...]
        middle_ref[:, :SIDE] += dot_nt(mixed, out_own[...])
        middle_ref[:, SIDE:] += dot_nt(mixed, out_other[...])

    @pl.when(step == 3)
    def _():
        middle = middle_ref[...]
        normed_ref[...] = (middle * norm_rows(middle) * gain_ref[...]).astype(bf16)
        total_s[...] = middle

    @pl.when(step >= 4)
    def _():
        left = normed_ref[:, :SIDE]
        right = normed_ref[:, SIDE:]
        gate = dot_nn(left, gate_own[...]) + dot_nn(right, gate_other[...])
        up = dot_nn(left, up_own[...]) + dot_nn(right, up_other[...])
        act = (gate * jax.nn.sigmoid(gate) * up).astype(bf16)
        if keep:
            gate_ref[...] = gate.astype(bf16)
            up_ref[...] = up.astype(bf16)
            act_ref[...] = act
        total_s[:, :SIDE] += dot_nt(act, down_own[...])
        total_s[:, SIDE:] += dot_nt(act, down_other[...])

    @pl.when(step == 7)
    def _():
        low_ref[...] = total_s[...].astype(bf16)


def pinned(own, other):
    return [
        pltpu.with_memory_space_constraint(own, pltpu.VMEM),
        pltpu.with_memory_space_constraint(other, pltpu.VMEM),
    ]


def b_block(start, skipped):
    return pl.BlockSpec(
        (SIDE, 512), lambda step, *pick: (0, start + jnp.clip(step - skipped, 0, 3))
    )


def b_blocks(parts):
    return [b_block(start, skipped) for start, skipped in parts for _ in range(2)]


def feed_forward(row, rows, mixed, gain, own, other, held=None):
    keep = held is not None
    at = row if rows.shape[0] > TOK else 0

    def late(step):
        return (row, jnp.clip(step - 4, 0, 3))

    wide = pl.BlockSpec((TOK, 512), late)
    full = pl.BlockSpec((TOK, D), lambda step: (row, 0))
    scratch = [pltpu.VMEM((TOK, D), f32)]
    if keep:
        out_specs = [full, full, full, wide, wide, wide]
        out_shape = [
            pltpu.HBM((MB * TOK, width), kind)
            for width, kind in ((D, bf16), (D, f32), (D, bf16), (FF, bf16), (FF, bf16), (FF, bf16))
        ]
    else:
        out_specs = [whole_block((TOK, D))]
        out_shape = [jax.ShapeDtypeStruct((TOK, D), bf16)]
        scratch = [pltpu.VMEM((TOK, D), f32), pltpu.VMEM((TOK, D), bf16)] + scratch
    mixed, *held = (
        pltpu.with_memory_space_constraint(one, pltpu.HBM) for one in (mixed, *(held or ()))
    )
    return pl.pallas_call(
        functools.partial(feed_forward_kernel, keep),
        grid=(8,),
        in_specs=[
            pl.BlockSpec((TOK, D), lambda step: (at, 0)),
            pl.BlockSpec((TOK, 512), lambda step: (row, jnp.clip(step, 0, 3))),
            whole_block((1, D)),
        ]
        + b_blocks(((0, 0), (4, 4), (8, 4), (12, 4)))
        + [pl.BlockSpec(memory_space=pl.ANY)] * len(held),
        out_specs=out_specs,
        out_shape=out_shape,
        scratch_shapes=scratch,
        input_output_aliases={11 + index: index for index in range(len(held))},
        compiler_params=pltpu.CompilerParams(vmem_limit_bytes=(FF_VMEM if keep else 18) * MIB),
        cost_estimate=pl.CostEstimate(
            flops=2 * TOK * D * WIDE_B, bytes_accessed=2 * D * WIDE_B, transcendentals=0
        ),
        name="feed_forward",
    )(rows, mixed, gain, *((pinned(own, other) if keep else [own, other]) * 4), *held)


def feed_back_kernel(
    pick_ref, cot_ref, gate_ref, up_ref, middle_ref, gain_ref,
    down_own, down_other, gate_own, gate_other, up_own, up_other, out_own, out_other,
    d_gate_ref, d_up_ref, d_middle_ref, low_ref, d_mixed_ref, gain_grad_ref,
    total_s,
):
    step = pl.program_id(0)

    @pl.when(step == 0)
    def _():
        total_s[...] = jnp.zeros_like(total_s)

    @pl.when(step < 4)
    def _():
        arrived = dot_nn(cot_ref[:, :SIDE], down_own[...]) + dot_nn(
            cot_ref[:, SIDE:], down_other[...]
        )
        gate = gate_ref[...].astype(f32)
        opened = jax.nn.sigmoid(gate)
        d_gate = (arrived * up_ref[...].astype(f32) * silu_slope(gate, opened)).astype(bf16)
        d_up = (arrived * (gate * opened)).astype(bf16)
        d_gate_ref[...] = d_gate
        d_up_ref[...] = d_up
        total_s[:, :SIDE] += dot_nt(d_gate, gate_own[...]) + dot_nt(d_up, up_own[...])
        total_s[:, SIDE:] += dot_nt(d_gate, gate_other[...]) + dot_nt(d_up, up_other[...])

    @pl.when(step == 3)
    def _():
        d_norm, gain_grad = norm_back(middle_ref[...], gain_ref[...], total_s[...])
        d_middle = cot_ref[...].astype(f32) + d_norm
        d_middle_ref[...] = d_middle
        low_ref[...] = d_middle.astype(bf16)
        gain_grad_ref[...] = gain_grad

    @pl.when(step >= 4)
    def _():
        d_mixed_ref[...] = dot_nn(low_ref[:, :SIDE], out_own[...]) + dot_nn(
            low_ref[:, SIDE:], out_other[...]
        )


def feed_back(row, cotangent, gate, up, middle, gain, own, other):
    saved = pl.BlockSpec((TOK, 512), lambda step, pick: (pick[0], jnp.clip(step, 0, 3)))
    early = pl.BlockSpec((TOK, 512), lambda step, pick: (0, jnp.clip(step, 0, 3)))
    late = pl.BlockSpec((TOK, 512), lambda step, pick: (0, jnp.clip(step - 4, 0, 3)))
    full = pl.BlockSpec((TOK, D), lambda step, pick: (0, 0))
    gain_block = pl.BlockSpec((1, D), lambda step, pick: (0, 0))
    return pl.pallas_call(
        feed_back_kernel,
        grid_spec=pltpu.PrefetchScalarGridSpec(
            num_scalar_prefetch=1,
            grid=(8,),
            in_specs=[
                full,
                saved,
                saved,
                pl.BlockSpec((TOK, D), lambda step, pick: (pick[0], 0)),
                gain_block,
            ]
            + b_blocks(((12, 0), (4, 0), (8, 0), (0, 4))),
            out_specs=[early, early, full, full, late, gain_block],
            scratch_shapes=[pltpu.VMEM((TOK, D), f32)],
        ),
        out_shape=[
            pltpu.HBM((TOK, FF), bf16),
            pltpu.HBM((TOK, FF), bf16),
            jax.ShapeDtypeStruct((TOK, D), f32),
            jax.ShapeDtypeStruct((TOK, D), bf16),
            jax.ShapeDtypeStruct((TOK, MIXED), f32),
            jax.ShapeDtypeStruct((1, D), f32),
        ],
        compiler_params=pltpu.CompilerParams(vmem_limit_bytes=FB_VMEM * MIB),
        cost_estimate=pl.CostEstimate(
            flops=2 * TOK * D * WIDE_B, bytes_accessed=2 * D * WIDE_B, transcendentals=0
        ),
        name="feed_back",
    )(
        row, cotangent, *(pltpu.with_memory_space_constraint(one, pltpu.HBM) for one in (gate, up)),
        pltpu.with_memory_space_constraint(middle, pltpu.HBM), gain, *(pinned(own, other) * 4),
    )


def project_back_kernel(
    pick_ref, grad_ref, rows_ref, d_middle_ref, gain_ref, own_ref, other_ref,
    d_rows_ref, low_ref, gain_grad_ref, total_s,
):
    step = pl.program_id(0)

    @pl.when(step == 0)
    def _():
        total_s[...] = jnp.zeros_like(total_s)

    total_s[:, :SIDE] += dot_nt(grad_ref[...], own_ref[...])
    total_s[:, SIDE:] += dot_nt(grad_ref[...], other_ref[...])

    @pl.when(step == 2)
    def _():
        d_norm, gain_grad = norm_back(rows_ref[...].astype(f32), gain_ref[...], total_s[...])
        d_rows = d_middle_ref[...] + d_norm
        d_rows_ref[...] = d_rows
        low_ref[...] = d_rows.astype(bf16)
        gain_grad_ref[...] = gain_grad


def project_back(row, proj_low, start_rows, d_middle, gain, own, other):
    tile = WIDE_A // 3
    weight = pl.BlockSpec((SIDE, tile), lambda step, pick: (0, step))
    full = pl.BlockSpec((TOK, D), lambda step, pick: (0, 0))
    gain_block = pl.BlockSpec((1, D), lambda step, pick: (0, 0))
    return pl.pallas_call(
        project_back_kernel,
        grid_spec=pltpu.PrefetchScalarGridSpec(
            num_scalar_prefetch=1,
            grid=(3,),
            in_specs=[
                pl.BlockSpec((TOK, tile), lambda step, pick: (0, step)),
                pl.BlockSpec((TOK, D), lambda step, pick: (pick[0], 0)),
                full,
                gain_block,
                weight,
                weight,
            ],
            out_specs=[full, full, gain_block],
            scratch_shapes=[pltpu.VMEM((TOK, D), f32)],
        ),
        out_shape=[
            jax.ShapeDtypeStruct((TOK, D), f32),
            jax.ShapeDtypeStruct((TOK, D), bf16),
            jax.ShapeDtypeStruct((1, D), f32),
        ],
        compiler_params=pltpu.CompilerParams(vmem_limit_bytes=15 * MIB),
        cost_estimate=pl.CostEstimate(
            flops=2 * TOK * D * WIDE_A, bytes_accessed=2 * D * WIDE_A, transcendentals=0
        ),
        name="project_back",
    )(row, proj_low, start_rows, d_middle, gain, own, other)


def weight_grad_kernel(groups, pick_ref, *refs):
    lefts = refs[: 4 * len(groups)]
    rights = refs[4 * len(groups) : 8 * len(groups)]
    sum_ref, left_s = refs[8 * len(groups) :]
    step = pl.program_id(0)
    for index, (start, count) in enumerate(groups):
        four = lefts[4 * index : 4 * index + 4]
        blocks = rights[4 * index : 4 * index + 4]

        @pl.when(step == start)
        def _(four=four):
            for place, ref in enumerate(four):
                left_s[:, place * TOK : (place + 1) * TOK] = ref[...].astype(f32).T.astype(bf16)

        @pl.when((step >= start) & (step < start + count))
        def _(blocks=blocks):
            right = jnp.concatenate([ref[...] for ref in blocks], axis=0)
            sum_ref[...] = dot_nn(left_s[...], right).astype(bf16)


def weight_grad(picks, tile, groups):
    steps = []
    in_left = []
    in_right = []
    operands_left = []
    operands_right = []
    start = 0
    for left, right in groups:
        count = right[0][0].shape[1] // tile
        steps.append((start, count))
        for array, which, column in left:
            in_left.append(
                pl.BlockSpec(
                    (TOK, SIDE),
                    lambda step, pick, which=which, column=column: (
                        0 if which is None else pick[which],
                        column,
                    ),
                )
            )
            operands_left.append(array)
        for array, which in right:
            in_right.append(
                pl.BlockSpec(
                    (TOK, tile),
                    lambda step, pick, which=which, start=start, count=count: (
                        0 if which is None else pick[which],
                        jnp.clip(step - start, 0, count - 1),
                    ),
                )
            )
            operands_right.append(array)
        start += count
    return pl.pallas_call(
        functools.partial(weight_grad_kernel, tuple(steps)),
        grid_spec=pltpu.PrefetchScalarGridSpec(
            num_scalar_prefetch=1,
            grid=(start,),
            in_specs=in_left + in_right,
            out_specs=pl.BlockSpec((SIDE, tile), lambda step, pick: (0, step)),
            scratch_shapes=[pltpu.VMEM((SIDE, 4 * TOK), bf16)],
        ),
        out_shape=jax.ShapeDtypeStruct((SIDE, start * tile), bf16),
        compiler_params=pltpu.CompilerParams(vmem_limit_bytes=16 * MIB),
        cost_estimate=pl.CostEstimate(
            flops=8 * TOK * SIDE * start * tile,
            bytes_accessed=4 * SIDE * start * tile,
            transcendentals=0,
        ),
        name="weight_grad",
    )(picks, *operands_left, *operands_right)


def row_layout(doc_ids):
    rows = doc_ids.shape[0]
    positions = jnp.arange(TOK, dtype=jnp.int32)
    earlier = jnp.sum((doc_ids[:, None, :] < doc_ids[:, :, None]).astype(jnp.int32), axis=2)
    places = positions[None, :] - earlier
    half_dim = HD // 2
    inverse_freq = rope_base ** (-jnp.arange(half_dim, dtype=f32) / half_dim)
    angles = places.astype(f32)[:, :, None] * inverse_freq[None, None, :]
    repeats = LANES // half_dim
    rope = jnp.concatenate([jnp.cos(angles)] * repeats + [jnp.sin(angles)] * repeats, axis=-1)
    masks = jnp.concatenate(
        [
            jnp.broadcast_to((places >= shift).astype(f32)[:, :, None], (rows, TOK, LANES))
            for shift in (1, 2, 3)
        ],
        axis=-1,
    )
    doc_cols = jnp.broadcast_to(doc_ids[:, :, None], (rows, TOK, LANES))
    doc_rows = jnp.broadcast_to(doc_ids[:, None, :], (rows, 8, TOK))
    return (rope, masks, doc_cols, doc_rows)


def core_params(conv_weight, conv_bias, step_bias, decay_log, skip_scale, mixer_gain):
    taps = jnp.concatenate([conv_weight, conv_bias[None], jnp.zeros((3, CH), f32)], axis=0)
    heads = jnp.zeros((8, LANES), f32)
    heads = heads.at[0, :MH].set(step_bias).at[1, :MH].set(jnp.exp(decay_log))
    wide = jnp.concatenate(
        [jnp.repeat(skip_scale, MP)[None], mixer_gain[None], jnp.zeros((6, E), f32)], axis=0
    )
    return (taps, heads, wide)


def swapped(value):
    return lax.ppermute(value, "core", [(0, 1), (1, 0)])


def ring_order(chips):
    return [2 * step for step in range(chips // 2)] + [
        2 * step + 1 for step in reversed(range(chips // 2))
    ]


def ring_place(chip, chips):
    return jnp.where(chip % 2 == 0, chip // 2, chips - 1 - chip // 2)


def onward(value, steps):
    order = ring_order(lax.axis_size("chip"))
    chips = len(order)
    return lax.ppermute(
        value, "chip", [(order[at], order[(at + steps) % chips]) for at in range(chips)]
    )


def slot_offsets(chips):
    offsets = [0]
    for far in range(1, chips // 2):
        offsets += [-far, far]
    return offsets + [chips // 2]


def tied(*values):
    return lax.optimization_barrier(values)


class RingGather:
    def __init__(self, shard):
        self.slots = [shard]
        self.ahead = self.back = shard
        self.left = lax.axis_size("chip") // 2

    def operands(self):
        half = self.ahead.shape[0] // 2
        if self.left == 1:
            return self.ahead[:half], self.back[half:]
        return self.ahead, self.back

    def send(self, ahead, back):
        self.ahead, self.back = tied(onward(ahead, 1), onward(back, -1))
        self.slots += [self.ahead, self.back]
        self.left -= 1
        return self.ahead

    def step(self):
        return self.send(*self.operands())

    def last(self):
        while self.left > 1:
            self.step()

    def hold(self, value):
        self.ahead, self.back, _ = tied(self.ahead, self.back, value)
        self.slots[-2:] = [self.ahead, self.back]


class RingReduce:
    def __init__(self, sums):
        self.sums = sums
        self.chips = lax.axis_size("chip")
        self.size = sums.shape[0] // self.chips
        self.left = self.chips // 2
        self.ahead = self.back = None

    def slot(self, index, start=0, stop=None):
        stop = self.size if stop is None else stop
        return self.sums[index * self.size + start : index * self.size + stop]

    def operands(self):
        half = self.size // 2
        if self.ahead is None:
            last = self.chips - 1
            return self.slot(last, 0, half), self.slot(last, half)
        ahead, back = self.ahead.astype(f32), self.back.astype(f32)
        if self.left == self.chips // 2 - 1:
            ahead = jnp.pad(ahead, ((0, half), (0, 0)))
            back = jnp.pad(back, ((half, 0), (0, 0)))
        return (
            (self.slot(2 * self.left).astype(f32) + ahead).astype(bf16),
            (self.slot(2 * self.left - 1).astype(f32) + back).astype(bf16),
        )

    def send(self, ahead, back):
        self.ahead, self.back = tied(onward(ahead, 1), onward(back, -1))
        self.left -= 1
        return self.ahead

    def step(self):
        return self.send(*self.operands())

    def hold(self, value):
        self.ahead, self.back, _ = tied(self.ahead, self.back, value)

    def columns(self, start, stop):
        part = RingReduce(self.sums[:, start:stop])
        part.left = self.left
        part.ahead, part.back = self.ahead[:, start:stop], self.back[:, start:stop]
        return part

    def total(self):
        while self.left > 0:
            self.step()
        return self.slot(0).astype(f32) + self.ahead.astype(f32) + self.back.astype(f32)


def small_hops(chips):
    if chips & (chips - 1):
        return [lambda value: lax.psum(value, ("chip", "core")) - value]
    hops = [swapped]
    for bit in range(chips.bit_length() - 1):
        pairs = [(chip, chip ^ (1 << bit)) for chip in range(chips)]
        hops.append(lambda value, pairs=pairs: lax.ppermute(value, "chip", pairs))
    return hops


def ring_columns(core):
    chips = lax.axis_size("chip")
    place = ring_place(lax.axis_index("chip"), chips)
    own = []
    for offset in slot_offsets(chips):
        at = (place + offset) % chips
        own.append(jnp.where(at < chips // 2, 2 * at, 2 * (chips - 1 - at) + 1))
    own = jnp.stack(own)
    width = D // (2 * chips)
    starts = jnp.concatenate([2 * own + core, 2 * own + 1 - core]) * width
    wanted = (starts[:, None] + jnp.arange(width)[None, :]).reshape(D)
    return (jnp.arange(D)[:, None] == wanted[None, :]).astype(bf16)


def per_device(
    inputs, out_grad, doc_ids, row_live, pre_gain, mlp_gain, mixer_gain, conv_weight, conv_bias,
    step_bias, decay_log, skip_scale, mixer_in_weight, mixer_out_weight, query_weight, key_weight,
    value_weight, attend_weight, gate_up_weight, down_weight,
):
    is_first = lax.axis_index("section") == 0
    core = lax.axis_index("core")
    shard = mixer_in_weight.shape[1]
    packed_a = jnp.concatenate(
        [
            mixer_in_weight[0, :, :AT_Q],
            query_weight[0],
            key_weight[0],
            value_weight[0],
            mixer_in_weight[0, :, AT_Q:],
            jnp.zeros((shard, LANES - MH), bf16),
        ],
        axis=1,
    )
    packed_b = jnp.concatenate(
        [mixer_out_weight[0].T, attend_weight[0].T, gate_up_weight[0], down_weight[0].T], axis=1
    )

    layout = row_layout(doc_ids)
    params = core_params(
        conv_weight[0], conv_bias[0], step_bias[0], decay_log[0], skip_scale[0], mixer_gain[0]
    )
    turn = ring_columns(core)

    def own_order(values):
        if values.dtype == bf16:
            return dot_nn(values, turn).astype(bf16)
        return dot_exact(values, turn.astype(f32))

    def whole_order(values):
        if values.dtype == bf16:
            return dot_nt(values, turn).astype(bf16)
        return dot_exact(values, turn.astype(f32).T)

    pre_row = own_order(pre_gain)
    mlp_row = own_order(mlp_gain)
    first_rows = own_order(inputs)

    positions = jnp.arange(TOK, dtype=jnp.int32)
    live = (positions[None, :] < row_live[:, None]).reshape(MB * TOK, 1)
    from_loss = own_order(jnp.where(live, out_grad, jnp.zeros_like(out_grad)))
    first_rows, from_loss = tied(first_rows, from_loss)

    ring_a = RingGather(packed_a)
    ring_b = RingGather(packed_b)
    ring_a.step()
    ring_b.step()
    ring_a.last()
    now_a, now_b = tied(ring_a.operands(), ring_b.operands())
    ring_a.send(*now_a)
    ring_b.send(*now_b)
    own_a = jnp.concatenate(ring_a.slots, axis=0)
    pair_a = (own_a, swapped(own_a))
    now_b, gain_now, pair_a = tied(ring_b.operands(), pre_row, pair_a)
    ring_b.send(*now_b)
    projected = by_row(project(first_rows, gain_now, *pair_a))
    mixed = core_forward(0, projected, layout, params)
    ring_b.hold(mixed)
    now_b, mixed = tied(ring_b.operands(), mixed)
    ring_b.send(*now_b)
    mixed, _, _ = core_forward(1, projected, layout, params, held=mixed)
    ring_b.hold(mixed)
    while ring_b.left:
        ring_b.step()
    pair_b = (
        jnp.concatenate(ring_b.slots, axis=0),
        jnp.concatenate([swapped(slot) for slot in ring_b.slots], axis=0),
    )
    mixed = mixed.reshape(MB * TOK, MIXED)
    received = {}
    for row in (1, 0):
        (handed,) = feed_forward(row, first_rows, mixed, mlp_row, *pair_b)
        received[row] = passed_along(handed, "section", 1)

    def second_pass(row, projects=(), cores=(), forwards=()):
        start = jnp.where(is_first, first_rows[row * TOK : (row + 1) * TOK], received[row])
        projects = project(start, pre_row, *pair_a, row=row, held=projects)
        cores = core_forward(row, by_row(projects), layout, params, held=cores)
        mixed = cores[0].reshape(MB * TOK, MIXED)
        forwards = feed_forward(row, start, mixed, mlp_row, *pair_b, held=forwards)
        return start, projects, cores, forwards

    arrived = jnp.zeros((TOK, D), bf16)
    lefts = []
    rights = []
    rows = []
    picks = jnp.where(is_first, jnp.array([1, 0]), jnp.array([0, 1])).astype(jnp.int32)

    def tick_left(which):
        return [(lefts[1][which], None, 0), (lefts[2][which], None, 0)] + [
            (lefts[1][which + 2], None, 0), (lefts[2][which + 2], None, 0)
        ]

    def tick_right(which):
        return [(rights[tick][which + far], None) for far in (0, 2) for tick in (1, 2)]

    def saved_left(own, their):
        return [(own, 0, 0), (own, 1, 0), (their, 0, 0), (their, 1, 0)]

    def saved_right(own, their):
        return [(own, 0), (own, 1), (their, 0), (their, 1)]

    start, projects, cores, forwards = second_pass(1)
    starts = {1: start}
    start_rows = jnp.concatenate([start, start], axis=0)
    for tick in range(3):
        if tick == 1:
            (projects, cores, forwards), received[0], _ = tied(
                (projects, cores, forwards), received[0], d_low
            )
            starts[0], projects, cores, forwards = second_pass(0, projects, cores, forwards)
            start_rows = jnp.concatenate([starts[0], starts[1]], axis=0)
            arrived, forwards = tied(arrived, forwards)
        normed, projected = projects[0], by_row(projects)
        mixed, pre, yns = cores[0].reshape(MB * TOK, MIXED), cores[1], cores[2]
        result, middle, normed_two, gate, up, act = forwards
        row = jnp.where(is_first, (1, 1, 0)[tick], (1, 0, 1)[tick]).astype(jnp.int32).reshape(1)
        if tick == 2:
            row, lefts[1], rights[1], rows[1] = tied(row, lefts[1], rights[1], rows[1])
            section_out = whole_order(result)
            row, section_out = tied(row, section_out)
        loss_row = (1, 0, 1)[tick]
        cotangent = jnp.where(
            is_first, arrived, from_loss[loss_row * TOK : (loss_row + 1) * TOK]
        )
        if tick == 1:
            cotangent, swaps = tied(
                cotangent, (mixed, act, normed[:, SIDE:], normed_two[:, SIDE:])
            )
            their_mixed, their_act, their_normed, their_normed_two = map(swapped, swaps)
        d_gate, d_up, d_middle, middle_low, d_mixed, mlp_grad = feed_back(
            row, cotangent, gate, up, middle, mlp_row, *pair_b
        )
        lefts.append(
            (cotangent, middle_low, swapped(cotangent[:, SIDE:]), swapped(middle_low[:, SIDE:]))
        )
        rights.append((d_gate, d_up, swapped(d_gate), swapped(d_up)))
        if tick < 2:
            attended = attend_back(row, projected, d_mixed, layout)
            if tick == 1:
                row, their_mixed, their_act, their_normed, their_normed_two = tied(
                    row, their_mixed, their_act, their_normed, their_normed_two
                )
            proj_low, small = mixer_back(
                row, projected, pre, yns, d_mixed, attended, layout, params
            )
            their_low = swapped(proj_low)
        else:
            sum_c = weight_grad(
                picks,
                1024,
                [
                    (tick_left(1), saved_right(mixed, their_mixed)),
                    (tick_left(0), saved_right(act, their_act)),
                ],
            )
            ring_c = RingReduce(sum_c)
            now_c, row = tied(ring_c.operands(), row)
            ring_c.send(*now_c)
            attended = attend_back(row, projected, d_mixed, layout)
            ring_c.hold(attended)
            picks_now, now_c, rights[2] = tied(picks, ring_c.operands(), rights[2])
            ring_c.send(*now_c)
            sum_b = weight_grad(
                picks_now,
                1024,
                [
                    (saved_left(normed_two, their_normed_two), tick_right(0)),
                    (saved_left(normed_two, their_normed_two), tick_right(1)),
                ],
            )
            ring_b = RingReduce(sum_b)
            ring_c.hold(sum_b)
            now_b, now_c, row, attended = tied(
                ring_b.operands(), ring_c.operands(), row, attended
            )
            ring_c.send(*now_c)
            ring_b.send(*now_b)
            proj_low, small = mixer_back(
                row, projected, pre, yns, d_mixed, attended, layout, params
            )
            proj_low, ring_b.ahead, ring_b.back, ring_c.ahead, ring_c.back = tied(
                proj_low, ring_b.ahead, ring_b.back, ring_c.ahead, ring_c.back
            )
            their_low = swapped(proj_low)
            now_b, row = tied(ring_b.operands(), row)
            ring_b.send(*now_b)
            d_rows, d_low, pre_grad = project_back(
                row, proj_low, start_rows, d_middle, pre_row, *pair_a
            )
            now_c, their_low, d_rows, pre_grad = tied(
                ring_c.operands(), their_low, d_rows, pre_grad
            )
            ring_c.send(*now_c)
            small_two = (pre_grad, mlp_grad, small)
            pre_sum, mlp_sum, small_sum = (one + two for one, two in zip(rows[1][2:], small_two))
            gain_sums = whole_order(jnp.concatenate([pre_sum, mlp_sum], axis=0))
            small_sum = jnp.concatenate(
                [small_sum, jnp.pad(gain_sums, ((0, 6), (0, CH - D)))], axis=0
            )
            picks_now, now_c, small_sum = tied(picks, now_c, small_sum)
            (p_one, their_one), (p_two, their_two) = rows[1][1], (proj_low, their_low)
            sum_a = weight_grad(
                picks_now,
                WIDE_A // 3,
                [
                    (
                        saved_left(normed, their_normed),
                        [(p_one, None), (p_two, None), (their_one, None), (their_two, None)],
                    )
                ],
            )
            ring_b.hold(sum_a)
            ring_a = RingReduce(sum_a)
            ring_c.hold(sum_a)
            now_a, now_b, ring_c.ahead, ring_c.back = tied(
                ring_a.operands(), ring_b.operands(), ring_c.ahead, ring_c.back
            )
            ring_b.send(*now_b)
            ring_a.send(*now_a)
        if tick < 2:
            d_rows, d_low, pre_grad = project_back(
                row, proj_low, start_rows, d_middle, pre_row, *pair_a
            )
        rows.append((d_rows, (proj_low, their_low), pre_grad, mlp_grad, small))
        if tick < 2:
            arrived = passed_along(d_low, "section", -1)

    hops = small_hops(lax.axis_size("chip"))

    def hop_beside(small, ring):
        if not hops:
            return small
        small, moved, _ = tied(small, hops.pop(0)(small), ring.ahead)
        return small + moved

    small = hop_beside(small_sum, ring_a)
    ring_b.step()
    ring_a.step()
    ring_c.hold(ring_a.ahead)
    small = hop_beside(small, ring_a)
    while ring_a.left > 2:
        ring_a.step()
    d_last = tied(rows[2][0], ring_a.ahead)[0]
    rings_a = [ring_a.columns(0, CUT_A), ring_a.columns(CUT_A, WIDE_A)]
    while rings_a[0].left:
        for ring in rings_a:
            ring.step()
        small = hop_beside(small, rings_a[0])
    for hop in hops:
        small = small + hop(small)
    share_c = ring_c.total()
    share_b = ring_b.total()
    share_a = jnp.concatenate([ring.total() for ring in rings_a], axis=1)

    start_grad = jnp.concatenate(
        [
            jnp.where(is_first, d_last, rows[1][0]),
            jnp.where(is_first, rows[1][0], d_last),
        ],
        axis=0,
    )
    skip_sum = jnp.sum(small[6, :E].reshape(MH, MP), axis=1)
    mixer_in_grad = jnp.concatenate([share_a[:, :AT_Q], share_a[:, AT_DT : AT_DT + MH]], axis=1)
    return (
        section_out[None],
        whole_order(start_grad)[None],
        small[8:9, :D],
        small[9:10, :D],
        small[5:6, :E],
        small[None, :4],
        small[4:5],
        small[7:8, :MH],
        small[7:8, LANES : LANES + MH],
        skip_sum[None],
        mixer_in_grad[None],
        share_c[:, :E].T[None],
        share_a[:, AT_Q:AT_K][None],
        share_a[:, AT_K:AT_V][None],
        share_a[:, AT_V:AT_DT][None],
        share_c[:, E:MIXED].T[None],
        share_b[None],
        share_c[:, MIXED:].T[None],
    )


def solution(mesh):
    dp = mesh.shape["dp"]
    devices = mesh.devices.reshape(mesh.shape["section"], dp // 2, 2)
    paired = Mesh(devices, ("section", "chip", "core"))
    over = ("chip", "core")
    rows = P(over, None)
    small = P("section", None)
    by_row = P("section", over, None)
    by_col = P("section", None, over)
    small_specs = (small, small, small, P("section", None, None), small, small, small, small)
    big_specs = (by_row, by_col, by_row, by_row, by_row, by_col, by_row, by_col)
    in_specs = (rows, rows, rows, P(over)) + small_specs + big_specs
    out_specs = (by_row, by_row) + small_specs + big_specs
    return jax.shard_map(
        per_device, mesh=paired, in_specs=in_specs, out_specs=out_specs, check_vma=False
    )
```

```python
import functools
import math

import jax
import jax.numpy as jnp
from jax import lax
from jax.experimental import pallas as pl
from jax.experimental.pallas import tpu as pltpu
from jax.sharding import Mesh
from jax.sharding import PartitionSpec as P

D = 1024
FF = 2048
MH = 24
MP = 64
NS = 128
AH = 8
KVH = 2
HD = 64
MB = 2
TOK = 256
E = 1536
CH = 1792
HALF = TOK // 2
PAIRS = MH // 2
LANES = 128
SIDE = D // 2
MIB = 2**20
FF_VMEM = 22
FB_VMEM = 20

AT_W = E
AT_Q = E + CH
AT_K = AT_Q + AH * HD
AT_V = AT_K + KVH * HD
AT_DT = AT_V + KVH * HD
WIDE_A = AT_DT + LANES
CUT_A = 16 * LANES
MIXED = E + AH * HD
AT_GU = MIXED
AT_DN = AT_GU + 2 * FF
WIDE_B = AT_DN + FF

highest = lax.Precision.HIGHEST
epsilon = 1e-05
rope_base = 100000000000.0
bf16 = jnp.bfloat16
f32 = jnp.float32


def dot_nn(left, right):
    return lax.dot_general(left, right, (((1,), (0,)), ((), ())), preferred_element_type=f32)


def dot_nt(left, right):
    return lax.dot_general(left, right, (((1,), (1,)), ((), ())), preferred_element_type=f32)


def dot_tn(left, right):
    return lax.dot_general(left, right, (((0,), (0,)), ((), ())), preferred_element_type=f32)


def dot_exact(left, right):
    return lax.dot_general(
        left, right, (((1,), (0,)), ((), ())), precision=highest, preferred_element_type=f32
    )


def softplus(value):
    return jnp.maximum(value, 0.0) + jnp.log1p(jnp.exp(-jnp.abs(value)))


def lane_low(rows):
    return lax.broadcasted_iota(jnp.int32, (rows, LANES), 1) < HD


def rope_halves(rows):
    return (lax.broadcasted_iota(jnp.int32, (rows, LANES), 1) & (HD - 1)) < HD // 2


def rope_turn(tile, cosine, sine):
    swapped = jnp.where(
        rope_halves(tile.shape[0]),
        -pltpu.roll(tile, LANES - HD // 2, 1),
        pltpu.roll(tile, HD // 2, 1),
    )
    return tile * cosine + swapped * sine


def rope_back(tile, cosine, sine):
    swapped = jnp.where(
        rope_halves(tile.shape[0]),
        pltpu.roll(tile, LANES - HD // 2, 1),
        -pltpu.roll(tile, HD // 2, 1),
    )
    return tile * cosine + swapped * sine


def both_halves(tile):
    swapped = pltpu.roll(tile, HD, 1)
    low = lane_low(tile.shape[0])
    return (jnp.where(low, tile, swapped), jnp.where(low, swapped, tile))


def tile_at(index):
    return pl.ds(pl.multiple_of(index * LANES, LANES), LANES)


def tile_from(start, index):
    return pl.ds(pl.multiple_of(start + index * LANES, LANES), LANES)


def allowed_pairs(doc_col_ref, doc_row_ref):
    later = lax.broadcasted_iota(jnp.int32, (TOK, TOK), 0)
    early = lax.broadcasted_iota(jnp.int32, (TOK, TOK), 1)
    same = doc_col_ref[:, 0:1] == doc_row_ref[0:1, :]
    return (later >= early) & same


def pair_rows(tile):
    low = lane_low(tile.shape[0])
    zero = jnp.zeros_like(tile)
    return jnp.concatenate([jnp.where(low, tile, zero), jnp.where(low, zero, tile)], axis=0)


def pair_lanes(rows):
    half = rows.shape[0] // 2
    return jnp.where(lane_low(half), rows[:half], rows[half:])


def core_forward_kernel(
    held, pm_ref, pq_ref, pd_ref, rope_ref, mask_ref, doc_col_ref, doc_row_ref,
    taps_ref, head_ref, wide_ref, *refs,
):
    xb_ref, pre_ref, yns_ref, conv_s, cb_s, bias_s, sum_s = refs[3:] if held else refs

    def conv_tile(index, carry):
        rows = pm_ref[:, tile_from(AT_W, index)].astype(f32)
        at = tile_at(index)
        total = taps_ref[4:5, at] + taps_ref[3:4, at] * rows
        for shift in (1, 2, 3):
            moved = mask_ref[:, (shift - 1) * LANES : shift * LANES] * pltpu.roll(rows, shift, 0)
            total = total + taps_ref[3 - shift : 4 - shift, at] * moved
        total = total.astype(bf16)
        pre_ref[:, at] = total
        total = total.astype(f32)
        conv_s[:, at] = total * jax.nn.sigmoid(total)
        return carry

    lax.fori_loop(0, CH // LANES, conv_tile, 0)

    allowed = allowed_pairs(doc_col_ref, doc_row_ref)
    bias_s[...] = jnp.where(allowed, 0.0, -1e30)
    steps = softplus(pd_ref[...] + head_ref[0:1, :])
    rates = -steps * head_ref[1:2, :]
    totals = dot_exact(jnp.where(allowed, 1.0, 0.0), rates)
    totals_t = totals.T
    inward = conv_s[:, E : E + NS].astype(bf16)
    outward = conv_s[:, E + NS :].astype(bf16)
    cb_s[...] = jnp.where(allowed, dot_nt(outward, inward), 0.0)
    low = lane_low(TOK)
    for pair in range(PAIRS):
        lanes = slice(pair * LANES, (pair + 1) * LANES)
        first = 2 * pair
        step_pair = jnp.where(low, steps[:, first : first + 1], steps[:, first + 1 : first + 2])
        scaled = (conv_s[:, lanes] * step_pair).astype(bf16)
        mixes = []
        for head in (first, first + 1):
            apart = totals[:, head : head + 1] - totals_t[head : head + 1, :]
            mixes.append((jnp.exp(jnp.minimum(apart, 0.0)) * cb_s[...]).astype(bf16))
        yns_ref[:, lanes] = pair_lanes(dot_nn(jnp.concatenate(mixes, axis=0), scaled))

    sum_s[...] = jnp.zeros((TOK, LANES), f32)

    def gate_tile(index, carry):
        at = tile_at(index)
        gate = pm_ref[:, at].astype(f32)
        rows = yns_ref[:, at] + wide_ref[0:1, at] * conv_s[:, at]
        gated = rows * (gate * jax.nn.sigmoid(gate))
        sum_s[...] += gated * gated
        conv_s[:, at] = gated
        return carry

    lax.fori_loop(0, E // LANES, gate_tile, 0)
    scale = lax.rsqrt(jnp.sum(sum_s[...], axis=1, keepdims=True) * (1.0 / E) + epsilon)

    def norm_tile(index, carry):
        at = tile_at(index)
        xb_ref[:, at] = (conv_s[:, at] * scale * wide_ref[1:2, at]).astype(bf16)
        return carry

    lax.fori_loop(0, E // LANES, norm_tile, 0)

    cosine = rope_ref[:, :LANES]
    sine = rope_ref[:, LANES:]
    keys = both_halves(rope_turn(pq_ref[:, AH * HD : AH * HD + LANES].astype(f32), cosine, sine))
    values = both_halves(pq_ref[:, AH * HD + LANES :].astype(f32))
    keys = tuple(part.astype(bf16) for part in keys)
    values = tuple(part.astype(bf16) for part in values)
    for pair in range(AH // 2):
        group = pair // (AH // (2 * KVH))
        at = pair * LANES
        turned = rope_turn(pq_ref[:, at : at + LANES].astype(f32), cosine, sine)
        scores = dot_nt(pair_rows((turned * (1.0 / math.sqrt(HD))).astype(bf16)), keys[group])
        weights = []
        shares = []
        for part in (scores[:TOK], scores[TOK:]):
            part = part + bias_s[...]
            part = jnp.exp(part - jnp.max(part, axis=1, keepdims=True))
            shares.append(1.0 / jnp.sum(part, axis=1, keepdims=True))
            weights.append(part.astype(bf16))
        out = pair_lanes(dot_nn(jnp.concatenate(weights, axis=0), values[group]))
        out = out * jnp.where(low, shares[0], shares[1])
        xb_ref[:, E + pair * LANES : E + (pair + 1) * LANES] = out.astype(bf16)


def silu_slope(value, gate):
    return gate * (1.0 + value * (1.0 - gate))


def attend_back_kernel(
    pick_ref, pq_ref, dxb_ref, rope_ref, doc_col_ref, doc_row_ref, pg_ref, bias_s
):
    later = lax.broadcasted_iota(jnp.int32, (TOK, TOK), 1)
    early = lax.broadcasted_iota(jnp.int32, (TOK, TOK), 0)
    allowed_t = (later >= early) & (doc_col_ref[:, 0:1] == doc_row_ref[0:1, :])
    bias_s[...] = jnp.where(allowed_t, 0.0, -1e30)
    low = lane_low(TOK)
    cosine = rope_ref[:, :LANES]
    sine = rope_ref[:, LANES:]
    keys = both_halves(rope_turn(pq_ref[:, AH * HD : AH * HD + LANES].astype(f32), cosine, sine))
    values = both_halves(pq_ref[:, AH * HD + LANES :].astype(f32))
    root = 1.0 / math.sqrt(HD)
    d_keys = []
    d_values = []
    for group in range(KVH):
        key = keys[group].astype(bf16)
        key_rows = pair_rows(key)
        value_rows = pair_rows(values[group].astype(bf16))
        d_key = jnp.zeros((TOK, LANES), f32)
        d_value = jnp.zeros((TOK, LANES), f32)
        for pair in range(group * (AH // (2 * KVH)), (group + 1) * (AH // (2 * KVH))):
            at = pair * LANES
            turned = rope_turn(pq_ref[:, at : at + LANES].astype(f32), cosine, sine) * root
            query = turned.astype(bf16)
            d_out = dxb_ref[:, E + at : E + at + LANES].astype(bf16)
            scores = dot_nt(key_rows, query)
            d_weights = dot_nt(value_rows, d_out)
            weights = []
            d_scores = []
            for part in (slice(0, TOK), slice(TOK, 2 * TOK)):
                score = scores[part] + bias_s[...]
                weight = jnp.exp(score - jnp.max(score, axis=0, keepdims=True))
                weight = weight * (1.0 / jnp.sum(weight, axis=0, keepdims=True))
                d_weight = d_weights[part]
                offset = jnp.sum(weight * d_weight, axis=0, keepdims=True)
                weights.append(weight.astype(bf16))
                d_scores.append((weight * (d_weight - offset)).astype(bf16))
            d_value = d_value + pair_lanes(dot_nn(jnp.concatenate(weights, axis=0), d_out))
            d_key = d_key + pair_lanes(dot_nn(jnp.concatenate(d_scores, axis=0), query))
            d_query = pair_lanes(dot_tn(jnp.concatenate(d_scores, axis=1), key))
            pg_ref[:, at : at + LANES] = rope_back(d_query * root, cosine, sine).astype(bf16)
        d_keys.append(d_key + pltpu.roll(d_key, HD, 1))
        d_values.append(d_value + pltpu.roll(d_value, HD, 1))
    d_key = rope_back(jnp.where(low, d_keys[0], d_keys[1]), cosine, sine)
    pg_ref[:, AH * HD : AH * HD + LANES] = d_key.astype(bf16)
    pg_ref[:, AH * HD + LANES :] = jnp.where(low, d_values[0], d_values[1]).astype(bf16)


def mixer_back_kernel(
    pick_ref, pm_ref, pd_ref, pre_ref, yns_ref, dxb_ref, attend_ref, mask_ref, doc_col_ref,
    doc_row_ref, taps_ref, head_ref, wide_ref,
    pg_ref, small_ref,
    x_s, dx_s, dyb_s, cbt_s, dcbt_s, sum_s, ssum_s,
):
    small_ref[...] = jnp.zeros_like(small_ref)
    pg_ref[:, AT_Q:AT_DT] = attend_ref[...]
    sum_s[...] = jnp.zeros((TOK, LANES), f32)
    ssum_s[...] = jnp.zeros((TOK, LANES), f32)

    def start_tile(index, carry):
        at = tile_at(index)
        pre = pre_ref[:, at].astype(f32)
        heads_in = pre * jax.nn.sigmoid(pre)
        x_s[:, at] = heads_in
        gate = pm_ref[:, at].astype(f32)
        rows = yns_ref[:, at] + wide_ref[0:1, at] * heads_in
        gated = rows * (gate * jax.nn.sigmoid(gate))
        sum_s[...] += gated * gated
        ssum_s[...] += dxb_ref[:, at] * wide_ref[1:2, at] * gated
        return carry

    lax.fori_loop(0, E // LANES, start_tile, 0)
    scale = lax.rsqrt(jnp.sum(sum_s[...], axis=1, keepdims=True) * (1.0 / E) + epsilon)
    pull = jnp.sum(ssum_s[...], axis=1, keepdims=True) * (1.0 / E) * scale * scale * scale

    def gate_tile(index, carry):
        at = tile_at(index)
        heads_in = x_s[:, at]
        skip = wide_ref[0:1, at]
        gate = pm_ref[:, at].astype(f32)
        opened = jax.nn.sigmoid(gate)
        rows = yns_ref[:, at] + skip * heads_in
        gated = rows * (gate * opened)
        arrived = dxb_ref[:, at]
        d_gated = scale * (arrived * wide_ref[1:2, at]) - gated * pull
        small_ref[5:6, at] = jnp.sum(arrived * gated * scale, axis=0, keepdims=True)
        d_rows = d_gated * (gate * opened)
        pg_ref[:, at] = (d_gated * rows * silu_slope(gate, opened)).astype(bf16)
        small_ref[6:7, at] = jnp.sum(d_rows * heads_in, axis=0, keepdims=True)
        dyb_s[:, at] = d_rows.astype(bf16)
        dx_s[:, at] = skip * d_rows
        return carry

    lax.fori_loop(0, E // LANES, gate_tile, 0)

    def state_tile(index, carry):
        at = tile_from(E, index)
        pre = pre_ref[:, at].astype(f32)
        x_s[:, at] = pre * jax.nn.sigmoid(pre)
        return carry

    lax.fori_loop(0, 2, state_tile, 0)

    later = lax.broadcasted_iota(jnp.int32, (TOK, TOK), 1)
    early = lax.broadcasted_iota(jnp.int32, (TOK, TOK), 0)
    allowed_t = (later >= early) & (doc_col_ref[:, 0:1] == doc_row_ref[0:1, :])
    allowed = allowed_pairs(doc_col_ref, doc_row_ref)
    raw = pd_ref[...] + head_ref[0:1, :]
    steps = softplus(raw)
    decay = head_ref[1:2, :]
    rates = -steps * decay
    totals = dot_exact(jnp.where(allowed, 1.0, 0.0), rates)
    totals_t = totals.T
    inward = x_s[:, E : E + NS].astype(bf16)
    outward = x_s[:, E + NS :].astype(bf16)
    cbt_s[...] = jnp.where(allowed_t, dot_nt(inward, outward), 0.0)
    dcbt_s[...] = jnp.zeros((TOK, TOK), f32)
    low = lane_low(TOK)
    spread_row = lax.broadcasted_iota(jnp.int32, (2 * LANES, LANES), 0) // HD
    spread_col = lax.broadcasted_iota(jnp.int32, (2 * LANES, LANES), 1)
    sum_s[...] = jnp.zeros((TOK, LANES), f32)
    ssum_s[...] = jnp.zeros((TOK, LANES), f32)
    waiting = None
    for pair in range(PAIRS):
        lanes = slice(pair * LANES, (pair + 1) * LANES)
        first = 2 * pair
        step_pair = jnp.where(low, steps[:, first : first + 1], steps[:, first + 1 : first + 2])
        heads_in = x_s[:, lanes]
        scaled = (heads_in * step_pair).astype(bf16)
        d_rows = dyb_s[:, lanes]
        d_mix = dot_nt(pair_rows(scaled), d_rows)
        mixes = []
        d_pairs = None
        for side, head in enumerate((first, first + 1)):
            apart = totals_t[head : head + 1, :] - totals[:, head : head + 1]
            decays = jnp.exp(jnp.minimum(apart, 0.0))
            mixes.append((decays * cbt_s[...]).astype(bf16))
            part = d_mix[side * TOK : (side + 1) * TOK] * decays
            d_pairs = part if d_pairs is None else d_pairs + part
        dcbt_s[...] += d_pairs
        d_scaled = pair_lanes(dot_nn(jnp.concatenate(mixes, axis=0), d_rows))
        dx_s[:, lanes] += d_scaled * step_pair
        value = d_rows.astype(f32) * yns_ref[:, lanes] - scaled.astype(f32) * d_scaled
        coarse = value.astype(bf16)
        fine = (value - coarse.astype(f32)).astype(bf16)
        spread = (spread_col == first + (spread_row & 1)).astype(bf16)
        ssum_s[...] += dot_nn(jnp.concatenate([coarse, fine], axis=1), spread)
        value = (d_scaled * heads_in).astype(bf16)
        if pair % 2 == 0:
            waiting = value
        else:
            spread = (spread_col == first - 2 + spread_row).astype(bf16)
            sum_s[...] += dot_nn(jnp.concatenate([waiting, value], axis=1), spread)

    d_rates = dot_exact(jnp.where(allowed_t, 1.0, 0.0), ssum_s[...])
    d_steps = sum_s[...] - decay * d_rates
    d_raw = d_steps * jax.nn.sigmoid(raw)
    pg_ref[:, AT_DT:] = d_raw.astype(bf16)
    small_ref[7:8, :LANES] = jnp.sum(d_raw, axis=0, keepdims=True)
    small_ref[7:8, LANES : 2 * LANES] = jnp.sum(d_rates * rates, axis=0, keepdims=True)
    d_pairs = jnp.where(allowed_t, dcbt_s[...], 0.0).astype(bf16)
    dx_s[:, E : E + NS] = dot_nn(d_pairs, outward)
    dx_s[:, E + NS :] = dot_tn(d_pairs, inward)

    def conv_tile(index, carry):
        at = tile_at(index)
        pre = pre_ref[:, at].astype(f32)
        d_pre = dx_s[:, at] * silu_slope(pre, jax.nn.sigmoid(pre))
        rows = pm_ref[:, tile_from(AT_W, index)].astype(f32)
        small_ref[4:5, at] = jnp.sum(d_pre, axis=0, keepdims=True)
        small_ref[3:4, at] = jnp.sum(d_pre * rows, axis=0, keepdims=True)
        back = taps_ref[3:4, at] * d_pre
        for shift in (1, 2, 3):
            held = mask_ref[:, (shift - 1) * LANES : shift * LANES] * d_pre
            small_ref[3 - shift : 4 - shift, at] = jnp.sum(
                held * pltpu.roll(rows, shift, 0), axis=0, keepdims=True
            )
            back = back + taps_ref[3 - shift : 4 - shift, at] * pltpu.roll(held, TOK - shift, 0)
        pg_ref[:, tile_from(AT_W, index)] = back.astype(bf16)
        return carry

    lax.fori_loop(0, CH // LANES, conv_tile, 0)


def whole_block(shape):
    return pl.BlockSpec(shape, lambda *steps: (0,) * len(shape))


def once(shape, place):
    return pl.BlockSpec(shape, place, pipeline_mode=pl.Buffered(1))


def core_forward(row, projected, layout, params, held=()):
    operands = (*projected, *layout)

    def block(array):
        return once((None,) + array.shape[1:], lambda step: (row, 0, 0))

    outs = [
        jax.ShapeDtypeStruct((MB, TOK, MIXED), bf16),
        jax.ShapeDtypeStruct((MB, TOK, CH), bf16),
        jax.ShapeDtypeStruct((MB, TOK, E), f32),
    ]
    return pl.pallas_call(
        functools.partial(core_forward_kernel, bool(held)),
        grid=(1,),
        in_specs=[block(array) for array in operands]
        + [once(array.shape, lambda step: (0, 0)) for array in params]
        + [pl.BlockSpec(memory_space=pl.ANY)] * len(held),
        out_specs=[block(array) for array in outs],
        out_shape=outs,
        scratch_shapes=[
            pltpu.VMEM((TOK, CH), f32),
            pltpu.VMEM((TOK, TOK), f32),
            pltpu.VMEM((TOK, TOK), f32),
            pltpu.VMEM((TOK, LANES), f32),
        ],
        input_output_aliases={10: 0, 11: 1, 12: 2} if held else {},
        compiler_params=pltpu.CompilerParams(vmem_limit_bytes=12 * MIB),
        cost_estimate=pl.CostEstimate(
            flops=4 * 10**8, bytes_accessed=12 * 2**20, transcendentals=10**6
        ),
        name="core_forward",
    )(*operands, *params, *held)


def core_back_specs(by_row, plain):
    return [
        once((None,) + array.shape[1:], lambda step, pick: (pick[0], 0, 0)) if chosen
        else once(array.shape, lambda step, pick: (0, 0))
        for chosen, arrays in ((True, by_row), (False, plain))
        for array in arrays
    ]


def attend_back(row, projected, d_mixed, layout):
    rope, masks, doc_cols, doc_rows = layout
    return pl.pallas_call(
        attend_back_kernel,
        grid_spec=pltpu.PrefetchScalarGridSpec(
            num_scalar_prefetch=1,
            grid=(1,),
            in_specs=core_back_specs([projected[1]], [d_mixed])
            + core_back_specs([rope, doc_cols, doc_rows], []),
            out_specs=once((TOK, AT_DT - AT_Q), lambda step, pick: (0, 0)),
            scratch_shapes=[pltpu.VMEM((TOK, TOK), f32)],
        ),
        out_shape=jax.ShapeDtypeStruct((TOK, AT_DT - AT_Q), bf16),
        compiler_params=pltpu.CompilerParams(vmem_limit_bytes=6 * MIB),
        cost_estimate=pl.CostEstimate(
            flops=3 * 10**8, bytes_accessed=4 * 2**20, transcendentals=6 * 10**5
        ),
        name="attend_back",
    )(row, projected[1], d_mixed, rope, doc_cols, doc_rows)


def mixer_back(row, projected, pre, yns, d_mixed, attended, layout, params):
    rope, masks, doc_cols, doc_rows = layout
    return pl.pallas_call(
        mixer_back_kernel,
        grid_spec=pltpu.PrefetchScalarGridSpec(
            num_scalar_prefetch=1,
            grid=(1,),
            in_specs=core_back_specs(
                [projected[0], projected[2], pre, yns], [d_mixed, attended]
            )
            + core_back_specs([masks, doc_cols, doc_rows], params),
            out_specs=[
                once((TOK, WIDE_A), lambda step, pick: (0, 0)),
                once((8, CH), lambda step, pick: (0, 0)),
            ],
            scratch_shapes=[
                pltpu.VMEM((TOK, CH), f32),
                pltpu.VMEM((TOK, CH), f32),
                pltpu.VMEM((TOK, E), bf16),
                pltpu.VMEM((TOK, TOK), f32),
                pltpu.VMEM((TOK, TOK), f32),
                pltpu.VMEM((TOK, LANES), f32),
                pltpu.VMEM((TOK, LANES), f32),
            ],
        ),
        out_shape=[
            jax.ShapeDtypeStruct((TOK, WIDE_A), bf16),
            jax.ShapeDtypeStruct((8, CH), f32),
        ],
        compiler_params=pltpu.CompilerParams(vmem_limit_bytes=15 * MIB),
        cost_estimate=pl.CostEstimate(
            flops=7 * 10**8, bytes_accessed=10 * 2**20, transcendentals=15 * 10**5
        ),
        name="mixer_back",
    )(
        row, projected[0], projected[2], pre, yns, d_mixed, attended, masks, doc_cols, doc_rows,
        *params,
    )


def passed_along(value, axis, steps):
    count = lax.axis_size(axis)
    leading, last = (max(0, -steps), min(count, count - steps))
    return lax.ppermute(value, axis, [(source, source + steps) for source in range(leading, last)])


def norm_rows(values):
    return lax.rsqrt(jnp.mean(values * values, axis=-1, keepdims=True) + epsilon)


def norm_back(values, gain, arrived):
    scale = norm_rows(values)
    weighted = arrived * gain
    pull = jnp.mean(weighted * values, axis=-1, keepdims=True) * scale * scale * scale
    gain_grad = jnp.sum(arrived * values * scale, axis=0, keepdims=True)
    return (weighted * scale - values * pull, gain_grad)


def project_kernel(rows_ref, gain_ref, own_ref, other_ref, *refs):
    normed_ref, pm_ref, pq_ref, pd_ref = refs[-4:]
    step = pl.program_id(0)

    @pl.when(step == 0)
    def _():
        rows = rows_ref[...].astype(f32)
        normed_ref[...] = (rows * norm_rows(rows) * gain_ref[...]).astype(bf16)

    out = dot_nn(normed_ref[:, :SIDE], own_ref[...]) + dot_nn(normed_ref[:, SIDE:], other_ref[...])
    tile = WIDE_A // 3
    for index in range(2):
        @pl.when(step == index)
        def _(index=index):
            pm_ref[:, index * tile : (index + 1) * tile] = out.astype(bf16)

    @pl.when(step == 2)
    def _():
        pm_ref[:, 2 * tile :] = out[:, : AT_Q - 2 * tile].astype(bf16)
        pq_ref[...] = out[:, AT_Q - 2 * tile : AT_DT - 2 * tile].astype(bf16)
        pd_ref[...] = out[:, AT_DT - 2 * tile :]


def project(rows, gain, own, other, row=None, held=()):
    count = rows.shape[0]
    tile = WIDE_A // 3
    weight = pl.BlockSpec((SIDE, tile), lambda step: (0, step))
    at = row or 0
    total = count if row is None else MB * TOK
    widths = ((D, bf16), (AT_Q, bf16), (AT_DT - AT_Q, bf16), (LANES, f32))
    return pl.pallas_call(
        project_kernel,
        grid=(3,),
        in_specs=[whole_block((count, D)), whole_block((1, D)), weight, weight]
        + [pl.BlockSpec(memory_space=pl.ANY)] * len(held),
        out_specs=[pl.BlockSpec((count, width), lambda step: (at, 0)) for width, _ in widths],
        out_shape=[jax.ShapeDtypeStruct((total, width), kind) for width, kind in widths],
        input_output_aliases={4 + index: index for index in range(len(held))},
        compiler_params=pltpu.CompilerParams(vmem_limit_bytes=15 * MIB),
        cost_estimate=pl.CostEstimate(
            flops=2 * count * D * WIDE_A,
            bytes_accessed=2 * D * WIDE_A + 2 * count * WIDE_A,
            transcendentals=0,
        ),
        name="project",
    )(rows, gain, own, other, *held)


def by_row(projected):
    return tuple(array.reshape(MB, TOK, -1) for array in projected[1:])


def feed_forward_kernel(
    keep, rows_ref, mixed_ref, gain_ref,
    out_own, out_other, gate_own, gate_other, up_own, up_other, down_own, down_other,
    *refs,
):
    if keep:
        low_ref, middle_ref, normed_ref, gate_ref, up_ref, act_ref, total_s = refs[-7:]
    else:
        low_ref, middle_ref, normed_ref, total_s = refs
    step = pl.program_id(0)

    @pl.when(step == 0)
    def _():
        middle_ref[...] = rows_ref[...].astype(f32)

    @pl.when(step < 4)
    def _():
        mixed = mixed_ref[...]
        middle_ref[:, :SIDE] += dot_nt(mixed, out_own[...])
        middle_ref[:, SIDE:] += dot_nt(mixed, out_other[...])

    @pl.when(step == 3)
    def _():
        middle = middle_ref[...]
        normed_ref[...] = (middle * norm_rows(middle) * gain_ref[...]).astype(bf16)
        total_s[...] = middle

    @pl.when(step >= 4)
    def _():
        left = normed_ref[:, :SIDE]
        right = normed_ref[:, SIDE:]
        gate = dot_nn(left, gate_own[...]) + dot_nn(right, gate_other[...])
        up = dot_nn(left, up_own[...]) + dot_nn(right, up_other[...])
        act = (gate * jax.nn.sigmoid(gate) * up).astype(bf16)
        if keep:
            gate_ref[...] = gate.astype(bf16)
            up_ref[...] = up.astype(bf16)
            act_ref[...] = act
        total_s[:, :SIDE] += dot_nt(act, down_own[...])
        total_s[:, SIDE:] += dot_nt(act, down_other[...])

    @pl.when(step == 7)
    def _():
        low_ref[...] = total_s[...].astype(bf16)


def pinned(own, other, kept=True):
    return [
        pltpu.with_memory_space_constraint(own, pltpu.VMEM if kept else pltpu.HBM),
        pltpu.with_memory_space_constraint(other, pltpu.HBM),
    ]


def b_block(start, skipped):
    return pl.BlockSpec(
        (SIDE, 512), lambda step, *pick: (0, start + jnp.clip(step - skipped, 0, 3))
    )


def b_blocks(parts):
    return [b_block(start, skipped) for start, skipped in parts for _ in range(2)]


def feed_forward(row, rows, mixed, gain, own, other, held=None):
    keep = held is not None
    at = row if rows.shape[0] > TOK else 0

    def late(step):
        return (row, jnp.clip(step - 4, 0, 3))

    wide = pl.BlockSpec((TOK, 512), late)
    full = pl.BlockSpec((TOK, D), lambda step: (row, 0))
    scratch = [pltpu.VMEM((TOK, D), f32)]
    if keep:
        out_specs = [full, full, full, wide, wide, wide]
        out_shape = [
            pltpu.HBM((MB * TOK, width), kind)
            for width, kind in ((D, bf16), (D, f32), (D, bf16), (FF, bf16), (FF, bf16), (FF, bf16))
        ]
    else:
        out_specs = [whole_block((TOK, D))]
        out_shape = [jax.ShapeDtypeStruct((TOK, D), bf16)]
        scratch = [pltpu.VMEM((TOK, D), f32), pltpu.VMEM((TOK, D), bf16)] + scratch
    held = tuple(pltpu.with_memory_space_constraint(one, pltpu.HBM) for one in held or ())
    return pl.pallas_call(
        functools.partial(feed_forward_kernel, keep),
        grid=(8,),
        in_specs=[
            pl.BlockSpec((TOK, D), lambda step: (at, 0)),
            pl.BlockSpec((TOK, 512), lambda step: (row, jnp.clip(step, 0, 3))),
            whole_block((1, D)),
        ]
        + b_blocks(((0, 0), (4, 4), (8, 4), (12, 4)))
        + [pl.BlockSpec(memory_space=pl.ANY)] * len(held),
        out_specs=out_specs,
        out_shape=out_shape,
        scratch_shapes=scratch,
        input_output_aliases={11 + index: index for index in range(len(held))},
        compiler_params=pltpu.CompilerParams(vmem_limit_bytes=(FF_VMEM if keep else 18) * MIB),
        cost_estimate=pl.CostEstimate(
            flops=2 * TOK * D * WIDE_B, bytes_accessed=2 * D * WIDE_B, transcendentals=0
        ),
        name="feed_forward",
    )(rows, mixed, gain, *((pinned(own, other) if keep else [own, other]) * 4), *held)


def feed_back_kernel(
    pick_ref, cot_ref, gate_ref, up_ref, middle_ref, gain_ref,
    down_own, down_other, gate_own, gate_other, up_own, up_other, out_own, out_other,
    d_gate_ref, d_up_ref, d_middle_ref, low_ref, d_mixed_ref, gain_grad_ref,
    total_s,
):
    step = pl.program_id(0)

    @pl.when(step == 0)
    def _():
        total_s[...] = jnp.zeros_like(total_s)

    @pl.when(step < 4)
    def _():
        arrived = dot_nn(cot_ref[:, :SIDE], down_own[...]) + dot_nn(
            cot_ref[:, SIDE:], down_other[...]
        )
        gate = gate_ref[...].astype(f32)
        opened = jax.nn.sigmoid(gate)
        d_gate = (arrived * up_ref[...].astype(f32) * silu_slope(gate, opened)).astype(bf16)
        d_up = (arrived * (gate * opened)).astype(bf16)
        d_gate_ref[...] = d_gate
        d_up_ref[...] = d_up
        total_s[:, :SIDE] += dot_nt(d_gate, gate_own[...]) + dot_nt(d_up, up_own[...])
        total_s[:, SIDE:] += dot_nt(d_gate, gate_other[...]) + dot_nt(d_up, up_other[...])

    @pl.when(step == 3)
    def _():
        d_norm, gain_grad = norm_back(middle_ref[...], gain_ref[...], total_s[...])
        d_middle = cot_ref[...].astype(f32) + d_norm
        d_middle_ref[...] = d_middle
        low_ref[...] = d_middle.astype(bf16)
        gain_grad_ref[...] = gain_grad

    @pl.when(step >= 4)
    def _():
        d_mixed_ref[...] = dot_nn(low_ref[:, :SIDE], out_own[...]) + dot_nn(
            low_ref[:, SIDE:], out_other[...]
        )


def feed_back(row, cotangent, gate, up, middle, gain, own, other, kept):
    saved = pl.BlockSpec((TOK, 512), lambda step, pick: (pick[0], jnp.clip(step, 0, 3)))
    early = pl.BlockSpec((TOK, 512), lambda step, pick: (0, jnp.clip(step, 0, 3)))
    late = pl.BlockSpec((TOK, 512), lambda step, pick: (0, jnp.clip(step - 4, 0, 3)))
    full = pl.BlockSpec((TOK, D), lambda step, pick: (0, 0))
    gain_block = pl.BlockSpec((1, D), lambda step, pick: (0, 0))
    return pl.pallas_call(
        feed_back_kernel,
        grid_spec=pltpu.PrefetchScalarGridSpec(
            num_scalar_prefetch=1,
            grid=(8,),
            in_specs=[
                full,
                saved,
                saved,
                pl.BlockSpec((TOK, D), lambda step, pick: (pick[0], 0)),
                gain_block,
            ]
            + b_blocks(((12, 0), (4, 0), (8, 0), (0, 4))),
            out_specs=[early, early, full, full, late, gain_block],
            scratch_shapes=[pltpu.VMEM((TOK, D), f32)],
        ),
        out_shape=[
            jax.ShapeDtypeStruct((TOK, FF), bf16),
            jax.ShapeDtypeStruct((TOK, FF), bf16),
            jax.ShapeDtypeStruct((TOK, D), f32),
            jax.ShapeDtypeStruct((TOK, D), bf16),
            jax.ShapeDtypeStruct((TOK, MIXED), f32),
            jax.ShapeDtypeStruct((1, D), f32),
        ],
        compiler_params=pltpu.CompilerParams(vmem_limit_bytes=FB_VMEM * MIB),
        cost_estimate=pl.CostEstimate(
            flops=2 * TOK * D * WIDE_B, bytes_accessed=2 * D * WIDE_B, transcendentals=0
        ),
        name="feed_back",
    )(
        row, cotangent, *(pltpu.with_memory_space_constraint(one, pltpu.HBM) for one in (gate, up)),
        pltpu.with_memory_space_constraint(middle, pltpu.HBM), gain,
        *(pinned(own, other, kept) * 4),
    )


def project_back_kernel(
    pick_ref, grad_ref, rows_ref, d_middle_ref, gain_ref, own_ref, other_ref,
    d_rows_ref, low_ref, gain_grad_ref, total_s,
):
    step = pl.program_id(0)

    @pl.when(step == 0)
    def _():
        total_s[...] = jnp.zeros_like(total_s)

    total_s[:, :SIDE] += dot_nt(grad_ref[...], own_ref[...])
    total_s[:, SIDE:] += dot_nt(grad_ref[...], other_ref[...])

    @pl.when(step == 2)
    def _():
        d_norm, gain_grad = norm_back(rows_ref[...].astype(f32), gain_ref[...], total_s[...])
        d_rows = d_middle_ref[...] + d_norm
        d_rows_ref[...] = d_rows
        low_ref[...] = d_rows.astype(bf16)
        gain_grad_ref[...] = gain_grad


def project_back(row, proj_low, start_rows, d_middle, gain, own, other):
    tile = WIDE_A // 3
    weight = pl.BlockSpec((SIDE, tile), lambda step, pick: (0, step))
    full = pl.BlockSpec((TOK, D), lambda step, pick: (0, 0))
    gain_block = pl.BlockSpec((1, D), lambda step, pick: (0, 0))
    return pl.pallas_call(
        project_back_kernel,
        grid_spec=pltpu.PrefetchScalarGridSpec(
            num_scalar_prefetch=1,
            grid=(3,),
            in_specs=[
                pl.BlockSpec((TOK, tile), lambda step, pick: (0, step)),
                pl.BlockSpec((TOK, D), lambda step, pick: (pick[0], 0)),
                full,
                gain_block,
                weight,
                weight,
            ],
            out_specs=[full, full, gain_block],
            scratch_shapes=[pltpu.VMEM((TOK, D), f32)],
        ),
        out_shape=[
            jax.ShapeDtypeStruct((TOK, D), f32),
            jax.ShapeDtypeStruct((TOK, D), bf16),
            jax.ShapeDtypeStruct((1, D), f32),
        ],
        compiler_params=pltpu.CompilerParams(vmem_limit_bytes=15 * MIB),
        cost_estimate=pl.CostEstimate(
            flops=2 * TOK * D * WIDE_A, bytes_accessed=2 * D * WIDE_A, transcendentals=0
        ),
        name="project_back",
    )(row, proj_low, start_rows, d_middle, gain, own, other)


def weight_grad_kernel(groups, pick_ref, *refs):
    lefts = refs[: 4 * len(groups)]
    rights = refs[4 * len(groups) : 8 * len(groups)]
    sum_ref, left_s = refs[8 * len(groups) :]
    step = pl.program_id(0)
    for index, (start, count) in enumerate(groups):
        four = lefts[4 * index : 4 * index + 4]
        blocks = rights[4 * index : 4 * index + 4]

        @pl.when(step == start)
        def _(four=four):
            for place, ref in enumerate(four):
                left_s[:, place * TOK : (place + 1) * TOK] = ref[...].astype(f32).T.astype(bf16)

        @pl.when((step >= start) & (step < start + count))
        def _(blocks=blocks):
            right = jnp.concatenate([ref[...] for ref in blocks], axis=0)
            sum_ref[...] = dot_nn(left_s[...], right).astype(bf16)


def weight_grad(picks, tile, groups):
    steps = []
    in_left = []
    in_right = []
    operands_left = []
    operands_right = []
    start = 0
    for left, right in groups:
        count = right[0][0].shape[1] // tile
        steps.append((start, count))
        for array, which, column in left:
            in_left.append(
                pl.BlockSpec(
                    (TOK, SIDE),
                    lambda step, pick, which=which, column=column: (
                        0 if which is None else pick[which],
                        column,
                    ),
                )
            )
            operands_left.append(array)
        for array, which in right:
            in_right.append(
                pl.BlockSpec(
                    (TOK, tile),
                    lambda step, pick, which=which, start=start, count=count: (
                        0 if which is None else pick[which],
                        jnp.clip(step - start, 0, count - 1),
                    ),
                )
            )
            operands_right.append(array)
        start += count
    return pl.pallas_call(
        functools.partial(weight_grad_kernel, tuple(steps)),
        grid_spec=pltpu.PrefetchScalarGridSpec(
            num_scalar_prefetch=1,
            grid=(start,),
            in_specs=in_left + in_right,
            out_specs=pl.BlockSpec((SIDE, tile), lambda step, pick: (0, step)),
            scratch_shapes=[pltpu.VMEM((SIDE, 4 * TOK), bf16)],
        ),
        out_shape=jax.ShapeDtypeStruct((SIDE, start * tile), bf16),
        compiler_params=pltpu.CompilerParams(vmem_limit_bytes=16 * MIB),
        cost_estimate=pl.CostEstimate(
            flops=8 * TOK * SIDE * start * tile,
            bytes_accessed=4 * SIDE * start * tile,
            transcendentals=0,
        ),
        name="weight_grad",
    )(picks, *operands_left, *operands_right)


def row_layout(doc_ids):
    rows = doc_ids.shape[0]
    positions = jnp.arange(TOK, dtype=jnp.int32)
    earlier = jnp.sum((doc_ids[:, None, :] < doc_ids[:, :, None]).astype(jnp.int32), axis=2)
    places = positions[None, :] - earlier
    half_dim = HD // 2
    inverse_freq = rope_base ** (-jnp.arange(half_dim, dtype=f32) / half_dim)
    angles = places.astype(f32)[:, :, None] * inverse_freq[None, None, :]
    repeats = LANES // half_dim
    rope = jnp.concatenate([jnp.cos(angles)] * repeats + [jnp.sin(angles)] * repeats, axis=-1)
    masks = jnp.concatenate(
        [
            jnp.broadcast_to((places >= shift).astype(f32)[:, :, None], (rows, TOK, LANES))
            for shift in (1, 2, 3)
        ],
        axis=-1,
    )
    doc_cols = jnp.broadcast_to(doc_ids[:, :, None], (rows, TOK, LANES))
    doc_rows = jnp.broadcast_to(doc_ids[:, None, :], (rows, 8, TOK))
    return (rope, masks, doc_cols, doc_rows)


def core_params(conv_weight, conv_bias, step_bias, decay_log, skip_scale, mixer_gain):
    taps = jnp.concatenate([conv_weight, conv_bias[None], jnp.zeros((3, CH), f32)], axis=0)
    heads = jnp.zeros((8, LANES), f32)
    heads = heads.at[0, :MH].set(step_bias).at[1, :MH].set(jnp.exp(decay_log))
    wide = jnp.concatenate(
        [jnp.repeat(skip_scale, MP)[None], mixer_gain[None], jnp.zeros((6, E), f32)], axis=0
    )
    return (taps, heads, wide)


def swapped(value):
    return lax.ppermute(value, "core", [(0, 1), (1, 0)])


def ring_order(chips):
    return [2 * step for step in range(chips // 2)] + [
        2 * step + 1 for step in reversed(range(chips // 2))
    ]


def ring_place(chip, chips):
    return jnp.where(chip % 2 == 0, chip // 2, chips - 1 - chip // 2)


def onward(value, steps):
    order = ring_order(lax.axis_size("chip"))
    chips = len(order)
    return lax.ppermute(
        value, "chip", [(order[at], order[(at + steps) % chips]) for at in range(chips)]
    )


def slot_offsets(chips):
    offsets = [0]
    for far in range(1, chips // 2):
        offsets += [-far, far]
    return offsets + [chips // 2]


def tied(*values):
    return lax.optimization_barrier(values)


class RingGather:
    def __init__(self, shard):
        self.slots = [shard]
        self.ahead = self.back = shard
        self.left = lax.axis_size("chip") // 2

    def operands(self):
        half = self.ahead.shape[0] // 2
        if self.left == 1:
            return self.ahead[:half], self.back[half:]
        return self.ahead, self.back

    def send(self, ahead, back):
        self.ahead, self.back = tied(onward(ahead, 1), onward(back, -1))
        self.slots += [self.ahead, self.back]
        self.left -= 1
        return self.ahead

    def step(self):
        return self.send(*self.operands())

    def last(self):
        while self.left > 1:
            self.step()

    def hold(self, value):
        self.ahead, self.back, _ = tied(self.ahead, self.back, value)
        self.slots[-2:] = [self.ahead, self.back]


class RingReduce:
    def __init__(self, sums):
        self.sums = sums
        self.chips = lax.axis_size("chip")
        self.size = sums.shape[0] // self.chips
        self.left = self.chips // 2
        self.ahead = self.back = None

    def slot(self, index, start=0, stop=None):
        stop = self.size if stop is None else stop
        return self.sums[index * self.size + start : index * self.size + stop]

    def operands(self):
        half = self.size // 2
        if self.ahead is None:
            last = self.chips - 1
            return self.slot(last, 0, half), self.slot(last, half)
        ahead, back = self.ahead.astype(f32), self.back.astype(f32)
        if self.left == self.chips // 2 - 1:
            ahead = jnp.pad(ahead, ((0, half), (0, 0)))
            back = jnp.pad(back, ((half, 0), (0, 0)))
        return (
            (self.slot(2 * self.left).astype(f32) + ahead).astype(bf16),
            (self.slot(2 * self.left - 1).astype(f32) + back).astype(bf16),
        )

    def send(self, ahead, back):
        self.ahead, self.back = tied(onward(ahead, 1), onward(back, -1))
        self.left -= 1
        return self.ahead

    def step(self):
        return self.send(*self.operands())

    def hold(self, value):
        self.ahead, self.back, _ = tied(self.ahead, self.back, value)

    def columns(self, start, stop):
        part = RingReduce(self.sums[:, start:stop])
        part.left = self.left
        part.ahead, part.back = self.ahead[:, start:stop], self.back[:, start:stop]
        return part

    def total(self):
        while self.left > 0:
            self.step()
        return self.slot(0).astype(f32) + self.ahead.astype(f32) + self.back.astype(f32)


def small_hops(chips):
    if chips & (chips - 1):
        return [lambda value: lax.psum(value, ("chip", "core")) - value]
    hops = [swapped]
    for bit in range(chips.bit_length() - 1):
        pairs = [(chip, chip ^ (1 << bit)) for chip in range(chips)]
        hops.append(lambda value, pairs=pairs: lax.ppermute(value, "chip", pairs))
    return hops


def ring_columns(core):
    chips = lax.axis_size("chip")
    place = ring_place(lax.axis_index("chip"), chips)
    own = []
    for offset in slot_offsets(chips):
        at = (place + offset) % chips
        own.append(jnp.where(at < chips // 2, 2 * at, 2 * (chips - 1 - at) + 1))
    own = jnp.stack(own)
    width = D // (2 * chips)
    starts = jnp.concatenate([2 * own + core, 2 * own + 1 - core]) * width
    wanted = (starts[:, None] + jnp.arange(width)[None, :]).reshape(D)
    return (jnp.arange(D)[:, None] == wanted[None, :]).astype(bf16)


def per_device(
    inputs, out_grad, doc_ids, row_live, pre_gain, mlp_gain, mixer_gain, conv_weight, conv_bias,
    step_bias, decay_log, skip_scale, mixer_in_weight, mixer_out_weight, query_weight, key_weight,
    value_weight, attend_weight, gate_up_weight, down_weight,
):
    is_first = lax.axis_index("section") == 0
    core = lax.axis_index("core")
    shard = mixer_in_weight.shape[1]
    packed_a = jnp.concatenate(
        [
            mixer_in_weight[0, :, :AT_Q],
            query_weight[0],
            key_weight[0],
            value_weight[0],
            mixer_in_weight[0, :, AT_Q:],
            jnp.zeros((shard, LANES - MH), bf16),
        ],
        axis=1,
    )
    packed_b = jnp.concatenate(
        [mixer_out_weight[0].T, attend_weight[0].T, gate_up_weight[0], down_weight[0].T], axis=1
    )

    layout = row_layout(doc_ids)
    params = core_params(
        conv_weight[0], conv_bias[0], step_bias[0], decay_log[0], skip_scale[0], mixer_gain[0]
    )
    turn = ring_columns(core)

    def own_order(values):
        if values.dtype == bf16:
            return dot_nn(values, turn).astype(bf16)
        return dot_exact(values, turn.astype(f32))

    def whole_order(values):
        if values.dtype == bf16:
            return dot_nt(values, turn).astype(bf16)
        high = values.astype(bf16)
        return dot_nt(high, turn) + dot_nt((values - high.astype(f32)).astype(bf16), turn)

    pre_row = own_order(pre_gain)
    mlp_row = own_order(mlp_gain)
    first_rows = own_order(inputs)

    positions = jnp.arange(TOK, dtype=jnp.int32)
    live = (positions[None, :] < row_live[:, None]).reshape(MB * TOK, 1)
    from_loss = own_order(jnp.where(live, out_grad, jnp.zeros_like(out_grad)))
    first_rows, from_loss = tied(first_rows, from_loss)

    ring_a = RingGather(packed_a)
    ring_b = RingGather(packed_b)
    ring_a.step()
    ring_b.step()
    ring_a.last()
    now_a, now_b = tied(ring_a.operands(), ring_b.operands())
    ring_a.send(*now_a)
    ring_b.send(*now_b)
    own_a = jnp.concatenate(ring_a.slots, axis=0)
    pair_a = (own_a, swapped(own_a))
    now_b, gain_now, pair_a = tied(ring_b.operands(), pre_row, pair_a)
    ring_b.send(*now_b)
    projected = by_row(project(first_rows, gain_now, *pair_a))
    mixed = core_forward(0, projected, layout, params)
    ring_b.hold(mixed)
    now_b, mixed = tied(ring_b.operands(), mixed)
    ring_b.send(*now_b)
    mixed, _, _ = core_forward(1, projected, layout, params, held=mixed)
    ring_b.hold(mixed)
    while ring_b.left:
        ring_b.step()
    pair_b = (
        jnp.concatenate(ring_b.slots, axis=0),
        jnp.concatenate([swapped(slot) for slot in ring_b.slots], axis=0),
    )
    mixed = mixed.reshape(MB * TOK, MIXED)
    received = {}
    for row in (1, 0):
        (handed,) = feed_forward(row, first_rows, mixed, mlp_row, *pair_b)
        received[row] = passed_along(handed, "section", 1)

    def second_pass(row, projects=(), cores=(), forwards=()):
        start = jnp.where(is_first, first_rows[row * TOK : (row + 1) * TOK], received[row])
        projects = project(start, pre_row, *pair_a, row=row, held=projects)
        cores = core_forward(row, by_row(projects), layout, params, held=cores)
        mixed = cores[0].reshape(MB * TOK, MIXED)
        forwards = feed_forward(row, start, mixed, mlp_row, *pair_b, held=forwards)
        return start, projects, cores, forwards

    arrived = jnp.zeros((TOK, D), bf16)
    lefts = []
    rights = []
    rows = []
    picks = jnp.where(is_first, jnp.array([1, 0]), jnp.array([0, 1])).astype(jnp.int32)

    def tick_left(which):
        return [(lefts[1][which], None, 0), (lefts[2][which], None, 0)] + [
            (lefts[1][which + 2], None, 0), (lefts[2][which + 2], None, 0)
        ]

    def tick_right(which):
        return [(rights[tick][which + far], None) for far in (0, 2) for tick in (1, 2)]

    def saved_left(own, their):
        return [(own, 0, 0), (own, 1, 0), (their, 0, 0), (their, 1, 0)]

    def saved_right(own, their):
        return [(own, 0), (own, 1), (their, 0), (their, 1)]

    start, projects, cores, forwards = second_pass(1)
    starts = {1: start}
    start_rows = jnp.concatenate([start, start], axis=0)
    for tick in range(3):
        if tick == 1:
            (projects, cores, forwards), received[0], _ = tied(
                (projects, cores, forwards), received[0], d_low
            )
            starts[0], projects, cores, forwards = second_pass(0, projects, cores, forwards)
            start_rows = jnp.concatenate([starts[0], starts[1]], axis=0)
            arrived, forwards = tied(arrived, forwards)
        normed, projected = projects[0], by_row(projects)
        mixed, pre, yns = cores[0].reshape(MB * TOK, MIXED), cores[1], cores[2]
        result, middle, normed_two, gate, up, act = forwards
        row = jnp.where(is_first, (1, 1, 0)[tick], (1, 0, 1)[tick]).astype(jnp.int32).reshape(1)
        if tick == 2:
            row, lefts[1], rights[1], rows[1] = tied(row, lefts[1], rights[1], rows[1])
            section_out = whole_order(result)
            d_early = whole_order(rows[1][0])
            row, section_out = tied(row, section_out)
        loss_row = (1, 0, 1)[tick]
        cotangent = jnp.where(
            is_first, arrived, from_loss[loss_row * TOK : (loss_row + 1) * TOK]
        )
        if tick == 1:
            cotangent, swaps = tied(
                cotangent, (mixed, act, normed[:, SIDE:], normed_two[:, SIDE:])
            )
            their_mixed, their_act, their_normed, their_normed_two = map(swapped, swaps)
        d_gate, d_up, d_middle, middle_low, d_mixed, mlp_grad = feed_back(
            row, cotangent, gate, up, middle, mlp_row, *pair_b, kept=tick == 0
        )
        lefts.append(
            (cotangent, middle_low, swapped(cotangent[:, SIDE:]), swapped(middle_low[:, SIDE:]))
        )
        rights.append((d_gate, d_up, swapped(d_gate), swapped(d_up)))
        if tick < 2:
            attended = attend_back(row, projected, d_mixed, layout)
            if tick == 1:
                row, their_mixed, their_act, their_normed, their_normed_two = tied(
                    row, their_mixed, their_act, their_normed, their_normed_two
                )
            proj_low, small = mixer_back(
                row, projected, pre, yns, d_mixed, attended, layout, params
            )
            their_low = swapped(proj_low)
        else:
            sum_c = weight_grad(
                picks,
                1024,
                [
                    (tick_left(1), saved_right(mixed, their_mixed)),
                    (tick_left(0), saved_right(act, their_act)),
                ],
            )
            ring_c = RingReduce(sum_c)
            now_c, row = tied(ring_c.operands(), row)
            ring_c.send(*now_c)
            attended = attend_back(row, projected, d_mixed, layout)
            ring_c.hold(attended)
            picks_now, now_c, rights[2] = tied(picks, ring_c.operands(), rights[2])
            ring_c.send(*now_c)
            sum_b = weight_grad(
                picks_now,
                1024,
                [
                    (saved_left(normed_two, their_normed_two), tick_right(0)),
                    (saved_left(normed_two, their_normed_two), tick_right(1)),
                ],
            )
            ring_b = RingReduce(sum_b)
            ring_c.hold(sum_b)
            now_b, now_c, row, attended = tied(
                ring_b.operands(), ring_c.operands(), row, attended
            )
            ring_c.send(*now_c)
            ring_b.send(*now_b)
            proj_low, small = mixer_back(
                row, projected, pre, yns, d_mixed, attended, layout, params
            )
            proj_low, ring_b.ahead, ring_b.back, ring_c.ahead, ring_c.back = tied(
                proj_low, ring_b.ahead, ring_b.back, ring_c.ahead, ring_c.back
            )
            their_low = swapped(proj_low)
            now_b, row = tied(ring_b.operands(), row)
            ring_b.send(*now_b)
            d_rows, d_low, pre_grad = project_back(
                row, proj_low, start_rows, d_middle, pre_row, *pair_a
            )
            small_two = (pre_grad, mlp_grad, small)
            pre_sum, mlp_sum, small_sum = (one + two for one, two in zip(rows[1][2:], small_two))
            gain_sums = whole_order(jnp.concatenate([pre_sum, mlp_sum], axis=0))
            small_sum = jnp.concatenate(
                [small_sum, jnp.pad(gain_sums, ((0, 6), (0, CH - D)))], axis=0
            )
            now_c, their_low, d_rows, small_sum = tied(
                ring_c.operands(), their_low, d_rows, small_sum
            )
            ring_c.send(*now_c)
            picks_now, now_c = tied(picks, now_c)
            (p_one, their_one), (p_two, their_two) = rows[1][1], (proj_low, their_low)
            sum_a = weight_grad(
                picks_now,
                WIDE_A // 3,
                [
                    (
                        saved_left(normed, their_normed),
                        [(p_one, None), (p_two, None), (their_one, None), (their_two, None)],
                    )
                ],
            )
            ring_b.hold(sum_a)
            ring_a = RingReduce(sum_a)
            ring_c.hold(sum_a)
            now_a, now_b, ring_c.ahead, ring_c.back = tied(
                ring_a.operands(), ring_b.operands(), ring_c.ahead, ring_c.back
            )
            ring_b.send(*now_b)
            ring_a.send(*now_a)
        if tick < 2:
            d_rows, d_low, pre_grad = project_back(
                row, proj_low, start_rows, d_middle, pre_row, *pair_a
            )
        rows.append((d_rows, (proj_low, their_low), pre_grad, mlp_grad, small))
        if tick < 2:
            arrived = passed_along(d_low, "section", -1)

    hops = small_hops(lax.axis_size("chip"))

    def hop_beside(small, ring):
        if not hops:
            return small
        small, moved, _ = tied(small, hops.pop(0)(small), ring.ahead)
        return small + moved

    small = hop_beside(small_sum, ring_a)
    ring_b.step()
    ring_a.step()
    ring_c.hold(ring_a.ahead)
    small = hop_beside(small, ring_a)
    while ring_a.left > 2:
        ring_a.step()
    d_last = whole_order(tied(rows[2][0], ring_a.ahead)[0])
    rings_a = [ring_a.columns(0, CUT_A), ring_a.columns(CUT_A, WIDE_A)]
    while rings_a[0].left:
        for ring in rings_a:
            ring.step()
        small = hop_beside(small, rings_a[0])
    for hop in hops:
        small = small + hop(small)
    share_c = ring_c.total()
    share_b = ring_b.total()
    share_a = jnp.concatenate([ring.total() for ring in rings_a], axis=1)

    start_grad = jnp.concatenate(
        [
            jnp.where(is_first, d_last, d_early),
            jnp.where(is_first, d_early, d_last),
        ],
        axis=0,
    )
    skip_sum = jnp.sum(small[6, :E].reshape(MH, MP), axis=1)
    mixer_in_grad = jnp.concatenate([share_a[:, :AT_Q], share_a[:, AT_DT : AT_DT + MH]], axis=1)
    return (
        section_out[None],
        start_grad[None],
        small[8:9, :D],
        small[9:10, :D],
        small[5:6, :E],
        small[None, :4],
        small[4:5],
        small[7:8, :MH],
        small[7:8, LANES : LANES + MH],
        skip_sum[None],
        mixer_in_grad[None],
        share_c[:, :E].T[None],
        share_a[:, AT_Q:AT_K][None],
        share_a[:, AT_K:AT_V][None],
        share_a[:, AT_V:AT_DT][None],
        share_c[:, E:MIXED].T[None],
        share_b[None],
        share_c[:, MIXED:].T[None],
    )


def solution(mesh):
    dp = mesh.shape["dp"]
    devices = mesh.devices.reshape(mesh.shape["section"], dp // 2, 2)
    paired = Mesh(devices, ("section", "chip", "core"))
    over = ("chip", "core")
    rows = P(over, None)
    small = P("section", None)
    by_row = P("section", over, None)
    by_col = P("section", None, over)
    small_specs = (small, small, small, P("section", None, None), small, small, small, small)
    big_specs = (by_row, by_col, by_row, by_row, by_row, by_col, by_row, by_col)
    in_specs = (rows, rows, rows, P(over)) + small_specs + big_specs
    out_specs = (by_row, by_row) + small_specs + big_specs
    return jax.shard_map(
        per_device, mesh=paired, in_specs=in_specs, out_specs=out_specs, check_vma=False
    )
```
